32 devices in a mesh: ctx: 8 (over y, x, core), fsdp: 4 (over z).
Axes of the slice: x: 2, y: 2, z: 4, core: 2. Of those that a mesh axis runs over, the one named last changes fastest.
Arguments:
- tokens: bfloat16 [8, 2048, 1536], P('fsdp', 'ctx'), may hold values from -16 to 16
- block_pairs: int32 [8, 2], replicated, may hold values from 0 to 15, as said below
- cotangent: bfloat16 [8, 2048, 1536], P('fsdp', 'ctx'), may hold values from -6 to 6
- attention_gain: bfloat16 [1536], P('fsdp'), may hold values from 0.099609375 to 1.8984375
- query_weight: bfloat16 [1536, 1536], P('fsdp'), may hold values from -0.15625 to 0.15625
- key_matrix: bfloat16 [1536, 768], P('fsdp'), may hold values from -0.15625 to 0.15625
- value_matrix: bfloat16 [1536, 768], P('fsdp'), may hold values from -0.15625 to 0.15625
- output_weight: bfloat16 [1536, 1536], P('fsdp'), may hold values from -4 to 4
- feedforward_gain: bfloat16 [1536], P('fsdp'), may hold values from 0.099609375 to 1.8984375
- gate_weight: bfloat16 [1536, 4096], P('fsdp'), may hold values from -0.15625 to 0.15625
- up_weight: bfloat16 [1536, 4096], P('fsdp'), may hold values from -0.15625 to 0.15625
- down_weight: bfloat16 [4096, 1536], P('fsdp'), may hold values from -0.09375 to 0.09375
Outputs:
- layer_out: bfloat16 [8, 2048, 1536], P('fsdp', 'ctx')
- tokens_grad: bfloat16 [8, 2048, 1536], P('fsdp', 'ctx')
- attention_gain_grad: float32 [1536], P('fsdp')
- query_grad: float32 [1536, 1536], P('fsdp')
- key_grad: float32 [1536, 768], P('fsdp')
- value_grad: float32 [1536, 768], P('fsdp')
- output_grad: float32 [1536, 1536], P('fsdp')
- feedforward_gain_grad: float32 [1536], P('fsdp')
- gate_grad: float32 [1536, 4096], P('fsdp')
- up_grad: float32 [1536, 4096], P('fsdp')
- down_grad: float32 [4096, 1536], P('fsdp')
The draws below stay inside these ranges and needn't reach their ends.
Inputs may be any that keep to these rules, and one draw needn't show every extreme that they name: `block_pairs`: row c names block b and block 15 - b for some b below 8, in either order; every block is named once.
All inputs are finite; a program needn't handle non-finite values.
Results may differ from the reference program's by a relative error of at most 0.023.
Values may be sent and summed in bfloat16 or wider, within the bound.
A program may use at most 448 MiB of HBM per device.

```python
import math
import jax
import jax.numpy as jnp
from jax import lax

MODEL_WIDTH = 1536
QUERY_HEADS = 16
KEY_HEADS = 8
HEAD_WIDTH = 96
FF = 4096
BLK = 128
BLOCKS = 16
TOKEN_COUNT = 2048
SEQS = 8


def draw_tokens(key, part):
    key = jax.random.fold_in(key, 11)
    first, second, third = jax.random.split(key, 3)
    row_scale = jnp.exp(jax.random.uniform(first, (SEQS, TOKEN_COUNT, 1), minval=jnp.log(0.3), maxval=jnp.log(3.0)))
    column_scale = jnp.exp(jax.random.uniform(second, (1, 1, MODEL_WIDTH), minval=jnp.log(0.3), maxval=jnp.log(3.0)))
    value_rows = jax.random.normal(third, (SEQS, TOKEN_COUNT, MODEL_WIDTH)) * row_scale * column_scale
    return jnp.clip(value_rows, -16.0, 16.0).astype(jnp.float32).astype(jnp.bfloat16)


def draw_block_pairs(key, part):
    key = jax.random.fold_in(key, 5)
    first, second = jax.random.split(key)
    early = jax.random.permutation(first, BLOCKS // 2).astype(jnp.int32)
    late = (BLOCKS - 1 - early).astype(jnp.int32)
    flipped = jax.random.randint(second, (BLOCKS // 2,), 0, 2)
    leading = jnp.where(flipped == 1, late, early)
    trailing = jnp.where(flipped == 1, early, late)
    return jnp.stack([leading, trailing], axis=1).astype(jnp.int32)


def level_of(rng, dims, cuts, low, largest):
    level = 1.0
    for position, shards_of in cuts:
        draws = jax.random.uniform(jax.random.fold_in(jax.random.fold_in(rng, 6), position), (shards_of,), jnp.float32, low / len(cuts), largest / len(cuts))
        level = level * jnp.repeat(jnp.exp(draws), dims[position] // shards_of).reshape((-1,) + (1,) * (len(dims) - 1 - position))
    return level


def normal_values(own_key, dims, spread, limit, cuts=(), kind=jnp.bfloat16):
    values = jax.random.normal(own_key, dims, jnp.float32) * spread
    if len(cuts) > 0:
        values = level_of(own_key, dims, cuts, -0.22, 0.18) * values
    return jnp.clip(values, min=-limit, max=limit).astype(kind)


def setup_inputs(seed: int = 0) -> dict:
    keys = jax.random.split(jax.random.key(seed), 13)
    return {
        "tokens": draw_tokens(jax.random.fold_in(keys[12], 71), 0),
        "block_pairs": draw_block_pairs(jax.random.fold_in(keys[12], 71), 0),
        "cotangent": normal_values(keys[2], (SEQS, TOKEN_COUNT, MODEL_WIDTH), 1.0, 6.0, ((0, 4), (1, 8))),
        "attention_gain": jnp.clip(1.0 + 0.18 * jax.random.normal(keys[3], (MODEL_WIDTH,), jnp.float32), 0.099609375, 1.8984375).astype(jnp.bfloat16),
        "query_weight": normal_values(keys[4], (MODEL_WIDTH, QUERY_HEADS * HEAD_WIDTH), MODEL_WIDTH ** -0.5, 0.15625, ((0, 4),)),
        "key_matrix": normal_values(keys[5], (MODEL_WIDTH, KEY_HEADS * HEAD_WIDTH), MODEL_WIDTH ** -0.5, 0.15625, ((0, 4),)),
        "value_matrix": normal_values(keys[6], (MODEL_WIDTH, KEY_HEADS * HEAD_WIDTH), MODEL_WIDTH ** -0.5, 0.15625, ((0, 4),)),
        "output_weight": normal_values(keys[7], (QUERY_HEADS * HEAD_WIDTH, MODEL_WIDTH), 2 ** -0.5, 4.0, ((0, 4),)),
        "feedforward_gain": jnp.clip(1.0 + 0.18 * jax.random.normal(keys[8], (MODEL_WIDTH,), jnp.float32), 0.099609375, 1.8984375).astype(jnp.bfloat16),
        "gate_weight": normal_values(keys[9], (MODEL_WIDTH, FF), MODEL_WIDTH ** -0.5, 0.15625, ((0, 4),)),
        "up_weight": normal_values(keys[10], (MODEL_WIDTH, FF), MODEL_WIDTH ** -0.5, 0.15625, ((0, 4),)),
        "down_weight": normal_values(keys[11], (FF, MODEL_WIDTH), FF ** -0.5, 0.09375, ((0, 4),)),
    }


EPS = 1e-05
THETA = 100000.0

@jax.custom_vjp
def reduced_forward(v):
    return lax.optimization_barrier(v.astype(jnp.bfloat16)).astype(jnp.float32)

@jax.custom_vjp
def reduced_backward(v):
    return v

def low_keep(v):
    return (reduced_forward(v), None)

def low_pass(kept, grad):
    return (grad,)

def back_keep(v):
    return (v, None)

def back_low(kept, grad):
    return (reduced_forward(grad),)
reduced_forward.defvjp(low_keep, low_pass)
reduced_backward.defvjp(back_keep, back_low)

def rope_tables(positions):
    half_size = HEAD_WIDTH // 2
    frequency = THETA ** (-jnp.arange(half_size, dtype=jnp.float32) * 2.0 / HEAD_WIDTH)
    angles = positions.astype(jnp.float32)[:, None] * frequency[None, :]
    cosine_lookup = jnp.cos(angles)
    sine_lookup = jnp.sin(angles)
    return (jnp.concatenate([cosine_lookup, cosine_lookup], -1), jnp.concatenate([sine_lookup, sine_lookup], -1))

def rotary_apply(value_rows, cosine_lookup, sine_lookup):
    half_size = value_rows.shape[-1] // 2
    turned = jnp.concatenate([-value_rows[..., half_size:], value_rows[..., :half_size]], -1)
    return value_rows * cosine_lookup + turned * sine_lookup

def matrix_product(left, right):
    return jnp.dot(left, right, precision=lax.Precision.HIGHEST, preferred_element_type=jnp.float32)

def rms_norm(value_rows, gain):
    return value_rows * lax.rsqrt(lax.optimization_barrier(jnp.mean(value_rows * value_rows, -1, keepdims=True)) + EPS) * gain

def attend(query_rows, key_rows, value_rows, positions):
    query_tile_block = math.gcd(TOKEN_COUNT, 512)
    block_number = TOKEN_COUNT // query_tile_block
    launch_lattice = query_rows.reshape(block_number, query_tile_block, KEY_HEADS, QUERY_HEADS // KEY_HEADS, HEAD_WIDTH)
    query_positions = positions.reshape(block_number, query_tile_block)

    def one_block(pieces):
        block_queries, block_positions = pieces
        scores = jnp.einsum('igrd,jgd->grij', block_queries, key_rows, precision=lax.Precision.HIGHEST) * HEAD_WIDTH ** (-0.5)
        scores = reduced_backward(scores)
        allowed = block_positions[:, None] >= positions[None, :]
        scores = jnp.where(allowed[None, None], scores, -jnp.inf)
        weights = jax.nn.softmax(scores, axis=-1)
        mixed = jnp.einsum('grij,jgd->igrd', reduced_forward(weights), value_rows, precision=lax.Precision.HIGHEST)
        return mixed.reshape(query_tile_block, QUERY_HEADS * HEAD_WIDTH)
    return lax.map(jax.checkpoint(one_block), (launch_lattice, query_positions)).reshape(TOKEN_COUNT, QUERY_HEADS * HEAD_WIDTH)

def layer(residual_in, positions, gain_first, query_weight, key_matrix, value_matrix, output_weight, gain_second, gate_weight, up_weight, down_weight):
    cosine_lookup, sine_lookup = rope_tables(positions)
    cosine_lookup = cosine_lookup[:, None, :]
    sine_lookup = sine_lookup[:, None, :]
    first_normalized = reduced_forward(rms_norm(residual_in, gain_first))
    query_rows = reduced_forward(rotary_apply(reduced_backward(matrix_product(first_normalized, query_weight)).reshape(TOKEN_COUNT, QUERY_HEADS, HEAD_WIDTH), cosine_lookup, sine_lookup))
    key_rows = reduced_forward(rotary_apply(reduced_backward(matrix_product(first_normalized, key_matrix)).reshape(TOKEN_COUNT, KEY_HEADS, HEAD_WIDTH), cosine_lookup, sine_lookup))
    value_rows = reduced_forward(reduced_backward(matrix_product(first_normalized, value_matrix))).reshape(TOKEN_COUNT, KEY_HEADS, HEAD_WIDTH)
    mixed = reduced_forward(reduced_backward(attend(query_rows, key_rows, value_rows, positions)))
    residual_mid = residual_in + reduced_backward(matrix_product(mixed, output_weight))
    normed_second = reduced_forward(rms_norm(residual_mid, gain_second))
    gate_pre = reduced_backward(matrix_product(normed_second, gate_weight))
    up_pre = reduced_backward(matrix_product(normed_second, up_weight))
    hidden = reduced_forward(jax.nn.silu(gate_pre) * up_pre)
    return residual_mid + reduced_backward(matrix_product(hidden, down_weight))

def reference(tokens, block_pairs, cotangent, attention_gain, query_weight, key_matrix, value_matrix, output_weight, feedforward_gain, gate_weight, up_weight, down_weight):
    offsets = jnp.arange(BLK, dtype=jnp.int32)
    positions = (block_pairs[:, :, None] * BLK + offsets[None, None, :]).reshape(TOKEN_COUNT).astype(jnp.int32)
    weights = tuple((tensor.astype(jnp.float32) for tensor in (attention_gain, query_weight, key_matrix, value_matrix, output_weight, feedforward_gain, gate_weight, up_weight, down_weight)))

    def one_sequence(totals, pieces):
        sequence_in, sequence_cot = pieces
        layer_out, pull_back = jax.vjp(lambda inputs, *params: layer(inputs, positions, *params), sequence_in, *weights)
        gradients = pull_back(sequence_cot)
        totals = tuple((total_old + update for total_old, update in zip(totals, gradients[1:])))
        return (totals, (layer_out.astype(jnp.bfloat16), gradients[0].astype(jnp.bfloat16)))
    start_totals = tuple((jnp.zeros_like(tensor) for tensor in weights))
    totals, (layer_out, tokens_grad) = lax.scan(one_sequence, start_totals, (tokens.astype(jnp.float32), cotangent.astype(jnp.float32)))
    return (layer_out, tokens_grad, totals[0], totals[1], totals[2], totals[3], totals[4], totals[5], totals[6], totals[7], totals[8])
```

```python
import functools

import jax
import jax.numpy as jnp
from jax import lax
from jax.experimental import pallas as pl
from jax.experimental.pallas import tpu as pltpu
from jax.sharding import PartitionSpec as P

QUERY_HEADS = 16
KEY_HEADS = 8
HEAD_WIDTH = 96
EPS = 1e-05
THETA = 100000.0
BLK = 128
SCALE = HEAD_WIDTH ** -0.5
BF = jnp.bfloat16
F32 = jnp.float32

LOG2E = 1.4426950408889634

def attn_setup(nchip, g_refs, nat, tr):
    for r in range(nchip):
        for j in range(g_refs[r].shape[1] // 128):
            n = r * (g_refs[r].shape[1] // 128) + j
            block = g_refs[r][:, 128 * j:128 * (j + 1)]
            if nat is not None:
                nat[n] = block.T
            if tr is not None:
                tr[n] = block


def fwd_kernel(nchip, scale, ids_ref, inv_ref, q_ref, *rest):
    k_refs, v_refs = rest[:nchip], rest[nchip:2 * nchip]
    o_ref, lse_ref, knat, vtr, qs, m_s, l_s, acc = rest[2 * nchip:]
    nq = q_ref.shape[1] // 128
    nb = knat.shape[0]
    c = scale * LOG2E
    attn_setup(nchip, k_refs, knat, None)
    attn_setup(nchip, v_refs, None, vtr)
    for qi in range(nq):
        qs[qi] = jnp.concatenate([q_ref[0:96, 128 * qi:128 * (qi + 1)], q_ref[96:192, 128 * qi:128 * (qi + 1)]], axis=1)
    m_s[...] = jnp.full(m_s.shape, -1e30, jnp.float32)
    l_s[...] = jnp.zeros(l_s.shape, jnp.float32)
    acc[...] = jnp.zeros(acc.shape, jnp.float32)
    diff = lax.broadcasted_iota(jnp.int32, (128, 256), 0) - lax.rem(lax.broadcasted_iota(jnp.int32, (128, 256), 1), 128)

    def step(t, _):
        for sl in range(nq // 2):
            first = ids_ref[2 * sl]
            late = (t > first).astype(jnp.int32)
            qi = 2 * sl + late
            kpos = t - late * (first + 1)
            qid = ids_ref[qi]
            n = inv_ref[kpos]
            s = jnp.dot(knat[n], qs[qi], preferred_element_type=jnp.float32)
            s = jnp.where(diff <= (qid - kpos) * 128, s, -jnp.inf)
            m_old = m_s[qi]
            m_new = jnp.maximum(m_old, jnp.max(s, axis=0, keepdims=True))
            p = jnp.exp2((s - m_new) * c)
            alpha = jnp.exp2((m_old - m_new) * c)
            l_s[qi] = l_s[qi] * alpha + jnp.sum(p, axis=0, keepdims=True)
            m_s[qi] = m_new
            acc[qi] = acc[qi] * alpha + jnp.dot(vtr[n], p.astype(jnp.bfloat16), preferred_element_type=jnp.float32)
        return 0

    lax.fori_loop(0, nb + 1, step, 0)
    for qi in range(nq):
        l = l_s[qi]
        o = acc[qi] / l
        lse_ref[qi] = m_s[qi] * c + jnp.log2(l)
        o_ref[0:96, 128 * qi:128 * (qi + 1)] = o[:, :128].astype(jnp.bfloat16)
        o_ref[96:192, 128 * qi:128 * (qi + 1)] = o[:, 128:].astype(jnp.bfloat16)


def attn_fwd(ids, inv, qT, ks, vs, heads):
    nchip = len(ks)
    T = qT.shape[1]
    nq = T // 128
    nb = nchip * nq
    grid_spec = pltpu.PrefetchScalarGridSpec(
        num_scalar_prefetch=2,
        grid=(heads,),
        in_specs=[pl.BlockSpec((192, T), lambda g, *_: (g, 0))] + [pl.BlockSpec((96, T), lambda g, *_: (g, 0))] * (2 * nchip),
        out_specs=[pl.BlockSpec((192, T), lambda g, *_: (g, 0)), pl.BlockSpec((None, nq, 1, 256), lambda g, *_: (g, 0, 0, 0))],
        scratch_shapes=[
            pltpu.VMEM((nb, 128, 96), jnp.bfloat16),
            pltpu.VMEM((nb, 96, 128), jnp.bfloat16),
            pltpu.VMEM((nq, 96, 256), jnp.bfloat16),
            pltpu.VMEM((nq, 1, 256), jnp.float32),
            pltpu.VMEM((nq, 1, 256), jnp.float32),
            pltpu.VMEM((nq, 96, 256), jnp.float32),
        ],
    )
    return pl.pallas_call(
        functools.partial(fwd_kernel, nchip, SCALE),
        grid_spec=grid_spec,
        out_shape=[jax.ShapeDtypeStruct((heads * 192, T), jnp.bfloat16), jax.ShapeDtypeStruct((heads, nq, 1, 256), jnp.float32)],
        name="attention_forward",
    )(ids, inv, qT, *ks, *vs)


def bwd_kernel(nchip, scale, ids_ref, inv_ref, q_ref, o_ref, do_ref, lse_ref, *rest):
    k_refs, v_refs = rest[:nchip], rest[nchip:2 * nchip]
    dq_ref = rest[2 * nchip]
    dk_refs, dv_refs = rest[2 * nchip + 1:3 * nchip + 1], rest[3 * nchip + 1:4 * nchip + 1]
    knat, ktr, vnat, qs, dos, delta, dq_s, dk_s, dv_s = rest[4 * nchip + 1:]
    nq = q_ref.shape[1] // 128
    nb = knat.shape[0]
    nsl = nq // 2
    c = scale * LOG2E
    attn_setup(nchip, k_refs, knat, ktr)
    attn_setup(nchip, v_refs, vnat, None)
    for qi in range(nq):
        lanes = slice(128 * qi, 128 * (qi + 1))
        qs[qi] = jnp.concatenate([q_ref[0:96, lanes], q_ref[96:192, lanes]], axis=1)
        do = jnp.concatenate([do_ref[0:96, lanes], do_ref[96:192, lanes]], axis=1)
        dos[qi] = do
        o = jnp.concatenate([o_ref[0:96, lanes], o_ref[96:192, lanes]], axis=1)
        delta[qi] = jnp.sum(o.astype(jnp.float32) * do.astype(jnp.float32), axis=0, keepdims=True)
    dq_s[...] = jnp.zeros(dq_s.shape, jnp.float32)
    dk_s[...] = jnp.zeros(dk_s.shape, jnp.float32)
    dv_s[...] = jnp.zeros(dv_s.shape, jnp.float32)
    diff = lax.broadcasted_iota(jnp.int32, (128, 256), 0) - lax.rem(lax.broadcasted_iota(jnp.int32, (128, 256), 1), 128)
    nt = (((1,), (1,)), ((), ()))

    def step(t, _):
        for sl in range(nsl):
            first = ids_ref[2 * sl]
            late = (t > first).astype(jnp.int32)
            qi = 2 * sl + late
            kpos = t - late * (first + 1)
            qid = ids_ref[qi]
            n = inv_ref[kpos]
            q, do = qs[qi], dos[qi]
            s = jnp.dot(knat[n], q, preferred_element_type=jnp.float32)
            p = jnp.exp2(jnp.where(diff <= (qid - kpos) * 128, s * c - lse_ref[qi], -jnp.inf))
            dp = jnp.dot(vnat[n], do, preferred_element_type=jnp.float32)
            ds = (p * (dp - delta[qi])).astype(jnp.bfloat16)
            dv_s[sl, n] += lax.dot_general(do, p.astype(jnp.bfloat16), nt, preferred_element_type=jnp.float32)
            dk_s[sl, n] += lax.dot_general(q, ds, nt, preferred_element_type=jnp.float32)
            dq_s[qi] += jnp.dot(ktr[n], ds, preferred_element_type=jnp.float32)
        return 0

    lax.fori_loop(0, nb + 1, step, 0)
    for qi in range(nq):
        lanes = slice(128 * qi, 128 * (qi + 1))
        dq_ref[0:96, lanes] = dq_s[qi][:, :128] * scale
        dq_ref[96:192, lanes] = dq_s[qi][:, 128:] * scale
    for r in range(nchip):
        for j in range(nq):
            n = r * nq + j
            dk = dk_s[0, n]
            dv = dv_s[0, n]
            for sl in range(1, nsl):
                dk = dk + dk_s[sl, n]
                dv = dv + dv_s[sl, n]
            dk_refs[r][:, 128 * j:128 * (j + 1)] = (dk * scale).astype(jnp.bfloat16)
            dv_refs[r][:, 128 * j:128 * (j + 1)] = dv.astype(jnp.bfloat16)


def attn_bwd(ids, inv, qT, oT, doT, lse, ks, vs, heads):
    nchip = len(ks)
    T = qT.shape[1]
    nq = T // 128
    nb = nchip * nq
    wide = pl.BlockSpec((192, T), lambda g, *_: (g, 0))
    slim = pl.BlockSpec((96, T), lambda g, *_: (g, 0))
    grid_spec = pltpu.PrefetchScalarGridSpec(
        num_scalar_prefetch=2,
        grid=(heads,),
        in_specs=[wide, wide, wide, pl.BlockSpec((None, nq, 1, 256), lambda g, *_: (g, 0, 0, 0))] + [slim] * (2 * nchip),
        out_specs=[wide] + [slim] * (2 * nchip),
        scratch_shapes=[
            pltpu.VMEM((nb, 128, 96), jnp.bfloat16),
            pltpu.VMEM((nb, 96, 128), jnp.bfloat16),
            pltpu.VMEM((nb, 128, 96), jnp.bfloat16),
            pltpu.VMEM((nq, 96, 256), jnp.bfloat16),
            pltpu.VMEM((nq, 96, 256), jnp.bfloat16),
            pltpu.VMEM((nq, 1, 256), jnp.float32),
            pltpu.VMEM((nq, 96, 256), jnp.float32),
            pltpu.VMEM((nq // 2, nb, 96, 128), jnp.float32),
            pltpu.VMEM((nq // 2, nb, 96, 128), jnp.float32),
        ],
    )
    slab = jax.ShapeDtypeStruct((heads * 96, T), jnp.bfloat16)
    outs = pl.pallas_call(
        functools.partial(bwd_kernel, nchip, SCALE),
        grid_spec=grid_spec,
        out_shape=[jax.ShapeDtypeStruct((heads * 192, T), jnp.float32)] + [slab] * (2 * nchip),
        name="attention_backward",
    )(ids, inv, qT, oT, doT, lse, *ks, *vs)
    return outs[0], outs[1:1 + nchip], outs[1 + nchip:]


def mm(left, right, left_dim, right_dim):
    return lax.dot_general(left, right, (((left_dim,), (right_dim,)), ((), ())), preferred_element_type=F32)


def swap(a):
    return lax.ppermute(a, "ctx", [(i, i ^ 1) for i in range(lax.axis_size("ctx"))])


def hop(a, r):
    return lax.ppermute(a, "ctx", [(i, i ^ (2 * r)) for i in range(lax.axis_size("ctx"))])


def ring(a):
    n = lax.axis_size("fsdp")
    return lax.ppermute(a, "fsdp", [(i, (i + 1) % n) for i in range(n)])


def pick(a, index, axis=0):
    return lax.dynamic_index_in_dim(a, index, axis, keepdims=False)


def place(buffer, piece, index, axis=0):
    return lax.dynamic_update_slice_in_dim(buffer, jnp.expand_dims(piece, axis), index, axis)


def depth_gather(piece, depth):
    n = lax.axis_size("fsdp")
    buffer = place(jnp.zeros((n,) + piece.shape, piece.dtype), piece, depth)
    for s in range(1, n):
        piece = ring(piece)
        buffer = place(buffer, piece, lax.rem(depth + n - s, n))
    return buffer


def depth_scatter(parts, depth):
    n = lax.axis_size("fsdp")
    total = pick(parts, lax.rem(depth + n - 1, n))
    for s in range(n - 1):
        total = ring(total.astype(BF))
        total = total.astype(F32) + pick(parts, lax.rem(depth + 2 * n - 2 - s, n)).astype(F32)
    return total


def plane_gather(piece, index):
    n = lax.axis_size("ctx")
    chips = n // 2
    pieces = jnp.stack([piece] + [hop(piece, r) for r in range(1, chips)])
    others = swap(pieces)
    buffer = jnp.zeros((n,) + piece.shape, piece.dtype)
    for r in range(chips):
        buffer = place(buffer, pieces[r], index ^ (2 * r))
        buffer = place(buffer, others[r], index ^ (2 * r + 1))
    return buffer


def rotate(v, cosine, sine):
    heads = v.reshape(-1, 2, HEAD_WIDTH // 2, v.shape[-1])
    a, b = heads[:, 0], heads[:, 1]
    return jnp.stack([a * cosine - b * sine, b * cosine + a * sine], 1).reshape(v.shape)


def rotate_back(v, cosine, sine):
    heads = v.reshape(-1, 2, HEAD_WIDTH // 2, v.shape[-1])
    a, b = heads[:, 0], heads[:, 1]
    return jnp.stack([a * cosine + b * sine, b * cosine - a * sine], 1).reshape(v.shape)


def norm_back(incoming, unit, inverse, gain):
    scaled = incoming * gain
    return inverse * (scaled - unit * jnp.mean(scaled * unit, -1, keepdims=True))


def body(
    tokens,
    block_pairs,
    cotangent,
    attention_gain,
    query_weight,
    key_matrix,
    value_matrix,
    output_weight,
    feedforward_gain,
    gate_weight,
    up_weight,
    down_weight,
):
    slice_len, width = tokens.shape[1], tokens.shape[2]
    ctx = lax.axis_size("ctx")
    zsize = lax.axis_size("fsdp")
    chips = ctx // 2
    diag = chips - 1
    near = range(1, chips - 1)
    index = lax.axis_index("ctx")
    chip, core = index // 2, lax.rem(index, 2)
    depth = lax.axis_index("fsdp")
    rows = width // zsize
    strip = rows // ctx
    hidden_rows = down_weight.shape[0]
    fine = hidden_rows // ctx
    chunk = fine * zsize
    kv_rows = KEY_HEADS * HEAD_WIDTH

    gains = jnp.stack([attention_gain, feedforward_gain])
    gain_buffer = place(jnp.zeros((zsize, 2, rows), BF), gains, depth)
    for s in range(1, zsize):
        moved = lax.ppermute(gains, "fsdp", [(k, (k + s) % zsize) for k in range(zsize)])
        gain_buffer = place(gain_buffer, moved, lax.rem(depth + zsize - s, zsize))
    gains_full = jnp.transpose(gain_buffer, (1, 0, 2)).reshape(2, width).astype(F32)
    gain_first, gain_second = gains_full[0], gains_full[1]

    def gather_square(shard):
        strips = shard.reshape(ctx, strip, shard.shape[1])
        pair = jnp.stack([pick(strips, index), pick(strips, index ^ (2 * diag))])
        pair = depth_gather(pair, depth)
        own, far = pair[:, 0], pair[:, 1]
        found = {0: own, diag: far}
        for r in near:
            found[r] = hop(own, r)
        full = jnp.zeros((zsize, ctx, strip, shard.shape[1]), BF)
        for r in range(chips):
            full = place(full, found[r], index ^ (2 * r), 1)
            full = place(full, swap(found[r]), index ^ (2 * r + 1), 1)
        return full.reshape(width, shard.shape[1])

    key_value_full = gather_square(jnp.concatenate([key_matrix, value_matrix], 1))
    query_full = gather_square(query_weight)
    output_full = gather_square(output_weight)

    gate_cut = gate_weight.reshape(rows, zsize, 2, chips, fine)
    up_cut = up_weight.reshape(rows, zsize, 2, chips, fine)
    down_cut = down_weight.reshape(2, chips, fine, width)

    def own_piece(r):
        gate = pick(pick(gate_cut, core, 2), chip ^ r, 2).reshape(rows, chunk)
        up = pick(pick(up_cut, core, 2), chip ^ r, 2).reshape(rows, chunk)
        down = pick(pick(down_cut, core), chip ^ r)
        return jnp.concatenate([gate, up], 1), down

    gate_up, down = {}, {}
    for r in (0, diag):
        wide, tall = own_piece(r)
        gate_up[r] = depth_gather(wide, depth).reshape(width, 2 * chunk)
        down[r] = depth_gather(tall, depth).reshape(chunk, width)
    for r in near:
        gate_up[r] = hop(gate_up[0], r)
        down[r] = hop(down[0], r)

    x = jnp.concatenate([pick(tokens, core), swap(pick(tokens, 1 - core))]).astype(F32)
    cot_there = swap(cotangent)
    cot = jnp.concatenate(
        [pick(cotangent, core), pick(cot_there, core), pick(cot_there, 1 - core), pick(cotangent, 1 - core)]
    )
    length = x.shape[0]

    ids_all = jnp.concatenate([pick(block_pairs, index ^ r) for r in range(ctx)])
    ids = ids_all[:4]
    blocks = ids_all.shape[0]
    order = jnp.sum(
        jnp.where(ids_all[None, :] == jnp.arange(blocks, dtype=jnp.int32)[:, None], jnp.arange(blocks, dtype=jnp.int32)[None, :], 0), 1
    )
    positions = (ids[:, None] * BLK + jnp.arange(BLK, dtype=jnp.int32)[None, :]).reshape(length)
    half = HEAD_WIDTH // 2
    frequency = THETA ** (-jnp.arange(half, dtype=F32) * 2.0 / HEAD_WIDTH)
    angles = frequency[:, None] * positions.astype(F32)[None, :]
    cosine, sine = jnp.cos(angles), jnp.sin(angles)

    inverse_first = lax.rsqrt(jnp.mean(x * x, -1, keepdims=True) + EPS)
    unit_first = x * inverse_first
    first = (unit_first * gain_first).astype(BF)
    first_t = jnp.transpose(first)
    kv = mm(key_value_full, first_t, 0, 0)
    keys = {0: rotate(kv[:kv_rows], cosine, sine).astype(BF)}
    values = {0: kv[kv_rows:].astype(BF)}
    top = 1
    while top < chips:
        top *= 2
    for r in range(1, chips):
        high = 1 << (r.bit_length() - 1)
        low = r & -r
        keys[r] = hop(keys[r ^ high], high)
        values[r] = hop(values[r ^ low], low)
    query = rotate(mm(query_full, first_t, 0, 0), cosine, sine).astype(BF)
    key_list = [keys[r] for r in range(chips)]
    value_list = [values[r] for r in range(chips)]
    attended, log_total = attn_fwd(ids, order, query, key_list, value_list, KEY_HEADS)

    middle = x + mm(attended, output_full, 0, 0)
    inverse_second = lax.rsqrt(jnp.mean(middle * middle, -1, keepdims=True) + EPS)
    unit_second = middle * inverse_second
    second = (unit_second * gain_second).astype(BF)
    second = jnp.concatenate([second, swap(second)])
    out_part = 0.0
    second_grad = 0.0
    wide_grad, tall_grad = {}, {}
    for r in list(near) + [0, diag]:
        pre = mm(second, gate_up[r], 1, 0)
        gate_pre, up_pre = pre[:, :chunk], pre[:, chunk:]
        hidden_grad = mm(cot, down[r], 1, 1)
        sigmoid = jax.nn.sigmoid(gate_pre)
        silu = gate_pre * sigmoid
        hidden = (silu * up_pre).astype(BF)
        gate_low = (hidden_grad * up_pre * sigmoid * (1.0 + gate_pre * (1.0 - sigmoid))).astype(BF)
        up_low = (hidden_grad * silu).astype(BF)
        both_low = jnp.concatenate([gate_low, up_low], 1)
        tall_grad[r] = mm(hidden, cot, 0, 0).astype(BF)
        wide_grad[r] = mm(second, both_low, 0, 0).astype(BF)
        out_part = out_part + mm(hidden, down[r], 1, 0)
        second_grad = second_grad + mm(both_low, gate_up[r], 1, 1)

    q = slice_len
    out_part = jnp.concatenate([out_part[:length] + middle, out_part[length:]])
    came = swap(jnp.concatenate([out_part[2 * q:3 * q], out_part[q:2 * q]]))
    out_here = (out_part[:q] + came[:q]).astype(BF)
    out_there = (out_part[3 * q:] + came[q:]).astype(BF)

    def stored(here, there):
        return jnp.where(core == 0, jnp.stack([here, there]), jnp.stack([there, here]))

    layer_out = stored(out_here, out_there)

    second_grad = second_grad[:length] + swap(second_grad[length:])
    gain_second_part = jnp.sum(second_grad * unit_second, 0)
    middle_grad = cot[:length].astype(F32) + norm_back(second_grad, unit_second, inverse_second, gain_second)

    def scatter(parts):
        total = parts[0].astype(F32)
        for r in near:
            total = total + hop(parts[r], r).astype(F32)
        far = hop(depth_scatter(parts[diag], depth).astype(BF), diag)
        total = depth_scatter(total.astype(BF), depth) + far.astype(F32)
        return total.astype(BF)

    tall_piece = scatter({r: tall_grad[r].reshape(zsize, fine, width) for r in range(chips)})
    wide_piece = scatter({r: wide_grad[r].reshape(zsize, rows, 2 * chunk) for r in range(chips)})
    tall_all = plane_gather(tall_piece, index)
    wide_all = plane_gather(wide_piece, index)
    down_grad = jnp.transpose(tall_all.reshape(chips, 2, fine, width), (1, 0, 2, 3)).reshape(hidden_rows, width).astype(F32)
    wide_all = wide_all.reshape(chips, 2, rows, 2, zsize, fine)
    gate_grad = jnp.transpose(wide_all[:, :, :, 0], (2, 3, 1, 0, 4)).reshape(rows, -1).astype(F32)
    up_grad = jnp.transpose(wide_all[:, :, :, 1], (2, 3, 1, 0, 4)).reshape(rows, -1).astype(F32)

    middle_low = middle_grad.astype(BF)
    attended_grad = mm(output_full, middle_low, 1, 1).astype(BF)
    query_total, key_parts, value_parts = attn_bwd(
        ids, order, query, attended, attended_grad, log_total, key_list, value_list, KEY_HEADS
    )
    key_sum = [part for part in key_parts]
    value_sum = [part for part in value_parts]
    for r in range(chips - 1, 0, -1):
        high = 1 << (r.bit_length() - 1)
        low = r & -r
        key_sum[r ^ high] = key_sum[r ^ high].astype(F32) + hop(key_sum[r].astype(BF), high).astype(F32)
        value_sum[r ^ low] = value_sum[r ^ low].astype(F32) + hop(value_sum[r].astype(BF), low).astype(F32)
    query_low = rotate_back(query_total, cosine, sine).astype(BF)
    key_low = rotate_back(key_sum[0], cosine, sine).astype(BF)
    value_low = value_sum[0].astype(BF)
    kv_low = jnp.concatenate([key_low, value_low])

    def halves(a):
        cut = a.reshape(zsize, chips, 2, strip, length)
        here = pick(cut, core, 2).reshape(-1, length)
        there = swap(pick(cut, 1 - core, 2).reshape(-1, length))
        return jnp.concatenate([here, there], 1)

    def square_grad(product):
        parts = product.astype(BF).reshape(zsize, chips, strip, width)
        piece = scatter({r: pick(parts, chip ^ r, 1) for r in range(chips)})
        return plane_gather(piece, index).reshape(rows, width).astype(F32)

    first_half = halves(first_t)
    output_grad = square_grad(mm(halves(attended), jnp.concatenate([middle_low, swap(middle_low)]), 1, 0))
    query_grad = square_grad(mm(first_half, jnp.concatenate([query_low, swap(query_low)], 1), 1, 1))
    kv_grad = square_grad(mm(first_half, jnp.concatenate([kv_low, swap(kv_low)], 1), 1, 1))

    first_grad = mm(query_low, query_full, 0, 1) + mm(kv_low, key_value_full, 0, 1)
    gain_first_part = jnp.sum(first_grad * unit_first, 0)
    tokens_part = (middle_grad + norm_back(first_grad, unit_first, inverse_first, gain_first)).astype(BF)
    tokens_grad = stored(tokens_part[:q], swap(tokens_part[q:]))

    def gain_total(part):
        return lax.dynamic_slice_in_dim(lax.psum(part, ("ctx", "fsdp")), depth * rows, rows)

    return (
        layer_out,
        tokens_grad,
        gain_total(gain_first_part),
        query_grad,
        kv_grad[:, :kv_rows],
        kv_grad[:, kv_rows:],
        output_grad,
        gain_total(gain_second_part),
        gate_grad,
        up_grad,
        down_grad,
    )


def solution(mesh):
    line, square, grid = P("fsdp"), P("fsdp", None), P("fsdp", "ctx", None)
    in_specs = (grid, P(), grid, line, square, square, square, square, line, square, square, square)
    out_specs = (grid, grid, line, square, square, square, square, line, square, square, square)
    return jax.shard_map(body, mesh=mesh, in_specs=in_specs, out_specs=out_specs, check_vma=False)
```

```python
import functools

import jax
import jax.numpy as jnp
from jax import lax
from jax.experimental import pallas as pl
from jax.experimental.pallas import tpu as pltpu
from jax.sharding import PartitionSpec as P

QUERY_HEADS = 16
KEY_HEADS = 8
HEAD_WIDTH = 96
EPS = 1e-05
THETA = 100000.0
BLK = 128
SCALE = HEAD_WIDTH ** -0.5
BF = jnp.bfloat16
F32 = jnp.float32

LOG2E = 1.4426950408889634

def attn_setup(nchip, g_refs, nat, tr):
    for r in range(nchip):
        for j in range(g_refs[r].shape[1] // 128):
            n = r * (g_refs[r].shape[1] // 128) + j
            block = g_refs[r][:, 128 * j:128 * (j + 1)]
            if nat is not None:
                nat[n] = block.T
            if tr is not None:
                tr[n] = block


def fwd_kernel(nchip, scale, ids_ref, inv_ref, q_ref, *rest):
    k_refs, v_refs = rest[:nchip], rest[nchip:2 * nchip]
    o_ref, lse_ref, knat, vtr, qs, m_s, l_s, acc = rest[2 * nchip:]
    nq = q_ref.shape[1] // 128
    nb = knat.shape[0]
    c = scale * LOG2E
    attn_setup(nchip, k_refs, knat, None)
    attn_setup(nchip, v_refs, None, vtr)
    for qi in range(nq):
        qs[qi] = jnp.concatenate([q_ref[0:96, 128 * qi:128 * (qi + 1)], q_ref[96:192, 128 * qi:128 * (qi + 1)]], axis=1)
    m_s[...] = jnp.full(m_s.shape, -1e30, jnp.float32)
    l_s[...] = jnp.zeros(l_s.shape, jnp.float32)
    acc[...] = jnp.zeros(acc.shape, jnp.float32)
    diff = lax.broadcasted_iota(jnp.int32, (128, 256), 0) - lax.rem(lax.broadcasted_iota(jnp.int32, (128, 256), 1), 128)

    def step(t, _):
        for sl in range(nq // 2):
            first = ids_ref[2 * sl]
            late = (t > first).astype(jnp.int32)
            qi = 2 * sl + late
            kpos = t - late * (first + 1)
            qid = ids_ref[qi]
            n = inv_ref[kpos]
            s = jnp.dot(knat[n], qs[qi], preferred_element_type=jnp.float32)
            s = jnp.where(diff <= (qid - kpos) * 128, s, -jnp.inf)
            m_old = m_s[qi]
            m_new = jnp.maximum(m_old, jnp.max(s, axis=0, keepdims=True))
            p = jnp.exp2((s - m_new) * c)
            alpha = jnp.exp2((m_old - m_new) * c)
            l_s[qi] = l_s[qi] * alpha + jnp.sum(p, axis=0, keepdims=True)
            m_s[qi] = m_new
            acc[qi] = acc[qi] * alpha + jnp.dot(vtr[n], p.astype(jnp.bfloat16), preferred_element_type=jnp.float32)
        return 0

    lax.fori_loop(0, nb + 1, step, 0)
    for qi in range(nq):
        l = l_s[qi]
        o = acc[qi] / l
        lse_ref[qi] = m_s[qi] * c + jnp.log2(l)
        o_ref[0:96, 128 * qi:128 * (qi + 1)] = o[:, :128].astype(jnp.bfloat16)
        o_ref[96:192, 128 * qi:128 * (qi + 1)] = o[:, 128:].astype(jnp.bfloat16)


def attn_fwd(ids, inv, qT, ks, vs, heads):
    nchip = len(ks)
    T = qT.shape[1]
    nq = T // 128
    nb = nchip * nq
    grid_spec = pltpu.PrefetchScalarGridSpec(
        num_scalar_prefetch=2,
        grid=(heads,),
        in_specs=[pl.BlockSpec((192, T), lambda g, *_: (g, 0))] + [pl.BlockSpec((96, T), lambda g, *_: (g, 0))] * (2 * nchip),
        out_specs=[pl.BlockSpec((192, T), lambda g, *_: (g, 0)), pl.BlockSpec((None, nq, 1, 256), lambda g, *_: (g, 0, 0, 0))],
        scratch_shapes=[
            pltpu.VMEM((nb, 128, 96), jnp.bfloat16),
            pltpu.VMEM((nb, 96, 128), jnp.bfloat16),
            pltpu.VMEM((nq, 96, 256), jnp.bfloat16),
            pltpu.VMEM((nq, 1, 256), jnp.float32),
            pltpu.VMEM((nq, 1, 256), jnp.float32),
            pltpu.VMEM((nq, 96, 256), jnp.float32),
        ],
    )
    return pl.pallas_call(
        functools.partial(fwd_kernel, nchip, SCALE),
        grid_spec=grid_spec,
        out_shape=[jax.ShapeDtypeStruct((heads * 192, T), jnp.bfloat16), jax.ShapeDtypeStruct((heads, nq, 1, 256), jnp.float32)],
        cost_estimate=pl.CostEstimate(flops=90 * 10**9, bytes_accessed=16 * 2**20, transcendentals=0),
        name="attention_forward",
    )(ids, inv, qT, *ks, *vs)


def bwd_kernel(nchip, scale, ids_ref, inv_ref, q_ref, o_ref, do_ref, lse_ref, *rest):
    k_refs, v_refs = rest[:nchip], rest[nchip:2 * nchip]
    dq_ref = rest[2 * nchip]
    dk_refs, dv_refs = rest[2 * nchip + 1:3 * nchip + 1], rest[3 * nchip + 1:4 * nchip + 1]
    knat, ktr, vnat, qs, dos, delta, dq_s, dk_s, dv_s = rest[4 * nchip + 1:]
    nq = q_ref.shape[1] // 128
    nb = knat.shape[0]
    nsl = nq // 2
    c = scale * LOG2E
    attn_setup(nchip, k_refs, knat, ktr)
    attn_setup(nchip, v_refs, vnat, None)
    for qi in range(nq):
        lanes = slice(128 * qi, 128 * (qi + 1))
        qs[qi] = jnp.concatenate([q_ref[0:96, lanes], q_ref[96:192, lanes]], axis=1)
        do = jnp.concatenate([do_ref[0:96, lanes], do_ref[96:192, lanes]], axis=1)
        dos[qi] = do
        o = jnp.concatenate([o_ref[0:96, lanes], o_ref[96:192, lanes]], axis=1)
        delta[qi] = jnp.sum(o.astype(jnp.float32) * do.astype(jnp.float32), axis=0, keepdims=True)
    dq_s[...] = jnp.zeros(dq_s.shape, jnp.float32)
    dk_s[...] = jnp.zeros(dk_s.shape, jnp.float32)
    dv_s[...] = jnp.zeros(dv_s.shape, jnp.float32)
    diff = lax.broadcasted_iota(jnp.int32, (128, 256), 0) - lax.rem(lax.broadcasted_iota(jnp.int32, (128, 256), 1), 128)
    nt = (((1,), (1,)), ((), ()))

    def step(t, _):
        for sl in range(nsl):
            first = ids_ref[2 * sl]
            late = (t > first).astype(jnp.int32)
            qi = 2 * sl + late
            kpos = t - late * (first + 1)
            qid = ids_ref[qi]
            n = inv_ref[kpos]
            q, do = qs[qi], dos[qi]
            s = jnp.dot(knat[n], q, preferred_element_type=jnp.float32)
            p = jnp.exp2(jnp.where(diff <= (qid - kpos) * 128, s * c - lse_ref[qi], -jnp.inf))
            dp = jnp.dot(vnat[n], do, preferred_element_type=jnp.float32)
            ds = (p * (dp - delta[qi])).astype(jnp.bfloat16)
            dv_s[sl, n] += lax.dot_general(do, p.astype(jnp.bfloat16), nt, preferred_element_type=jnp.float32)
            dk_s[sl, n] += lax.dot_general(q, ds, nt, preferred_element_type=jnp.float32)
            dq_s[qi] += jnp.dot(ktr[n], ds, preferred_element_type=jnp.float32)
        return 0

    lax.fori_loop(0, nb + 1, step, 0)
    for qi in range(nq):
        lanes = slice(128 * qi, 128 * (qi + 1))
        dq_ref[0:96, lanes] = dq_s[qi][:, :128] * scale
        dq_ref[96:192, lanes] = dq_s[qi][:, 128:] * scale
    for r in range(nchip):
        for j in range(nq):
            n = r * nq + j
            dk = dk_s[0, n]
            dv = dv_s[0, n]
            for sl in range(1, nsl):
                dk = dk + dk_s[sl, n]
                dv = dv + dv_s[sl, n]
            dk_refs[r][:, 128 * j:128 * (j + 1)] = (dk * scale).astype(jnp.bfloat16)
            dv_refs[r][:, 128 * j:128 * (j + 1)] = dv.astype(jnp.bfloat16)


def attn_bwd(ids, inv, qT, oT, doT, lse, ks, vs, heads):
    nchip = len(ks)
    T = qT.shape[1]
    nq = T // 128
    nb = nchip * nq
    wide = pl.BlockSpec((192, T), lambda g, *_: (g, 0))
    slim = pl.BlockSpec((96, T), lambda g, *_: (g, 0))
    grid_spec = pltpu.PrefetchScalarGridSpec(
        num_scalar_prefetch=2,
        grid=(heads,),
        in_specs=[wide, wide, wide, pl.BlockSpec((None, nq, 1, 256), lambda g, *_: (g, 0, 0, 0))] + [slim] * (2 * nchip),
        out_specs=[wide] + [slim] * (2 * nchip),
        scratch_shapes=[
            pltpu.VMEM((nb, 128, 96), jnp.bfloat16),
            pltpu.VMEM((nb, 96, 128), jnp.bfloat16),
            pltpu.VMEM((nb, 128, 96), jnp.bfloat16),
            pltpu.VMEM((nq, 96, 256), jnp.bfloat16),
            pltpu.VMEM((nq, 96, 256), jnp.bfloat16),
            pltpu.VMEM((nq, 1, 256), jnp.float32),
            pltpu.VMEM((nq, 96, 256), jnp.float32),
            pltpu.VMEM((nq // 2, nb, 96, 128), jnp.float32),
            pltpu.VMEM((nq // 2, nb, 96, 128), jnp.float32),
        ],
    )
    slab = jax.ShapeDtypeStruct((heads * 96, T), jnp.bfloat16)
    outs = pl.pallas_call(
        functools.partial(bwd_kernel, nchip, SCALE),
        grid_spec=grid_spec,
        out_shape=[jax.ShapeDtypeStruct((heads * 192, T), jnp.float32)] + [slab] * (2 * nchip),
        cost_estimate=pl.CostEstimate(flops=90 * 10**9, bytes_accessed=24 * 2**20, transcendentals=0),
        name="attention_backward",
    )(ids, inv, qT, oT, doT, lse, *ks, *vs)
    return outs[0], outs[1:1 + nchip], outs[1 + nchip:]


def front_kernel(zsize, *refs):
    (tok, gains, key_w, value_w, query_w, out_w, gate_w, up_w, down_w, cos, sin) = refs[:11]
    (full_kv, full_q, full_o, wide, tall, far_wide, far_tall, x_out, first, q_out, gains_out, k0, k1, k2, k3, v0, v1, v2, v3) = refs[11:30]
    x_s, gain_s, kv_w, q_w, kv_s, ss, rs, ls, gs, gr = refs[30:]
    ks, vs = (k0, k1, k2, k3), (v0, v1, v2, v3)
    index, depth = lax.axis_index("ctx"), lax.axis_index("fsdp")
    chip, core = index // 2, lax.rem(index, 2)
    fine = tall.shape[1]
    chunk = fine * zsize
    width = first.shape[1]
    length = first.shape[0]
    kv_rows = k0.shape[0]
    nxt, prv = lax.rem(depth + 1, zsize), lax.rem(depth + zsize - 1, zsize)
    to_next, to_prev = (index, nxt), (index, prv)
    chip_x, chip_y, chip_d = chip + 1 - 2 * lax.rem(chip, 2), lax.rem(chip + 2, 4), 3 - chip
    to_x, to_y, to_core = (chip_x * 2 + core, depth), (chip_y * 2 + core, depth), (chip * 2 + 1 - core, depth)

    barrier = pltpu.get_barrier_semaphore()
    for target in (to_next, to_prev, to_x, to_y, to_core):
        pl.semaphore_signal(barrier, inc=1, device_id=target, device_id_type=pl.DeviceIdType.MESH)
    pl.semaphore_wait(barrier, 5)

    count = [0, 0]
    sent = []

    def send(src, dst, target):
        k = count[0]
        count[0] += 1
        copy = pltpu.make_async_remote_copy(
            src_ref=src, dst_ref=dst, send_sem=ss.at[k], recv_sem=rs.at[k], device_id=target, device_id_type=pl.DeviceIdType.MESH
        )
        copy.start()
        sent.append(copy)
        return copy

    def local(src, dst):
        k = count[1]
        count[1] += 1
        copy = pltpu.make_async_copy(src, dst, ls.at[k])
        copy.start()
        return copy

    def slot(s):
        return lax.rem(depth + zsize - s, zsize)

    steps = range(1, zsize)
    last = zsize - 1
    tokens_there = send(tok.at[1 - core], x_s.at[1], to_core)
    own_kv = [local(key_w, full_kv.at[depth, :, :, :, pl.ds(0, kv_rows)]), local(value_w, full_kv.at[depth, :, :, :, pl.ds(kv_rows, kv_rows)])]
    gain_s[depth] = gains[...]
    for copy in own_kv:
        copy.wait()

    weights = {"kv": full_kv, "q": full_q, "o": full_o}
    shards = {"q": query_w, "o": out_w}
    moves = {}

    def ring_step(name, s):
        full = weights[name]
        place = full.at[slot(s - 1), chip, core]
        source = shards[name].at[chip, core] if name in shards and s == 1 else place
        moves[name, "ring", s] = send(source, place, to_next)

    def spread(name, s):
        place = weights[name].at[slot(s), chip, core]
        moves[name, "x", s] = send(place, place, to_x)
        moves[name, "y", s] = send(place, place, to_y)

    def forward(name, s):
        mid = width // 2
        moves[name, "x", s].wait_recv()
        left = weights[name].at[slot(s), chip_x, core, :, pl.ds(0, mid)]
        moves[name, "fy", s] = send(left, left, to_y)
        moves[name, "y", s].wait_recv()
        right = weights[name].at[slot(s), chip_y, core, :, pl.ds(mid, mid)]
        moves[name, "fx", s] = send(right, right, to_x)

    def cross(name, s):
        moves[name, "fx", s].wait_recv()
        moves[name, "fy", s].wait_recv()
        column = weights[name].at[slot(s), :, core]
        moves[name, "core", s] = send(column, column, to_core)

    def gain_step(s):
        place = gain_s.at[slot(s - 1)]
        copy = pltpu.make_async_remote_copy(
            src_ref=place, dst_ref=place, send_sem=gs.at[s], recv_sem=gr.at[s], device_id=to_next, device_id_type=pl.DeviceIdType.MESH
        )
        copy.start()
        sent.append(copy)
        moves["gain", s] = copy

    ring_step("kv", 1)
    gain_step(1)
    own_late = [local(query_w, full_q.at[depth]), local(out_w, full_o.at[depth])]
    own_ffn = [local(down_w.at[pl.ds(pl.multiple_of(core * (4 * fine) + chip * fine, fine), fine)], tall.at[depth])]
    for part in range(zsize):
        column = pl.multiple_of(part * (8 * fine) + core * (4 * fine) + chip * fine, fine)
        own_ffn.append(local(gate_w.at[:, pl.ds(column, fine)], wide.at[depth, :, pl.ds(part * fine, fine)]))
        own_ffn.append(local(up_w.at[:, pl.ds(column, fine)], wide.at[depth, :, pl.ds(chunk + part * fine, fine)]))
    far_ffn = [local(down_w.at[pl.ds(pl.multiple_of(core * (4 * fine) + chip_d * fine, fine), fine)], far_tall)]
    for part in range(zsize):
        column = pl.multiple_of(part * (8 * fine) + core * (4 * fine) + chip_d * fine, fine)
        far_ffn.append(local(gate_w.at[:, pl.ds(column, fine)], far_wide.at[:, pl.ds(part * fine, fine)]))
        far_ffn.append(local(up_w.at[:, pl.ds(column, fine)], far_wide.at[:, pl.ds(chunk + part * fine, fine)]))

    for s in steps:
        moves["kv", "ring", s].wait_recv()
        moves["gain", s].wait_recv()
        if s < last:
            ring_step("kv", s + 1)
            gain_step(s + 1)
        else:
            ring_step("q", 1)
        spread("kv", s)
    for s in steps:
        forward("kv", s)
        moves["q", "ring", s].wait_recv()
        ring_step("q", s + 1) if s < last else ring_step("o", 1)
        spread("q", s)
    for s in steps:
        cross("kv", s)

    tokens_there.wait_recv()
    x_out[0:length // 2] = tok[core]
    x_out[length // 2:] = x_s[1]
    gain_rows = [gain_s[place] for place in range(zsize)]
    gains_full = jnp.concatenate(gain_rows, axis=1)
    gains_out[...] = gains_full
    gain = gains_full[0:1]
    rows = 64

    def normalize(t, _):
        part = pl.ds(pl.multiple_of(t * rows, rows), rows)
        v = x_out[part].astype(F32)
        inverse = lax.rsqrt(jnp.mean(v * v, -1, keepdims=True) + EPS)
        first[part] = (v * inverse * gain).astype(BF)
        return 0

    lax.fori_loop(0, length // rows, normalize, 0)

    moves["o", "ring", 1].wait_recv()
    if last > 1:
        ring_step("o", 2)
    spread("o", 1)
    for s in steps:
        moves["kv", "core", s].wait_recv()
    load_kv = local(full_kv, kv_w)
    if last > 1:
        moves["o", "ring", 2].wait_recv()
        if last > 2:
            ring_step("o", 3)
        spread("o", 2)
    load_kv.wait()
    tile = 384

    def project(weight, t, turn):
        cols = pl.ds(pl.multiple_of(t * tile, tile), tile)
        w = weight[:, :, :, :, cols].reshape(width, tile)
        r = jnp.dot(first[...], w, preferred_element_type=F32).T
        if turn:
            r = rotate(r, cos[...], sin[...])
        return r.astype(BF)

    def project_kv(t, turn):
        kv_s[pl.ds(pl.multiple_of(t * tile, tile), tile)] = project(kv_w, t, turn)
        return 0

    per = kv_rows // tile
    lax.fori_loop(0, per, lambda t, _: project_kv(t, True), 0)
    k_here, v_here = kv_s.at[pl.ds(0, kv_rows)], kv_s.at[pl.ds(kv_rows, kv_rows)]
    k_x, k_y = send(k_here, k1, to_x), send(k_here, k2, to_y)
    lax.fori_loop(per, 2 * per, lambda t, _: project_kv(t, False), 0)
    v_y, v_x = send(v_here, v2, to_y), send(v_here, v1, to_x)
    keep = [local(k_here, k0), local(v_here, v0)]

    for s in range(3, zsize):
        moves["o", "ring", s].wait_recv()
        if s < last:
            ring_step("o", s + 1)
        spread("o", s)
    for copy in own_ffn:
        copy.wait()

    def ffn_step(s):
        a, b = wide.at[slot(s - 1)], tall.at[slot(s - 1)]
        moves["ffn", s] = (send(a, a, to_next), send(b, b, to_next))

    ffn_step(1)
    for s in steps:
        forward("q", s)
    for s in steps:
        cross("q", s)
    for s in steps:
        forward("o", s)
    for s in steps:
        cross("o", s)
    for s in steps:
        moves["q", "core", s].wait_recv()
    for copy in own_late:
        copy.wait()
    local(full_q, q_w).wait()

    def project_q(t, _):
        q_out[pl.ds(pl.multiple_of(t * tile, tile), tile)] = project(q_w, t, True)
        return 0

    lax.fori_loop(0, width // tile, project_q, 0)
    k_x.wait_recv()
    k_d = send(k1, k3, to_y)
    v_y.wait_recv()
    v_d = send(v2, v3, to_x)
    for s in steps:
        for copy in moves["ffn", s]:
            copy.wait_recv()
        if s < last:
            ffn_step(s + 1)
    for s in steps:
        moves["o", "core", s].wait_recv()
    for copy in (k_y, v_x, k_d, v_d):
        copy.wait_recv()
    for copy in keep + far_ffn:
        copy.wait()
    for copy in sent:
        copy.wait_send()


def front(tokens, gains, key_w, value_w, query_w, out_w, gate_w, up_w, down_w, cosine, sine, zsize, ctx):
    width = tokens.shape[2]
    length = 2 * tokens.shape[1]
    rows = width // zsize
    strip = rows // ctx
    fine = down_w.shape[0] // ctx
    chunk = fine * zsize
    kv_rows = key_w.shape[1]
    chips = ctx // 2
    cut = lambda w: w.reshape(chips, 2, strip, w.shape[1])
    square = jax.ShapeDtypeStruct((zsize, chips, 2, strip, width), BF)
    flat = jax.ShapeDtypeStruct((kv_rows, length), BF)
    hbm, vmem = pl.BlockSpec(memory_space=pl.ANY), pl.BlockSpec(memory_space=pltpu.VMEM)
    copies = 18 * (zsize - 1) + 2 * (zsize - 1) + 8
    return pl.pallas_call(
        functools.partial(front_kernel, zsize),
        out_shape=[
            square, square, square,
            jax.ShapeDtypeStruct((zsize, rows, 2 * chunk), BF),
            jax.ShapeDtypeStruct((zsize, fine, width), BF),
            jax.ShapeDtypeStruct((rows, 2 * chunk), BF),
            jax.ShapeDtypeStruct((fine, width), BF),
            jax.ShapeDtypeStruct((length, width), BF),
            jax.ShapeDtypeStruct((length, width), BF),
            jax.ShapeDtypeStruct((width, length), BF),
            jax.ShapeDtypeStruct((2, width), F32),
        ] + [flat] * 8,
        in_specs=[vmem, vmem] + [hbm] * 7 + [vmem] * 2,
        out_specs=[hbm] * 7 + [vmem] * 4 + [hbm] * 8,
        scratch_shapes=[
            pltpu.VMEM((2, length // 2, width), BF),
            pltpu.VMEM((zsize, 2, rows), F32),
            pltpu.VMEM(square.shape, BF),
            pltpu.VMEM(square.shape, BF),
            pltpu.VMEM((2 * kv_rows, length), BF),
            pltpu.SemaphoreType.DMA((copies,)),
            pltpu.SemaphoreType.DMA((copies,)),
            pltpu.SemaphoreType.DMA((10 + 4 * zsize,)),
            pltpu.SemaphoreType.DMA((zsize,)),
            pltpu.SemaphoreType.DMA((zsize,)),
        ],
        compiler_params=pltpu.CompilerParams(collective_id=0, has_side_effects=True, vmem_limit_bytes=40 * 2**20),
        name="front",
    )(tokens, gains, cut(key_w), cut(value_w), cut(query_w), cut(out_w), gate_w, up_w, down_w, cosine, sine)


def mm(left, right, left_dim, right_dim):
    return lax.dot_general(left, right, (((left_dim,), (right_dim,)), ((), ())), preferred_element_type=F32)


def swap(a):
    return lax.ppermute(a, "ctx", [(i, i ^ 1) for i in range(lax.axis_size("ctx"))])


def hop(a, r):
    return lax.ppermute(a, "ctx", [(i, i ^ (2 * r)) for i in range(lax.axis_size("ctx"))])


def ring(a):
    n = lax.axis_size("fsdp")
    return lax.ppermute(a, "fsdp", [(i, (i + 1) % n) for i in range(n)])


def pick(a, index, axis=0):
    return lax.dynamic_index_in_dim(a, index, axis, keepdims=False)


def place(buffer, piece, index, axis=0):
    return lax.dynamic_update_slice_in_dim(buffer, jnp.expand_dims(piece, axis), index, axis)


def depth_gather(piece, depth):
    n = lax.axis_size("fsdp")
    buffer = place(jnp.zeros((n,) + piece.shape, piece.dtype), piece, depth)
    for s in range(1, n):
        piece = ring(piece)
        buffer = place(buffer, piece, lax.rem(depth + n - s, n))
    return buffer


def depth_gather_direct(piece, depth):
    n = lax.axis_size("fsdp")
    buffer = place(jnp.zeros((n,) + piece.shape, piece.dtype), piece, depth)
    for s in range(1, n):
        moved = lax.ppermute(piece, "fsdp", [(k, (k + s) % n) for k in range(n)])
        buffer = place(buffer, moved, lax.rem(depth + n - s, n))
    return buffer


def depth_scatter(parts, depth):
    n = lax.axis_size("fsdp")
    total = pick(parts, lax.rem(depth + n - 1, n))
    for s in range(n - 1):
        total = ring(total.astype(BF))
        total = total.astype(F32) + pick(parts, lax.rem(depth + 2 * n - 2 - s, n)).astype(F32)
    return total


def plane_gather(piece, index):
    n = lax.axis_size("ctx")
    chips = n // 2
    pieces = jnp.stack([piece] + [hop(piece, r) for r in range(1, chips)])
    others = swap(pieces)
    buffer = jnp.zeros((n,) + piece.shape, piece.dtype)
    for r in range(chips):
        buffer = place(buffer, pieces[r], index ^ (2 * r))
        buffer = place(buffer, others[r], index ^ (2 * r + 1))
    return buffer


def rotate(v, cosine, sine):
    heads = v.reshape(-1, 2, HEAD_WIDTH // 2, v.shape[-1])
    a, b = heads[:, 0], heads[:, 1]
    return jnp.stack([a * cosine - b * sine, b * cosine + a * sine], 1).reshape(v.shape)


def rotate_back(v, cosine, sine):
    heads = v.reshape(-1, 2, HEAD_WIDTH // 2, v.shape[-1])
    a, b = heads[:, 0], heads[:, 1]
    return jnp.stack([a * cosine + b * sine, b * cosine - a * sine], 1).reshape(v.shape)


def norm_back(incoming, unit, inverse, gain):
    scaled = incoming * gain
    return inverse * (scaled - unit * jnp.mean(scaled * unit, -1, keepdims=True))


def body(
    tokens,
    block_pairs,
    cotangent,
    attention_gain,
    query_weight,
    key_matrix,
    value_matrix,
    output_weight,
    feedforward_gain,
    gate_weight,
    up_weight,
    down_weight,
):
    slice_len, width = tokens.shape[1], tokens.shape[2]
    ctx = lax.axis_size("ctx")
    zsize = lax.axis_size("fsdp")
    chips = ctx // 2
    diag = chips - 1
    near = range(1, chips - 1)
    index = lax.axis_index("ctx")
    chip, core = index // 2, lax.rem(index, 2)
    depth = lax.axis_index("fsdp")
    rows = width // zsize
    strip = rows // ctx
    hidden_rows = down_weight.shape[0]
    fine = hidden_rows // ctx
    chunk = fine * zsize
    kv_rows = KEY_HEADS * HEAD_WIDTH

    cot_there = swap(cotangent)
    cot = jnp.concatenate(
        [pick(cotangent, core), pick(cot_there, core), pick(cot_there, 1 - core), pick(cotangent, 1 - core)]
    )
    length = 2 * slice_len

    ids_all = jnp.concatenate([pick(block_pairs, index ^ r) for r in range(ctx)])
    ids = ids_all[:4]
    blocks = ids_all.shape[0]
    order = jnp.sum(
        jnp.where(ids_all[None, :] == jnp.arange(blocks, dtype=jnp.int32)[:, None], jnp.arange(blocks, dtype=jnp.int32)[None, :], 0), 1
    )
    positions = (ids[:, None] * BLK + jnp.arange(BLK, dtype=jnp.int32)[None, :]).reshape(length)
    half = HEAD_WIDTH // 2
    frequency = THETA ** (-jnp.arange(half, dtype=F32) * 2.0 / HEAD_WIDTH)
    angles = frequency[:, None] * positions.astype(F32)[None, :]
    cosine, sine = jnp.cos(angles), jnp.sin(angles)

    gate_up, down, keys, values = {}, {}, {}, {}
    fast = chips == 4 and strip % 16 == 0 and fine % 128 == 0
    if fast:
        (key_value_full, query_full, output_full, wide, tall, far_wide, far_tall, x, first, query, gains_full, *kv) = front(
            tokens, jnp.stack([attention_gain, feedforward_gain]).astype(F32), key_matrix, value_matrix, query_weight,
            output_weight, gate_weight, up_weight, down_weight, cosine, sine, zsize, ctx,
        )
        key_value_full, query_full, output_full = (w.reshape(width, width) for w in (key_value_full, query_full, output_full))
        gate_up[0], down[0] = wide.reshape(width, 2 * chunk), tall.reshape(chunk, width)
        for r in range(chips):
            keys[r], values[r] = kv[r], kv[chips + r]
        x = x.astype(F32)
        gain_first, gain_second = gains_full[0], gains_full[1]
        inverse_first = lax.rsqrt(jnp.mean(x * x, -1, keepdims=True) + EPS)
        unit_first = x * inverse_first
        first_t = jnp.transpose(first)
        gate_up[diag] = depth_gather_direct(far_wide, depth).reshape(width, 2 * chunk)
        down[diag] = depth_gather_direct(far_tall, depth).reshape(chunk, width)
    else:
        gate_cut = gate_weight.reshape(rows, zsize, 2, chips, fine)
        up_cut = up_weight.reshape(rows, zsize, 2, chips, fine)
        down_cut = down_weight.reshape(2, chips, fine, width)

        def own_piece(r):
            gate = pick(pick(gate_cut, core, 2), chip ^ r, 2).reshape(rows, chunk)
            up = pick(pick(up_cut, core, 2), chip ^ r, 2).reshape(rows, chunk)
            down = pick(pick(down_cut, core), chip ^ r)
            return jnp.concatenate([gate, up], 1), down

        gains = jnp.stack([attention_gain, feedforward_gain])
        gain_buffer = place(jnp.zeros((zsize, 2, rows), BF), gains, depth)
        for s in range(1, zsize):
            moved = lax.ppermute(gains, "fsdp", [(k, (k + s) % zsize) for k in range(zsize)])
            gain_buffer = place(gain_buffer, moved, lax.rem(depth + zsize - s, zsize))
        gains_full = jnp.transpose(gain_buffer, (1, 0, 2)).reshape(2, width).astype(F32)
        gain_first, gain_second = gains_full[0], gains_full[1]

        def gather_square(shard):
            strips = shard.reshape(ctx, strip, shard.shape[1])
            pair = jnp.stack([pick(strips, index), pick(strips, index ^ (2 * diag))])
            pair = depth_gather(pair, depth)
            own, far = pair[:, 0], pair[:, 1]
            found = {0: own, diag: far}
            for r in near:
                found[r] = hop(own, r)
            full = jnp.zeros((zsize, ctx, strip, shard.shape[1]), BF)
            for r in range(chips):
                full = place(full, found[r], index ^ (2 * r), 1)
                full = place(full, swap(found[r]), index ^ (2 * r + 1), 1)
            return full.reshape(width, shard.shape[1])

        key_value_full = gather_square(jnp.concatenate([key_matrix, value_matrix], 1))
        query_full = gather_square(query_weight)
        output_full = gather_square(output_weight)

        x = jnp.concatenate([pick(tokens, core), swap(pick(tokens, 1 - core))]).astype(F32)
        wide, tall = own_piece(0)
        gate_up[0] = depth_gather(wide, depth).reshape(width, 2 * chunk)
        down[0] = depth_gather(tall, depth).reshape(chunk, width)
        inverse_first = lax.rsqrt(jnp.mean(x * x, -1, keepdims=True) + EPS)
        unit_first = x * inverse_first
        first = (unit_first * gain_first).astype(BF)
        first_t = jnp.transpose(first)
        kv = mm(key_value_full, first_t, 0, 0)
        keys[0] = rotate(kv[:kv_rows], cosine, sine).astype(BF)
        values[0] = kv[kv_rows:].astype(BF)
        for r in range(1, chips):
            high = 1 << (r.bit_length() - 1)
            low = r & -r
            keys[r] = hop(keys[r ^ high], high)
            values[r] = hop(values[r ^ low], low)
        query = rotate(mm(query_full, first_t, 0, 0), cosine, sine).astype(BF)
        wide, tall = own_piece(diag)
        gate_up[diag] = depth_gather(wide, depth).reshape(width, 2 * chunk)
        down[diag] = depth_gather(tall, depth).reshape(chunk, width)

    for r in near:
        gate_up[r] = hop(gate_up[0], r)
        down[r] = hop(down[0], r)

    key_list = [keys[r] for r in range(chips)]
    value_list = [values[r] for r in range(chips)]
    attended, log_total = attn_fwd(ids, order, query, key_list, value_list, KEY_HEADS)

    middle = x + mm(attended, output_full, 0, 0)
    inverse_second = lax.rsqrt(jnp.mean(middle * middle, -1, keepdims=True) + EPS)
    unit_second = middle * inverse_second
    second = (unit_second * gain_second).astype(BF)
    second = jnp.concatenate([second, swap(second)])
    out_part = 0.0
    second_grad = 0.0
    wide_grad, tall_grad = {}, {}
    for r in [0] + list(near) + [diag]:
        pre = mm(second, gate_up[r], 1, 0)
        gate_pre, up_pre = pre[:, :chunk], pre[:, chunk:]
        hidden_grad = mm(cot, down[r], 1, 1)
        sigmoid = jax.nn.sigmoid(gate_pre)
        silu = gate_pre * sigmoid
        hidden = (silu * up_pre).astype(BF)
        gate_low = (hidden_grad * up_pre * sigmoid * (1.0 + gate_pre * (1.0 - sigmoid))).astype(BF)
        up_low = (hidden_grad * silu).astype(BF)
        both_low = jnp.concatenate([gate_low, up_low], 1)
        tall_grad[r] = mm(hidden, cot, 0, 0).astype(BF)
        wide_grad[r] = mm(second, both_low, 0, 0).astype(BF)
        out_part = out_part + mm(hidden, down[r], 1, 0)
        second_grad = second_grad + mm(both_low, gate_up[r], 1, 1)

    q = slice_len
    out_part = jnp.concatenate([out_part[:length] + middle, out_part[length:]])
    came = swap(jnp.concatenate([out_part[2 * q:3 * q], out_part[q:2 * q]]))
    out_here = (out_part[:q] + came[:q]).astype(BF)
    out_there = (out_part[3 * q:] + came[q:]).astype(BF)

    def stored(here, there):
        return jnp.where(core == 0, jnp.stack([here, there]), jnp.stack([there, here]))

    layer_out = stored(out_here, out_there)

    second_grad = second_grad[:length] + swap(second_grad[length:])
    gain_second_part = jnp.sum(second_grad * unit_second, 0)
    middle_grad = cot[:length].astype(F32) + norm_back(second_grad, unit_second, inverse_second, gain_second)

    def scatter(parts):
        total = parts[0].astype(F32)
        for r in near:
            total = total + hop(parts[r], r).astype(F32)
        far = hop(depth_scatter(parts[diag], depth).astype(BF), diag)
        total = depth_scatter(total.astype(BF), depth) + far.astype(F32)
        return total.astype(BF)

    tall_piece = scatter({r: tall_grad[r].reshape(zsize, fine, width) for r in range(chips)})
    wide_piece = scatter({r: wide_grad[r].reshape(zsize, rows, 2 * chunk) for r in range(chips)})
    tall_all = plane_gather(tall_piece, index)
    wide_all = plane_gather(wide_piece, index)
    down_grad = jnp.transpose(tall_all.reshape(chips, 2, fine, width), (1, 0, 2, 3)).reshape(hidden_rows, width).astype(F32)
    wide_all = wide_all.reshape(chips, 2, rows, 2, zsize, fine)
    gate_grad = jnp.transpose(wide_all[:, :, :, 0], (2, 3, 1, 0, 4)).reshape(rows, -1).astype(F32)
    up_grad = jnp.transpose(wide_all[:, :, :, 1], (2, 3, 1, 0, 4)).reshape(rows, -1).astype(F32)

    middle_low = middle_grad.astype(BF)
    attended_grad = mm(output_full, middle_low, 1, 1).astype(BF)
    query_total, key_parts, value_parts = attn_bwd(
        ids, order, query, attended, attended_grad, log_total, key_list, value_list, KEY_HEADS
    )
    key_sum = [part for part in key_parts]
    value_sum = [part for part in value_parts]
    for r in range(chips - 1, 0, -1):
        high = 1 << (r.bit_length() - 1)
        low = r & -r
        key_sum[r ^ high] = key_sum[r ^ high].astype(F32) + hop(key_sum[r].astype(BF), high).astype(F32)
        value_sum[r ^ low] = value_sum[r ^ low].astype(F32) + hop(value_sum[r].astype(BF), low).astype(F32)
    query_low = rotate_back(query_total, cosine, sine).astype(BF)
    key_low = rotate_back(key_sum[0], cosine, sine).astype(BF)
    value_low = value_sum[0].astype(BF)
    kv_low = jnp.concatenate([key_low, value_low])

    def halves(a):
        cut = a.reshape(zsize, chips, 2, strip, length)
        here = pick(cut, core, 2).reshape(-1, length)
        there = swap(pick(cut, 1 - core, 2).reshape(-1, length))
        return jnp.concatenate([here, there], 1)

    def square_grad(product):
        parts = product.astype(BF).reshape(zsize, chips, strip, width)
        piece = scatter({r: pick(parts, chip ^ r, 1) for r in range(chips)})
        return plane_gather(piece, index).reshape(rows, width).astype(F32)

    first_half = halves(first_t)
    output_grad = square_grad(mm(halves(attended), jnp.concatenate([middle_low, swap(middle_low)]), 1, 0))
    query_grad = square_grad(mm(first_half, jnp.concatenate([query_low, swap(query_low)], 1), 1, 1))
    kv_grad = square_grad(mm(first_half, jnp.concatenate([kv_low, swap(kv_low)], 1), 1, 1))

    first_grad = mm(query_low, query_full, 0, 1) + mm(kv_low, key_value_full, 0, 1)
    gain_first_part = jnp.sum(first_grad * unit_first, 0)
    tokens_part = (middle_grad + norm_back(first_grad, unit_first, inverse_first, gain_first)).astype(BF)
    tokens_grad = stored(tokens_part[:q], swap(tokens_part[q:]))

    def gain_total(part):
        cut = part.reshape(zsize, rows)
        total = pick(cut, depth)
        for s in range(1, zsize):
            total = total + lax.ppermute(
                pick(cut, lax.rem(depth + s, zsize)), "fsdp", [(k, (k + s) % zsize) for k in range(zsize)]
            )
        total = total + swap(total)
        bit = 1
        while bit < chips:
            total = total + hop(total, bit)
            bit *= 2
        return total

    return (
        layer_out,
        tokens_grad,
        gain_total(gain_first_part),
        query_grad,
        kv_grad[:, :kv_rows],
        kv_grad[:, kv_rows:],
        output_grad,
        gain_total(gain_second_part),
        gate_grad,
        up_grad,
        down_grad,
    )


def solution(mesh):
    line, square, grid = P("fsdp"), P("fsdp", None), P("fsdp", "ctx", None)
    in_specs = (grid, P(), grid, line, square, square, square, square, line, square, square, square)
    out_specs = (grid, grid, line, square, square, square, square, line, square, square, square)
    return jax.shard_map(body, mesh=mesh, in_specs=in_specs, out_specs=out_specs, check_vma=False)
```

```python
import functools

import jax
import jax.numpy as jnp
from jax import lax
from jax.experimental import pallas as pl
from jax.experimental.pallas import tpu as pltpu
from jax.sharding import PartitionSpec as P

QUERY_HEADS = 16
KEY_HEADS = 8
HEAD_WIDTH = 96
EPS = 1e-05
THETA = 100000.0
BLK = 128
SCALE = HEAD_WIDTH ** -0.5
BF = jnp.bfloat16
F32 = jnp.float32

LOG2E = 1.4426950408889634

def attn_setup(nchip, g_refs, nat, tr):
    for r in range(nchip):
        for j in range(g_refs[r].shape[1] // 128):
            n = r * (g_refs[r].shape[1] // 128) + j
            block = g_refs[r][:, 128 * j:128 * (j + 1)]
            if nat is not None:
                nat[n] = block.T
            if tr is not None:
                tr[n] = block


def fwd_kernel(nchip, scale, ids_ref, inv_ref, q_ref, *rest):
    k_refs, v_refs = rest[:nchip], rest[nchip:2 * nchip]
    o_ref, lse_ref, knat, vtr, qs, m_s, l_s, acc = rest[2 * nchip:]
    nq = q_ref.shape[1] // 128
    nb = knat.shape[0]
    c = scale * LOG2E
    attn_setup(nchip, k_refs, knat, None)
    attn_setup(nchip, v_refs, None, vtr)
    for qi in range(nq):
        qs[qi] = jnp.concatenate([q_ref[0:96, 128 * qi:128 * (qi + 1)], q_ref[96:192, 128 * qi:128 * (qi + 1)]], axis=1)
    m_s[...] = jnp.full(m_s.shape, -1e30, jnp.float32)
    l_s[...] = jnp.zeros(l_s.shape, jnp.float32)
    acc[...] = jnp.zeros(acc.shape, jnp.float32)
    diff = lax.broadcasted_iota(jnp.int32, (128, 256), 0) - lax.rem(lax.broadcasted_iota(jnp.int32, (128, 256), 1), 128)

    def step(t, _):
        for sl in range(nq // 2):
            first = ids_ref[2 * sl]
            late = (t > first).astype(jnp.int32)
            qi = 2 * sl + late
            kpos = t - late * (first + 1)
            qid = ids_ref[qi]
            n = inv_ref[kpos]
            s = jnp.dot(knat[n], qs[qi], preferred_element_type=jnp.float32)
            s = jnp.where(diff <= (qid - kpos) * 128, s, -jnp.inf)
            m_old = m_s[qi]
            m_new = jnp.maximum(m_old, jnp.max(s, axis=0, keepdims=True))
            p = jnp.exp2((s - m_new) * c)
            alpha = jnp.exp2((m_old - m_new) * c)
            l_s[qi] = l_s[qi] * alpha + jnp.sum(p, axis=0, keepdims=True)
            m_s[qi] = m_new
            acc[qi] = acc[qi] * alpha + jnp.dot(vtr[n], p.astype(jnp.bfloat16), preferred_element_type=jnp.float32)
        return 0

    lax.fori_loop(0, nb + 1, step, 0)
    for qi in range(nq):
        l = l_s[qi]
        o = acc[qi] / l
        lse_ref[qi] = m_s[qi] * c + jnp.log2(l)
        o_ref[0:96, 128 * qi:128 * (qi + 1)] = o[:, :128].astype(jnp.bfloat16)
        o_ref[96:192, 128 * qi:128 * (qi + 1)] = o[:, 128:].astype(jnp.bfloat16)


def attn_fwd(ids, inv, qT, ks, vs, heads):
    nchip = len(ks)
    T = qT.shape[1]
    nq = T // 128
    nb = nchip * nq
    grid_spec = pltpu.PrefetchScalarGridSpec(
        num_scalar_prefetch=2,
        grid=(heads,),
        in_specs=[pl.BlockSpec((192, T), lambda g, *_: (g, 0))] + [pl.BlockSpec((96, T), lambda g, *_: (g, 0))] * (2 * nchip),
        out_specs=[pl.BlockSpec((192, T), lambda g, *_: (g, 0)), pl.BlockSpec((None, nq, 1, 256), lambda g, *_: (g, 0, 0, 0))],
        scratch_shapes=[
            pltpu.VMEM((nb, 128, 96), jnp.bfloat16),
            pltpu.VMEM((nb, 96, 128), jnp.bfloat16),
            pltpu.VMEM((nq, 96, 256), jnp.bfloat16),
            pltpu.VMEM((nq, 1, 256), jnp.float32),
            pltpu.VMEM((nq, 1, 256), jnp.float32),
            pltpu.VMEM((nq, 96, 256), jnp.float32),
        ],
    )
    return pl.pallas_call(
        functools.partial(fwd_kernel, nchip, SCALE),
        grid_spec=grid_spec,
        out_shape=[jax.ShapeDtypeStruct((heads * 192, T), jnp.bfloat16), jax.ShapeDtypeStruct((heads, nq, 1, 256), jnp.float32)],
        cost_estimate=pl.CostEstimate(flops=90 * 10**9, bytes_accessed=16 * 2**20, transcendentals=0),
        name="attention_forward",
    )(ids, inv, qT, *ks, *vs)


def bwd_kernel(nchip, scale, ids_ref, inv_ref, q_ref, o_ref, do_ref, lse_ref, cos_ref, sin_ref, *rest):
    k_refs, v_refs = rest[:nchip], rest[nchip:2 * nchip]
    dq_ref = rest[2 * nchip]
    dk_refs, dv_refs = rest[2 * nchip + 1:3 * nchip + 1], rest[3 * nchip + 1:4 * nchip + 1]
    knat, ktr, vnat, qs, dos, delta, dq_s, dk_s, dv_s = rest[4 * nchip + 1:]
    nq = q_ref.shape[1] // 128
    nb = knat.shape[0]
    nsl = nq // 2
    c = scale * LOG2E
    attn_setup(nchip, k_refs, knat, ktr)
    attn_setup(nchip, v_refs, vnat, None)
    for qi in range(nq):
        lanes = slice(128 * qi, 128 * (qi + 1))
        qs[qi] = jnp.concatenate([q_ref[0:96, lanes], q_ref[96:192, lanes]], axis=1)
        do = jnp.concatenate([do_ref[0:96, lanes], do_ref[96:192, lanes]], axis=1)
        dos[qi] = do
        o = jnp.concatenate([o_ref[0:96, lanes], o_ref[96:192, lanes]], axis=1)
        delta[qi] = jnp.sum(o.astype(jnp.float32) * do.astype(jnp.float32), axis=0, keepdims=True)
    dq_s[...] = jnp.zeros(dq_s.shape, jnp.float32)
    dk_s[...] = jnp.zeros(dk_s.shape, jnp.float32)
    dv_s[...] = jnp.zeros(dv_s.shape, jnp.float32)
    diff = lax.broadcasted_iota(jnp.int32, (128, 256), 0) - lax.rem(lax.broadcasted_iota(jnp.int32, (128, 256), 1), 128)
    nt = (((1,), (1,)), ((), ()))

    def step(t, _):
        for sl in range(nsl):
            first = ids_ref[2 * sl]
            late = (t > first).astype(jnp.int32)
            qi = 2 * sl + late
            kpos = t - late * (first + 1)
            qid = ids_ref[qi]
            n = inv_ref[kpos]
            q, do = qs[qi], dos[qi]
            s = jnp.dot(knat[n], q, preferred_element_type=jnp.float32)
            p = jnp.exp2(jnp.where(diff <= (qid - kpos) * 128, s * c - lse_ref[qi], -jnp.inf))
            dp = jnp.dot(vnat[n], do, preferred_element_type=jnp.float32)
            ds = (p * (dp - delta[qi])).astype(jnp.bfloat16)
            dv_s[sl, n] += lax.dot_general(do, p.astype(jnp.bfloat16), nt, preferred_element_type=jnp.float32)
            dk_s[sl, n] += lax.dot_general(q, ds, nt, preferred_element_type=jnp.float32)
            dq_s[qi] += jnp.dot(ktr[n], ds, preferred_element_type=jnp.float32)
        return 0

    lax.fori_loop(0, nb + 1, step, 0)
    for qi in range(nq):
        lanes = slice(128 * qi, 128 * (qi + 1))
        cos, sin = cos_ref[:, lanes], sin_ref[:, lanes]
        for h in range(2):
            a = dq_s[qi, 0:48, 128 * h:128 * (h + 1)] * scale
            b = dq_s[qi, 48:96, 128 * h:128 * (h + 1)] * scale
            dq_ref[96 * h:96 * h + 48, lanes] = (a * cos + b * sin).astype(jnp.bfloat16)
            dq_ref[96 * h + 48:96 * h + 96, lanes] = (b * cos - a * sin).astype(jnp.bfloat16)
    for r in range(nchip):
        for j in range(nq):
            n = r * nq + j
            dk = dk_s[0, n]
            dv = dv_s[0, n]
            for sl in range(1, nsl):
                dk = dk + dk_s[sl, n]
                dv = dv + dv_s[sl, n]
            dk_refs[r][:, 128 * j:128 * (j + 1)] = (dk * scale).astype(jnp.bfloat16)
            dv_refs[r][:, 128 * j:128 * (j + 1)] = dv.astype(jnp.bfloat16)


def attn_bwd(ids, inv, qT, oT, doT, lse, cosine, sine, ks, vs, heads):
    nchip = len(ks)
    T = qT.shape[1]
    nq = T // 128
    nb = nchip * nq
    wide = pl.BlockSpec((192, T), lambda g, *_: (g, 0))
    slim = pl.BlockSpec((96, T), lambda g, *_: (g, 0))
    grid_spec = pltpu.PrefetchScalarGridSpec(
        num_scalar_prefetch=2,
        grid=(heads,),
        in_specs=[wide, wide, wide, pl.BlockSpec((None, nq, 1, 256), lambda g, *_: (g, 0, 0, 0))]
        + [pl.BlockSpec((48, T), lambda g, *_: (0, 0))] * 2 + [slim] * (2 * nchip),
        out_specs=[wide] + [slim] * (2 * nchip),
        scratch_shapes=[
            pltpu.VMEM((nb, 128, 96), jnp.bfloat16),
            pltpu.VMEM((nb, 96, 128), jnp.bfloat16),
            pltpu.VMEM((nb, 128, 96), jnp.bfloat16),
            pltpu.VMEM((nq, 96, 256), jnp.bfloat16),
            pltpu.VMEM((nq, 96, 256), jnp.bfloat16),
            pltpu.VMEM((nq, 1, 256), jnp.float32),
            pltpu.VMEM((nq, 96, 256), jnp.float32),
            pltpu.VMEM((nq // 2, nb, 96, 128), jnp.float32),
            pltpu.VMEM((nq // 2, nb, 96, 128), jnp.float32),
        ],
    )
    slab = jax.ShapeDtypeStruct((heads * 96, T), jnp.bfloat16)
    outs = pl.pallas_call(
        functools.partial(bwd_kernel, nchip, SCALE),
        grid_spec=grid_spec,
        out_shape=[jax.ShapeDtypeStruct((heads * 192, T), jnp.bfloat16)] + [slab] * (2 * nchip),
        cost_estimate=pl.CostEstimate(flops=90 * 10**9, bytes_accessed=24 * 2**20, transcendentals=0),
        name="attention_backward",
    )(ids, inv, qT, oT, doT, lse, cosine, sine, *ks, *vs)
    return outs[0], outs[1:1 + nchip], outs[1 + nchip:]


def front_kernel(zsize, *refs):
    (tok, gains, key_w, value_w, query_w, out_w, gate_w, up_w, down_w, cos, sin) = refs[:11]
    (full_kv, full_q, full_o, wide, tall, far_wide, far_tall, x_out, first, q_out, gains_out, k0, k1, k2, k3, v0, v1, v2, v3) = refs[11:30]
    x_s, gain_s, kv_w, q_w, kv_s, ss, rs, ls, gs, gr = refs[30:]
    ks, vs = (k0, k1, k2, k3), (v0, v1, v2, v3)
    index, depth = lax.axis_index("ctx"), lax.axis_index("fsdp")
    chip, core = index // 2, lax.rem(index, 2)
    fine = tall.shape[1]
    chunk = fine * zsize
    width = first.shape[1]
    length = first.shape[0]
    kv_rows = k0.shape[0]
    nxt, prv = lax.rem(depth + 1, zsize), lax.rem(depth + zsize - 1, zsize)
    to_next, to_prev = (index, nxt), (index, prv)
    chip_x, chip_y, chip_d = chip + 1 - 2 * lax.rem(chip, 2), lax.rem(chip + 2, 4), 3 - chip
    to_x, to_y, to_core = (chip_x * 2 + core, depth), (chip_y * 2 + core, depth), (chip * 2 + 1 - core, depth)

    barrier = pltpu.get_barrier_semaphore()
    for target in (to_next, to_prev, to_x, to_y, to_core):
        pl.semaphore_signal(barrier, inc=1, device_id=target, device_id_type=pl.DeviceIdType.MESH)
    pl.semaphore_wait(barrier, 5)

    count = [0, 0]
    sent = []

    def send(src, dst, target):
        k = count[0]
        count[0] += 1
        copy = pltpu.make_async_remote_copy(
            src_ref=src, dst_ref=dst, send_sem=ss.at[k], recv_sem=rs.at[k], device_id=target, device_id_type=pl.DeviceIdType.MESH
        )
        copy.start()
        sent.append(copy)
        return copy

    def local(src, dst):
        k = count[1]
        count[1] += 1
        copy = pltpu.make_async_copy(src, dst, ls.at[k])
        copy.start()
        return copy

    def slot(s):
        return lax.rem(depth + zsize - s, zsize)

    steps = range(1, zsize)
    last = zsize - 1
    tokens_there = send(tok.at[1 - core], x_s.at[1], to_core)
    own_kv = [local(key_w, full_kv.at[depth, :, :, :, pl.ds(0, kv_rows)]), local(value_w, full_kv.at[depth, :, :, :, pl.ds(kv_rows, kv_rows)])]
    gain_s[depth] = gains[...]
    for copy in own_kv:
        copy.wait()

    weights = {"kv": full_kv, "q": full_q, "o": full_o}
    shards = {"q": query_w, "o": out_w}
    moves = {}

    def ring_step(name, s):
        full = weights[name]
        place = full.at[slot(s - 1), chip, core]
        source = shards[name].at[chip, core] if name in shards and s == 1 else place
        moves[name, "ring", s] = send(source, place, to_next)

    def spread(name, s):
        place = weights[name].at[slot(s), chip, core]
        moves[name, "x", s] = send(place, place, to_x)
        moves[name, "y", s] = send(place, place, to_y)

    def forward(name, s):
        mid = width // 2
        moves[name, "x", s].wait_recv()
        left = weights[name].at[slot(s), chip_x, core, :, pl.ds(0, mid)]
        moves[name, "fy", s] = send(left, left, to_y)
        moves[name, "y", s].wait_recv()
        right = weights[name].at[slot(s), chip_y, core, :, pl.ds(mid, mid)]
        moves[name, "fx", s] = send(right, right, to_x)

    def cross(name, s):
        moves[name, "fx", s].wait_recv()
        moves[name, "fy", s].wait_recv()
        column = weights[name].at[slot(s), :, core]
        moves[name, "core", s] = send(column, column, to_core)

    def gain_step(s):
        place = gain_s.at[slot(s - 1)]
        copy = pltpu.make_async_remote_copy(
            src_ref=place, dst_ref=place, send_sem=gs.at[s], recv_sem=gr.at[s], device_id=to_next, device_id_type=pl.DeviceIdType.MESH
        )
        copy.start()
        sent.append(copy)
        moves["gain", s] = copy

    ring_step("kv", 1)
    gain_step(1)
    own_late = [local(query_w, full_q.at[depth]), local(out_w, full_o.at[depth])]
    own_ffn = [local(down_w.at[pl.ds(pl.multiple_of(core * (4 * fine) + chip * fine, fine), fine)], tall.at[depth])]
    for part in range(zsize):
        column = pl.multiple_of(part * (8 * fine) + core * (4 * fine) + chip * fine, fine)
        own_ffn.append(local(gate_w.at[:, pl.ds(column, fine)], wide.at[depth, :, pl.ds(part * fine, fine)]))
        own_ffn.append(local(up_w.at[:, pl.ds(column, fine)], wide.at[depth, :, pl.ds(chunk + part * fine, fine)]))
    far_ffn = [local(down_w.at[pl.ds(pl.multiple_of(core * (4 * fine) + chip_d * fine, fine), fine)], far_tall)]
    for part in range(zsize):
        column = pl.multiple_of(part * (8 * fine) + core * (4 * fine) + chip_d * fine, fine)
        far_ffn.append(local(gate_w.at[:, pl.ds(column, fine)], far_wide.at[:, pl.ds(part * fine, fine)]))
        far_ffn.append(local(up_w.at[:, pl.ds(column, fine)], far_wide.at[:, pl.ds(chunk + part * fine, fine)]))

    for s in steps:
        moves["kv", "ring", s].wait_recv()
        moves["gain", s].wait_recv()
        if s < last:
            ring_step("kv", s + 1)
            gain_step(s + 1)
        else:
            ring_step("q", 1)
        spread("kv", s)
    for s in steps:
        forward("kv", s)
        moves["q", "ring", s].wait_recv()
        ring_step("q", s + 1) if s < last else ring_step("o", 1)
        spread("q", s)
    for s in steps:
        cross("kv", s)

    tokens_there.wait_recv()
    x_out[0:length // 2] = tok[core]
    x_out[length // 2:] = x_s[1]
    gain_rows = [gain_s[place] for place in range(zsize)]
    gains_full = jnp.concatenate(gain_rows, axis=1)
    gains_out[...] = gains_full
    gain = gains_full[0:1]
    rows = 64

    def normalize(t, _):
        part = pl.ds(pl.multiple_of(t * rows, rows), rows)
        v = x_out[part].astype(F32)
        inverse = lax.rsqrt(jnp.mean(v * v, -1, keepdims=True) + EPS)
        first[part] = (v * inverse * gain).astype(BF)
        return 0

    lax.fori_loop(0, length // rows, normalize, 0)

    moves["o", "ring", 1].wait_recv()
    if last > 1:
        ring_step("o", 2)
    spread("o", 1)
    for s in steps:
        moves["kv", "core", s].wait_recv()
    load_kv = local(full_kv, kv_w)
    if last > 1:
        moves["o", "ring", 2].wait_recv()
        if last > 2:
            ring_step("o", 3)
        spread("o", 2)
    load_kv.wait()
    tile = 384

    def project(weight, t, turn):
        cols = pl.ds(pl.multiple_of(t * tile, tile), tile)
        w = weight[:, :, :, :, cols].reshape(width, tile)
        r = jnp.dot(first[...], w, preferred_element_type=F32).T
        if turn:
            r = rotate(r, cos[...], sin[...])
        return r.astype(BF)

    def project_kv(t, turn):
        kv_s[pl.ds(pl.multiple_of(t * tile, tile), tile)] = project(kv_w, t, turn)
        return 0

    per = kv_rows // tile
    lax.fori_loop(0, per, lambda t, _: project_kv(t, True), 0)
    k_here, v_here = kv_s.at[pl.ds(0, kv_rows)], kv_s.at[pl.ds(kv_rows, kv_rows)]
    k_x, k_y = send(k_here, k1, to_x), send(k_here, k2, to_y)
    lax.fori_loop(per, 2 * per, lambda t, _: project_kv(t, False), 0)
    v_y, v_x = send(v_here, v2, to_y), send(v_here, v1, to_x)
    keep = [local(k_here, k0), local(v_here, v0)]

    for s in range(3, zsize):
        moves["o", "ring", s].wait_recv()
        if s < last:
            ring_step("o", s + 1)
        spread("o", s)
    for copy in own_ffn:
        copy.wait()

    def ffn_step(s):
        a, b = wide.at[slot(s - 1)], tall.at[slot(s - 1)]
        moves["ffn", s] = (send(a, a, to_next), send(b, b, to_next))

    ffn_step(1)
    for s in steps:
        forward("q", s)
    for s in steps:
        cross("q", s)
    for s in steps:
        forward("o", s)
    for s in steps:
        cross("o", s)
    for s in steps:
        moves["q", "core", s].wait_recv()
    for copy in own_late:
        copy.wait()
    local(full_q, q_w).wait()

    def project_q(t, _):
        q_out[pl.ds(pl.multiple_of(t * tile, tile), tile)] = project(q_w, t, True)
        return 0

    lax.fori_loop(0, width // tile, project_q, 0)
    k_x.wait_recv()
    k_d = send(k1, k3, to_y)
    v_y.wait_recv()
    v_d = send(v2, v3, to_x)
    for s in steps:
        for copy in moves["ffn", s]:
            copy.wait_recv()
        if s < last:
            ffn_step(s + 1)
    for s in steps:
        moves["o", "core", s].wait_recv()
    for copy in (k_y, v_x, k_d, v_d):
        copy.wait_recv()
    for copy in keep + far_ffn:
        copy.wait()
    for copy in sent:
        copy.wait_send()


def front(tokens, gains, key_w, value_w, query_w, out_w, gate_w, up_w, down_w, cosine, sine, zsize, ctx):
    width = tokens.shape[2]
    length = 2 * tokens.shape[1]
    rows = width // zsize
    strip = rows // ctx
    fine = down_w.shape[0] // ctx
    chunk = fine * zsize
    kv_rows = key_w.shape[1]
    chips = ctx // 2
    cut = lambda w: w.reshape(chips, 2, strip, w.shape[1])
    square = jax.ShapeDtypeStruct((zsize, chips, 2, strip, width), BF)
    flat = jax.ShapeDtypeStruct((kv_rows, length), BF)
    hbm, vmem = pl.BlockSpec(memory_space=pl.ANY), pl.BlockSpec(memory_space=pltpu.VMEM)
    copies = 18 * (zsize - 1) + 2 * (zsize - 1) + 8
    return pl.pallas_call(
        functools.partial(front_kernel, zsize),
        out_shape=[
            square, square, square,
            jax.ShapeDtypeStruct((zsize, rows, 2 * chunk), BF),
            jax.ShapeDtypeStruct((zsize, fine, width), BF),
            jax.ShapeDtypeStruct((rows, 2 * chunk), BF),
            jax.ShapeDtypeStruct((fine, width), BF),
            jax.ShapeDtypeStruct((length, width), BF),
            jax.ShapeDtypeStruct((length, width), BF),
            jax.ShapeDtypeStruct((width, length), BF),
            jax.ShapeDtypeStruct((2, width), F32),
        ] + [flat] * 8,
        in_specs=[vmem, vmem] + [hbm] * 7 + [vmem] * 2,
        out_specs=[hbm] * 7 + [vmem] * 4 + [hbm] * 8,
        scratch_shapes=[
            pltpu.VMEM((2, length // 2, width), BF),
            pltpu.VMEM((zsize, 2, rows), F32),
            pltpu.VMEM(square.shape, BF),
            pltpu.VMEM(square.shape, BF),
            pltpu.VMEM((2 * kv_rows, length), BF),
            pltpu.SemaphoreType.DMA((copies,)),
            pltpu.SemaphoreType.DMA((copies,)),
            pltpu.SemaphoreType.DMA((10 + 4 * zsize,)),
            pltpu.SemaphoreType.DMA((zsize,)),
            pltpu.SemaphoreType.DMA((zsize,)),
        ],
        compiler_params=pltpu.CompilerParams(collective_id=0, has_side_effects=True, vmem_limit_bytes=40 * 2**20),
        name="front",
    )(tokens, gains, cut(key_w), cut(value_w), cut(query_w), cut(out_w), gate_w, up_w, down_w, cosine, sine)


def tail_kernel(zsize, *refs):
    dk, dv = refs[0:4], refs[4:8]
    dq, cos, sin, first_half, out_grad = refs[8:13]
    wide_in, tall_in = refs[13:16], refs[16:19]
    far_wide_in, far_tall_in = refs[19:19 + zsize], refs[19 + zsize:19 + 2 * zsize]
    rest = refs[19 + 2 * zsize:]
    o_all, q_all, kv_all, wide_all, tall_all, kv_low = rest[:6]
    (got, held, dq_pair, kv_pair, half, grads, gl, gr, gx, gy, gz, piece, wide_s, tall_s, wide_0, tall_0, wide_z, tall_z,
     wide_f, tall_f, wide_r, tall_r, wide_p, tall_p, ss, rs, ls) = rest[6:]
    index, depth = lax.axis_index("ctx"), lax.axis_index("fsdp")
    chip, core = index // 2, lax.rem(index, 2)
    chip_x, chip_y, chip_d = chip + 1 - 2 * lax.rem(chip, 2), lax.rem(chip + 2, 4), 3 - chip
    nxt, prv = lax.rem(depth + 1, zsize), lax.rem(depth + zsize - 1, zsize)
    to_next, to_prev = (index, nxt), (index, prv)
    to_x, to_y, to_core = (chip_x * 2 + core, depth), (chip_y * 2 + core, depth), (chip * 2 + 1 - core, depth)
    to_far = (chip_d * 2 + core, depth)
    last = zsize - 1
    kv_rows = dk[0].shape[0]
    width = first_half.shape[0] * 2
    strip = piece.shape[1]
    length = dq.shape[1]

    barrier = pltpu.get_barrier_semaphore()
    for target in (to_next, to_prev, to_x, to_y, to_core, to_far):
        pl.semaphore_signal(barrier, inc=1, device_id=target, device_id_type=pl.DeviceIdType.MESH)
    pl.semaphore_wait(barrier, 6)

    count = [0, 0]
    sent, kept = [], []

    def send(src, dst, target):
        k = count[0]
        count[0] += 1
        copy = pltpu.make_async_remote_copy(
            src_ref=src, dst_ref=dst, send_sem=ss.at[k], recv_sem=rs.at[k], device_id=target, device_id_type=pl.DeviceIdType.MESH
        )
        copy.start()
        sent.append(copy)
        return copy

    def local(src, dst):
        k = count[1]
        count[1] += 1
        copy = pltpu.make_async_copy(src, dst, ls.at[k])
        copy.start()
        return copy

    def wait_all(copies):
        for copy in copies:
            copy.wait()

    def received(*copies):
        for copy in copies:
            copy.wait_recv()

    def add_rows(target, sources, block):
        def one(t, _):
            part = pl.ds(pl.multiple_of(t * block, block), block)
            total = target[part].astype(F32)
            for source in sources:
                total = total + source[part].astype(F32)
            target[part] = total.astype(BF)
            return 0

        lax.fori_loop(0, target.shape[0] // block, one, 0)

    def place_at(j):
        return lax.rem(depth + 2 * zsize - 1 - j, zsize)

    k3, v3 = send(dk[3], got.at[0], to_y), send(dv[3], got.at[1], to_x)
    q_swap = send(dq, dq_pair.at[1], to_core)

    def load_ffn(j):
        slot = lax.rem(j, 2) if not isinstance(j, int) else j % 2
        return [local(wide_in[n].at[place_at(j)], wide_s.at[slot, n]) for n in range(3)] + [
            local(tall_in[n].at[place_at(j)], tall_s.at[slot, n]) for n in range(3)]

    ffn_loads = {0: load_ffn(0)}
    load_o = local(out_grad, grads.at[0])
    load_q = [local(dq, dq_pair.at[0]), local(first_half, half)]
    load_kv = [local(dk[0], held.at[0]), local(dk[1], held.at[1]), local(dv[0], held.at[2]), local(dv[2], held.at[3])]
    load_far = [local(far_wide_in[0].at[depth], wide_f.at[0]), local(far_tall_in[0].at[depth], tall_f.at[0])]
    for n in range(1, zsize):
        load_far += [local(far_wide_in[n], wide_f.at[n]), local(far_tall_in[n], tall_f.at[n])]

    moves = {}

    def ffn_step(j):
        if j + 1 <= last:
            ffn_loads[j + 1] = load_ffn(j + 1)
        wait_all(ffn_loads[j])
        w = [wide_s.at[j % 2, n] for n in range(3)]
        t = [tall_s.at[j % 2, n] for n in range(3)]
        if j == 0:
            sum_rows(wide_0, w, 64)
            sum_rows(tall_0, t, 64)
            moves["wide", 0], moves["tall", 0] = send(wide_0, wide_z.at[0], to_next), send(tall_0, tall_z.at[0], to_next)
            return
        received(moves["tall", j - 1])
        add_rows(tall_z.at[j - 1], t, 64)
        if j < last:
            moves["tall", j] = send(tall_z.at[j - 1], tall_z.at[j], to_next)
        received(moves["wide", j - 1])
        add_rows(wide_z.at[j - 1], w, 64)
        if j < last:
            moves["wide", j] = send(wide_z.at[j - 1], wide_z.at[j], to_next)

    def sum_rows(target, sources, block):
        def one(t, _):
            part = pl.ds(pl.multiple_of(t * block, block), block)
            total = sources[0][part].astype(F32)
            for source in sources[1:]:
                total = total + source[part].astype(F32)
            target[part] = total.astype(BF)
            return 0

        lax.fori_loop(0, target.shape[0] // block, one, 0)

    mid = width // 2
    tiles = 512

    def stage_1(m):
        moves["l", m] = send(grads.at[m, :, chip_d, :, pl.ds(0, mid)], gl.at[m], to_y)
        moves["r", m] = send(grads.at[m, :, chip_d, :, pl.ds(mid, mid)], gr.at[m], to_x)

    def stage_2(m):
        received(moves["l", m])

        def left(zz, _):
            grads[m, zz, chip_x, :, 0:mid] = (grads[m, zz, chip_x, :, 0:mid].astype(F32) + gl[m, zz].astype(F32)).astype(BF)
            return 0

        lax.fori_loop(0, zsize, left, 0)
        moves["x", m] = send(grads.at[m, :, chip_x], gx.at[m], to_x)
        received(moves["r", m])

        def right(zz, _):
            grads[m, zz, chip_y, :, mid:] = (grads[m, zz, chip_y, :, mid:].astype(F32) + gr[m, zz].astype(F32)).astype(BF)
            return 0

        lax.fori_loop(0, zsize, right, 0)
        moves["y", m] = send(grads.at[m, :, chip_y], gy.at[m], to_y)

    def stage_3(m):
        received(moves["x", m], moves["y", m])

        def own(zz, _):
            grads[m, zz, chip] = (grads[m, zz, chip].astype(F32) + gx[m, zz].astype(F32) + gy[m, zz].astype(F32)).astype(BF)
            return 0

        lax.fori_loop(0, zsize, own, 0)
        moves["z", m, 0] = send(grads.at[m, place_at(0), chip], gz.at[m, 0], to_next)

    def ring_step(m, j):
        received(moves["z", m, j - 1])
        total = gz[m, j - 1].astype(F32) + grads[m, place_at(j), chip].astype(F32)
        if j < last:
            gz[m, j - 1] = total.astype(BF)
            moves["z", m, j] = send(gz.at[m, j - 1], gz.at[m, j], to_next)
        else:
            piece[m] = total.astype(BF)

    def spread(name, source, target):
        kept.append(local(source, target.at[chip, core]))
        moves[name, "x"] = send(source, target.at[chip, core], to_x)
        moves[name, "y"] = send(source, target.at[chip, core], to_y)

    def forward(name, target):
        middle = target.shape[3] // 2
        received(moves[name, "x"])
        left = target.at[chip_x, core, :, pl.ds(0, middle)]
        moves[name, "fy"] = send(left, left, to_y)
        received(moves[name, "y"])
        right = target.at[chip_y, core, :, pl.ds(middle, middle)]
        moves[name, "fx"] = send(right, right, to_x)

    def cross(name, target):
        received(moves[name, "fx"], moves[name, "fy"])
        column = target.at[:, core]
        moves[name, "core"] = send(column, column, to_core)

    def product(m, pair):
        per = width // tiles

        def one(t, _):
            zz = t // per
            cols = pl.ds(pl.multiple_of(lax.rem(t, per) * tiles, tiles), tiles)
            rows = pl.ds(pl.multiple_of(zz * (4 * strip), 4 * strip), 4 * strip)
            nt = (((1,), (1,)), ((), ()))
            r = lax.dot_general(half[rows, 0:length], pair[0, cols], nt, preferred_element_type=F32)
            r = r + lax.dot_general(half[rows, length:], pair[1, cols], nt, preferred_element_type=F32)
            grads[m, zz, :, :, cols] = r.astype(BF).reshape(4, strip, tiles)
            return 0

        lax.fori_loop(0, zsize * per, one, 0)

    ffn_step(0)
    load_o.wait()
    stage_1(0)
    received(q_swap)
    wait_all(load_q)
    product(1, dq_pair)
    stage_1(1)

    received(k3)
    wait_all(load_kv)
    add_rows(held.at[1], [got.at[0]], 96)
    k1 = send(held.at[1], got.at[2], to_x)
    received(v3)
    add_rows(held.at[3], [got.at[1]], 96)
    v2 = send(held.at[3], got.at[3], to_y)
    k2, v1 = send(dk[2], got.at[4], to_y), send(dv[1], got.at[5], to_x)
    if last > 1:
        ffn_step(1)
    received(k1, k2, v1, v2)

    def finish_keys(h, _):
        rows = pl.ds(pl.multiple_of(h * 96, 96), 96)
        v = held[0, rows].astype(F32) + got[2, rows].astype(F32) + got[4, rows].astype(F32)
        kv_pair[0, rows] = rotate_back(v, cos[...], sin[...]).astype(BF)
        return 0

    def finish_values(h, _):
        rows = pl.ds(pl.multiple_of(h * 96, 96), 96)
        v = held[2, rows].astype(F32) + got[3, rows].astype(F32) + got[5, rows].astype(F32)
        kv_pair[0, pl.ds(pl.multiple_of(kv_rows + h * 96, 96), 96)] = v.astype(BF)
        return 0

    lax.fori_loop(0, kv_rows // 96, finish_keys, 0)
    lax.fori_loop(0, kv_rows // 96, finish_values, 0)
    kv_swap = send(kv_pair.at[0], kv_pair.at[1], to_core)
    kept.append(local(kv_pair.at[0], kv_low))
    stage_2(0)
    stage_2(1)
    if last > 2:
        ffn_step(2)
    wait_all(load_far)
    add_rows(wide_f.at[0], [wide_f.at[n] for n in range(1, zsize)], 64)
    add_rows(tall_f.at[0], [tall_f.at[n] for n in range(1, zsize)], 64)
    far = send(wide_f.at[0], wide_r, to_far), send(tall_f.at[0], tall_r, to_far)
    received(kv_swap)
    product(2, kv_pair)
    stage_1(2)
    stage_3(0)
    stage_3(1)
    stage_2(2)
    for j in range(3, last):
        ffn_step(j)
    ffn_step(last)
    received(*far)

    def whole_wide(t, _):
        part = pl.ds(pl.multiple_of(t * 64, 64), 64)
        wide_p[part] = (wide_z[last - 1, part].astype(F32) + wide_r[part].astype(F32)).astype(BF)
        return 0

    def whole_tall(t, _):
        part = pl.ds(pl.multiple_of(t * 64, 64), 64)
        tall_p[part] = (tall_z[last - 1, part].astype(F32) + tall_r[part].astype(F32)).astype(BF)
        return 0

    lax.fori_loop(0, tall_p.shape[0] // 64, whole_tall, 0)
    spread("tall", tall_p, tall_all)
    lax.fori_loop(0, wide_p.shape[0] // 64, whole_wide, 0)
    spread("wide", wide_p, wide_all)
    for j in range(1, zsize):
        ring_step(0, j)
        ring_step(1, j)
        if j == 1:
            stage_3(2)
    spread(0, piece.at[0], o_all)
    spread(1, piece.at[1], q_all)
    for j in range(1, zsize):
        ring_step(2, j)
    spread(2, piece.at[2], kv_all)
    targets = (("tall", tall_all), ("wide", wide_all), (0, o_all), (1, q_all), (2, kv_all))
    for name, target in targets:
        forward(name, target)
    wait_all(kept)
    for name, target in targets:
        cross(name, target)
    for name, target in targets:
        received(moves[name, "core"])
    for copy in sent:
        copy.wait_send()


def tail(dk, dv, dq, cosine, sine, first_half, out_grad, wide, tall, far_wide, far_tall, zsize, chips):
    kv_rows, length = dk[0].shape
    width = 2 * kv_rows
    strip = out_grad.shape[2]
    rows, two = wide[0].shape[1:]
    fine = tall[0].shape[1]
    hbm, vmem = pl.BlockSpec(memory_space=pl.ANY), pl.BlockSpec(memory_space=pltpu.VMEM)
    shape = lambda *s: jax.ShapeDtypeStruct(s, BF)
    store = lambda *s: pltpu.VMEM(s, BF)
    copies = 6 + 2 + 1 + 2 * (zsize - 1) + 3 * (4 + zsize - 1) + 5 * 5 + 2
    inputs = [*dk, *dv, dq, cosine, sine, first_half, out_grad, *wide, *tall, *far_wide, *far_tall]
    last = zsize - 1
    return pl.pallas_call(
        functools.partial(tail_kernel, zsize),
        out_shape=[shape(chips, 2, strip, width)] * 3 + [shape(chips, 2, rows, two), shape(chips, 2, fine, width), shape(width, length)],
        in_specs=[hbm] * 9 + [vmem] * 2 + [hbm] * (len(inputs) - 11),
        out_specs=[hbm] * 6,
        scratch_shapes=[
            store(6, kv_rows, length), store(4, kv_rows, length), store(2, width, length), store(2, width, length),
            store(width // 2, 2 * length), store(3, zsize, chips, strip, width),
            store(3, zsize, strip, width // 2), store(3, zsize, strip, width // 2),
            store(3, zsize, strip, width), store(3, zsize, strip, width),
            store(3, last, strip, width), store(3, strip, width),
            store(2, 3, rows, two), store(2, 3, fine, width), store(rows, two), store(fine, width),
            store(last, rows, two), store(last, fine, width),
            store(zsize, rows, two), store(zsize, fine, width), store(rows, two), store(fine, width), store(rows, two), store(fine, width),
            pltpu.SemaphoreType.DMA((copies,)), pltpu.SemaphoreType.DMA((copies,)),
            pltpu.SemaphoreType.DMA((6 * zsize + 8 + 2 * zsize + 6,)),
        ],
        compiler_params=pltpu.CompilerParams(collective_id=1, has_side_effects=True, vmem_limit_bytes=60 * 2**20),
        name="tail",
    )(*inputs)


def mm(left, right, left_dim, right_dim):
    return lax.dot_general(left, right, (((left_dim,), (right_dim,)), ((), ())), preferred_element_type=F32)


def swap(a):
    return lax.ppermute(a, "ctx", [(i, i ^ 1) for i in range(lax.axis_size("ctx"))])


def hop(a, r):
    return lax.ppermute(a, "ctx", [(i, i ^ (2 * r)) for i in range(lax.axis_size("ctx"))])


def ring(a):
    n = lax.axis_size("fsdp")
    return lax.ppermute(a, "fsdp", [(i, (i + 1) % n) for i in range(n)])


def pick(a, index, axis=0):
    return lax.dynamic_index_in_dim(a, index, axis, keepdims=False)


def place(buffer, piece, index, axis=0):
    return lax.dynamic_update_slice_in_dim(buffer, jnp.expand_dims(piece, axis), index, axis)


def depth_gather(piece, depth):
    n = lax.axis_size("fsdp")
    buffer = place(jnp.zeros((n,) + piece.shape, piece.dtype), piece, depth)
    for s in range(1, n):
        piece = ring(piece)
        buffer = place(buffer, piece, lax.rem(depth + n - s, n))
    return buffer


def depth_gather_direct(piece, depth):
    n = lax.axis_size("fsdp")
    buffer = place(jnp.zeros((n,) + piece.shape, piece.dtype), piece, depth)
    for s in range(1, n):
        moved = lax.ppermute(piece, "fsdp", [(k, (k + s) % n) for k in range(n)])
        buffer = place(buffer, moved, lax.rem(depth + n - s, n))
    return buffer


def depth_scatter(parts, depth):
    n = lax.axis_size("fsdp")
    total = pick(parts, lax.rem(depth + n - 1, n))
    for s in range(n - 1):
        total = ring(total.astype(BF))
        total = total.astype(F32) + pick(parts, lax.rem(depth + 2 * n - 2 - s, n)).astype(F32)
    return total


def plane_gather(piece, index):
    n = lax.axis_size("ctx")
    chips = n // 2
    pieces = jnp.stack([piece] + [hop(piece, r) for r in range(1, chips)])
    others = swap(pieces)
    buffer = jnp.zeros((n,) + piece.shape, piece.dtype)
    for r in range(chips):
        buffer = place(buffer, pieces[r], index ^ (2 * r))
        buffer = place(buffer, others[r], index ^ (2 * r + 1))
    return buffer


def rotate(v, cosine, sine):
    heads = v.reshape(-1, 2, HEAD_WIDTH // 2, v.shape[-1])
    a, b = heads[:, 0], heads[:, 1]
    return jnp.stack([a * cosine - b * sine, b * cosine + a * sine], 1).reshape(v.shape)


def rotate_back(v, cosine, sine):
    heads = v.reshape(-1, 2, HEAD_WIDTH // 2, v.shape[-1])
    a, b = heads[:, 0], heads[:, 1]
    return jnp.stack([a * cosine + b * sine, b * cosine - a * sine], 1).reshape(v.shape)


def norm_back(incoming, unit, inverse, gain):
    scaled = incoming * gain
    return inverse * (scaled - unit * jnp.mean(scaled * unit, -1, keepdims=True))


def body(
    tokens,
    block_pairs,
    cotangent,
    attention_gain,
    query_weight,
    key_matrix,
    value_matrix,
    output_weight,
    feedforward_gain,
    gate_weight,
    up_weight,
    down_weight,
):
    slice_len, width = tokens.shape[1], tokens.shape[2]
    ctx = lax.axis_size("ctx")
    zsize = lax.axis_size("fsdp")
    chips = ctx // 2
    diag = chips - 1
    near = range(1, chips - 1)
    index = lax.axis_index("ctx")
    chip, core = index // 2, lax.rem(index, 2)
    depth = lax.axis_index("fsdp")
    rows = width // zsize
    strip = rows // ctx
    hidden_rows = down_weight.shape[0]
    fine = hidden_rows // ctx
    chunk = fine * zsize
    kv_rows = KEY_HEADS * HEAD_WIDTH

    cot_there = swap(cotangent)
    cot = jnp.concatenate(
        [pick(cotangent, core), pick(cot_there, core), pick(cot_there, 1 - core), pick(cotangent, 1 - core)]
    )
    length = 2 * slice_len

    ids_all = jnp.concatenate([pick(block_pairs, index ^ r) for r in range(ctx)])
    ids = ids_all[:4]
    blocks = ids_all.shape[0]
    order = jnp.sum(
        jnp.where(ids_all[None, :] == jnp.arange(blocks, dtype=jnp.int32)[:, None], jnp.arange(blocks, dtype=jnp.int32)[None, :], 0), 1
    )
    positions = (ids[:, None] * BLK + jnp.arange(BLK, dtype=jnp.int32)[None, :]).reshape(length)
    half = HEAD_WIDTH // 2
    frequency = THETA ** (-jnp.arange(half, dtype=F32) * 2.0 / HEAD_WIDTH)
    angles = frequency[:, None] * positions.astype(F32)[None, :]
    cosine, sine = jnp.cos(angles), jnp.sin(angles)

    gate_up, down, keys, values = {}, {}, {}, {}
    fast = chips == 4 and strip % 16 == 0 and fine % 128 == 0
    if fast:
        (key_value_full, query_full, output_full, wide, tall, far_wide, far_tall, x, first, query, gains_full, *kv) = front(
            tokens, jnp.stack([attention_gain, feedforward_gain]).astype(F32), key_matrix, value_matrix, query_weight,
            output_weight, gate_weight, up_weight, down_weight, cosine, sine, zsize, ctx,
        )
        key_value_full, query_full, output_full = (w.reshape(width, width) for w in (key_value_full, query_full, output_full))
        gate_up[0], down[0] = wide.reshape(width, 2 * chunk), tall.reshape(chunk, width)
        for r in range(chips):
            keys[r], values[r] = kv[r], kv[chips + r]
        x = x.astype(F32)
        gain_first, gain_second = gains_full[0], gains_full[1]
        inverse_first = lax.rsqrt(jnp.mean(x * x, -1, keepdims=True) + EPS)
        unit_first = x * inverse_first
        first_t = jnp.transpose(first)
        gate_up[diag] = depth_gather_direct(far_wide, depth).reshape(width, 2 * chunk)
        down[diag] = depth_gather_direct(far_tall, depth).reshape(chunk, width)
    else:
        gate_cut = gate_weight.reshape(rows, zsize, 2, chips, fine)
        up_cut = up_weight.reshape(rows, zsize, 2, chips, fine)
        down_cut = down_weight.reshape(2, chips, fine, width)

        def own_piece(r):
            gate = pick(pick(gate_cut, core, 2), chip ^ r, 2).reshape(rows, chunk)
            up = pick(pick(up_cut, core, 2), chip ^ r, 2).reshape(rows, chunk)
            down = pick(pick(down_cut, core), chip ^ r)
            return jnp.concatenate([gate, up], 1), down

        gains = jnp.stack([attention_gain, feedforward_gain])
        gain_buffer = place(jnp.zeros((zsize, 2, rows), BF), gains, depth)
        for s in range(1, zsize):
            moved = lax.ppermute(gains, "fsdp", [(k, (k + s) % zsize) for k in range(zsize)])
            gain_buffer = place(gain_buffer, moved, lax.rem(depth + zsize - s, zsize))
        gains_full = jnp.transpose(gain_buffer, (1, 0, 2)).reshape(2, width).astype(F32)
        gain_first, gain_second = gains_full[0], gains_full[1]

        def gather_square(shard):
            strips = shard.reshape(ctx, strip, shard.shape[1])
            pair = jnp.stack([pick(strips, index), pick(strips, index ^ (2 * diag))])
            pair = depth_gather(pair, depth)
            own, far = pair[:, 0], pair[:, 1]
            found = {0: own, diag: far}
            for r in near:
                found[r] = hop(own, r)
            full = jnp.zeros((zsize, ctx, strip, shard.shape[1]), BF)
            for r in range(chips):
                full = place(full, found[r], index ^ (2 * r), 1)
                full = place(full, swap(found[r]), index ^ (2 * r + 1), 1)
            return full.reshape(width, shard.shape[1])

        key_value_full = gather_square(jnp.concatenate([key_matrix, value_matrix], 1))
        query_full = gather_square(query_weight)
        output_full = gather_square(output_weight)

        x = jnp.concatenate([pick(tokens, core), swap(pick(tokens, 1 - core))]).astype(F32)
        wide, tall = own_piece(0)
        gate_up[0] = depth_gather(wide, depth).reshape(width, 2 * chunk)
        down[0] = depth_gather(tall, depth).reshape(chunk, width)
        inverse_first = lax.rsqrt(jnp.mean(x * x, -1, keepdims=True) + EPS)
        unit_first = x * inverse_first
        first = (unit_first * gain_first).astype(BF)
        first_t = jnp.transpose(first)
        kv = mm(key_value_full, first_t, 0, 0)
        keys[0] = rotate(kv[:kv_rows], cosine, sine).astype(BF)
        values[0] = kv[kv_rows:].astype(BF)
        for r in range(1, chips):
            high = 1 << (r.bit_length() - 1)
            low = r & -r
            keys[r] = hop(keys[r ^ high], high)
            values[r] = hop(values[r ^ low], low)
        query = rotate(mm(query_full, first_t, 0, 0), cosine, sine).astype(BF)
        wide, tall = own_piece(diag)
        gate_up[diag] = depth_gather(wide, depth).reshape(width, 2 * chunk)
        down[diag] = depth_gather(tall, depth).reshape(chunk, width)

    for r in near:
        gate_up[r] = hop(gate_up[0], r)
        down[r] = hop(down[0], r)

    key_list = [keys[r] for r in range(chips)]
    value_list = [values[r] for r in range(chips)]
    attended, log_total = attn_fwd(ids, order, query, key_list, value_list, KEY_HEADS)

    middle = x + mm(attended, output_full, 0, 0)
    inverse_second = lax.rsqrt(jnp.mean(middle * middle, -1, keepdims=True) + EPS)
    unit_second = middle * inverse_second
    second = (unit_second * gain_second).astype(BF)
    second = jnp.concatenate([second, swap(second)])
    out_part = 0.0
    second_grad = 0.0
    wide_grad, tall_grad = {}, {}
    for r in [0] + list(near) + [diag]:
        pre = mm(second, gate_up[r], 1, 0)
        gate_pre, up_pre = pre[:, :chunk], pre[:, chunk:]
        hidden_grad = mm(cot, down[r], 1, 1)
        sigmoid = jax.nn.sigmoid(gate_pre)
        silu = gate_pre * sigmoid
        hidden = (silu * up_pre).astype(BF)
        gate_low = (hidden_grad * up_pre * sigmoid * (1.0 + gate_pre * (1.0 - sigmoid))).astype(BF)
        up_low = (hidden_grad * silu).astype(BF)
        both_low = jnp.concatenate([gate_low, up_low], 1)
        tall_grad[r] = mm(hidden, cot, 0, 0).astype(BF)
        wide_grad[r] = mm(second, both_low, 0, 0).astype(BF)
        out_part = out_part + mm(hidden, down[r], 1, 0)
        second_grad = second_grad + mm(both_low, gate_up[r], 1, 1)

    q = slice_len
    out_part = jnp.concatenate([out_part[:length] + middle, out_part[length:]])
    came = swap(jnp.concatenate([out_part[2 * q:3 * q], out_part[q:2 * q]]))
    out_here = (out_part[:q] + came[:q]).astype(BF)
    out_there = (out_part[3 * q:] + came[q:]).astype(BF)

    def stored(here, there):
        return jnp.where(core == 0, jnp.stack([here, there]), jnp.stack([there, here]))

    layer_out = stored(out_here, out_there)

    second_grad = second_grad[:length] + swap(second_grad[length:])
    gain_second_part = jnp.sum(second_grad * unit_second, 0)
    middle_grad = cot[:length].astype(F32) + norm_back(second_grad, unit_second, inverse_second, gain_second)

    def halves(a):
        cut = a.reshape(zsize, chips, 2, strip, length)
        here = pick(cut, core, 2).reshape(-1, length)
        there = swap(pick(cut, 1 - core, 2).reshape(-1, length))
        return jnp.concatenate([here, there], 1)

    first_half = halves(first_t)
    middle_low = middle_grad.astype(BF)
    out_part_grad = mm(halves(attended), jnp.concatenate([middle_low, swap(middle_low)]), 1, 0)
    attended_grad = mm(output_full, middle_low, 1, 1).astype(BF)
    query_low, key_parts, value_parts = attn_bwd(
        ids, order, query, attended, attended_grad, log_total, cosine, sine, key_list, value_list, KEY_HEADS
    )
    wide_cut = {r: wide_grad[r].reshape(zsize, rows, 2 * chunk) for r in range(chips)}
    tall_cut = {r: tall_grad[r].reshape(zsize, fine, width) for r in range(chips)}
    if fast:
        def shifted(parts):
            return [parts] + [
                lax.ppermute(pick(parts, lax.rem(depth + s, zsize)), "fsdp", [(k, (k + s) % zsize) for k in range(zsize)])
                for s in range(1, zsize)
            ]

        o_all, q_all, kv_all, wide_all, tall_all, kv_low = tail(
            key_parts, value_parts, query_low, cosine, sine, first_half,
            out_part_grad.astype(BF).reshape(zsize, chips, strip, width),
            [wide_cut[0], hop(wide_cut[1], 1), hop(wide_cut[2], 2)], [tall_cut[0], hop(tall_cut[1], 1), hop(tall_cut[2], 2)],
            shifted(wide_cut[diag]), shifted(tall_cut[diag]), zsize, chips,
        )
        output_grad, query_grad, kv_grad = (a.reshape(rows, width).astype(F32) for a in (o_all, q_all, kv_all))
    else:
        key_sum = [part for part in key_parts]
        value_sum = [part for part in value_parts]
        for r in range(chips - 1, 0, -1):
            high = 1 << (r.bit_length() - 1)
            low = r & -r
            key_sum[r ^ high] = key_sum[r ^ high].astype(F32) + hop(key_sum[r].astype(BF), high).astype(F32)
            value_sum[r ^ low] = value_sum[r ^ low].astype(F32) + hop(value_sum[r].astype(BF), low).astype(F32)
        key_low = rotate_back(key_sum[0], cosine, sine).astype(BF)
        value_low = value_sum[0].astype(BF)
        kv_low = jnp.concatenate([key_low, value_low])

        def scatter(parts):
            total = parts[0].astype(F32)
            for r in near:
                total = total + hop(parts[r], r).astype(F32)
            far = hop(depth_scatter(parts[diag], depth).astype(BF), diag)
            total = depth_scatter(total.astype(BF), depth) + far.astype(F32)
            return total.astype(BF)

        tall_piece = scatter(tall_cut)
        wide_piece = scatter(wide_cut)
        tall_all = plane_gather(tall_piece, index)
        wide_all = plane_gather(wide_piece, index)
        def square_grad(product):
            parts = product.astype(BF).reshape(zsize, chips, strip, width)
            piece = scatter({r: pick(parts, chip ^ r, 1) for r in range(chips)})
            return plane_gather(piece, index).reshape(rows, width).astype(F32)

        output_grad = square_grad(out_part_grad)
        query_grad = square_grad(mm(first_half, jnp.concatenate([query_low, swap(query_low)], 1), 1, 1))
        kv_grad = square_grad(mm(first_half, jnp.concatenate([kv_low, swap(kv_low)], 1), 1, 1))


    down_grad = jnp.transpose(tall_all.reshape(chips, 2, fine, width), (1, 0, 2, 3)).reshape(hidden_rows, width).astype(F32)
    wide_all = wide_all.reshape(chips, 2, rows, 2, zsize, fine)
    gate_grad = jnp.transpose(wide_all[:, :, :, 0], (2, 3, 1, 0, 4)).reshape(rows, -1).astype(F32)
    up_grad = jnp.transpose(wide_all[:, :, :, 1], (2, 3, 1, 0, 4)).reshape(rows, -1).astype(F32)

    first_grad = mm(query_low, query_full, 0, 1) + mm(kv_low, key_value_full, 0, 1)
    gain_first_part = jnp.sum(first_grad * unit_first, 0)
    tokens_part = (middle_grad + norm_back(first_grad, unit_first, inverse_first, gain_first)).astype(BF)
    tokens_grad = stored(tokens_part[:q], swap(tokens_part[q:]))

    def gain_total(part):
        cut = part.reshape(zsize, rows)
        total = pick(cut, depth)
        for s in range(1, zsize):
            total = total + lax.ppermute(
                pick(cut, lax.rem(depth + s, zsize)), "fsdp", [(k, (k + s) % zsize) for k in range(zsize)]
            )
        total = total + swap(total)
        bit = 1
        while bit < chips:
            total = total + hop(total, bit)
            bit *= 2
        return total

    return (
        layer_out,
        tokens_grad,
        gain_total(gain_first_part),
        query_grad,
        kv_grad[:, :kv_rows],
        kv_grad[:, kv_rows:],
        output_grad,
        gain_total(gain_second_part),
        gate_grad,
        up_grad,
        down_grad,
    )


def solution(mesh):
    line, square, grid = P("fsdp"), P("fsdp", None), P("fsdp", "ctx", None)
    in_specs = (grid, P(), grid, line, square, square, square, square, line, square, square, square)
    out_specs = (grid, grid, line, square, square, square, square, line, square, square, square)
    return jax.shard_map(body, mesh=mesh, in_specs=in_specs, out_specs=out_specs, check_vma=False)
```

```python
import functools

import jax
import jax.numpy as jnp
from jax import lax
from jax.experimental import pallas as pl
from jax.experimental.pallas import tpu as pltpu
from jax.sharding import PartitionSpec as P

QUERY_HEADS = 16
KEY_HEADS = 8
HEAD_WIDTH = 96
EPS = 1e-05
THETA = 100000.0
BLK = 128
SCALE = HEAD_WIDTH ** -0.5
BF = jnp.bfloat16
F32 = jnp.float32

ATT_COST = 8
LOG2E = 1.4426950408889634
NT = (((1,), (1,)), ((), ()))


def block_tasks(ids_ref, inv_ref, slices, t):
    tasks = []
    for sl in range(slices):
        first = ids_ref[2 * sl]
        late = (t > first).astype(jnp.int32)
        kpos = t - late * (first + 1)
        tasks.append((sl, late, inv_ref[kpos], (ids_ref[2 * sl + late] - kpos) * BLK))
    return tasks


def causal_difference():
    return lax.broadcasted_iota(jnp.int32, (BLK, 2 * BLK), 0) - lax.rem(lax.broadcasted_iota(jnp.int32, (BLK, 2 * BLK), 1), BLK)


def fwd_kernel(nchip, heads, ids_ref, inv_ref, q_ref, *rest):
    k_refs, v_refs = rest[:nchip], rest[nchip:2 * nchip]
    o_ref, lse_ref, knat, vtr = rest[2 * nchip:2 * nchip + 4]
    state = rest[2 * nchip + 4:]
    nq = q_ref.shape[1] // BLK
    slices = nq // 2
    nb = nchip * nq
    c = SCALE * LOG2E
    chains = [(h, sl) for h in range(heads) for sl in range(slices)]
    qs, m_s, l_s, acc = ({chain: state[4 * n + k] for n, chain in enumerate(chains)} for k in range(4))
    for h in range(heads):
        for n in range(nb):
            r, lanes = n // nq, slice(BLK * (n % nq), BLK * (n % nq + 1))
            knat[h, n] = k_refs[r][96 * h:96 * (h + 1), lanes].T
            vtr[h, n] = v_refs[r][96 * h:96 * (h + 1), lanes]
        for sl in range(slices):
            for half in range(2):
                lanes = slice(BLK * (2 * sl + half), BLK * (2 * sl + half + 1))
                qs[h, sl][half] = jnp.concatenate([q_ref[192 * h:192 * h + 96, lanes], q_ref[192 * h + 96:192 * h + 192, lanes]], axis=1)
            m_s[h, sl][...] = jnp.full((2, 1, 2 * BLK), -1e30, F32)
            l_s[h, sl][...] = jnp.zeros((2, 1, 2 * BLK), F32)
            acc[h, sl][...] = jnp.zeros((2, 96, 2 * BLK), F32)
    diff = causal_difference()

    def step(t, _):
        tasks = block_tasks(ids_ref, inv_ref, slices, t)
        todo = [(h, *task) for h in range(heads) for task in tasks]
        scores = [
            jnp.where(diff <= offset, jnp.dot(knat[h, n], qs[h, sl][late], preferred_element_type=F32), -jnp.inf)
            for h, sl, late, n, offset in todo
        ]
        old = [(m_s[h, sl][late], l_s[h, sl][late], acc[h, sl][late]) for h, sl, late, n, offset in todo]
        peaks = [jnp.maximum(m, jnp.max(s, axis=0, keepdims=True)) for s, (m, _l, _a) in zip(scores, old)]
        weights = [jnp.exp2((s - peak) * c) for s, peak in zip(scores, peaks)]
        shrink = [jnp.exp2((m - peak) * c) for peak, (m, _l, _a) in zip(peaks, old)]
        totals = [l * a + jnp.sum(p, axis=0, keepdims=True) for (_m, l, _a), a, p in zip(old, shrink, weights)]
        mixed = [
            o * a + jnp.dot(vtr[h, n], p.astype(BF), preferred_element_type=F32)
            for (h, sl, late, n, offset), (_m, _l, o), a, p in zip(todo, old, shrink, weights)
        ]
        for (h, sl, late, n, offset), peak, total, o in zip(todo, peaks, totals, mixed):
            m_s[h, sl][late] = peak
            l_s[h, sl][late] = total
            acc[h, sl][late] = o
        return 0

    lax.fori_loop(0, nb + 1, step, 0)
    for h, sl in chains:
        for half in range(2):
            lanes = slice(BLK * (2 * sl + half), BLK * (2 * sl + half + 1))
            l = l_s[h, sl][half]
            o = acc[h, sl][half] / l
            lse_ref[h, 2 * sl + half] = m_s[h, sl][half] * c + jnp.log2(l)
            o_ref[192 * h:192 * h + 96, lanes] = o[:, :BLK].astype(BF)
            o_ref[192 * h + 96:192 * h + 192, lanes] = o[:, BLK:].astype(BF)


def attn_fwd(ids, inv, qT, ks, vs, heads):
    nchip = len(ks)
    T = qT.shape[1]
    nq = T // BLK
    nb = nchip * nq
    per = 4 if nb <= 16 else 2
    wide = pl.BlockSpec((192 * per, T), lambda g, *_: (g, 0))
    slim = pl.BlockSpec((96 * per, T), lambda g, *_: (g, 0))
    chain = [
        pltpu.VMEM((2, 96, 2 * BLK), BF),
        pltpu.VMEM((2, 1, 2 * BLK), F32),
        pltpu.VMEM((2, 1, 2 * BLK), F32),
        pltpu.VMEM((2, 96, 2 * BLK), F32),
    ]
    grid_spec = pltpu.PrefetchScalarGridSpec(
        num_scalar_prefetch=2,
        grid=(heads // per,),
        in_specs=[wide] + [slim] * (2 * nchip),
        out_specs=[wide, pl.BlockSpec((per, nq, 1, 2 * BLK), lambda g, *_: (g, 0, 0, 0))],
        scratch_shapes=[pltpu.VMEM((per, nb, BLK, 96), BF), pltpu.VMEM((per, nb, 96, BLK), BF)] + chain * (per * nq // 2),
    )
    return pl.pallas_call(
        functools.partial(fwd_kernel, nchip, per),
        grid_spec=grid_spec,
        out_shape=[jax.ShapeDtypeStruct((heads * 192, T), BF), jax.ShapeDtypeStruct((heads, nq, 1, 2 * BLK), F32)],
        cost_estimate=pl.CostEstimate(flops=ATT_COST * 10**9, bytes_accessed=16 * 2**20, transcendentals=0),
        compiler_params=pltpu.CompilerParams(vmem_limit_bytes=48 * 2**20),
        name="attention_forward",
    )(ids, inv, qT, *ks, *vs)


def bwd_kernel(nchip, heads, ids_ref, inv_ref, q_ref, o_ref, do_ref, lse_ref, cos_ref, sin_ref, *rest):
    k_refs, v_refs = rest[:nchip], rest[nchip:2 * nchip]
    dq_ref = rest[2 * nchip]
    dk_refs, dv_refs = rest[2 * nchip + 1:3 * nchip + 1], rest[3 * nchip + 1:4 * nchip + 1]
    knat, ktr, vnat = rest[4 * nchip + 1:4 * nchip + 4]
    state = rest[4 * nchip + 4:]
    nq = q_ref.shape[1] // BLK
    slices = nq // 2
    nb = nchip * nq
    c = SCALE * LOG2E
    chains = [(h, sl) for h in range(heads) for sl in range(slices)]
    qs, dos, stat, dq_s, dk_s, dv_s = ({chain: state[6 * n + k] for n, chain in enumerate(chains)} for k in range(6))
    for h in range(heads):
        for n in range(nb):
            r, lanes = n // nq, slice(BLK * (n % nq), BLK * (n % nq + 1))
            block = k_refs[r][96 * h:96 * (h + 1), lanes]
            knat[h, n] = block.T
            ktr[h, n] = block
            vnat[h, n] = v_refs[r][96 * h:96 * (h + 1), lanes].T
    for h, sl in chains:
        for half in range(2):
            lanes = slice(BLK * (2 * sl + half), BLK * (2 * sl + half + 1))
            pair = lambda ref: jnp.concatenate([ref[192 * h:192 * h + 96, lanes], ref[192 * h + 96:192 * h + 192, lanes]], axis=1)
            do = pair(do_ref)
            qs[h, sl][half] = pair(q_ref)
            dos[h, sl][half] = do
            stat[h, sl][half, 0:1] = lse_ref[h, 2 * sl + half]
            stat[h, sl][half, 1:2] = jnp.sum(pair(o_ref).astype(F32) * do.astype(F32), axis=0, keepdims=True)
        dq_s[h, sl][...] = jnp.zeros((2, 96, 2 * BLK), F32)
        dk_s[h, sl][...] = jnp.zeros((nb, 96, BLK), F32)
        dv_s[h, sl][...] = jnp.zeros((nb, 96, BLK), F32)
    diff = causal_difference()

    def step(t, _):
        tasks = block_tasks(ids_ref, inv_ref, slices, t)
        todo = [(h, *task) for h in range(heads) for task in tasks]
        q = [qs[h, sl][late] for h, sl, late, n, offset in todo]
        do = [dos[h, sl][late] for h, sl, late, n, offset in todo]
        scores = [jnp.dot(knat[h, n], x, preferred_element_type=F32) for (h, sl, late, n, offset), x in zip(todo, q)]
        grads = [jnp.dot(vnat[h, n], x, preferred_element_type=F32) for (h, sl, late, n, offset), x in zip(todo, do)]
        weights = [
            jnp.exp2(jnp.where(diff <= offset, s * c - stat[h, sl][late, 0:1], -jnp.inf))
            for (h, sl, late, n, offset), s in zip(todo, scores)
        ]
        low = [(p * (g - stat[h, sl][late, 1:2])).astype(BF) for (h, sl, late, n, offset), p, g in zip(todo, weights, grads)]
        dv = [lax.dot_general(x, p.astype(BF), NT, preferred_element_type=F32) for x, p in zip(do, weights)]
        dk = [lax.dot_general(x, ds, NT, preferred_element_type=F32) for x, ds in zip(q, low)]
        dq = [jnp.dot(ktr[h, n], ds, preferred_element_type=F32) for (h, sl, late, n, offset), ds in zip(todo, low)]
        for (h, sl, late, n, offset), a, b, d in zip(todo, dv, dk, dq):
            dv_s[h, sl][n] += a
            dk_s[h, sl][n] += b
            dq_s[h, sl][late] += d
        return 0

    lax.fori_loop(0, nb + 1, step, 0)
    for h, sl in chains:
        for half in range(2):
            lanes = slice(BLK * (2 * sl + half), BLK * (2 * sl + half + 1))
            cos, sin = cos_ref[:, lanes], sin_ref[:, lanes]
            for e in range(2):
                a = dq_s[h, sl][half, 0:48, BLK * e:BLK * (e + 1)] * SCALE
                b = dq_s[h, sl][half, 48:96, BLK * e:BLK * (e + 1)] * SCALE
                at = 192 * h + 96 * e
                dq_ref[at:at + 48, lanes] = (a * cos + b * sin).astype(BF)
                dq_ref[at + 48:at + 96, lanes] = (b * cos - a * sin).astype(BF)
    for h in range(heads):
        for n in range(nb):
            r, lanes = n // nq, slice(BLK * (n % nq), BLK * (n % nq + 1))
            dk = sum(dk_s[h, sl][n] for sl in range(slices))
            dv = sum(dv_s[h, sl][n] for sl in range(slices))
            dk_refs[r][96 * h:96 * (h + 1), lanes] = (dk * SCALE).astype(BF)
            dv_refs[r][96 * h:96 * (h + 1), lanes] = dv.astype(BF)


def attn_bwd(ids, inv, qT, oT, doT, lse, cosine, sine, ks, vs, heads):
    nchip = len(ks)
    T = qT.shape[1]
    nq = T // BLK
    nb = nchip * nq
    per = 4 if nb <= 16 else 2
    wide = pl.BlockSpec((192 * per, T), lambda g, *_: (g, 0))
    slim = pl.BlockSpec((96 * per, T), lambda g, *_: (g, 0))
    chain = [
        pltpu.VMEM((2, 96, 2 * BLK), BF),
        pltpu.VMEM((2, 96, 2 * BLK), BF),
        pltpu.VMEM((2, 2, 2 * BLK), F32),
        pltpu.VMEM((2, 96, 2 * BLK), F32),
        pltpu.VMEM((nb, 96, BLK), F32),
        pltpu.VMEM((nb, 96, BLK), F32),
    ]
    grid_spec = pltpu.PrefetchScalarGridSpec(
        num_scalar_prefetch=2,
        grid=(heads // per,),
        in_specs=[wide, wide, wide, pl.BlockSpec((per, nq, 1, 2 * BLK), lambda g, *_: (g, 0, 0, 0))]
        + [pl.BlockSpec((48, T), lambda g, *_: (0, 0))] * 2 + [slim] * (2 * nchip),
        out_specs=[wide] + [slim] * (2 * nchip),
        scratch_shapes=[pltpu.VMEM((per, nb, BLK, 96), BF), pltpu.VMEM((per, nb, 96, BLK), BF), pltpu.VMEM((per, nb, BLK, 96), BF)]
        + chain * (per * nq // 2),
    )
    slab = jax.ShapeDtypeStruct((heads * 96, T), BF)
    outs = pl.pallas_call(
        functools.partial(bwd_kernel, nchip, per),
        grid_spec=grid_spec,
        out_shape=[jax.ShapeDtypeStruct((heads * 192, T), BF)] + [slab] * (2 * nchip),
        cost_estimate=pl.CostEstimate(flops=ATT_COST * 10**9, bytes_accessed=24 * 2**20, transcendentals=0),
        compiler_params=pltpu.CompilerParams(vmem_limit_bytes=48 * 2**20),
        name="attention_backward",
    )(ids, inv, qT, oT, doT, lse, cosine, sine, *ks, *vs)
    return outs[0], outs[1:1 + nchip], outs[1 + nchip:]


def pack_width(rows, fine, zsize, width):
    return 2 * fine * zsize + width * fine // rows


def front_kernel(zsize, *refs):
    (tok, gains, key_w, value_w, query_w, out_w, gate_w, up_w, down_w, cos, sin) = refs[:11]
    (full_kv, full_q, full_o, pack, far_pack, x_out, first, q_out, gains_out, k0, k1, k2, k3, v0, v1, v2, v3) = refs[11:28]
    x_s, gain_s, kv_w, q_w, kv_s, ss, rs, ls, gs, gr = refs[28:]
    ks, vs = (k0, k1, k2, k3), (v0, v1, v2, v3)
    index, depth = lax.axis_index("ctx"), lax.axis_index("fsdp")
    chip, core = index // 2, lax.rem(index, 2)
    fine = down_w.shape[0] // 8
    chunk = fine * zsize
    folds = pack.shape[1] // fine
    fold = first.shape[1] // folds
    width = first.shape[1]
    length = first.shape[0]
    kv_rows = k0.shape[0]
    nxt, prv = lax.rem(depth + 1, zsize), lax.rem(depth + zsize - 1, zsize)
    to_next, to_prev = (index, nxt), (index, prv)
    chip_x, chip_y, chip_d = chip + 1 - 2 * lax.rem(chip, 2), lax.rem(chip + 2, 4), 3 - chip
    to_x, to_y, to_core = (chip_x * 2 + core, depth), (chip_y * 2 + core, depth), (chip * 2 + 1 - core, depth)

    barrier = pltpu.get_barrier_semaphore()
    for target in (to_next, to_prev, to_x, to_y, to_core):
        pl.semaphore_signal(barrier, inc=1, device_id=target, device_id_type=pl.DeviceIdType.MESH)
    pl.semaphore_wait(barrier, 5)

    count = [0, 0]
    sent = []

    def send(src, dst, target):
        k = count[0]
        count[0] += 1
        copy = pltpu.make_async_remote_copy(
            src_ref=src, dst_ref=dst, send_sem=ss.at[k], recv_sem=rs.at[k], device_id=target, device_id_type=pl.DeviceIdType.MESH
        )
        copy.start()
        sent.append(copy)
        return copy

    def local(src, dst):
        k = count[1]
        count[1] += 1
        copy = pltpu.make_async_copy(src, dst, ls.at[k])
        copy.start()
        return copy

    def slot(s):
        return lax.rem(depth + zsize - s, zsize)

    steps = range(1, zsize)
    last = zsize - 1
    tokens_there = send(tok.at[1 - core], x_s.at[1], to_core)
    own_kv = [local(key_w, full_kv.at[depth, :, :, :, pl.ds(0, kv_rows)]), local(value_w, full_kv.at[depth, :, :, :, pl.ds(kv_rows, kv_rows)])]
    gain_s[depth] = gains[...]
    for copy in own_kv:
        copy.wait()

    weights = {"kv": full_kv, "q": full_q, "o": full_o}
    shards = {"q": query_w, "o": out_w}
    moves = {}

    def ring_step(name, s):
        full = weights[name]
        place = full.at[slot(s - 1), chip, core]
        source = shards[name].at[chip, core] if name in shards and s == 1 else place
        moves[name, "ring", s] = send(source, place, to_next)

    def spread(name, s):
        place = weights[name].at[slot(s), chip, core]
        moves[name, "x", s] = send(place, place, to_x)
        moves[name, "y", s] = send(place, place, to_y)

    def forward(name, s):
        mid = width // 2
        moves[name, "x", s].wait_recv()
        left = weights[name].at[slot(s), chip_x, core, :, pl.ds(0, mid)]
        moves[name, "fy", s] = send(left, left, to_y)
        moves[name, "y", s].wait_recv()
        right = weights[name].at[slot(s), chip_y, core, :, pl.ds(mid, mid)]
        moves[name, "fx", s] = send(right, right, to_x)

    def cross(name, s):
        moves[name, "fx", s].wait_recv()
        moves[name, "fy", s].wait_recv()
        column = weights[name].at[slot(s), :, core]
        moves[name, "core", s] = send(column, column, to_core)

    def gain_step(s):
        place = gain_s.at[slot(s - 1)]
        copy = pltpu.make_async_remote_copy(
            src_ref=place, dst_ref=place, send_sem=gs.at[s], recv_sem=gr.at[s], device_id=to_next, device_id_type=pl.DeviceIdType.MESH
        )
        copy.start()
        sent.append(copy)
        moves["gain", s] = copy

    ring_step("kv", 1)
    gain_step(1)
    own_late = [local(query_w, full_q.at[depth]), local(out_w, full_o.at[depth])]
    def cut_pack(which, target):
        copies = []
        for part in range(zsize):
            column = pl.multiple_of(part * (8 * fine) + core * (4 * fine) + which * fine, fine)
            copies.append(local(gate_w.at[:, pl.ds(column, fine)], target.at[:, pl.ds(part * fine, fine)]))
            copies.append(local(up_w.at[:, pl.ds(column, fine)], target.at[:, pl.ds(chunk + part * fine, fine)]))
        row = pl.multiple_of(core * (4 * fine) + which * fine, fine)
        for n in range(folds):
            copies.append(local(down_w.at[pl.ds(row, fine), pl.ds(n * fold, fold)], target.at[pl.ds(n * fine, fine), pl.ds(2 * chunk, fold)]))
        return copies

    own_ffn = cut_pack(chip, pack.at[depth])
    far_ffn = cut_pack(chip_d, far_pack)

    for s in steps:
        moves["kv", "ring", s].wait_recv()
        moves["gain", s].wait_recv()
        if s < last:
            ring_step("kv", s + 1)
            gain_step(s + 1)
        else:
            ring_step("q", 1)
        spread("kv", s)
    for s in steps:
        forward("kv", s)
        moves["q", "ring", s].wait_recv()
        ring_step("q", s + 1) if s < last else ring_step("o", 1)
        spread("q", s)
    for s in steps:
        cross("kv", s)

    tokens_there.wait_recv()
    x_out[0:length // 2] = tok[core]
    x_out[length // 2:] = x_s[1]
    gain_rows = [gain_s[place] for place in range(zsize)]
    gains_full = jnp.concatenate(gain_rows, axis=1)
    gains_out[...] = gains_full
    gain = gains_full[0:1]
    rows = 64

    def normalize(t, _):
        part = pl.ds(pl.multiple_of(t * rows, rows), rows)
        v = x_out[part].astype(F32)
        inverse = lax.rsqrt(jnp.mean(v * v, -1, keepdims=True) + EPS)
        first[part] = (v * inverse * gain).astype(BF)
        return 0

    lax.fori_loop(0, length // rows, normalize, 0)

    moves["o", "ring", 1].wait_recv()
    if last > 1:
        ring_step("o", 2)
    spread("o", 1)
    for s in steps:
        moves["kv", "core", s].wait_recv()
    load_kv = local(full_kv, kv_w)
    if last > 1:
        moves["o", "ring", 2].wait_recv()
        if last > 2:
            ring_step("o", 3)
        spread("o", 2)
    load_kv.wait()
    tile = 384

    def project(weight, t, turn):
        cols = pl.ds(pl.multiple_of(t * tile, tile), tile)
        w = weight[:, :, :, :, cols].reshape(width, tile)
        r = jnp.dot(first[...], w, preferred_element_type=F32).T
        if turn:
            r = rotate(r, cos[...], sin[...])
        return r.astype(BF)

    def project_kv(t, turn):
        kv_s[pl.ds(pl.multiple_of(t * tile, tile), tile)] = project(kv_w, t, turn)
        return 0

    per = kv_rows // tile
    lax.fori_loop(0, per, lambda t, _: project_kv(t, True), 0)
    k_here, v_here = kv_s.at[pl.ds(0, kv_rows)], kv_s.at[pl.ds(kv_rows, kv_rows)]
    k_x, k_y = send(k_here, k1, to_x), send(k_here, k2, to_y)
    lax.fori_loop(per, 2 * per, lambda t, _: project_kv(t, False), 0)
    v_y, v_x = send(v_here, v2, to_y), send(v_here, v1, to_x)
    keep = [local(k_here, k0), local(v_here, v0)]

    for s in range(3, zsize):
        moves["o", "ring", s].wait_recv()
        if s < last:
            ring_step("o", s + 1)
        spread("o", s)
    for copy in own_ffn:
        copy.wait()

    def ffn_step(s):
        a = pack.at[slot(s - 1)]
        moves["ffn", s] = send(a, a, to_next)

    ffn_step(1)
    for s in steps:
        forward("q", s)
    for s in steps:
        cross("q", s)
    for s in steps:
        forward("o", s)
    for s in steps:
        cross("o", s)
    for s in steps:
        moves["q", "core", s].wait_recv()
    for copy in own_late:
        copy.wait()
    local(full_q, q_w).wait()

    def project_q(t, _):
        q_out[pl.ds(pl.multiple_of(t * tile, tile), tile)] = project(q_w, t, True)
        return 0

    lax.fori_loop(0, width // tile, project_q, 0)
    k_x.wait_recv()
    k_d = send(k1, k3, to_y)
    v_y.wait_recv()
    v_d = send(v2, v3, to_x)
    for s in steps:
        moves["ffn", s].wait_recv()
        if s < last:
            ffn_step(s + 1)
    for s in steps:
        moves["o", "core", s].wait_recv()
    for copy in (k_y, v_x, k_d, v_d):
        copy.wait_recv()
    for copy in keep + far_ffn:
        copy.wait()
    for copy in sent:
        copy.wait_send()


def front(tokens, gains, key_w, value_w, query_w, out_w, gate_w, up_w, down_w, cosine, sine, zsize, ctx):
    width = tokens.shape[2]
    length = 2 * tokens.shape[1]
    rows = width // zsize
    strip = rows // ctx
    fine = down_w.shape[0] // ctx
    packed = pack_width(rows, fine, zsize, width)
    kv_rows = key_w.shape[1]
    chips = ctx // 2
    cut = lambda w: w.reshape(chips, 2, strip, w.shape[1])
    square = jax.ShapeDtypeStruct((zsize, chips, 2, strip, width), BF)
    flat = jax.ShapeDtypeStruct((kv_rows, length), BF)
    hbm, vmem = pl.BlockSpec(memory_space=pl.ANY), pl.BlockSpec(memory_space=pltpu.VMEM)
    copies = 19 * (zsize - 1) + 8
    return pl.pallas_call(
        functools.partial(front_kernel, zsize),
        out_shape=[
            square, square, square,
            jax.ShapeDtypeStruct((zsize, rows, packed), BF),
            jax.ShapeDtypeStruct((rows, packed), BF),
            jax.ShapeDtypeStruct((length, width), BF),
            jax.ShapeDtypeStruct((length, width), BF),
            jax.ShapeDtypeStruct((width, length), BF),
            jax.ShapeDtypeStruct((2, width), F32),
        ] + [flat] * 8,
        in_specs=[vmem, vmem] + [hbm] * 7 + [vmem] * 2,
        out_specs=[hbm] * 5 + [vmem] * 4 + [hbm] * 8,
        scratch_shapes=[
            pltpu.VMEM((2, length // 2, width), BF),
            pltpu.VMEM((zsize, 2, rows), F32),
            pltpu.VMEM(square.shape, BF),
            pltpu.VMEM(square.shape, BF),
            pltpu.VMEM((2 * kv_rows, length), BF),
            pltpu.SemaphoreType.DMA((copies,)),
            pltpu.SemaphoreType.DMA((copies,)),
            pltpu.SemaphoreType.DMA((8 + 4 * zsize + 2 * (rows // fine),)),
            pltpu.SemaphoreType.DMA((zsize,)),
            pltpu.SemaphoreType.DMA((zsize,)),
        ],
        compiler_params=pltpu.CompilerParams(collective_id=0, has_side_effects=True, vmem_limit_bytes=40 * 2**20),
        name="front",
    )(tokens, gains, cut(key_w), cut(value_w), cut(query_w), cut(out_w), gate_w, up_w, down_w, cosine, sine)


def tail_kernel(zsize, *refs):
    dk, dv = refs[0:4], refs[4:8]
    dq, cos, sin, first_half, out_grad = refs[8:13]
    pack_in, far_in = refs[13:16], refs[16:16 + zsize]
    rest = refs[16 + zsize:]
    o_all, q_all, kv_all, pack_all, kv_low = rest[:5]
    (got, held, dq_pair, kv_pair, half, grads, gl, gr, gx, gy, gz, piece,
     pack_s, pack_0, pack_z, far_s, far_r, pack_p, ss, rs, ls) = rest[5:]
    index, depth = lax.axis_index("ctx"), lax.axis_index("fsdp")
    chip, core = index // 2, lax.rem(index, 2)
    chip_x, chip_y, chip_d = chip + 1 - 2 * lax.rem(chip, 2), lax.rem(chip + 2, 4), 3 - chip
    nxt, prv = lax.rem(depth + 1, zsize), lax.rem(depth + zsize - 1, zsize)
    to_next, to_prev = (index, nxt), (index, prv)
    to_x, to_y, to_core = (chip_x * 2 + core, depth), (chip_y * 2 + core, depth), (chip * 2 + 1 - core, depth)
    to_far = (chip_d * 2 + core, depth)
    last = zsize - 1
    kv_rows = dk[0].shape[0]
    width = first_half.shape[0] * 2
    strip = piece.shape[1]
    length = dq.shape[1]

    barrier = pltpu.get_barrier_semaphore()
    for target in (to_next, to_prev, to_x, to_y, to_core, to_far):
        pl.semaphore_signal(barrier, inc=1, device_id=target, device_id_type=pl.DeviceIdType.MESH)
    pl.semaphore_wait(barrier, 6)

    count = [0, 0]
    sent, kept = [], []

    def send(src, dst, target):
        k = count[0]
        count[0] += 1
        copy = pltpu.make_async_remote_copy(
            src_ref=src, dst_ref=dst, send_sem=ss.at[k], recv_sem=rs.at[k], device_id=target, device_id_type=pl.DeviceIdType.MESH
        )
        copy.start()
        sent.append(copy)
        return copy

    def local(src, dst):
        k = count[1]
        count[1] += 1
        copy = pltpu.make_async_copy(src, dst, ls.at[k])
        copy.start()
        return copy

    def wait_all(copies):
        for copy in copies:
            copy.wait()

    def received(*copies):
        for copy in copies:
            copy.wait_recv()

    def add_rows(target, sources, block):
        def one(t, _):
            part = pl.ds(pl.multiple_of(t * block, block), block)
            total = target[part].astype(F32)
            for source in sources:
                total = total + source[part].astype(F32)
            target[part] = total.astype(BF)
            return 0

        lax.fori_loop(0, target.shape[0] // block, one, 0)

    def place_at(j):
        return lax.rem(depth + 2 * zsize - 1 - j, zsize)

    k3, v3 = send(dk[3], got.at[0], to_y), send(dv[3], got.at[1], to_x)
    q_swap = send(dq, dq_pair.at[1], to_core)

    part = pack_0.shape[0] // 2
    parts = [pl.ds(h * part, part) for h in range(2)]

    def load_ffn(j):
        return [local(pack_in[n].at[place_at(j)], pack_s.at[j % 2, n]) for n in range(3)]

    ffn_loads = {0: load_ffn(0)}
    load_o = local(out_grad, grads.at[0])
    load_q = [local(dq, dq_pair.at[0]), local(first_half, half)]
    load_kv = [local(dk[0], held.at[0]), local(dk[1], held.at[1]), local(dv[0], held.at[2]), local(dv[2], held.at[3])]
    load_far = [local(far_in[n], far_s.at[n]) for n in range(zsize)]

    moves = {}

    def ffn_step(j):
        if j + 1 <= last:
            ffn_loads[j + 1] = load_ffn(j + 1)
        wait_all(ffn_loads[j])
        for h in range(2):
            mine = [pack_s.at[j % 2, n, parts[h]] for n in range(3)]
            if j == 0:
                sum_rows(pack_0.at[parts[h]], mine, 64)
                moves["pack", h, 0] = send(pack_0.at[parts[h]], pack_z.at[0, parts[h]], to_next)
                continue
            received(moves["pack", h, j - 1])
            here = pack_z.at[j - 1, parts[h]]
            add_rows(here, mine, 64)
            if j < last:
                moves["pack", h, j] = send(here, pack_z.at[j, parts[h]], to_next)

    def sum_rows(target, sources, block):
        def one(t, _):
            part = pl.ds(pl.multiple_of(t * block, block), block)
            total = sources[0][part].astype(F32)
            for source in sources[1:]:
                total = total + source[part].astype(F32)
            target[part] = total.astype(BF)
            return 0

        lax.fori_loop(0, target.shape[0] // block, one, 0)

    mid = width // 2
    tiles = 512

    def stage_1(m):
        moves["l", m] = send(grads.at[m, :, chip_d, :, pl.ds(0, mid)], gl.at[m], to_y)
        moves["r", m] = send(grads.at[m, :, chip_d, :, pl.ds(mid, mid)], gr.at[m], to_x)

    def stage_2(m):
        received(moves["l", m])

        def left(zz, _):
            grads[m, zz, chip_x, :, 0:mid] = (grads[m, zz, chip_x, :, 0:mid].astype(F32) + gl[m, zz].astype(F32)).astype(BF)
            return 0

        lax.fori_loop(0, zsize, left, 0)
        moves["x", m] = send(grads.at[m, :, chip_x], gx.at[m], to_x)
        received(moves["r", m])

        def right(zz, _):
            grads[m, zz, chip_y, :, mid:] = (grads[m, zz, chip_y, :, mid:].astype(F32) + gr[m, zz].astype(F32)).astype(BF)
            return 0

        lax.fori_loop(0, zsize, right, 0)
        moves["y", m] = send(grads.at[m, :, chip_y], gy.at[m], to_y)

    def stage_3(m):
        received(moves["x", m], moves["y", m])

        def own(zz, _):
            grads[m, zz, chip] = (grads[m, zz, chip].astype(F32) + gx[m, zz].astype(F32) + gy[m, zz].astype(F32)).astype(BF)
            return 0

        lax.fori_loop(0, zsize, own, 0)
        moves["z", m, 0] = send(grads.at[m, place_at(0), chip], gz.at[m, 0], to_next)

    def ring_step(m, j):
        received(moves["z", m, j - 1])
        total = gz[m, j - 1].astype(F32) + grads[m, place_at(j), chip].astype(F32)
        if j < last:
            gz[m, j - 1] = total.astype(BF)
            moves["z", m, j] = send(gz.at[m, j - 1], gz.at[m, j], to_next)
        else:
            piece[m] = total.astype(BF)

    def spread(name, source, target):
        kept.append(local(source, target(chip, core)))
        moves[name, "x"] = send(source, target(chip, core), to_x)
        moves[name, "y"] = send(source, target(chip, core), to_y)

    def forward(name, target):
        received(moves[name, "x"])
        left = target(chip_x, core, pl.ds(0, mid))
        moves[name, "fy"] = send(left, left, to_y)
        received(moves[name, "y"])
        right = target(chip_y, core, pl.ds(mid, mid))
        moves[name, "fx"] = send(right, right, to_x)

    def cross(name, target):
        received(moves[name, "fx"], moves[name, "fy"])
        column = target(slice(None), core)
        moves[name, "core"] = send(column, column, to_core)

    def whole(ref):
        def at(p, c, cols=None):
            return ref.at[p, c] if cols is None else ref.at[p, c, :, cols]

        return at

    def half_rows(ref, h):
        def at(p, c, cols=None):
            return ref.at[p, c, parts[h]] if cols is None else ref.at[p, c, parts[h], cols]

        return at

    def product(m, pair):
        per = width // tiles

        def one(t, _):
            zz = t // per
            cols = pl.ds(pl.multiple_of(lax.rem(t, per) * tiles, tiles), tiles)
            rows = pl.ds(pl.multiple_of(zz * (4 * strip), 4 * strip), 4 * strip)
            nt = (((1,), (1,)), ((), ()))
            r = lax.dot_general(half[rows, 0:length], pair[0, cols], nt, preferred_element_type=F32)
            r = r + lax.dot_general(half[rows, length:], pair[1, cols], nt, preferred_element_type=F32)
            grads[m, zz, :, :, cols] = r.astype(BF).reshape(4, strip, tiles)
            return 0

        lax.fori_loop(0, zsize * per, one, 0)

    ffn_step(0)
    load_o.wait()
    stage_1(0)
    received(q_swap)
    wait_all(load_q)
    product(1, dq_pair)
    stage_1(1)

    received(k3)
    wait_all(load_kv)
    add_rows(held.at[1], [got.at[0]], 96)
    k1 = send(held.at[1], got.at[2], to_x)
    received(v3)
    add_rows(held.at[3], [got.at[1]], 96)
    v2 = send(held.at[3], got.at[3], to_y)
    k2, v1 = send(dk[2], got.at[4], to_y), send(dv[1], got.at[5], to_x)
    if last > 1:
        ffn_step(1)
    received(k1, k2, v1, v2)

    def finish_keys(h, _):
        rows = pl.ds(pl.multiple_of(h * 96, 96), 96)
        v = held[0, rows].astype(F32) + got[2, rows].astype(F32) + got[4, rows].astype(F32)
        kv_pair[0, rows] = rotate_back(v, cos[...], sin[...]).astype(BF)
        return 0

    def finish_values(h, _):
        rows = pl.ds(pl.multiple_of(h * 96, 96), 96)
        v = held[2, rows].astype(F32) + got[3, rows].astype(F32) + got[5, rows].astype(F32)
        kv_pair[0, pl.ds(pl.multiple_of(kv_rows + h * 96, 96), 96)] = v.astype(BF)
        return 0

    lax.fori_loop(0, kv_rows // 96, finish_keys, 0)
    lax.fori_loop(0, kv_rows // 96, finish_values, 0)
    kv_swap = send(kv_pair.at[0], kv_pair.at[1], to_core)
    kept.append(local(kv_pair.at[0], kv_low))
    stage_2(0)
    stage_2(1)
    if last > 2:
        ffn_step(2)
    wait_all(load_far)
    add_rows(far_s.at[0], [far_s.at[n] for n in range(1, zsize)], 64)
    far = send(far_s.at[0], far_r, to_far)
    received(kv_swap)
    product(2, kv_pair)
    stage_1(2)
    stage_3(0)
    stage_3(1)
    stage_2(2)
    for j in range(3, last):
        ffn_step(j)
    ffn_step(last)
    received(far)
    for h in range(2):
        sum_rows(pack_p.at[parts[h]], [pack_z.at[last - 1, parts[h]], far_r.at[parts[h]]], 64)
        spread(("pack", h), pack_p.at[parts[h]], half_rows(pack_all, h))
    for j in range(1, zsize):
        ring_step(0, j)
        ring_step(1, j)
        if j == 1:
            stage_3(2)
    spread(0, piece.at[0], whole(o_all))
    spread(1, piece.at[1], whole(q_all))
    for j in range(1, zsize):
        ring_step(2, j)
    spread(2, piece.at[2], whole(kv_all))
    targets = [(("pack", h), half_rows(pack_all, h)) for h in range(2)]
    targets += [(m, whole(ref)) for m, ref in enumerate((o_all, q_all, kv_all))]
    for name, target in targets:
        forward(name, target)
    wait_all(kept)
    for name, target in targets:
        cross(name, target)
    for name, target in targets:
        received(moves[name, "core"])
    for copy in sent:
        copy.wait_send()


def tail(dk, dv, dq, cosine, sine, first_half, out_grad, packs, far_packs, zsize, chips):
    kv_rows, length = dk[0].shape
    width = 2 * kv_rows
    strip = out_grad.shape[2]
    rows, packed = packs[0].shape[1:]
    hbm, vmem = pl.BlockSpec(memory_space=pl.ANY), pl.BlockSpec(memory_space=pltpu.VMEM)
    shape = lambda *s: jax.ShapeDtypeStruct(s, BF)
    store = lambda *s: pltpu.VMEM(s, BF)
    copies = 9 + 2 * (zsize - 1) + 3 * (4 + zsize - 1) + 5 * 5
    inputs = [*dk, *dv, dq, cosine, sine, first_half, out_grad, *packs, *far_packs]
    last = zsize - 1
    return pl.pallas_call(
        functools.partial(tail_kernel, zsize),
        out_shape=[shape(chips, 2, strip, width)] * 3 + [shape(chips, 2, rows, packed), shape(width, length)],
        in_specs=[hbm] * 9 + [vmem] * 2 + [hbm] * (len(inputs) - 11),
        out_specs=[hbm] * 5,
        scratch_shapes=[
            store(6, kv_rows, length), store(4, kv_rows, length), store(2, width, length), store(2, width, length),
            store(width // 2, 2 * length), store(3, zsize, chips, strip, width),
            store(3, zsize, strip, width // 2), store(3, zsize, strip, width // 2),
            store(3, zsize, strip, width), store(3, zsize, strip, width),
            store(3, last, strip, width), store(3, strip, width),
            store(2, 3, rows, packed), store(rows, packed), store(last, rows, packed),
            store(zsize, rows, packed), store(rows, packed), store(rows, packed),
            pltpu.SemaphoreType.DMA((copies,)), pltpu.SemaphoreType.DMA((copies,)),
            pltpu.SemaphoreType.DMA((4 * zsize + 13,)),
        ],
        compiler_params=pltpu.CompilerParams(collective_id=1, has_side_effects=True, vmem_limit_bytes=60 * 2**20),
        name="tail",
    )(*inputs)


def unfold(refs, wide, tall, start):
    zsize, fine = tall.shape[0], tall.shape[1]
    folds = wide.shape[1] // fine
    fold = tall.shape[2] // folds
    two = wide.shape[2]
    whole = len(refs) == 1
    depth = 0 if whole else lax.axis_index("fsdp")
    for s in range(1 if whole else zsize):
        at = slice(None) if whole else lax.rem(depth + zsize - s, zsize)
        lead = (slice(None),) if whole else ()
        start(refs[s].at[(*lead, slice(None), pl.ds(0, two))], wide.at[at])
        for n in range(folds):
            cols = pl.ds(n * fold, fold)
            start(refs[s].at[(*lead, pl.ds(n * fine, fine), pl.ds(two, fold))], tall.at[at, :, cols])


def ffn_kernel(pieces, second, second_t, cot, *refs):
    weights, (hidden_o, low_o), grads = refs[:pieces], refs[pieces:pieces + 2], refs[pieces + 2:2 * pieces + 2]
    s_v, st_v, c_v, wi_v, wo_v, h_v, ht_v, l_v, w_v, t_v, sem = refs[2 * pieces + 2:]
    tokens, width = second.shape
    zsize, fine = wo_v.shape[:2]
    rows = wi_v.shape[1]
    chunk = zsize * fine
    loads = []

    def load(src, dst):
        copy = pltpu.make_async_copy(src, dst, sem.at[len(loads)])
        copy.start()
        loads.append(copy)

    unfold(weights, wi_v, wo_v, load)
    load(second, s_v)
    load(cot, c_v)
    load(second_t, st_v)
    for copy in loads[:-1]:
        copy.wait()
    nt = (((1,), (1,)), ((), ()))
    tile = 256

    def one(t, _):
        part = pl.ds(pl.multiple_of(t * tile, tile), tile)
        pre = jnp.dot(s_v[part], wi_v[...].reshape(width, 2 * chunk), preferred_element_type=F32)
        hidden_grad = lax.dot_general(c_v[part], wo_v[...].reshape(chunk, width), nt, preferred_element_type=F32)
        gate, up = pre[:, :chunk], pre[:, chunk:]
        sigmoid = jax.nn.sigmoid(gate)
        silu = gate * sigmoid
        hidden = silu * up
        h_v[part] = hidden.astype(BF)
        ht_v[:, part] = hidden.T.astype(BF)
        l_v[part, 0:chunk] = (hidden_grad * up * sigmoid * (1.0 + gate * (1.0 - sigmoid))).astype(BF)
        l_v[part, chunk:] = (hidden_grad * silu).astype(BF)
        return 0

    lax.fori_loop(0, tokens // tile, one, 0)
    stores = []

    def store(src, dst):
        copy = pltpu.make_async_copy(src, dst, sem.at[len(loads) + len(stores)])
        copy.start()
        stores.append(copy)

    store(h_v, hidden_o)
    store(l_v, low_o)
    loads[-1].wait()
    depth = 0 if pieces == 1 else lax.axis_index("fsdp")
    grad_at = lambda n: grads[0].at[n] if pieces == 1 else grads[n]

    def place(n):
        return n if pieces == 1 else lax.rem(depth + n, zsize)

    for n in range(zsize):
        z = place(n)
        part = pl.ds(pl.multiple_of(z * rows, rows), rows)
        w_v[z] = jnp.dot(st_v[part], l_v[...], preferred_element_type=F32).astype(BF)
        store(w_v.at[z], grad_at(n).at[:, pl.ds(0, 2 * chunk)])
    folds = rows // fine
    fold = width // folds
    for n in range(folds):
        cols = slice(fold * n, fold * (n + 1))
        t_v[:, :, cols] = jnp.dot(ht_v[...], c_v[:, cols], preferred_element_type=F32).astype(BF).reshape(zsize, fine, fold)
        if pieces == 1:
            store(t_v.at[:, :, cols], grads[0].at[:, pl.ds(n * fine, fine), pl.ds(2 * chunk, fold)])
        else:
            for k in range(zsize):
                store(t_v.at[place(k), :, cols], grads[k].at[pl.ds(n * fine, fine), pl.ds(2 * chunk, fold)])
    for copy in stores:
        copy.wait()


def ffn_chunk(second, second_t, cot, weights, zsize, fine):
    pieces = len(weights)
    tokens, width = second.shape
    chunk = zsize * fine
    rows = width // zsize
    folds = rows // fine
    shape = lambda *s: jax.ShapeDtypeStruct(s, BF)
    store = lambda *s: pltpu.VMEM(s, BF)
    hbm = pl.BlockSpec(memory_space=pl.ANY)
    out = pl.pallas_call(
        functools.partial(ffn_kernel, pieces),
        out_shape=[shape(tokens, chunk), shape(tokens, 2 * chunk)] + [shape(*w.shape) for w in weights],
        in_specs=[hbm] * (3 + pieces),
        out_specs=[hbm] * (2 + pieces),
        scratch_shapes=[
            store(tokens, width), store(width, tokens), store(tokens, width), store(zsize, rows, 2 * chunk), store(zsize, fine, width),
            store(tokens, chunk), store(chunk, tokens), store(tokens, 2 * chunk), store(zsize, rows, 2 * chunk), store(zsize, fine, width),
            pltpu.SemaphoreType.DMA((5 + zsize + pieces * (2 * folds + 1),)),
        ],
        cost_estimate=pl.CostEstimate(flops=16 * 10**9, bytes_accessed=24 * 2**20, transcendentals=0),
        compiler_params=pltpu.CompilerParams(vmem_limit_bytes=50 * 2**20),
        name="ffn_chunk",
    )(second, second_t, cot, *weights)
    return out[0], out[1], out[2:]

def combine_kernel(counts, *refs):
    count = len(counts)
    hidden, low = refs[:count], refs[count:2 * count]
    weights, at = [], 2 * count
    for n in counts:
        weights.append(refs[at:at + n])
        at += n
    out, grad, h_v, l_v, wi_v, wo_v, o_v, g_v, sem = refs[at:]
    tokens, chunk = hidden[0].shape
    width = out.shape[1]
    loads = []

    def load(src, dst):
        copy = pltpu.make_async_copy(src, dst, sem.at[len(loads)])
        copy.start()
        loads.append(copy)

    for r in range(count):
        load(hidden[r], h_v.at[:, pl.ds(r * chunk, chunk)])
        unfold(weights[r], wi_v.at[:, :, pl.ds(2 * r * chunk, 2 * chunk)], wo_v.at[r], load)
    for r in range(count):
        load(low[r], l_v.at[:, pl.ds(2 * r * chunk, 2 * chunk)])
    nt = (((1,), (1,)), ((), ()))
    tile = 256
    steps = tokens // tile
    stores = []

    def store(src, dst):
        copy = pltpu.make_async_copy(src, dst, sem.at[len(loads) + len(stores)])
        copy.start()
        stores.append(copy)

    for copy in loads[:-count]:
        copy.wait()
    for t in range(steps):
        rows = slice(tile * t, tile * (t + 1))
        if t >= 2:
            stores[t - 2].wait()
        o_v[t % 2] = jnp.dot(h_v[rows], wo_v[...].reshape(count * chunk, width), preferred_element_type=F32)
        store(o_v.at[t % 2], out.at[rows])
    for copy in loads[-count:]:
        copy.wait()
    for t in range(steps):
        rows = slice(tile * t, tile * (t + 1))
        if t >= 2:
            stores[steps + t - 2].wait()
        g_v[t % 2] = lax.dot_general(l_v[rows], wi_v[...].reshape(width, 2 * count * chunk), nt, preferred_element_type=F32)
        store(g_v.at[t % 2], grad.at[rows])
    for t in range(max(steps - 2, 0), steps):
        stores[t].wait()
        stores[steps + t].wait()


def combine(hidden, low, weights, zsize, fine):
    counts = tuple(len(w) for w in weights)
    count = len(counts)
    tokens, chunk = hidden[0].shape
    rows = weights[0][0].shape[-2]
    width = rows * zsize
    hbm = pl.BlockSpec(memory_space=pl.ANY)
    shape = jax.ShapeDtypeStruct((tokens, width), F32)
    inputs = [*hidden, *low] + [piece for w in weights for piece in w]
    return pl.pallas_call(
        functools.partial(combine_kernel, counts),
        out_shape=[shape, shape],
        in_specs=[hbm] * len(inputs),
        out_specs=[hbm] * 2,
        scratch_shapes=[
            pltpu.VMEM((tokens, count * chunk), BF), pltpu.VMEM((tokens, 2 * count * chunk), BF),
            pltpu.VMEM((zsize, rows, 2 * count * chunk), BF), pltpu.VMEM((count, zsize, fine, width), BF),
            pltpu.VMEM((2, 256, width), F32), pltpu.VMEM((2, 256, width), F32),
            pltpu.SemaphoreType.DMA((2 * count + sum(counts) * (1 + rows // fine) + 2 * (tokens // 256),)),
        ],
        cost_estimate=pl.CostEstimate(flops=26 * 10**9, bytes_accessed=48 * 2**20, transcendentals=0),
        compiler_params=pltpu.CompilerParams(vmem_limit_bytes=56 * 2**20),
        name="ffn_combine",
    )(*inputs)


def assemble_kernel(zsize, wide, tall, o, q, kv, gate_o, up_o, down_o, o_o, q_o, k_o, v_o):
    fold = tall.shape[3]
    folds = down_o.shape[1] // fold
    fine = tall.shape[2] // folds
    kv_rows = k_o.shape[1]
    for p in range(4):
        for c in range(2):
            for part in range(zsize):
                at = slice((part * 8 + c * 4 + p) * fine, (part * 8 + c * 4 + p + 1) * fine)
                gate_o[:, at] = wide[p, c, :, part * fine:(part + 1) * fine].astype(F32)
                up_o[:, at] = wide[p, c, :, (zsize + part) * fine:(zsize + part + 1) * fine].astype(F32)
    for p in range(2):
        for n in range(folds):
            down_o[p * fine:(p + 1) * fine, n * fold:(n + 1) * fold] = tall[p, 0, n * fine:(n + 1) * fine].astype(F32)
    o_o[...] = o[...].astype(F32)
    q_o[...] = q[...].astype(F32)
    k_o[...] = kv[:, 0:kv_rows].astype(F32)
    v_o[...] = kv[:, kv_rows:].astype(F32)


def assemble(packs, o, q, kv, zsize, fine):
    chips, cores, rows, packed = packs.shape
    width = o.shape[1]
    steps = 4
    block = rows // steps
    two = 2 * fine * zsize
    fold = packed - two
    flat = lambda n: pl.BlockSpec((block, n), lambda i: (i, 0))
    out = lambda r, c: jax.ShapeDtypeStruct((r, c), F32)
    ff = fine * chips * cores
    return pl.pallas_call(
        functools.partial(assemble_kernel, zsize),
        grid=(steps,),
        out_shape=[out(rows, ff * zsize), out(rows, ff * zsize), out(ff, width), out(rows, width), out(rows, width), out(rows, width // 2), out(rows, width // 2)],
        in_specs=[
            pl.BlockSpec((chips, cores, block, two), lambda i: (0, 0, i, 0)),
            pl.BlockSpec((2, 1, rows, fold), lambda i: (i % 2, i // 2, 0, two // fold)),
            flat(width), flat(width), flat(width),
        ],
        out_specs=[flat(ff * zsize), flat(ff * zsize), pl.BlockSpec((ff // steps, width), lambda i: (i, 0)), flat(width), flat(width), flat(width // 2), flat(width // 2)],
        cost_estimate=pl.CostEstimate(flops=0, bytes_accessed=39 * 2**20, transcendentals=0),
        compiler_params=pltpu.CompilerParams(vmem_limit_bytes=40 * 2**20),
        name="assemble",
    )(packs, packs, o, q, kv)


def mm(left, right, left_dim, right_dim):
    return lax.dot_general(left, right, (((left_dim,), (right_dim,)), ((), ())), preferred_element_type=F32)


def swap(a):
    return lax.ppermute(a, "ctx", [(i, i ^ 1) for i in range(lax.axis_size("ctx"))])


def hop(a, r):
    return lax.ppermute(a, "ctx", [(i, i ^ (2 * r)) for i in range(lax.axis_size("ctx"))])


def ring(a):
    n = lax.axis_size("fsdp")
    return lax.ppermute(a, "fsdp", [(i, (i + 1) % n) for i in range(n)])


def pick(a, index, axis=0):
    return lax.dynamic_index_in_dim(a, index, axis, keepdims=False)


def place(buffer, piece, index, axis=0):
    return lax.dynamic_update_slice_in_dim(buffer, jnp.expand_dims(piece, axis), index, axis)


def shift(a, s):
    n = lax.axis_size("fsdp")
    return lax.ppermute(a, "fsdp", [(i, (i + s) % n) for i in range(n)])


def depth_gather(piece, depth):
    n = lax.axis_size("fsdp")
    buffer = place(jnp.zeros((n,) + piece.shape, piece.dtype), piece, depth)
    for s in range(1, n):
        piece = ring(piece)
        buffer = place(buffer, piece, lax.rem(depth + n - s, n))
    return buffer


def depth_scatter(parts, depth):
    n = lax.axis_size("fsdp")
    total = pick(parts, lax.rem(depth + n - 1, n))
    for s in range(n - 1):
        total = ring(total.astype(BF))
        total = total.astype(F32) + pick(parts, lax.rem(depth + 2 * n - 2 - s, n)).astype(F32)
    return total


def plane_gather(piece, index):
    n = lax.axis_size("ctx")
    chips = n // 2
    pieces = jnp.stack([piece] + [hop(piece, r) for r in range(1, chips)])
    others = swap(pieces)
    buffer = jnp.zeros((n,) + piece.shape, piece.dtype)
    for r in range(chips):
        buffer = place(buffer, pieces[r], index ^ (2 * r))
        buffer = place(buffer, others[r], index ^ (2 * r + 1))
    return buffer


def rotate(v, cosine, sine):
    heads = v.reshape(-1, 2, HEAD_WIDTH // 2, v.shape[-1])
    a, b = heads[:, 0], heads[:, 1]
    return jnp.stack([a * cosine - b * sine, b * cosine + a * sine], 1).reshape(v.shape)


def rotate_back(v, cosine, sine):
    heads = v.reshape(-1, 2, HEAD_WIDTH // 2, v.shape[-1])
    a, b = heads[:, 0], heads[:, 1]
    return jnp.stack([a * cosine + b * sine, b * cosine - a * sine], 1).reshape(v.shape)


def norm_back(incoming, unit, inverse, gain):
    scaled = incoming * gain
    return inverse * (scaled - unit * jnp.mean(scaled * unit, -1, keepdims=True))


def body(
    tokens,
    block_pairs,
    cotangent,
    attention_gain,
    query_weight,
    key_matrix,
    value_matrix,
    output_weight,
    feedforward_gain,
    gate_weight,
    up_weight,
    down_weight,
):
    slice_len, width = tokens.shape[1], tokens.shape[2]
    ctx = lax.axis_size("ctx")
    zsize = lax.axis_size("fsdp")
    chips = ctx // 2
    diag = chips - 1
    near = range(1, chips - 1)
    index = lax.axis_index("ctx")
    chip, core = index // 2, lax.rem(index, 2)
    depth = lax.axis_index("fsdp")
    rows = width // zsize
    strip = rows // ctx
    hidden_rows = down_weight.shape[0]
    fine = hidden_rows // ctx
    chunk = fine * zsize
    kv_rows = KEY_HEADS * HEAD_WIDTH

    cot_there = swap(cotangent)
    cot = jnp.concatenate(
        [pick(cotangent, core), pick(cot_there, core), pick(cot_there, 1 - core), pick(cotangent, 1 - core)]
    )
    length = 2 * slice_len

    ids_all = jnp.concatenate([pick(block_pairs, index ^ r) for r in range(ctx)])
    ids = ids_all[:4]
    blocks = ids_all.shape[0]
    order = jnp.sum(
        jnp.where(ids_all[None, :] == jnp.arange(blocks, dtype=jnp.int32)[:, None], jnp.arange(blocks, dtype=jnp.int32)[None, :], 0), 1
    )
    positions = (ids[:, None] * BLK + jnp.arange(BLK, dtype=jnp.int32)[None, :]).reshape(length)
    half = HEAD_WIDTH // 2
    frequency = THETA ** (-jnp.arange(half, dtype=F32) * 2.0 / HEAD_WIDTH)
    angles = frequency[:, None] * positions.astype(F32)[None, :]
    cosine, sine = jnp.cos(angles), jnp.sin(angles)

    packs, keys, values = {}, {}, {}
    folds = rows // fine
    fast = chips == 4 and strip % 16 == 0 and fine % 128 == 0
    if fast:
        (key_value_full, query_full, output_full, pack, far_pack, x, first, query, gains_full, *kv) = front(
            tokens, jnp.stack([attention_gain, feedforward_gain]).astype(F32), key_matrix, value_matrix, query_weight,
            output_weight, gate_weight, up_weight, down_weight, cosine, sine, zsize, ctx,
        )
        key_value_full, query_full, output_full = (w.reshape(width, width) for w in (key_value_full, query_full, output_full))
        packs[0] = [pack]
        for r in range(chips):
            keys[r], values[r] = kv[r], kv[chips + r]
        x = x.astype(F32)
        gain_first, gain_second = gains_full[0], gains_full[1]
        inverse_first = lax.rsqrt(jnp.mean(x * x, -1, keepdims=True) + EPS)
        unit_first = x * inverse_first
        first_t = jnp.transpose(first)
        packs[diag] = [far_pack] + [shift(far_pack, s) for s in range(1, zsize)]
    else:
        gate_cut = gate_weight.reshape(rows, zsize, 2, chips, fine)
        up_cut = up_weight.reshape(rows, zsize, 2, chips, fine)
        down_cut = down_weight.reshape(2, chips, fine, width)

        def own_piece(r):
            gate = pick(pick(gate_cut, core, 2), chip ^ r, 2).reshape(rows, chunk)
            up = pick(pick(up_cut, core, 2), chip ^ r, 2).reshape(rows, chunk)
            down = pick(pick(down_cut, core), chip ^ r)
            folded = jnp.transpose(down.reshape(fine, folds, width // folds), (1, 0, 2)).reshape(rows, width // folds)
            return jnp.concatenate([gate, up, folded], 1)

        gains = jnp.stack([attention_gain, feedforward_gain])
        gain_buffer = place(jnp.zeros((zsize, 2, rows), BF), gains, depth)
        for s in range(1, zsize):
            moved = lax.ppermute(gains, "fsdp", [(k, (k + s) % zsize) for k in range(zsize)])
            gain_buffer = place(gain_buffer, moved, lax.rem(depth + zsize - s, zsize))
        gains_full = jnp.transpose(gain_buffer, (1, 0, 2)).reshape(2, width).astype(F32)
        gain_first, gain_second = gains_full[0], gains_full[1]

        def gather_square(shard):
            strips = shard.reshape(ctx, strip, shard.shape[1])
            pair = jnp.stack([pick(strips, index), pick(strips, index ^ (2 * diag))])
            pair = depth_gather(pair, depth)
            own, far = pair[:, 0], pair[:, 1]
            found = {0: own, diag: far}
            for r in near:
                found[r] = hop(own, r)
            full = jnp.zeros((zsize, ctx, strip, shard.shape[1]), BF)
            for r in range(chips):
                full = place(full, found[r], index ^ (2 * r), 1)
                full = place(full, swap(found[r]), index ^ (2 * r + 1), 1)
            return full.reshape(width, shard.shape[1])

        key_value_full = gather_square(jnp.concatenate([key_matrix, value_matrix], 1))
        query_full = gather_square(query_weight)
        output_full = gather_square(output_weight)

        x = jnp.concatenate([pick(tokens, core), swap(pick(tokens, 1 - core))]).astype(F32)
        packs[0] = [depth_gather(own_piece(0), depth)]
        inverse_first = lax.rsqrt(jnp.mean(x * x, -1, keepdims=True) + EPS)
        unit_first = x * inverse_first
        first = (unit_first * gain_first).astype(BF)
        first_t = jnp.transpose(first)
        kv = mm(key_value_full, first_t, 0, 0)
        keys[0] = rotate(kv[:kv_rows], cosine, sine).astype(BF)
        values[0] = kv[kv_rows:].astype(BF)
        for r in range(1, chips):
            high = 1 << (r.bit_length() - 1)
            low = r & -r
            keys[r] = hop(keys[r ^ high], high)
            values[r] = hop(values[r ^ low], low)
        query = rotate(mm(query_full, first_t, 0, 0), cosine, sine).astype(BF)
        packs[diag] = [depth_gather(own_piece(diag), depth)]

    for r in near:
        packs[r] = [hop(packs[0][0], r)]

    key_list = [keys[r] for r in range(chips)]
    value_list = [values[r] for r in range(chips)]
    attended, log_total = attn_fwd(ids, order, query, key_list, value_list, KEY_HEADS)

    middle = x + mm(attended, output_full, 0, 0)
    inverse_second = lax.rsqrt(jnp.mean(middle * middle, -1, keepdims=True) + EPS)
    unit_second = middle * inverse_second
    second = (unit_second * gain_second).astype(BF)
    second = jnp.concatenate([second, swap(second)])
    second_t = jnp.transpose(second)
    grads, hidden, low = {}, {}, {}
    for r in [0] + list(near) + [diag]:
        hidden[r], low[r], grads[r] = ffn_chunk(second, second_t, cot, packs[r], zsize, fine)
    every = range(chips)
    out_part, second_grad = combine([hidden[r] for r in every], [low[r] for r in every], [packs[r] for r in every], zsize, fine)

    q = slice_len
    out_part = jnp.concatenate([out_part[:length] + middle, out_part[length:]])
    came = swap(jnp.concatenate([out_part[2 * q:3 * q], out_part[q:2 * q]]))
    out_here = (out_part[:q] + came[:q]).astype(BF)
    out_there = (out_part[3 * q:] + came[q:]).astype(BF)

    def stored(here, there):
        return jnp.where(core == 0, jnp.stack([here, there]), jnp.stack([there, here]))

    layer_out = stored(out_here, out_there)

    second_grad = second_grad[:length] + swap(second_grad[length:])
    gain_second_part = jnp.sum(second_grad * unit_second, 0)
    middle_grad = cot[:length].astype(F32) + norm_back(second_grad, unit_second, inverse_second, gain_second)

    def halves(a):
        cut = a.reshape(zsize, chips, 2, strip, length)
        here = pick(cut, core, 2).reshape(-1, length)
        there = swap(pick(cut, 1 - core, 2).reshape(-1, length))
        return jnp.concatenate([here, there], 1)

    first_half = halves(first_t)
    middle_low = middle_grad.astype(BF)
    out_part_grad = mm(halves(attended), jnp.concatenate([middle_low, swap(middle_low)]), 1, 0)
    attended_grad = mm(output_full, middle_low, 1, 1).astype(BF)
    query_low, key_parts, value_parts = attn_bwd(
        ids, order, query, attended, attended_grad, log_total, cosine, sine, key_list, value_list, KEY_HEADS
    )
    if fast:
        o_all, q_all, kv_all, pack_all, kv_low = tail(
            key_parts, value_parts, query_low, cosine, sine, first_half,
            out_part_grad.astype(BF).reshape(zsize, chips, strip, width),
            [grads[0][0], hop(grads[1][0], 1), hop(grads[2][0], 2)],
            [grads[diag][0]] + [shift(grads[diag][s], s) for s in range(1, zsize)], zsize, chips,
        )
        gate_grad, up_grad, down_grad, output_grad, query_grad, key_grad, value_grad = assemble(
            pack_all, *(a.reshape(rows, width) for a in (o_all, q_all, kv_all)), zsize, fine
        )
    else:
        key_sum = [part for part in key_parts]
        value_sum = [part for part in value_parts]
        for r in range(chips - 1, 0, -1):
            high = 1 << (r.bit_length() - 1)
            low = r & -r
            key_sum[r ^ high] = key_sum[r ^ high].astype(F32) + hop(key_sum[r].astype(BF), high).astype(F32)
            value_sum[r ^ low] = value_sum[r ^ low].astype(F32) + hop(value_sum[r].astype(BF), low).astype(F32)
        key_low = rotate_back(key_sum[0], cosine, sine).astype(BF)
        value_low = value_sum[0].astype(BF)
        kv_low = jnp.concatenate([key_low, value_low])

        def scatter(parts):
            total = parts[0].astype(F32)
            for r in near:
                total = total + hop(parts[r], r).astype(F32)
            far = hop(depth_scatter(parts[diag], depth).astype(BF), diag)
            total = depth_scatter(total.astype(BF), depth) + far.astype(F32)
            return total.astype(BF)

        pack_all = plane_gather(scatter({r: grads[r][0] for r in range(chips)}), index)
        wide_all = pack_all[:, :, :2 * chunk]
        tall_all = jnp.transpose(pack_all[:, :, 2 * chunk:].reshape(ctx, folds, fine, width // folds), (0, 2, 1, 3))
        def square_grad(product):
            parts = product.astype(BF).reshape(zsize, chips, strip, width)
            piece = scatter({r: pick(parts, chip ^ r, 1) for r in range(chips)})
            return plane_gather(piece, index).reshape(rows, width).astype(F32)

        output_grad = square_grad(out_part_grad)
        query_grad = square_grad(mm(first_half, jnp.concatenate([query_low, swap(query_low)], 1), 1, 1))
        kv_grad = square_grad(mm(first_half, jnp.concatenate([kv_low, swap(kv_low)], 1), 1, 1))
        down_grad = jnp.transpose(tall_all.reshape(chips, 2, fine, width), (1, 0, 2, 3)).reshape(hidden_rows, width).astype(F32)
        wide_all = wide_all.reshape(chips, 2, rows, 2, zsize, fine)
        gate_grad = jnp.transpose(wide_all[:, :, :, 0], (2, 3, 1, 0, 4)).reshape(rows, -1).astype(F32)
        up_grad = jnp.transpose(wide_all[:, :, :, 1], (2, 3, 1, 0, 4)).reshape(rows, -1).astype(F32)
        key_grad, value_grad = kv_grad[:, :kv_rows], kv_grad[:, kv_rows:]

    first_grad = mm(query_low, query_full, 0, 1) + mm(kv_low, key_value_full, 0, 1)
    gain_first_part = jnp.sum(first_grad * unit_first, 0)
    tokens_part = (middle_grad + norm_back(first_grad, unit_first, inverse_first, gain_first)).astype(BF)
    tokens_grad = stored(tokens_part[:q], swap(tokens_part[q:]))

    def gain_total(part):
        cut = part.reshape(zsize, rows)
        total = pick(cut, depth)
        for s in range(1, zsize):
            total = total + lax.ppermute(
                pick(cut, lax.rem(depth + s, zsize)), "fsdp", [(k, (k + s) % zsize) for k in range(zsize)]
            )
        total = total + swap(total)
        bit = 1
        while bit < chips:
            total = total + hop(total, bit)
            bit *= 2
        return total

    return (
        layer_out,
        tokens_grad,
        gain_total(gain_first_part),
        query_grad,
        key_grad,
        value_grad,
        output_grad,
        gain_total(gain_second_part),
        gate_grad,
        up_grad,
        down_grad,
    )


def solution(mesh):
    line, square, grid = P("fsdp"), P("fsdp", None), P("fsdp", "ctx", None)
    in_specs = (grid, P(), grid, line, square, square, square, square, line, square, square, square)
    out_specs = (grid, grid, line, square, square, square, square, line, square, square, square)
    return jax.shard_map(body, mesh=mesh, in_specs=in_specs, out_specs=out_specs, check_vma=False)
```

```python
import functools

import jax
import jax.numpy as jnp
from jax import lax
from jax.experimental import pallas as pl
from jax.experimental.pallas import tpu as pltpu
from jax.sharding import PartitionSpec as P

QUERY_HEADS = 16
KEY_HEADS = 8
HEAD_WIDTH = 96
EPS = 1e-05
THETA = 100000.0
BLK = 128
SCALE = HEAD_WIDTH ** -0.5
BF = jnp.bfloat16
F32 = jnp.float32
NO_COST = pl.CostEstimate(flops=0, bytes_accessed=0, transcendentals=0)
LONG = pl.CostEstimate(flops=200 * 10**9, bytes_accessed=0, transcendentals=0)

LOG2E = 1.4426950408889634
NT = (((1,), (1,)), ((), ()))


def block_tasks(ids_ref, inv_ref, slices, t):
    tasks = []
    for sl in range(slices):
        first = ids_ref[2 * sl]
        late = (t > first).astype(jnp.int32)
        kpos = t - late * (first + 1)
        tasks.append((sl, late, inv_ref[kpos], (ids_ref[2 * sl + late] - kpos) * BLK))
    return tasks


def causal_difference():
    return lax.broadcasted_iota(jnp.int32, (BLK, 2 * BLK), 0) - lax.rem(lax.broadcasted_iota(jnp.int32, (BLK, 2 * BLK), 1), BLK)


def load_keys(refs, scratch, sem):
    copies = [pltpu.make_async_copy(ref, scratch.at[n], sem.at[n]) for n, ref in enumerate(refs)]

    @pl.when(pl.program_id(0) == 0)
    def _():
        for copy in copies:
            copy.start()
        for copy in copies:
            copy.wait()


def fwd_kernel(nchip, heads, ids_ref, inv_ref, q_ref, *rest):
    o_ref, lse_ref, kv_s, sem, knat, vtr = rest[2 * nchip:2 * nchip + 6]
    state = rest[2 * nchip + 6:]
    load_keys(rest[:2 * nchip], kv_s, sem)
    base = pl.program_id(0) * (96 * heads)
    nq = q_ref.shape[1] // BLK
    slices = nq // 2
    nb = nchip * nq
    c = SCALE * LOG2E
    chains = [(h, sl) for h in range(heads) for sl in range(slices)]
    qs, m_s, l_s, acc = ({chain: state[4 * n + k] for n, chain in enumerate(chains)} for k in range(4))
    for h in range(heads):
        for n in range(nb):
            r, lanes = n // nq, slice(BLK * (n % nq), BLK * (n % nq + 1))
            part = pl.ds(pl.multiple_of(base + 96 * h, 96), 96)
            knat[h, n] = kv_s[r, part, lanes].T
            vtr[h, n] = kv_s[nchip + r, part, lanes]
        for sl in range(slices):
            for half in range(2):
                lanes = slice(BLK * (2 * sl + half), BLK * (2 * sl + half + 1))
                qs[h, sl][half] = jnp.concatenate([q_ref[192 * h:192 * h + 96, lanes], q_ref[192 * h + 96:192 * h + 192, lanes]], axis=1)
            m_s[h, sl][...] = jnp.full((2, 1, 2 * BLK), -1e30, F32)
            l_s[h, sl][...] = jnp.zeros((2, 1, 2 * BLK), F32)
            acc[h, sl][...] = jnp.zeros((2, 96, 2 * BLK), F32)
    diff = causal_difference()

    def step(t, _):
        tasks = block_tasks(ids_ref, inv_ref, slices, t)
        todo = [(h, *task) for h in range(heads) for task in tasks]
        scores = [
            jnp.where(diff <= offset, jnp.dot(knat[h, n], qs[h, sl][late], preferred_element_type=F32), -jnp.inf)
            for h, sl, late, n, offset in todo
        ]
        old = [(m_s[h, sl][late], l_s[h, sl][late], acc[h, sl][late]) for h, sl, late, n, offset in todo]
        peaks = [jnp.maximum(m, jnp.max(s, axis=0, keepdims=True)) for s, (m, _l, _a) in zip(scores, old)]
        weights = [jnp.exp2((s - peak) * c) for s, peak in zip(scores, peaks)]
        shrink = [jnp.exp2((m - peak) * c) for peak, (m, _l, _a) in zip(peaks, old)]
        totals = [l * a + jnp.sum(p, axis=0, keepdims=True) for (_m, l, _a), a, p in zip(old, shrink, weights)]
        mixed = [
            o * a + jnp.dot(vtr[h, n], p.astype(BF), preferred_element_type=F32)
            for (h, sl, late, n, offset), (_m, _l, o), a, p in zip(todo, old, shrink, weights)
        ]
        for (h, sl, late, n, offset), peak, total, o in zip(todo, peaks, totals, mixed):
            m_s[h, sl][late] = peak
            l_s[h, sl][late] = total
            acc[h, sl][late] = o
        return 0

    lax.fori_loop(0, nb + 1, step, 0)
    for h, sl in chains:
        for half in range(2):
            lanes = slice(BLK * (2 * sl + half), BLK * (2 * sl + half + 1))
            l = l_s[h, sl][half]
            o = acc[h, sl][half] / l
            lse_ref[h, 2 * sl + half] = m_s[h, sl][half] * c + jnp.log2(l)
            o_ref[192 * h:192 * h + 96, lanes] = o[:, :BLK].astype(BF)
            o_ref[192 * h + 96:192 * h + 192, lanes] = o[:, BLK:].astype(BF)


def attn_fwd(ids, inv, qT, ks, vs, heads):
    nchip = len(ks)
    T = qT.shape[1]
    nq = T // BLK
    nb = nchip * nq
    per = 4 if nb <= 16 else 2
    wide = pl.BlockSpec((192 * per, T), lambda g, *_: (g, 0))
    slim = pl.BlockSpec((96 * per, T), lambda g, *_: (g, 0))
    chain = [
        pltpu.VMEM((2, 96, 2 * BLK), BF),
        pltpu.VMEM((2, 1, 2 * BLK), F32),
        pltpu.VMEM((2, 1, 2 * BLK), F32),
        pltpu.VMEM((2, 96, 2 * BLK), F32),
    ]
    grid_spec = pltpu.PrefetchScalarGridSpec(
        num_scalar_prefetch=2,
        grid=(heads // per,),
        in_specs=[wide] + [pl.BlockSpec(memory_space=pltpu.HBM)] * (2 * nchip),
        out_specs=[wide, pl.BlockSpec((per, nq, 1, 2 * BLK), lambda g, *_: (g, 0, 0, 0))],
        scratch_shapes=[
            pltpu.VMEM((2 * nchip, heads * 96, T), BF), pltpu.SemaphoreType.DMA((2 * nchip,)),
            pltpu.VMEM((per, nb, BLK, 96), BF), pltpu.VMEM((per, nb, 96, BLK), BF),
        ] + chain * (per * nq // 2),
    )
    return pl.pallas_call(
        functools.partial(fwd_kernel, nchip, per),
        grid_spec=grid_spec,
        out_shape=[jax.ShapeDtypeStruct((heads * 192, T), BF), jax.ShapeDtypeStruct((heads, nq, 1, 2 * BLK), F32)],
        cost_estimate=NO_COST,
        compiler_params=pltpu.CompilerParams(vmem_limit_bytes=56 * 2**20),
        name="attention_forward",
    )(ids, inv, qT, *ks, *vs)


def bwd_kernel(nchip, heads, ids_ref, inv_ref, q_ref, o_ref, do_ref, lse_ref, cos_ref, sin_ref, *rest):
    dq_ref = rest[2 * nchip]
    dk_refs, dv_refs = rest[2 * nchip + 1:3 * nchip + 1], rest[3 * nchip + 1:4 * nchip + 1]
    kv_s, sem, knat, ktr, vnat = rest[4 * nchip + 1:4 * nchip + 6]
    state = rest[4 * nchip + 6:]
    load_keys(rest[:2 * nchip], kv_s, sem)
    base = pl.program_id(0) * (96 * heads)
    nq = q_ref.shape[1] // BLK
    slices = nq // 2
    nb = nchip * nq
    c = SCALE * LOG2E
    chains = [(h, sl) for h in range(heads) for sl in range(slices)]
    qs, dos, stat, dq_s, dk_s, dv_s = ({chain: state[6 * n + k] for n, chain in enumerate(chains)} for k in range(6))
    for h in range(heads):
        for n in range(nb):
            r, lanes = n // nq, slice(BLK * (n % nq), BLK * (n % nq + 1))
            part = pl.ds(pl.multiple_of(base + 96 * h, 96), 96)
            block = kv_s[r, part, lanes]
            knat[h, n] = block.T
            ktr[h, n] = block
            vnat[h, n] = kv_s[nchip + r, part, lanes].T
    for h, sl in chains:
        for half in range(2):
            lanes = slice(BLK * (2 * sl + half), BLK * (2 * sl + half + 1))
            pair = lambda ref: jnp.concatenate([ref[192 * h:192 * h + 96, lanes], ref[192 * h + 96:192 * h + 192, lanes]], axis=1)
            do = pair(do_ref)
            qs[h, sl][half] = pair(q_ref)
            dos[h, sl][half] = do
            stat[h, sl][half, 0:1] = lse_ref[h, 2 * sl + half]
            stat[h, sl][half, 1:2] = jnp.sum(pair(o_ref).astype(F32) * do.astype(F32), axis=0, keepdims=True)
        dq_s[h, sl][...] = jnp.zeros((2, 96, 2 * BLK), F32)
        dk_s[h, sl][...] = jnp.zeros((nb, 96, BLK), F32)
        dv_s[h, sl][...] = jnp.zeros((nb, 96, BLK), F32)
    diff = causal_difference()

    def step(t, _):
        tasks = block_tasks(ids_ref, inv_ref, slices, t)
        todo = [(h, *task) for h in range(heads) for task in tasks]
        q = [qs[h, sl][late] for h, sl, late, n, offset in todo]
        do = [dos[h, sl][late] for h, sl, late, n, offset in todo]
        scores = [jnp.dot(knat[h, n], x, preferred_element_type=F32) for (h, sl, late, n, offset), x in zip(todo, q)]
        grads = [jnp.dot(vnat[h, n], x, preferred_element_type=F32) for (h, sl, late, n, offset), x in zip(todo, do)]
        weights = [
            jnp.exp2(jnp.where(diff <= offset, s * c - stat[h, sl][late, 0:1], -jnp.inf))
            for (h, sl, late, n, offset), s in zip(todo, scores)
        ]
        low = [(p * (g - stat[h, sl][late, 1:2])).astype(BF) for (h, sl, late, n, offset), p, g in zip(todo, weights, grads)]
        dv = [lax.dot_general(x, p.astype(BF), NT, preferred_element_type=F32) for x, p in zip(do, weights)]
        dk = [lax.dot_general(x, ds, NT, preferred_element_type=F32) for x, ds in zip(q, low)]
        dq = [jnp.dot(ktr[h, n], ds, preferred_element_type=F32) for (h, sl, late, n, offset), ds in zip(todo, low)]
        for (h, sl, late, n, offset), a, b, d in zip(todo, dv, dk, dq):
            dv_s[h, sl][n] += a
            dk_s[h, sl][n] += b
            dq_s[h, sl][late] += d
        return 0

    lax.fori_loop(0, nb + 1, step, 0)
    for h, sl in chains:
        for half in range(2):
            lanes = slice(BLK * (2 * sl + half), BLK * (2 * sl + half + 1))
            cos, sin = cos_ref[:, lanes], sin_ref[:, lanes]
            for e in range(2):
                a = dq_s[h, sl][half, 0:48, BLK * e:BLK * (e + 1)] * SCALE
                b = dq_s[h, sl][half, 48:96, BLK * e:BLK * (e + 1)] * SCALE
                at = 192 * h + 96 * e
                dq_ref[at:at + 48, lanes] = (a * cos + b * sin).astype(BF)
                dq_ref[at + 48:at + 96, lanes] = (b * cos - a * sin).astype(BF)
    for h in range(heads):
        for n in range(nb):
            r, lanes = n // nq, slice(BLK * (n % nq), BLK * (n % nq + 1))
            dk = sum(dk_s[h, sl][n] for sl in range(slices))
            dv = sum(dv_s[h, sl][n] for sl in range(slices))
            dk_refs[r][96 * h:96 * (h + 1), lanes] = (dk * SCALE).astype(BF)
            dv_refs[r][96 * h:96 * (h + 1), lanes] = dv.astype(BF)


def attn_bwd(ids, inv, qT, oT, doT, lse, cosine, sine, ks, vs, heads):
    nchip = len(ks)
    T = qT.shape[1]
    nq = T // BLK
    nb = nchip * nq
    per = 4 if nb <= 16 else 2
    wide = pl.BlockSpec((192 * per, T), lambda g, *_: (g, 0))
    slim = pl.BlockSpec((96 * per, T), lambda g, *_: (g, 0))
    chain = [
        pltpu.VMEM((2, 96, 2 * BLK), BF),
        pltpu.VMEM((2, 96, 2 * BLK), BF),
        pltpu.VMEM((2, 2, 2 * BLK), F32),
        pltpu.VMEM((2, 96, 2 * BLK), F32),
        pltpu.VMEM((nb, 96, BLK), F32),
        pltpu.VMEM((nb, 96, BLK), F32),
    ]
    grid_spec = pltpu.PrefetchScalarGridSpec(
        num_scalar_prefetch=2,
        grid=(heads // per,),
        in_specs=[wide, wide, wide, pl.BlockSpec((per, nq, 1, 2 * BLK), lambda g, *_: (g, 0, 0, 0))]
        + [pl.BlockSpec((48, T), lambda g, *_: (0, 0))] * 2 + [pl.BlockSpec(memory_space=pltpu.HBM)] * (2 * nchip),
        out_specs=[wide] + [slim] * (2 * nchip),
        scratch_shapes=[
            pltpu.VMEM((2 * nchip, heads * 96, T), BF), pltpu.SemaphoreType.DMA((2 * nchip,)),
            pltpu.VMEM((per, nb, BLK, 96), BF), pltpu.VMEM((per, nb, 96, BLK), BF), pltpu.VMEM((per, nb, BLK, 96), BF),
        ]
        + chain * (per * nq // 2),
    )
    slab = jax.ShapeDtypeStruct((heads * 96, T), BF)
    outs = pl.pallas_call(
        functools.partial(bwd_kernel, nchip, per),
        grid_spec=grid_spec,
        out_shape=[jax.ShapeDtypeStruct((heads * 192, T), BF)] + [slab] * (2 * nchip),
        cost_estimate=LONG,
        compiler_params=pltpu.CompilerParams(vmem_limit_bytes=56 * 2**20),
        name="attention_backward",
    )(ids, inv, qT, oT, doT, lse, cosine, sine, *ks, *vs)
    return outs[0], outs[1:1 + nchip], outs[1 + nchip:]


def pack_width(rows, fine, zsize, width):
    return 2 * fine * zsize + width * fine // rows


def front_kernel(zsize, *refs):
    (tok, cot_in, gains, key_w, value_w, query_w, out_w, gate_w, up_w, down_w, cos, sin) = refs[:12]
    (kv_all, q_all, o_all, pack, rest, pack_x, pack_y, far_pack, cot, first_half, x_out, first, q_out, gains_out) = refs[12:26]
    (k0, k1, k2, k3, v0, v1, v2, v3) = refs[26:34]
    x_s, gain_s, full_kv, full_q, full_o, kv_s, first_s, pack_s, cot_s, ss, rs, ls, gs, gr = refs[34:]
    ks, vs = (k0, k1, k2, k3), (v0, v1, v2, v3)
    index, depth = lax.axis_index("ctx"), lax.axis_index("fsdp")
    chip, core = index // 2, lax.rem(index, 2)
    fine = down_w.shape[0] // 8
    chunk = fine * zsize
    folds = pack.shape[0] // fine
    fold = first.shape[1] // folds
    width = first.shape[1]
    length = first.shape[0]
    kv_rows = k0.shape[0]
    nxt, prv = lax.rem(depth + 1, zsize), lax.rem(depth + zsize - 1, zsize)
    to_next, to_prev = (index, nxt), (index, prv)
    chip_x, chip_y, chip_d = chip + 1 - 2 * lax.rem(chip, 2), lax.rem(chip + 2, 4), 3 - chip
    to_x, to_y, to_core = (chip_x * 2 + core, depth), (chip_y * 2 + core, depth), (chip * 2 + 1 - core, depth)

    barrier = pltpu.get_barrier_semaphore()
    for target in (to_next, to_prev, to_x, to_y, to_core):
        pl.semaphore_signal(barrier, inc=1, device_id=target, device_id_type=pl.DeviceIdType.MESH)
    pl.semaphore_wait(barrier, 5)

    count = [0, 0]
    sent = []

    def send(src, dst, target):
        k = count[0]
        count[0] += 1
        copy = pltpu.make_async_remote_copy(
            src_ref=src, dst_ref=dst, send_sem=ss.at[k], recv_sem=rs.at[k], device_id=target, device_id_type=pl.DeviceIdType.MESH
        )
        copy.start()
        sent.append(copy)
        return copy

    def local(src, dst):
        k = count[1]
        count[1] += 1
        copy = pltpu.make_async_copy(src, dst, ls.at[k])
        copy.start()
        return copy

    def slot(s):
        return lax.rem(depth + zsize - s, zsize)

    steps = range(1, zsize)
    last = zsize - 1
    tokens_there = send(tok.at[1 - core], x_s.at[1], to_core)
    own_kv = [local(key_w, full_kv.at[depth, :, :, :, pl.ds(0, kv_rows)]), local(value_w, full_kv.at[depth, :, :, :, pl.ds(kv_rows, kv_rows)])]
    gain_s[depth] = gains[...]
    for copy in own_kv:
        copy.wait()

    weights = {"kv": full_kv, "q": full_q, "o": full_o}
    shards = {"q": query_w, "o": out_w}
    moves = {}

    def ring_step(name, s):
        full = weights[name]
        place = full.at[slot(s - 1), chip, core]
        source = shards[name].at[chip, core] if name in shards and s == 1 else place
        moves[name, "ring", s] = send(source, place, to_next)

    def spread(name, s):
        place = weights[name].at[slot(s), chip, core]
        moves[name, "x", s] = send(place, place, to_x)
        moves[name, "y", s] = send(place, place, to_y)

    def forward(name, s):
        mid = width // 2
        moves[name, "x", s].wait_recv()
        left = weights[name].at[slot(s), chip_x, core, :, pl.ds(0, mid)]
        moves[name, "fy", s] = send(left, left, to_y)
        moves[name, "y", s].wait_recv()
        right = weights[name].at[slot(s), chip_y, core, :, pl.ds(mid, mid)]
        moves[name, "fx", s] = send(right, right, to_x)

    def cross(name, s):
        moves[name, "fx", s].wait_recv()
        moves[name, "fy", s].wait_recv()
        column = weights[name].at[slot(s), :, core]
        moves[name, "core", s] = send(column, column, to_core)

    def gain_step(s):
        place = gain_s.at[slot(s - 1)]
        copy = pltpu.make_async_remote_copy(
            src_ref=place, dst_ref=place, send_sem=gs.at[s], recv_sem=gr.at[s], device_id=to_next, device_id_type=pl.DeviceIdType.MESH
        )
        copy.start()
        sent.append(copy)
        moves["gain", s] = copy

    def ffn_step(s):
        moves["ffn", s] = send(pack_s.at[0] if s == 1 else rest.at[s - 2], rest.at[s - 1], to_next)

    ring_step("kv", 1)
    gain_step(1)
    own_late = [local(query_w, full_q.at[depth]), local(out_w, full_o.at[depth])]
    def cut_pack(which, target):
        copies = []
        for part in range(zsize):
            column = pl.multiple_of(part * (8 * fine) + core * (4 * fine) + which * fine, fine)
            copies.append(local(gate_w.at[:, pl.ds(column, fine)], target.at[:, pl.ds(part * fine, fine)]))
            copies.append(local(up_w.at[:, pl.ds(column, fine)], target.at[:, pl.ds(chunk + part * fine, fine)]))
        row = pl.multiple_of(core * (4 * fine) + which * fine, fine)
        for n in range(folds):
            copies.append(local(down_w.at[pl.ds(row, fine), pl.ds(n * fold, fold)], target.at[pl.ds(n * fine, fine), pl.ds(2 * chunk, fold)]))
        return copies

    own_ffn = cut_pack(chip, pack_s.at[0])
    far_ffn = cut_pack(chip_d, pack_s.at[1]) + cut_pack(chip_x, pack_s.at[2]) + cut_pack(chip_y, pack_s.at[3])
    far_ffn += [local(cot_in.at[core], cot_s.at[0]), local(cot_in.at[1 - core], cot_s.at[1])]
    cot_moves = [send(cot_in.at[1 - core], cot.at[1], to_core), send(cot_in.at[core], cot.at[2], to_core)]

    for s in steps:
        moves["kv", "ring", s].wait_recv()
        moves["gain", s].wait_recv()
        if s < last:
            ring_step("kv", s + 1)
            gain_step(s + 1)
        else:
            for copy in own_ffn:
                copy.wait()
            ring_step("q", 1)
            ffn_step(1)
        spread("kv", s)
    for s in steps:
        forward("kv", s)
        moves["q", "ring", s].wait_recv()
        ring_step("q", s + 1) if s < last else ring_step("o", 1)
        spread("q", s)
    for s in steps:
        cross("kv", s)

    tokens_there.wait_recv()
    x_out[0:length // 2] = tok[core]
    x_out[length // 2:] = x_s[1]
    gain_rows = [gain_s[place] for place in range(zsize)]
    gains_full = jnp.concatenate(gain_rows, axis=1)
    gains_out[...] = gains_full
    gain = gains_full[0:1]
    rows = 64

    def normalize(t, _):
        part = pl.ds(pl.multiple_of(t * rows, rows), rows)
        v = x_out[part].astype(F32)
        inverse = lax.rsqrt(jnp.mean(v * v, -1, keepdims=True) + EPS)
        first[part] = (v * inverse * gain).astype(BF)
        return 0

    lax.fori_loop(0, length // rows, normalize, 0)

    moves["o", "ring", 1].wait_recv()
    if last > 1:
        ring_step("o", 2)
    spread("o", 1)
    for s in steps:
        forward("q", s)
    for s in steps:
        moves["kv", "core", s].wait_recv()
    keep = [local(full_kv, kv_all)]
    tile = 384

    def project(weight, t, turn):
        cols = pl.ds(pl.multiple_of(t * tile, tile), tile)
        w = weight[:, :, :, :, cols].reshape(width, tile)
        r = jnp.dot(first[...], w, preferred_element_type=F32).T
        if turn:
            r = rotate(r, cos[...], sin[...])
        return r.astype(BF)

    def project_kv(t, turn):
        kv_s[pl.ds(pl.multiple_of(t * tile, tile), tile)] = project(full_kv, t, turn)
        return 0

    per = kv_rows // tile
    lax.fori_loop(0, per, lambda t, _: project_kv(t, True), 0)
    k_here, v_here = kv_s.at[pl.ds(0, kv_rows)], kv_s.at[pl.ds(kv_rows, kv_rows)]
    k_x, k_y = send(k_here, k1, to_x), send(k_here, k2, to_y)
    if last > 1:
        moves["o", "ring", 2].wait_recv()
        if last > 2:
            ring_step("o", 3)
        spread("o", 2)
    lax.fori_loop(per, 2 * per, lambda t, _: project_kv(t, False), 0)
    v_y, v_x = send(v_here, v2, to_y), send(v_here, v1, to_x)
    for s in range(3, zsize):
        moves["o", "ring", s].wait_recv()
        if s < last:
            ring_step("o", s + 1)
        spread("o", s)
    keep += [local(k_here, k0), local(v_here, v0)]
    for copy in far_ffn:
        copy.wait()
    keep += [local(pack_s.at[n], out) for n, out in enumerate((pack, far_pack, pack_x, pack_y))]
    keep += [local(cot_s.at[0], cot.at[0]), local(cot_s.at[1], cot.at[3])]
    for s in steps:
        cross("q", s)
    if last > 1:
        moves["ffn", 1].wait_recv()
        ffn_step(2)
    for z in range(zsize):
        strips = first[:, z * tile:(z + 1) * tile].astype(F32).T.astype(BF)
        first_s[z] = strips.reshape(4, 2, strips.shape[0] // 8, length)
    keep.append(local(first_s.at[:, :, core], first_half.at[:, :, :, pl.ds(0, length)]))
    half_move = send(first_s.at[:, :, 1 - core], first_half.at[:, :, :, pl.ds(length, length)], to_core)
    for s in steps:
        moves["q", "core", s].wait_recv()
    for copy in own_late:
        copy.wait()
    keep.append(local(full_q, q_all))

    def project_q(t, _):
        q_out[pl.ds(pl.multiple_of(t * tile, tile), tile)] = project(full_q, t, True)
        return 0

    lax.fori_loop(0, width // tile, project_q, 0)
    for s in steps:
        forward("o", s)
    k_x.wait_recv()
    k_d = send(k1, k3, to_y)
    v_y.wait_recv()
    v_d = send(v2, v3, to_x)
    for s in range(2, last):
        moves["ffn", s].wait_recv()
        ffn_step(s + 1)
    for s in steps:
        cross("o", s)
    for s in steps:
        moves["o", "core", s].wait_recv()
    keep.append(local(full_o, o_all))
    moves["ffn", last].wait_recv()
    for copy in (k_y, v_x, k_d, v_d, half_move, *cot_moves):
        copy.wait_recv()
    for copy in keep:
        copy.wait()
    for copy in sent:
        copy.wait_send()


def front(tokens, cotangent, gains, key_w, value_w, query_w, out_w, gate_w, up_w, down_w, cosine, sine, zsize, ctx):
    width = tokens.shape[2]
    length = 2 * tokens.shape[1]
    rows = width // zsize
    strip = rows // ctx
    fine = down_w.shape[0] // ctx
    packed = pack_width(rows, fine, zsize, width)
    kv_rows = key_w.shape[1]
    chips = ctx // 2
    cut = lambda w: w.reshape(chips, 2, strip, w.shape[1])
    square = jax.ShapeDtypeStruct((zsize, chips, 2, strip, width), BF)
    flat = jax.ShapeDtypeStruct((kv_rows, length), BF)
    hbm, vmem = pl.BlockSpec(memory_space=pltpu.HBM), pl.BlockSpec(memory_space=pltpu.VMEM)
    copies = 19 * (zsize - 1) + 12
    return pl.pallas_call(
        functools.partial(front_kernel, zsize),
        out_shape=[
            square, square, square,
            jax.ShapeDtypeStruct((rows, packed), BF),
            jax.ShapeDtypeStruct((zsize - 1, rows, packed), BF),
            jax.ShapeDtypeStruct((rows, packed), BF),
            jax.ShapeDtypeStruct((rows, packed), BF),
            jax.ShapeDtypeStruct((rows, packed), BF),
            jax.ShapeDtypeStruct((4, length // 2, width), BF),
            jax.ShapeDtypeStruct((zsize, chips, strip, 2 * length), BF),
            jax.ShapeDtypeStruct((length, width), BF),
            jax.ShapeDtypeStruct((length, width), BF),
            jax.ShapeDtypeStruct((width, length), BF),
            jax.ShapeDtypeStruct((2, width), F32),
        ] + [flat] * 8,
        in_specs=[vmem, hbm, vmem] + [hbm] * 7 + [vmem] * 2,
        out_specs=[hbm] * 10 + [vmem] * 4 + [hbm] * 8,
        scratch_shapes=[
            pltpu.VMEM((2, length // 2, width), BF),
            pltpu.VMEM((zsize, 2, rows), F32),
            pltpu.VMEM(square.shape, BF),
            pltpu.VMEM(square.shape, BF),
            pltpu.VMEM(square.shape, BF),
            pltpu.VMEM((2 * kv_rows, length), BF),
            pltpu.VMEM((zsize, chips, 2, strip, length), BF),
            pltpu.VMEM((4, rows, packed), BF),
            pltpu.VMEM((2, length // 2, width), BF),
            pltpu.SemaphoreType.DMA((copies,)),
            pltpu.SemaphoreType.DMA((copies,)),
            pltpu.SemaphoreType.DMA((20 + 8 * zsize + 4 * (rows // fine),)),
            pltpu.SemaphoreType.DMA((zsize,)),
            pltpu.SemaphoreType.DMA((zsize,)),
        ],
        compiler_params=pltpu.CompilerParams(collective_id=0, has_side_effects=True, vmem_limit_bytes=50 * 2**20),
        name="front",
    )(tokens, cotangent, gains, cut(key_w), cut(value_w), cut(query_w), cut(out_w), gate_w, up_w, down_w, cosine, sine)


def tail_kernel(zsize, *refs):
    dk, dv = refs[0:4], refs[4:8]
    dq, cos, sin, first_half, att_half = refs[8:13]
    pack_in, far_in = refs[13:16], refs[16:16 + zsize]
    mid_t, query_w, kv_w, x_in, middle, gain, second_part = refs[16 + zsize:23 + zsize]
    rest = refs[23 + zsize:]
    o_all, q_all, kv_all, pack_all, tokens_out, gains_out = rest[:6]
    (got, held, dq_pair, kv_pair, half, grads, gl, gr, gx, gy, gz, piece,
     pack_s, pack_0, pack_z, far_s, far_r, pack_p, first_grad, tokens_s, gain_s, gain_r, ss, rs, ls) = rest[6:]
    index, depth = lax.axis_index("ctx"), lax.axis_index("fsdp")
    chip, core = index // 2, lax.rem(index, 2)
    chip_x, chip_y, chip_d = chip + 1 - 2 * lax.rem(chip, 2), lax.rem(chip + 2, 4), 3 - chip
    nxt, prv = lax.rem(depth + 1, zsize), lax.rem(depth + zsize - 1, zsize)
    to_next, to_prev = (index, nxt), (index, prv)
    to_x, to_y, to_core = (chip_x * 2 + core, depth), (chip_y * 2 + core, depth), (chip * 2 + 1 - core, depth)
    to_far = (chip_d * 2 + core, depth)
    last = zsize - 1
    kv_rows = dk[0].shape[0]
    width = kv_w.shape[2]
    strip = piece.shape[1]
    length = dq.shape[1]

    barrier = pltpu.get_barrier_semaphore()
    for target in (to_next, to_prev, to_x, to_y, to_core, to_far):
        pl.semaphore_signal(barrier, inc=1, device_id=target, device_id_type=pl.DeviceIdType.MESH)
    pl.semaphore_wait(barrier, 6)

    count = [0, 0]
    sent, kept = [], []

    def send(src, dst, target):
        k = count[0]
        count[0] += 1
        copy = pltpu.make_async_remote_copy(
            src_ref=src, dst_ref=dst, send_sem=ss.at[k], recv_sem=rs.at[k], device_id=target, device_id_type=pl.DeviceIdType.MESH
        )
        copy.start()
        sent.append(copy)
        return copy

    def settle(copy):
        copy.wait_send()
        sent[:] = [other for other in sent if other is not copy]

    def local(src, dst):
        k = count[1]
        count[1] += 1
        copy = pltpu.make_async_copy(src, dst, ls.at[k])
        copy.start()
        return copy

    def wait_all(copies):
        for copy in copies:
            copy.wait()

    def received(*copies):
        for copy in copies:
            copy.wait_recv()

    def add_rows(target, sources, block):
        def one(t, _):
            part = pl.ds(pl.multiple_of(t * block, block), block)
            total = target[part].astype(F32)
            for source in sources:
                total = total + source[part].astype(F32)
            target[part] = total.astype(BF)
            return 0

        lax.fori_loop(0, target.shape[0] // block, one, 0)

    def place_at(j):
        return lax.rem(depth + 2 * zsize - 1 - j, zsize)

    k3, v3 = send(dk[3], got.at[0], to_y), send(dv[3], got.at[1], to_x)
    mid_swap = send(mid_t, held.at[1], to_core)
    q_swap = send(dq, dq_pair.at[1], to_core)

    part = pack_0.shape[0] // 2
    parts = [pl.ds(h * part, part) for h in range(2)]

    def load_ffn(j):
        return [local(pack_in[n].at[place_at(j)], pack_s.at[j % 2, n]) for n in range(3)]

    ffn_loads = {0: load_ffn(0)}
    load_o = [local(mid_t, held.at[0]), local(att_half, half.at[0])]
    load_q = [local(dq, dq_pair.at[0]), local(first_half, half.at[1])]
    load_far = [local(far_in[n], far_s.at[n]) for n in range(zsize)]

    moves = {}

    def ffn_step(j):
        if j + 1 <= last:
            ffn_loads[j + 1] = load_ffn(j + 1)
        wait_all(ffn_loads[j])
        for h in range(2):
            mine = [pack_s.at[j % 2, n, parts[h]] for n in range(3)]
            if j == 0:
                sum_rows(pack_0.at[parts[h]], mine, 64)
                moves["pack", h, 0] = send(pack_0.at[parts[h]], pack_z.at[0, parts[h]], to_next)
                continue
            received(moves["pack", h, j - 1])
            here = pack_z.at[j - 1, parts[h]]
            add_rows(here, mine, 64)
            if j < last:
                moves["pack", h, j] = send(here, pack_z.at[j, parts[h]], to_next)

    def sum_rows(target, sources, block):
        def one(t, _):
            part = pl.ds(pl.multiple_of(t * block, block), block)
            total = sources[0][part].astype(F32)
            for source in sources[1:]:
                total = total + source[part].astype(F32)
            target[part] = total.astype(BF)
            return 0

        lax.fori_loop(0, target.shape[0] // block, one, 0)

    mid = width // 2
    tiles = 512

    def stage_1(m):
        moves["l", m] = send(grads.at[m, :, chip_d, :, pl.ds(0, mid)], gl.at[m], to_y)
        moves["r", m] = send(grads.at[m, :, chip_d, :, pl.ds(mid, mid)], gr.at[m], to_x)

    def stage_2(m):
        received(moves["l", m])

        def left(zz, _):
            grads[m, zz, chip_x, :, 0:mid] = (grads[m, zz, chip_x, :, 0:mid].astype(F32) + gl[m, zz].astype(F32)).astype(BF)
            return 0

        lax.fori_loop(0, zsize, left, 0)
        moves["x", m] = send(grads.at[m, :, chip_x], gx.at[m], to_x)
        received(moves["r", m])

        def right(zz, _):
            grads[m, zz, chip_y, :, mid:] = (grads[m, zz, chip_y, :, mid:].astype(F32) + gr[m, zz].astype(F32)).astype(BF)
            return 0

        lax.fori_loop(0, zsize, right, 0)
        moves["y", m] = send(grads.at[m, :, chip_y], gy.at[m], to_y)

    def stage_3(m):
        received(moves["x", m], moves["y", m])

        def own(zz, _):
            grads[m, zz, chip] = (grads[m, zz, chip].astype(F32) + gx[m, zz].astype(F32) + gy[m, zz].astype(F32)).astype(BF)
            return 0

        lax.fori_loop(0, zsize, own, 0)
        moves["z", m, 0] = send(grads.at[m, place_at(0), chip], gz.at[m, 0], to_next)

    def ring_step(m, j):
        received(moves["z", m, j - 1])
        total = gz[m, j - 1].astype(F32) + grads[m, place_at(j), chip].astype(F32)
        if j < last:
            gz[m, j - 1] = total.astype(BF)
            moves["z", m, j] = send(gz.at[m, j - 1], gz.at[m, j], to_next)
        else:
            piece[m] = total.astype(BF)

    def spread(name, source, target):
        kept.append(local(source, target(chip, core)))
        moves[name, "x"] = send(source, target(chip, core), to_x)
        moves[name, "y"] = send(source, target(chip, core), to_y)

    def forward(name, target):
        received(moves[name, "x"])
        left = target(chip_x, core, pl.ds(0, mid))
        moves[name, "fy"] = send(left, left, to_y)
        received(moves[name, "y"])
        right = target(chip_y, core, pl.ds(mid, mid))
        moves[name, "fx"] = send(right, right, to_x)

    def cross(name, target):
        received(moves[name, "fx"], moves[name, "fy"])
        column = target(slice(None), core)
        moves[name, "core"] = send(column, column, to_core)

    def whole(ref):
        def at(p, c, cols=None):
            return ref.at[p, c] if cols is None else ref.at[p, c, :, cols]

        return at

    def half_rows(ref, h):
        def at(p, c, cols=None):
            return ref.at[p, c, parts[h]] if cols is None else ref.at[p, c, parts[h], cols]

        return at

    def product(m, pair, which):
        per = width // tiles

        def one(t, _):
            zz = t // per
            cols = pl.ds(pl.multiple_of(lax.rem(t, per) * tiles, tiles), tiles)
            nt = (((1,), (1,)), ((), ()))
            left = half[which, zz].reshape(4 * strip, 2 * length)
            r = lax.dot_general(left[:, 0:length], pair[0, cols], nt, preferred_element_type=F32)
            r = r + lax.dot_general(left[:, length:], pair[1, cols], nt, preferred_element_type=F32)
            grads[m, zz, :, :, cols] = r.astype(BF).reshape(4, strip, tiles)
            return 0

        lax.fori_loop(0, zsize * per, one, 0)

    ffn_step(0)
    received(mid_swap)
    wait_all(load_o)
    product(0, held, 0)
    stage_1(0)
    keys_0, keys_1 = held.at[0, pl.ds(0, kv_rows)], held.at[0, pl.ds(kv_rows, kv_rows)]
    values_0, values_2 = held.at[1, pl.ds(0, kv_rows)], held.at[1, pl.ds(kv_rows, kv_rows)]
    load_kv = [local(dk[0], keys_0), local(dk[1], keys_1), local(dv[0], values_0), local(dv[2], values_2)]
    received(q_swap)
    wait_all(load_q)
    product(1, dq_pair, 1)
    stage_1(1)

    received(k3)
    wait_all(load_kv)
    add_rows(keys_1, [got.at[0]], 96)
    k1 = send(keys_1, got.at[2], to_x)
    received(v3)
    add_rows(values_2, [got.at[1]], 96)
    v2 = send(values_2, got.at[3], to_y)
    k2, v1 = send(dk[2], got.at[4], to_y), send(dv[1], got.at[5], to_x)
    if last > 1:
        ffn_step(1)
    received(k1, k2, v1, v2)

    def finish_keys(h, _):
        rows = pl.ds(pl.multiple_of(h * 96, 96), 96)
        v = keys_0[rows].astype(F32) + got[2, rows].astype(F32) + got[4, rows].astype(F32)
        kv_pair[0, rows] = rotate_back(v, cos[...], sin[...]).astype(BF)
        return 0

    def finish_values(h, _):
        rows = pl.ds(pl.multiple_of(h * 96, 96), 96)
        v = values_0[rows].astype(F32) + got[3, rows].astype(F32) + got[5, rows].astype(F32)
        kv_pair[0, pl.ds(pl.multiple_of(kv_rows + h * 96, 96), 96)] = v.astype(BF)
        return 0

    lax.fori_loop(0, kv_rows // 96, finish_keys, 0)
    lax.fori_loop(0, kv_rows // 96, finish_values, 0)
    kv_swap = send(kv_pair.at[0], kv_pair.at[1], to_core)
    stage_2(0)
    stage_2(1)
    if last > 2:
        ffn_step(2)
    wait_all(load_far)
    add_rows(far_s.at[0], [far_s.at[n] for n in range(1, zsize)], 64)
    far = send(far_s.at[0], far_r, to_far)
    received(kv_swap)
    product(2, kv_pair, 1)
    stage_1(2)
    stage_3(0)
    stage_3(1)
    stage_2(2)
    for j in range(3, last):
        ffn_step(j)
    ffn_step(last)
    received(far)
    for h in range(2):
        sum_rows(pack_p.at[parts[h]], [pack_z.at[last - 1, parts[h]], far_r.at[parts[h]]], 64)
        spread(("pack", h), pack_p.at[parts[h]], half_rows(pack_all, h))
    for j in range(1, zsize):
        ring_step(0, j)
        ring_step(1, j)
        if j == 1:
            stage_3(2)
    spread(0, piece.at[0], whole(o_all))
    spread(1, piece.at[1], whole(q_all))
    for j in range(1, zsize):
        ring_step(2, j)
    spread(2, piece.at[2], whole(kv_all))
    settle(far)
    weight_at = [(pack_s.at[k // 3, k % 3], far_s.at[k]) for k in range(zsize)]
    loads = [(local(query_w.at[k], a), local(kv_w.at[k], b)) for k, (a, b) in enumerate(weight_at)]
    rows = width // zsize
    for k, (a, b) in enumerate(weight_at):
        wait_all(loads[k])
        r = jnp.dot(a[...], dq_pair[0], preferred_element_type=F32) + jnp.dot(b[...], kv_pair[0], preferred_element_type=F32)
        first_grad[:, k * rows:(k + 1) * rows] = r.T
    gain_s[...] = jnp.zeros(gain_s.shape, F32)
    gain_s[1:2] = second_part[...]

    def finish_tokens(t, _):
        at = pl.ds(pl.multiple_of(t * 64, 64), 64)
        v = x_in[at].astype(F32)
        inverse = lax.rsqrt(jnp.mean(v * v, -1, keepdims=True) + EPS)
        unit = v * inverse
        d = first_grad[at]
        gain_s[0:1] += jnp.sum(d * unit, axis=0, keepdims=True)
        scaled = d * gain[...]
        tokens_s[at] = (middle[at] + inverse * (scaled - unit * jnp.mean(scaled * unit, -1, keepdims=True))).astype(BF)
        return 0

    lax.fori_loop(0, length // 64, finish_tokens, 0)
    near_half = pl.ds(0, length // 2)
    kept.append(local(tokens_s.at[near_half], tokens_out.at[core]))
    tokens_swap = send(tokens_s.at[pl.ds(length // 2, length // 2)], tokens_out.at[core], to_core)
    gain_swap = send(gain_s, gain_r.at[0], to_core)

    targets = [(("pack", h), half_rows(pack_all, h)) for h in range(2)]
    targets += [(m, whole(ref)) for m, ref in enumerate((o_all, q_all, kv_all))]
    for name, target in targets[:2]:
        forward(name, target)
    received(gain_swap)
    settle(gain_swap)
    gain_s[...] += gain_r[0]
    for n, target in ((1, to_x), (2, to_y)):
        copy = send(gain_s, gain_r.at[n], target)
        for name, at in targets[2 * n:2 * n + 2]:
            forward(name, at)
        received(copy)
        settle(copy)
        gain_s[...] += gain_r[n]
    copy = send(gain_s, gain_r.at[3], to_next)
    wait_all(kept)
    for name, target in targets:
        cross(name, target)
    total = gain_s[...]
    for s in range(1, zsize):
        received(copy)
        total = total + gain_r[2 + s]
        if s < last:
            copy = send(gain_r.at[2 + s], gain_r.at[3 + s], to_next)
    gains_out[...] = total
    received(tokens_swap)
    for name, target in targets:
        received(moves[name, "core"])
    for copy in sent:
        copy.wait_send()


def tail(dk, dv, dq, cosine, sine, first_half, att_half, packs, far_packs, mid_t, query_w, kv_w, x, middle, gain, second_part, zsize, chips):
    kv_rows, length = dk[0].shape
    width = 2 * kv_rows
    strip = att_half.shape[2]
    rows, packed = packs[0].shape[1:]
    hbm, vmem = pl.BlockSpec(memory_space=pltpu.HBM), pl.BlockSpec(memory_space=pltpu.VMEM)
    shape = lambda *s: jax.ShapeDtypeStruct(s, BF)
    store = lambda *s: pltpu.VMEM(s, BF)
    copies = 15 + 3 * (zsize - 1) + 3 * (4 + zsize - 1) + 5 * 5
    cut = lambda w: w.reshape(zsize, rows, width)
    inputs = [*dk, *dv, dq, cosine, sine, first_half, att_half, *packs, *far_packs, mid_t, cut(query_w), cut(kv_w), x, middle, gain, second_part]
    last = zsize - 1
    return pl.pallas_call(
        functools.partial(tail_kernel, zsize),
        out_shape=[shape(chips, 2, strip, width)] * 3 + [
            shape(chips, 2, rows, packed), shape(2, length // 2, width), jax.ShapeDtypeStruct((8, width), F32)],
        in_specs=[hbm] * 9 + [vmem] * 2 + [hbm] * (len(inputs) - 15) + [vmem] * 4,
        out_specs=[hbm] * 5 + [vmem],
        scratch_shapes=[
            store(6, kv_rows, length), store(2, width, length), store(2, width, length), store(2, width, length),
            store(2, zsize, chips, strip, 2 * length), store(3, zsize, chips, strip, width),
            store(3, zsize, strip, width // 2), store(3, zsize, strip, width // 2),
            store(3, zsize, strip, width), store(3, zsize, strip, width),
            store(3, last, strip, width), store(3, strip, width),
            store(2, 3, rows, packed), store(rows, packed), store(last, rows, packed),
            store(zsize, rows, packed), store(rows, packed), store(rows, packed),
            pltpu.VMEM((length, width), F32), store(length, width), pltpu.VMEM((8, width), F32), pltpu.VMEM((zsize + 2, 8, width), F32),
            pltpu.SemaphoreType.DMA((copies,)), pltpu.SemaphoreType.DMA((copies,)),
            pltpu.SemaphoreType.DMA((6 * zsize + 14,)),
        ],
        compiler_params=pltpu.CompilerParams(collective_id=1, has_side_effects=True, vmem_limit_bytes=62 * 2**20),
        name="tail",
    )(*inputs)


def unfold(refs, wide, tall, start):
    zsize, fine = tall.shape[0], tall.shape[1]
    folds = wide.shape[1] // fine
    fold = tall.shape[2] // folds
    two = wide.shape[2]
    if len(refs) == 1:
        sources = [(refs[0], slice(None), (slice(None),))]
    else:
        depth = lax.axis_index("fsdp")
        pieces = [refs[0]] + ([refs[1].at[s] for s in range(zsize - 1)] if len(refs) == 2 else list(refs[1:]))
        sources = [(piece, lax.rem(depth + zsize - s, zsize), ()) for s, piece in enumerate(pieces)]
    for source, at, lead in sources:
        start(source.at[(*lead, slice(None), pl.ds(0, two))], wide.at[at])
        for n in range(folds):
            cols = pl.ds(n * fold, fold)
            start(source.at[(*lead, pl.ds(n * fine, fine), pl.ds(two, fold))], tall.at[at, :, cols])


def ffn_kernel(given, pieces, before, second, second_t, cot, *refs):
    weights, (hidden_o, low_o), grads = refs[:given], refs[given:given + 2], refs[given + 2:given + pieces + 2]
    s_v, st_v, c_v, wi_v, wo_v, h_v, ht_v, l_v, w_v, t_v, sem = refs[given + pieces + 2:]
    tokens, width = second.shape
    zsize, fine = wo_v.shape[:2]
    rows = wi_v.shape[1]
    chunk = zsize * fine
    loads = []

    def load(src, dst):
        copy = pltpu.make_async_copy(src, dst, sem.at[len(loads)])
        copy.start()
        loads.append(copy)

    unfold(weights, wi_v, wo_v, load)
    load(second, s_v)
    load(cot, c_v)
    load(second_t, st_v)
    for copy in loads[:-1]:
        copy.wait()
    nt = (((1,), (1,)), ((), ()))
    tile = 256

    def one(t, _):
        part = pl.ds(pl.multiple_of(t * tile, tile), tile)
        pre = jnp.dot(s_v[part], wi_v[...].reshape(width, 2 * chunk), preferred_element_type=F32)
        hidden_grad = lax.dot_general(c_v[part], wo_v[...].reshape(chunk, width), nt, preferred_element_type=F32)
        gate, up = pre[:, :chunk], pre[:, chunk:]
        sigmoid = jax.nn.sigmoid(gate)
        silu = gate * sigmoid
        hidden = silu * up
        h_v[part] = hidden.astype(BF)
        ht_v[:, part] = hidden.T.astype(BF)
        l_v[part, 0:chunk] = (hidden_grad * up * sigmoid * (1.0 + gate * (1.0 - sigmoid))).astype(BF)
        l_v[part, chunk:] = (hidden_grad * silu).astype(BF)
        return 0

    lax.fori_loop(0, tokens // tile, one, 0)
    stores = []

    def store(src, dst):
        copy = pltpu.make_async_copy(src, dst, sem.at[len(loads) + len(stores)])
        copy.start()
        stores.append(copy)

    store(h_v, hidden_o)
    store(l_v, low_o)
    loads[-1].wait()
    depth = 0 if pieces == 1 else lax.axis_index("fsdp")
    grad_at = lambda n: grads[0].at[n] if pieces == 1 else grads[n]

    def place(n):
        return n if pieces == 1 else lax.rem(depth + n, zsize)

    for n in range(zsize):
        z = place(n)
        part = pl.ds(pl.multiple_of(z * rows, rows), rows)
        w_v[z] = jnp.dot(st_v[part], l_v[...], preferred_element_type=F32).astype(BF)
        store(w_v.at[z], grad_at(n).at[:, pl.ds(0, 2 * chunk)])
    folds = rows // fine
    fold = width // folds
    for n in range(folds):
        cols = slice(fold * n, fold * (n + 1))
        t_v[:, :, cols] = jnp.dot(ht_v[...], c_v[:, cols], preferred_element_type=F32).astype(BF).reshape(zsize, fine, fold)
        if pieces == 1:
            store(t_v.at[:, :, cols], grads[0].at[:, pl.ds(n * fine, fine), pl.ds(2 * chunk, fold)])
        else:
            for k in range(zsize):
                store(t_v.at[place(k), :, cols], grads[k].at[pl.ds(n * fine, fine), pl.ds(2 * chunk, fold)])
    for copy in stores:
        copy.wait()


def ffn_chunk(before, second, second_t, cot, weights, split, zsize, fine):
    pieces = zsize if split else 1
    tokens, width = second.shape
    chunk = zsize * fine
    rows = width // zsize
    folds = rows // fine
    shape = lambda *s: jax.ShapeDtypeStruct(s, BF)
    store = lambda *s: pltpu.VMEM(s, BF)
    hbm = pl.BlockSpec(memory_space=pltpu.HBM)
    packed = weights[0].shape[-1]
    piece = (rows, packed) if split else (zsize, rows, packed)
    out = pl.pallas_call(
        functools.partial(ffn_kernel, len(weights), pieces),
        out_shape=[shape(tokens, chunk), shape(tokens, 2 * chunk)] + [shape(*piece)] * pieces,
        in_specs=[hbm] * (4 + len(weights)),
        out_specs=[hbm] * (2 + pieces),
        scratch_shapes=[
            store(tokens, width), store(width, tokens), store(tokens, width), store(zsize, rows, 2 * chunk), store(zsize, fine, width),
            store(tokens, chunk), store(chunk, tokens), store(tokens, 2 * chunk), store(zsize, rows, 2 * chunk), store(zsize, fine, width),
            pltpu.SemaphoreType.DMA((5 + zsize + 2 * zsize * (folds + 1),)),
        ],
        cost_estimate=NO_COST,
        compiler_params=pltpu.CompilerParams(vmem_limit_bytes=50 * 2**20),
        name="ffn_chunk",
    )(before, second, second_t, cot, *weights)
    return out[0], out[1], out[2:]

def combine_kernel(counts, *refs):
    count = len(counts)
    hidden, low = refs[:count], refs[count:2 * count]
    weights, at = [], 2 * count
    for n in counts:
        weights.append(refs[at:at + n])
        at += n
    out, grad, h_v, l_v, wi_v, wo_v, o_v, g_v, sem = refs[at:]
    tokens, chunk = hidden[0].shape
    width = out.shape[1]
    loads = []

    def load(src, dst):
        copy = pltpu.make_async_copy(src, dst, sem.at[len(loads)])
        copy.start()
        loads.append(copy)

    for r in range(count):
        load(hidden[r], h_v.at[:, pl.ds(r * chunk, chunk)])
        unfold(weights[r], wi_v.at[:, :, pl.ds(2 * r * chunk, 2 * chunk)], wo_v.at[r], load)
    for r in range(count):
        load(low[r], l_v.at[:, pl.ds(2 * r * chunk, 2 * chunk)])
    nt = (((1,), (1,)), ((), ()))
    tile = 256
    steps = tokens // tile
    stores = []

    def store(src, dst):
        copy = pltpu.make_async_copy(src, dst, sem.at[len(loads) + len(stores)])
        copy.start()
        stores.append(copy)

    for copy in loads[:-count]:
        copy.wait()
    for t in range(steps):
        rows = slice(tile * t, tile * (t + 1))
        if t >= 2:
            stores[t - 2].wait()
        o_v[t % 2] = jnp.dot(h_v[rows], wo_v[...].reshape(count * chunk, width), preferred_element_type=F32)
        store(o_v.at[t % 2], out.at[rows])
    for copy in loads[-count:]:
        copy.wait()
    for t in range(steps):
        rows = slice(tile * t, tile * (t + 1))
        if t >= 2:
            stores[steps + t - 2].wait()
        g_v[t % 2] = lax.dot_general(l_v[rows], wi_v[...].reshape(width, 2 * count * chunk), nt, preferred_element_type=F32)
        store(g_v.at[t % 2], grad.at[rows])
    for t in range(max(steps - 2, 0), steps):
        stores[t].wait()
        stores[steps + t].wait()


def combine(hidden, low, weights, zsize, fine):
    counts = tuple(len(w) for w in weights)
    count = len(counts)
    tokens, chunk = hidden[0].shape
    rows = weights[0][0].shape[-2]
    width = rows * zsize
    hbm = pl.BlockSpec(memory_space=pltpu.HBM)
    shape = jax.ShapeDtypeStruct((tokens, width), F32)
    inputs = [*hidden, *low] + [piece for w in weights for piece in w]
    return pl.pallas_call(
        functools.partial(combine_kernel, counts),
        out_shape=[shape, shape],
        in_specs=[hbm] * len(inputs),
        out_specs=[hbm] * 2,
        scratch_shapes=[
            pltpu.VMEM((tokens, count * chunk), BF), pltpu.VMEM((tokens, 2 * count * chunk), BF),
            pltpu.VMEM((zsize, rows, 2 * count * chunk), BF), pltpu.VMEM((count, zsize, fine, width), BF),
            pltpu.VMEM((2, 256, width), F32), pltpu.VMEM((2, 256, width), F32),
            pltpu.SemaphoreType.DMA((2 * count + sum(counts) * (1 + rows // fine) + 2 * (tokens // 256),)),
        ],
        cost_estimate=NO_COST,
        compiler_params=pltpu.CompilerParams(vmem_limit_bytes=56 * 2**20),
        name="ffn_combine",
    )(*inputs)


def assemble_kernel(zsize, wide, tall, o, q, kv, gate_o, up_o, down_o, o_o, q_o, k_o, v_o):
    fold = tall.shape[3]
    folds = down_o.shape[1] // fold
    fine = tall.shape[2] // folds
    kv_rows = k_o.shape[1]
    for p in range(4):
        for c in range(2):
            for part in range(zsize):
                at = slice((part * 8 + c * 4 + p) * fine, (part * 8 + c * 4 + p + 1) * fine)
                gate_o[:, at] = wide[p, c, :, part * fine:(part + 1) * fine].astype(F32)
                up_o[:, at] = wide[p, c, :, (zsize + part) * fine:(zsize + part + 1) * fine].astype(F32)
    for p in range(2):
        for n in range(folds):
            down_o[p * fine:(p + 1) * fine, n * fold:(n + 1) * fold] = tall[p, 0, n * fine:(n + 1) * fine].astype(F32)
    o_o[...] = o[...].astype(F32)
    q_o[...] = q[...].astype(F32)
    k_o[...] = kv[:, 0:kv_rows].astype(F32)
    v_o[...] = kv[:, kv_rows:].astype(F32)


def assemble(packs, o, q, kv, zsize, fine):
    chips, cores, rows, packed = packs.shape
    width = o.shape[1]
    steps = 4
    block = rows // steps
    two = 2 * fine * zsize
    fold = packed - two
    flat = lambda n: pl.BlockSpec((block, n), lambda i: (i, 0))
    out = lambda r, c: jax.ShapeDtypeStruct((r, c), F32)
    ff = fine * chips * cores
    return pl.pallas_call(
        functools.partial(assemble_kernel, zsize),
        grid=(steps,),
        out_shape=[out(rows, ff * zsize), out(rows, ff * zsize), out(ff, width), out(rows, width), out(rows, width), out(rows, width // 2), out(rows, width // 2)],
        in_specs=[
            pl.BlockSpec((chips, cores, block, two), lambda i: (0, 0, i, 0)),
            pl.BlockSpec((2, 1, rows, fold), lambda i: (i % 2, i // 2, 0, two // fold)),
            flat(width), flat(width), flat(width),
        ],
        out_specs=[flat(ff * zsize), flat(ff * zsize), pl.BlockSpec((ff // steps, width), lambda i: (i, 0)), flat(width), flat(width), flat(width // 2), flat(width // 2)],
        cost_estimate=NO_COST,
        compiler_params=pltpu.CompilerParams(vmem_limit_bytes=40 * 2**20),
        name="assemble",
    )(packs, packs, o, q, kv)


MESH = pl.DeviceIdType.MESH


class Mover:
    def __init__(self, send_sems, recv_sems, local_sems):
        self.sems = send_sems, recv_sems, local_sems
        self.sent, self.kept, self.counts = [], [], [0, 0]

    def send(self, src, dst, target):
        k = self.counts[0]
        self.counts[0] += 1
        copy = pltpu.make_async_remote_copy(
            src_ref=src, dst_ref=dst, send_sem=self.sems[0].at[k], recv_sem=self.sems[1].at[k], device_id=target, device_id_type=MESH
        )
        copy.start()
        self.sent.append(copy)
        return copy

    def local(self, src, dst):
        k = self.counts[1]
        self.counts[1] += 1
        copy = pltpu.make_async_copy(src, dst, self.sems[2].at[k])
        copy.start()
        return copy

    def settle(self, copy):
        copy.wait_send()
        self.sent = [other for other in self.sent if other is not copy]

    def finish(self):
        for copy in self.sent:
            copy.wait_send()
        for copy in self.kept:
            copy.wait()


def greet_other_core():
    index, depth = lax.axis_index("ctx"), lax.axis_index("fsdp")
    core = lax.rem(index, 2)
    other = (index + 1 - 2 * core, depth)
    barrier = pltpu.get_barrier_semaphore()
    pl.semaphore_signal(barrier, inc=1, device_id=other, device_id_type=MESH)
    pl.semaphore_wait(barrier, 1)
    return core, other


def bridge_kernel(att, weight, x, gain, middle, second, second_t, att_half, att_s, w_s, low_s, low_t, ss, rs, ls):
    core, other = greet_other_core()
    move = Mover(ss, rs, ls)
    zsize, chips, _, strip, length = att.shape
    width = x.shape[1]
    loads = [move.local(att, att_s), move.local(weight, w_s)]
    arrive = [move.send(att.at[:, :, 1 - core], att_half.at[:, :, :, pl.ds(length, length)], other)]
    for copy in loads:
        copy.wait()
    move.kept.append(move.local(att_s.at[:, :, core], att_half.at[:, :, :, pl.ds(0, length)]))
    tile = 128
    for t in range(length // tile):
        rows = slice(tile * t, tile * (t + 1))
        left = att_s[:, :, :, :, rows].reshape(width, tile).astype(F32).T.astype(BF)
        y = x[rows].astype(F32) + jnp.dot(left, w_s[...], preferred_element_type=F32)
        middle[rows] = y
        inverse = lax.rsqrt(jnp.mean(y * y, -1, keepdims=True) + EPS)
        normed = y * inverse * gain[...]
        low_s[rows] = normed.astype(BF)
        low_t[:, rows] = normed.T.astype(BF)
        here, there = pl.ds(tile * t, tile), pl.ds(length + tile * t, tile)
        arrive.append(move.send(low_s.at[here], second.at[there], other))
        arrive.append(move.send(low_t.at[:, here], second_t.at[:, there], other))
    move.kept.append(move.local(low_s, second.at[pl.ds(0, length)]))
    move.kept.append(move.local(low_t, second_t.at[:, pl.ds(0, length)]))
    for copy in arrive:
        copy.wait_recv()
    move.finish()


def bridge(attended, weight, x, gain, zsize, chips):
    width, length = attended.shape
    strip = width // (zsize * chips * 2)
    hbm, vmem = pl.BlockSpec(memory_space=pltpu.HBM), pl.BlockSpec(memory_space=pltpu.VMEM)
    steps = length // 128
    return pl.pallas_call(
        bridge_kernel,
        out_shape=[
            jax.ShapeDtypeStruct((length, width), F32), jax.ShapeDtypeStruct((2 * length, width), BF),
            jax.ShapeDtypeStruct((width, 2 * length), BF), jax.ShapeDtypeStruct((zsize, chips, strip, 2 * length), BF),
        ],
        in_specs=[hbm, hbm, vmem, vmem],
        out_specs=[vmem, hbm, hbm, hbm],
        scratch_shapes=[
            pltpu.VMEM((zsize, chips, 2, strip, length), BF), pltpu.VMEM((width, width), BF),
            pltpu.VMEM((length, width), BF), pltpu.VMEM((width, length), BF),
            pltpu.SemaphoreType.DMA((1 + 2 * steps,)), pltpu.SemaphoreType.DMA((1 + 2 * steps,)), pltpu.SemaphoreType.DMA((5,)),
        ],
        compiler_params=pltpu.CompilerParams(collective_id=2, has_side_effects=True, vmem_limit_bytes=40 * 2**20),
        cost_estimate=NO_COST,
        name="bridge",
    )(attended.reshape(zsize, chips, 2, strip, length), weight, x, gain)


def middle_kernel(counts, *refs):
    count = len(counts)
    hidden, low = refs[:count], refs[count:2 * count]
    weights, at = [], 2 * count
    for n in counts:
        weights.append(refs[at:at + n])
        at += n
    y_in, cot_in, gain, out_w = refs[at:at + 4]
    layer_out, middle_grad, low_t, att_grad, gain_part = refs[at + 4:at + 9]
    h_v, l_v, wi_v, wo_v, send_s, got, own, out_s, ss, rs, ls = refs[at + 9:]
    core, other = greet_other_core()
    move = Mover(ss, rs, ls)
    tokens, chunk = hidden[0].shape
    length, width = y_in.shape
    loads = []
    load = lambda src, dst: loads.append(move.local(src, dst))
    late = []
    for r in range(count):
        load(low[r], l_v.at[:, pl.ds(2 * r * chunk, 2 * chunk)])
    for r in range(count):
        unfold(weights[r], wi_v.at[:, :, pl.ds(2 * r * chunk, 2 * chunk)], wo_v.at[r], load)
    for r in range(count):
        late.append(move.local(hidden[r], h_v.at[:, pl.ds(r * chunk, chunk)]))
    nt = (((1,), (1,)), ((), ()))
    tile = tokens // 4

    def grad_tile(t):
        return lax.dot_general(
            l_v[tile * t:tile * (t + 1)], wi_v[...].reshape(width, 2 * count * chunk), nt, preferred_element_type=F32
        )

    def out_tile(t):
        return jnp.dot(h_v[tile * t:tile * (t + 1)], wo_v[...].reshape(count * chunk, width), preferred_element_type=F32)

    for copy in loads:
        copy.wait()
    there = []
    for n in range(2):
        send_s[n] = grad_tile(2 + n)
        there.append(move.send(send_s.at[n], got.at[n], other))
    for n in range(2):
        own[tile * n:tile * (n + 1)] = grad_tile(n)
    load_out = move.local(out_w, wi_v.at[:, :, pl.ds(0, width)])
    for copy in late:
        copy.wait()
    for n in range(2):
        move.settle(there[n])
        send_s[n] = out_tile(2) if n == 0 else out_tile(1) + y_in[tile:2 * tile]
        there.append(move.send(send_s.at[n], got.at[2 + n], other))
    there[0].wait_recv()
    there[1].wait_recv()
    gain_part[...] = jnp.zeros(gain_part.shape, F32)
    step = 128

    for t in range(length // step):
        part = slice(step * t, step * (t + 1))
        y = y_in[part]
        inverse = lax.rsqrt(jnp.mean(y * y, -1, keepdims=True) + EPS)
        unit = y * inverse
        d = own[part] + got[step * t // tile, step * t % tile:step * t % tile + step]
        gain_part[...] += jnp.sum(d * unit, axis=0, keepdims=True)
        scaled = d * gain[...]
        g = cot_in[step * t // tile, step * t % tile:step * t % tile + step].astype(F32)
        g = g + inverse * (scaled - unit * jnp.mean(scaled * unit, -1, keepdims=True))
        middle_grad[part] = g
        low_t[:, part] = g.T.astype(BF)
    load_out.wait()
    rows = wi_v.shape[1]
    for z in range(wi_v.shape[0]):
        att_grad[z * rows:(z + 1) * rows] = jnp.dot(wi_v[z, :, 0:width], low_t[...], preferred_element_type=F32).astype(BF)
    first, last = out_tile(0) + y_in[0:tile], out_tile(3)
    there[2].wait_recv()
    out_s[0] = (first + got[2]).astype(BF)
    there[3].wait_recv()
    out_s[1] = (last + got[3]).astype(BF)
    move.kept.append(move.local(out_s.at[0], layer_out.at[core]))
    move.kept.append(move.local(out_s.at[1], layer_out.at[1 - core]))
    move.finish()


def middle_part(hidden, low, weights, y, cot, gain, out_w, zsize, fine):
    counts = tuple(len(w) for w in weights)
    count = len(counts)
    tokens, chunk = hidden[0].shape
    length, width = y.shape
    rows = width // zsize
    hbm, vmem = pl.BlockSpec(memory_space=pltpu.HBM), pl.BlockSpec(memory_space=pltpu.VMEM)
    inputs = [*hidden, *low] + [piece for w in weights for piece in w]
    tile = tokens // 4
    return pl.pallas_call(
        functools.partial(middle_kernel, counts),
        out_shape=[
            jax.ShapeDtypeStruct((2, length // 2, width), BF), jax.ShapeDtypeStruct((length, width), F32),
            jax.ShapeDtypeStruct((width, length), BF), jax.ShapeDtypeStruct((width, length), BF),
            jax.ShapeDtypeStruct((1, width), F32),
        ],
        in_specs=[hbm] * len(inputs) + [vmem, vmem, vmem, hbm],
        out_specs=[hbm] + [vmem] * 4,
        scratch_shapes=[
            pltpu.VMEM((tokens, count * chunk), BF), pltpu.VMEM((tokens, 2 * count * chunk), BF),
            pltpu.VMEM((zsize, rows, 2 * count * chunk), BF), pltpu.VMEM((count, zsize, fine, width), BF),
            pltpu.VMEM((2, tile, width), F32), pltpu.VMEM((4, tile, width), F32),
            pltpu.VMEM((length, width), F32), pltpu.VMEM((2, tile, width), BF),
            pltpu.SemaphoreType.DMA((4,)), pltpu.SemaphoreType.DMA((4,)),
            pltpu.SemaphoreType.DMA((2 * count + count * zsize * (1 + rows // fine) + 3,)),
        ],
        compiler_params=pltpu.CompilerParams(collective_id=3, has_side_effects=True, vmem_limit_bytes=61 * 2**20),
        cost_estimate=LONG,
        name="middle",
    )(*inputs, y, cot[:2], gain, out_w.reshape(zsize, rows, width))


def mm(left, right, left_dim, right_dim):
    return lax.dot_general(left, right, (((left_dim,), (right_dim,)), ((), ())), preferred_element_type=F32)


def swap(a):
    return lax.ppermute(a, "ctx", [(i, i ^ 1) for i in range(lax.axis_size("ctx"))])


def hop(a, r):
    return lax.ppermute(a, "ctx", [(i, i ^ (2 * r)) for i in range(lax.axis_size("ctx"))])


def ring(a):
    n = lax.axis_size("fsdp")
    return lax.ppermute(a, "fsdp", [(i, (i + 1) % n) for i in range(n)])


def pick(a, index, axis=0):
    return lax.dynamic_index_in_dim(a, index, axis, keepdims=False)


def place(buffer, piece, index, axis=0):
    return lax.dynamic_update_slice_in_dim(buffer, jnp.expand_dims(piece, axis), index, axis)


def shift(a, s):
    n = lax.axis_size("fsdp")
    return lax.ppermute(a, "fsdp", [(i, (i + s) % n) for i in range(n)])


def depth_gather(piece, depth):
    n = lax.axis_size("fsdp")
    buffer = place(jnp.zeros((n,) + piece.shape, piece.dtype), piece, depth)
    for s in range(1, n):
        piece = ring(piece)
        buffer = place(buffer, piece, lax.rem(depth + n - s, n))
    return buffer


def depth_scatter(parts, depth):
    n = lax.axis_size("fsdp")
    total = pick(parts, lax.rem(depth + n - 1, n))
    for s in range(n - 1):
        total = ring(total.astype(BF))
        total = total.astype(F32) + pick(parts, lax.rem(depth + 2 * n - 2 - s, n)).astype(F32)
    return total


def plane_gather(piece, index):
    n = lax.axis_size("ctx")
    chips = n // 2
    pieces = jnp.stack([piece] + [hop(piece, r) for r in range(1, chips)])
    others = swap(pieces)
    buffer = jnp.zeros((n,) + piece.shape, piece.dtype)
    for r in range(chips):
        buffer = place(buffer, pieces[r], index ^ (2 * r))
        buffer = place(buffer, others[r], index ^ (2 * r + 1))
    return buffer


def rotate(v, cosine, sine):
    heads = v.reshape(-1, 2, HEAD_WIDTH // 2, v.shape[-1])
    a, b = heads[:, 0], heads[:, 1]
    return jnp.stack([a * cosine - b * sine, b * cosine + a * sine], 1).reshape(v.shape)


def rotate_back(v, cosine, sine):
    heads = v.reshape(-1, 2, HEAD_WIDTH // 2, v.shape[-1])
    a, b = heads[:, 0], heads[:, 1]
    return jnp.stack([a * cosine + b * sine, b * cosine - a * sine], 1).reshape(v.shape)


def norm_back(incoming, unit, inverse, gain):
    scaled = incoming * gain
    return inverse * (scaled - unit * jnp.mean(scaled * unit, -1, keepdims=True))


def body(
    tokens,
    block_pairs,
    cotangent,
    attention_gain,
    query_weight,
    key_matrix,
    value_matrix,
    output_weight,
    feedforward_gain,
    gate_weight,
    up_weight,
    down_weight,
):
    slice_len, width = tokens.shape[1], tokens.shape[2]
    ctx = lax.axis_size("ctx")
    zsize = lax.axis_size("fsdp")
    chips = ctx // 2
    diag = chips - 1
    near = range(1, chips - 1)
    index = lax.axis_index("ctx")
    chip, core = index // 2, lax.rem(index, 2)
    depth = lax.axis_index("fsdp")
    rows = width // zsize
    strip = rows // ctx
    hidden_rows = down_weight.shape[0]
    fine = hidden_rows // ctx
    chunk = fine * zsize
    kv_rows = KEY_HEADS * HEAD_WIDTH

    length = 2 * slice_len

    ids_all = jnp.concatenate([pick(block_pairs, index ^ r) for r in range(ctx)])
    ids = ids_all[:4]
    blocks = ids_all.shape[0]
    order = jnp.sum(
        jnp.where(ids_all[None, :] == jnp.arange(blocks, dtype=jnp.int32)[:, None], jnp.arange(blocks, dtype=jnp.int32)[None, :], 0), 1
    )
    positions = (ids[:, None] * BLK + jnp.arange(BLK, dtype=jnp.int32)[None, :]).reshape(length)
    half = HEAD_WIDTH // 2
    frequency = THETA ** (-jnp.arange(half, dtype=F32) * 2.0 / HEAD_WIDTH)
    angles = frequency[:, None] * positions.astype(F32)[None, :]
    cosine, sine = jnp.cos(angles), jnp.sin(angles)

    packs, keys, values = {}, {}, {}
    folds = rows // fine
    fast = chips == 4 and strip % 16 == 0 and fine % 128 == 0 and pack_width(rows, fine, zsize, width) == width
    if fast:
        (key_value_full, query_full, output_full, pack, rest, pack_x, pack_y, far_pack, cot, first_half, x_low, first, query, gains_full, *kv) = front(
            tokens, cotangent, jnp.stack([attention_gain, feedforward_gain]).astype(F32), key_matrix, value_matrix, query_weight,
            output_weight, gate_weight, up_weight, down_weight, cosine, sine, zsize, ctx,
        )
        key_value_full, query_full, output_full = (w.reshape(width, width) for w in (key_value_full, query_full, output_full))
        packs[0], packs[1], packs[2] = [pack, rest], [pack_x, hop(rest, 1)], [pack_y, hop(rest, 2)]
        for r in range(chips):
            keys[r], values[r] = kv[r], kv[chips + r]
        gain_first, gain_second = gains_full[0], gains_full[1]
        packs[diag] = [far_pack] + [shift(far_pack, s) for s in range(1, zsize)]
    else:
        gate_cut = gate_weight.reshape(rows, zsize, 2, chips, fine)
        up_cut = up_weight.reshape(rows, zsize, 2, chips, fine)
        down_cut = down_weight.reshape(2, chips, fine, width)

        def own_piece(r):
            gate = pick(pick(gate_cut, core, 2), chip ^ r, 2).reshape(rows, chunk)
            up = pick(pick(up_cut, core, 2), chip ^ r, 2).reshape(rows, chunk)
            down = pick(pick(down_cut, core), chip ^ r)
            folded = jnp.transpose(down.reshape(fine, folds, width // folds), (1, 0, 2)).reshape(rows, width // folds)
            return jnp.concatenate([gate, up, folded], 1)

        gains = jnp.stack([attention_gain, feedforward_gain])
        gain_buffer = place(jnp.zeros((zsize, 2, rows), BF), gains, depth)
        for s in range(1, zsize):
            moved = lax.ppermute(gains, "fsdp", [(k, (k + s) % zsize) for k in range(zsize)])
            gain_buffer = place(gain_buffer, moved, lax.rem(depth + zsize - s, zsize))
        gains_full = jnp.transpose(gain_buffer, (1, 0, 2)).reshape(2, width).astype(F32)
        gain_first, gain_second = gains_full[0], gains_full[1]

        def gather_square(shard):
            strips = shard.reshape(ctx, strip, shard.shape[1])
            pair = jnp.stack([pick(strips, index), pick(strips, index ^ (2 * diag))])
            pair = depth_gather(pair, depth)
            own, far = pair[:, 0], pair[:, 1]
            found = {0: own, diag: far}
            for r in near:
                found[r] = hop(own, r)
            full = jnp.zeros((zsize, ctx, strip, shard.shape[1]), BF)
            for r in range(chips):
                full = place(full, found[r], index ^ (2 * r), 1)
                full = place(full, swap(found[r]), index ^ (2 * r + 1), 1)
            return full.reshape(width, shard.shape[1])

        key_value_full = gather_square(jnp.concatenate([key_matrix, value_matrix], 1))
        query_full = gather_square(query_weight)
        output_full = gather_square(output_weight)

        x = jnp.concatenate([pick(tokens, core), swap(pick(tokens, 1 - core))]).astype(F32)
        packs[0] = [depth_gather(own_piece(0), depth)]
        inverse_first = lax.rsqrt(jnp.mean(x * x, -1, keepdims=True) + EPS)
        unit_first = x * inverse_first
        first = (unit_first * gain_first).astype(BF)
        first_t = jnp.transpose(first)
        kv = mm(key_value_full, first_t, 0, 0)
        keys[0] = rotate(kv[:kv_rows], cosine, sine).astype(BF)
        values[0] = kv[kv_rows:].astype(BF)
        for r in range(1, chips):
            high = 1 << (r.bit_length() - 1)
            low = r & -r
            keys[r] = hop(keys[r ^ high], high)
            values[r] = hop(values[r ^ low], low)
        query = rotate(mm(query_full, first_t, 0, 0), cosine, sine).astype(BF)
        packs[diag] = [depth_gather(own_piece(diag), depth)]

        for r in near:
            packs[r] = [hop(packs[0][0], r)]
        cot_there = swap(cotangent)
        cot = jnp.concatenate(
            [pick(cotangent, core), pick(cot_there, core), pick(cot_there, 1 - core), pick(cotangent, 1 - core)]
        )

    key_list = [keys[r] for r in range(chips)]
    value_list = [values[r] for r in range(chips)]
    attended, log_total = attn_fwd(ids, order, query, key_list, value_list, KEY_HEADS)

    if fast:
        middle, second, second_t, att_half = bridge(attended, output_full, x_low, gain_second[None], zsize, chips)
    else:
        middle = x + mm(attended, output_full, 0, 0)
        inverse_second = lax.rsqrt(jnp.mean(middle * middle, -1, keepdims=True) + EPS)
        unit_second = middle * inverse_second
        second = (unit_second * gain_second).astype(BF)
        second = jnp.concatenate([second, swap(second)])
        second_t = jnp.transpose(second)
    grads, hidden, low = {}, {}, {}
    before = second
    for r in [0] + list(near) + [diag]:
        before, low[r], grads[r] = ffn_chunk(
            before, second, second_t, cot.reshape(2 * length, width), packs[r], fast and r == diag, zsize, fine
        )
        hidden[r] = before
    every = range(chips)
    hidden, low, packs = ([a[r] for r in every] for a in (hidden, low, packs))

    if fast:
        layer_out, middle_grad, middle_t, attended_grad, gain_second_part = middle_part(
            hidden, low, packs, middle, cot, gain_second[None], output_full, zsize, fine
        )
    else:
        out_part, second_grad = combine(hidden, low, packs, zsize, fine)

        q = slice_len
        out_part = jnp.concatenate([out_part[:length] + middle, out_part[length:]])
        came = swap(jnp.concatenate([out_part[2 * q:3 * q], out_part[q:2 * q]]))
        out_here = (out_part[:q] + came[:q]).astype(BF)
        out_there = (out_part[3 * q:] + came[q:]).astype(BF)

        def stored(here, there):
            return jnp.where(core == 0, jnp.stack([here, there]), jnp.stack([there, here]))

        layer_out = stored(out_here, out_there)

        second_grad = second_grad[:length] + swap(second_grad[length:])
        gain_second_part = jnp.sum(second_grad * unit_second, 0)
        middle_grad = cot[:length].astype(F32) + norm_back(second_grad, unit_second, inverse_second, gain_second)

        def halves(a):
            cut = a.reshape(zsize, chips, 2, strip, length)
            here = pick(cut, core, 2).reshape(-1, length)
            there = swap(pick(cut, 1 - core, 2).reshape(-1, length))
            return jnp.concatenate([here, there], 1)

        first_half = halves(first_t)
        middle_low = middle_grad.astype(BF)
        out_part_grad = mm(halves(attended), jnp.concatenate([middle_low, swap(middle_low)]), 1, 0)
        attended_grad = mm(output_full, middle_low, 1, 1).astype(BF)

    query_low, key_parts, value_parts = attn_bwd(
        ids, order, query, attended, attended_grad, log_total, cosine, sine, key_list, value_list, KEY_HEADS
    )
    if fast:
        o_all, q_all, kv_all, pack_all, tokens_grad, gain_sums = tail(
            key_parts, value_parts, query_low, cosine, sine, first_half,
            att_half,
            [grads[0][0], hop(grads[1][0], 1), hop(grads[2][0], 2)],
            [grads[diag][0]] + [shift(grads[diag][s], s) for s in range(1, zsize)],
            middle_t, query_full, key_value_full, x_low, middle_grad, gain_first[None], gain_second_part, zsize, chips,
        )
        gain_first_grad, gain_second_grad = (
            lax.dynamic_slice_in_dim(gain_sums[n], depth * rows, rows) for n in range(2)
        )
        gate_grad, up_grad, down_grad, output_grad, query_grad, key_grad, value_grad = assemble(
            pack_all, *(a.reshape(rows, width) for a in (o_all, q_all, kv_all)), zsize, fine
        )
    else:
        key_sum = [part for part in key_parts]
        value_sum = [part for part in value_parts]
        for r in range(chips - 1, 0, -1):
            high = 1 << (r.bit_length() - 1)
            low = r & -r
            key_sum[r ^ high] = key_sum[r ^ high].astype(F32) + hop(key_sum[r].astype(BF), high).astype(F32)
            value_sum[r ^ low] = value_sum[r ^ low].astype(F32) + hop(value_sum[r].astype(BF), low).astype(F32)
        key_low = rotate_back(key_sum[0], cosine, sine).astype(BF)
        value_low = value_sum[0].astype(BF)
        kv_low = jnp.concatenate([key_low, value_low])

        def scatter(parts):
            total = parts[0].astype(F32)
            for r in near:
                total = total + hop(parts[r], r).astype(F32)
            far = hop(depth_scatter(parts[diag], depth).astype(BF), diag)
            total = depth_scatter(total.astype(BF), depth) + far.astype(F32)
            return total.astype(BF)

        pack_all = plane_gather(scatter({r: grads[r][0] for r in range(chips)}), index)
        wide_all = pack_all[:, :, :2 * chunk]
        tall_all = jnp.transpose(pack_all[:, :, 2 * chunk:].reshape(ctx, folds, fine, width // folds), (0, 2, 1, 3))
        def square_grad(product):
            parts = product.astype(BF).reshape(zsize, chips, strip, width)
            piece = scatter({r: pick(parts, chip ^ r, 1) for r in range(chips)})
            return plane_gather(piece, index).reshape(rows, width).astype(F32)

        output_grad = square_grad(out_part_grad)
        query_grad = square_grad(mm(first_half, jnp.concatenate([query_low, swap(query_low)], 1), 1, 1))
        kv_grad = square_grad(mm(first_half, jnp.concatenate([kv_low, swap(kv_low)], 1), 1, 1))
        down_grad = jnp.transpose(tall_all.reshape(chips, 2, fine, width), (1, 0, 2, 3)).reshape(hidden_rows, width).astype(F32)
        wide_all = wide_all.reshape(chips, 2, rows, 2, zsize, fine)
        gate_grad = jnp.transpose(wide_all[:, :, :, 0], (2, 3, 1, 0, 4)).reshape(rows, -1).astype(F32)
        up_grad = jnp.transpose(wide_all[:, :, :, 1], (2, 3, 1, 0, 4)).reshape(rows, -1).astype(F32)
        key_grad, value_grad = kv_grad[:, :kv_rows], kv_grad[:, kv_rows:]

        def gain_total(part):
            cut = part.reshape(zsize, rows)
            total = pick(cut, depth)
            for s in range(1, zsize):
                total = total + lax.ppermute(
                    pick(cut, lax.rem(depth + s, zsize)), "fsdp", [(k, (k + s) % zsize) for k in range(zsize)]
                )
            total = total + swap(total)
            bit = 1
            while bit < chips:
                total = total + hop(total, bit)
                bit *= 2
            return total

        first_grad = mm(query_low, query_full, 0, 1) + mm(kv_low, key_value_full, 0, 1)
        gain_first_part = jnp.sum(first_grad * unit_first, 0)
        tokens_part = (middle_grad + norm_back(first_grad, unit_first, inverse_first, gain_first)).astype(BF)
        tokens_grad = stored(tokens_part[:q], swap(tokens_part[q:]))
        gain_first_grad, gain_second_grad = gain_total(gain_first_part), gain_total(gain_second_part)

    return (
        layer_out,
        tokens_grad,
        gain_first_grad,
        query_grad,
        key_grad,
        value_grad,
        output_grad,
        gain_second_grad,
        gate_grad,
        up_grad,
        down_grad,
    )


def solution(mesh):
    line, square, grid = P("fsdp"), P("fsdp", None), P("fsdp", "ctx", None)
    in_specs = (grid, P(), grid, line, square, square, square, square, line, square, square, square)
    out_specs = (grid, grid, line, square, square, square, square, line, square, square, square)
    return jax.shard_map(body, mesh=mesh, in_specs=in_specs, out_specs=out_specs, check_vma=False)
```

```python
import functools

import jax
import jax.numpy as jnp
from jax import lax
from jax.experimental import pallas as pl
from jax.experimental.pallas import tpu as pltpu
from jax.sharding import PartitionSpec as P

QUERY_HEADS = 16
KEY_HEADS = 8
HEAD_WIDTH = 96
EPS = 1e-05
THETA = 100000.0
BLK = 128
SCALE = HEAD_WIDTH ** -0.5
BF = jnp.bfloat16
F32 = jnp.float32
NO_COST = pl.CostEstimate(flops=0, bytes_accessed=0, transcendentals=0)
LONG = pl.CostEstimate(flops=52 * 10**9, bytes_accessed=0, transcendentals=0)

LOG2E = 1.4426950408889634
NT = (((1,), (1,)), ((), ()))


def block_tasks(ids_ref, inv_ref, slices, t):
    tasks = []
    for sl in range(slices):
        first = ids_ref[2 * sl]
        late = (t > first).astype(jnp.int32)
        kpos = t - late * (first + 1)
        tasks.append((sl, late, inv_ref[kpos], (ids_ref[2 * sl + late] - kpos) * BLK))
    return tasks


def causal_difference():
    return lax.broadcasted_iota(jnp.int32, (BLK, 2 * BLK), 0) - lax.rem(lax.broadcasted_iota(jnp.int32, (BLK, 2 * BLK), 1), BLK)


def load_keys(refs, scratch, sem):
    copies = [pltpu.make_async_copy(ref, scratch.at[n], sem.at[n]) for n, ref in enumerate(refs)]

    @pl.when(pl.program_id(0) == 0)
    def _():
        for copy in copies:
            copy.start()
        for copy in copies:
            copy.wait()


def fwd_kernel(nchip, heads, ids_ref, inv_ref, q_ref, *rest):
    o_ref, lse_ref, kv_s, sem, knat, vtr = rest[2 * nchip:2 * nchip + 6]
    state = rest[2 * nchip + 6:]
    load_keys(rest[:2 * nchip], kv_s, sem)
    base = pl.program_id(0) * (96 * heads)
    nq = q_ref.shape[1] // BLK
    slices = nq // 2
    nb = nchip * nq
    c = SCALE * LOG2E
    chains = [(h, sl) for h in range(heads) for sl in range(slices)]
    qs, m_s, l_s, acc = ({chain: state[4 * n + k] for n, chain in enumerate(chains)} for k in range(4))
    for h in range(heads):
        for n in range(nb):
            r, lanes = n // nq, slice(BLK * (n % nq), BLK * (n % nq + 1))
            part = pl.ds(pl.multiple_of(base + 96 * h, 96), 96)
            knat[h, n] = kv_s[r, part, lanes].T
            vtr[h, n] = kv_s[nchip + r, part, lanes]
        for sl in range(slices):
            for half in range(2):
                lanes = slice(BLK * (2 * sl + half), BLK * (2 * sl + half + 1))
                qs[h, sl][half] = jnp.concatenate([q_ref[192 * h:192 * h + 96, lanes], q_ref[192 * h + 96:192 * h + 192, lanes]], axis=1)
            m_s[h, sl][...] = jnp.full((2, 1, 2 * BLK), -1e30, F32)
            l_s[h, sl][...] = jnp.zeros((2, 1, 2 * BLK), F32)
            acc[h, sl][...] = jnp.zeros((2, 96, 2 * BLK), F32)
    diff = causal_difference()

    def step(t, _):
        tasks = block_tasks(ids_ref, inv_ref, slices, t)
        todo = [(h, *task) for h in range(heads) for task in tasks]
        scores = [
            jnp.where(diff <= offset, jnp.dot(knat[h, n], qs[h, sl][late], preferred_element_type=F32), -jnp.inf)
            for h, sl, late, n, offset in todo
        ]
        old = [(m_s[h, sl][late], l_s[h, sl][late], acc[h, sl][late]) for h, sl, late, n, offset in todo]
        peaks = [jnp.maximum(m, jnp.max(s, axis=0, keepdims=True)) for s, (m, _l, _a) in zip(scores, old)]
        weights = [jnp.exp2((s - peak) * c) for s, peak in zip(scores, peaks)]
        shrink = [jnp.exp2((m - peak) * c) for peak, (m, _l, _a) in zip(peaks, old)]
        totals = [l * a + jnp.sum(p, axis=0, keepdims=True) for (_m, l, _a), a, p in zip(old, shrink, weights)]
        mixed = [
            o * a + jnp.dot(vtr[h, n], p.astype(BF), preferred_element_type=F32)
            for (h, sl, late, n, offset), (_m, _l, o), a, p in zip(todo, old, shrink, weights)
        ]
        for (h, sl, late, n, offset), peak, total, o in zip(todo, peaks, totals, mixed):
            m_s[h, sl][late] = peak
            l_s[h, sl][late] = total
            acc[h, sl][late] = o
        return 0

    lax.fori_loop(0, nb + 1, step, 0)
    for h, sl in chains:
        for half in range(2):
            lanes = slice(BLK * (2 * sl + half), BLK * (2 * sl + half + 1))
            l = l_s[h, sl][half]
            o = acc[h, sl][half] / l
            lse_ref[h, 2 * sl + half] = m_s[h, sl][half] * c + jnp.log2(l)
            o_ref[192 * h:192 * h + 96, lanes] = o[:, :BLK].astype(BF)
            o_ref[192 * h + 96:192 * h + 192, lanes] = o[:, BLK:].astype(BF)


def attn_fwd(ids, inv, qT, ks, vs, heads):
    nchip = len(ks)
    T = qT.shape[1]
    nq = T // BLK
    nb = nchip * nq
    per = 4 if nb <= 16 else 2
    wide = pl.BlockSpec((192 * per, T), lambda g, *_: (g, 0))
    slim = pl.BlockSpec((96 * per, T), lambda g, *_: (g, 0))
    chain = [
        pltpu.VMEM((2, 96, 2 * BLK), BF),
        pltpu.VMEM((2, 1, 2 * BLK), F32),
        pltpu.VMEM((2, 1, 2 * BLK), F32),
        pltpu.VMEM((2, 96, 2 * BLK), F32),
    ]
    grid_spec = pltpu.PrefetchScalarGridSpec(
        num_scalar_prefetch=2,
        grid=(heads // per,),
        in_specs=[wide] + [pl.BlockSpec(memory_space=pltpu.HBM)] * (2 * nchip),
        out_specs=[wide, pl.BlockSpec((per, nq, 1, 2 * BLK), lambda g, *_: (g, 0, 0, 0))],
        scratch_shapes=[
            pltpu.VMEM((2 * nchip, heads * 96, T), BF), pltpu.SemaphoreType.DMA((2 * nchip,)),
            pltpu.VMEM((per, nb, BLK, 96), BF), pltpu.VMEM((per, nb, 96, BLK), BF),
        ] + chain * (per * nq // 2),
    )
    return pl.pallas_call(
        functools.partial(fwd_kernel, nchip, per),
        grid_spec=grid_spec,
        out_shape=[jax.ShapeDtypeStruct((heads * 192, T), BF), jax.ShapeDtypeStruct((heads, nq, 1, 2 * BLK), F32)],
        cost_estimate=NO_COST,
        compiler_params=pltpu.CompilerParams(vmem_limit_bytes=56 * 2**20),
        name="attention_forward",
    )(ids, inv, qT, *ks, *vs)


def bwd_kernel(nchip, heads, ids_ref, inv_ref, q_ref, o_ref, do_ref, lse_ref, cos_ref, sin_ref, before, *rest):
    dq_ref = rest[2 * nchip]
    dk_refs, dv_refs = rest[2 * nchip + 1:3 * nchip + 1], rest[3 * nchip + 1:4 * nchip + 1]
    kv_s, sem, knat, ktr, vnat = rest[4 * nchip + 1:4 * nchip + 6]
    state = rest[4 * nchip + 6:]
    load_keys(rest[:2 * nchip], kv_s, sem)
    base = pl.program_id(0) * (96 * heads)
    nq = q_ref.shape[1] // BLK
    slices = nq // 2
    nb = nchip * nq
    c = SCALE * LOG2E
    chains = [(h, sl) for h in range(heads) for sl in range(slices)]
    qs, dos, stat, dq_s, dk_s, dv_s = ({chain: state[6 * n + k] for n, chain in enumerate(chains)} for k in range(6))
    for h in range(heads):
        for n in range(nb):
            r, lanes = n // nq, slice(BLK * (n % nq), BLK * (n % nq + 1))
            part = pl.ds(pl.multiple_of(base + 96 * h, 96), 96)
            block = kv_s[r, part, lanes]
            knat[h, n] = block.T
            ktr[h, n] = block
            vnat[h, n] = kv_s[nchip + r, part, lanes].T
    for h, sl in chains:
        for half in range(2):
            lanes = slice(BLK * (2 * sl + half), BLK * (2 * sl + half + 1))
            pair = lambda ref: jnp.concatenate([ref[192 * h:192 * h + 96, lanes], ref[192 * h + 96:192 * h + 192, lanes]], axis=1)
            do = pair(do_ref)
            qs[h, sl][half] = pair(q_ref)
            dos[h, sl][half] = do
            stat[h, sl][half, 0:1] = lse_ref[h, 2 * sl + half]
            stat[h, sl][half, 1:2] = jnp.sum(pair(o_ref).astype(F32) * do.astype(F32), axis=0, keepdims=True)
        dq_s[h, sl][...] = jnp.zeros((2, 96, 2 * BLK), F32)
        dk_s[h, sl][...] = jnp.zeros((nb, 96, BLK), F32)
        dv_s[h, sl][...] = jnp.zeros((nb, 96, BLK), F32)
    diff = causal_difference()

    def step(t, _):
        tasks = block_tasks(ids_ref, inv_ref, slices, t)
        todo = [(h, *task) for h in range(heads) for task in tasks]
        q = [qs[h, sl][late] for h, sl, late, n, offset in todo]
        do = [dos[h, sl][late] for h, sl, late, n, offset in todo]
        scores = [jnp.dot(knat[h, n], x, preferred_element_type=F32) for (h, sl, late, n, offset), x in zip(todo, q)]
        grads = [jnp.dot(vnat[h, n], x, preferred_element_type=F32) for (h, sl, late, n, offset), x in zip(todo, do)]
        weights = [
            jnp.exp2(jnp.where(diff <= offset, s * c - stat[h, sl][late, 0:1], -jnp.inf))
            for (h, sl, late, n, offset), s in zip(todo, scores)
        ]
        low = [(p * (g - stat[h, sl][late, 1:2])).astype(BF) for (h, sl, late, n, offset), p, g in zip(todo, weights, grads)]
        dv = [lax.dot_general(x, p.astype(BF), NT, preferred_element_type=F32) for x, p in zip(do, weights)]
        dk = [lax.dot_general(x, ds, NT, preferred_element_type=F32) for x, ds in zip(q, low)]
        dq = [jnp.dot(ktr[h, n], ds, preferred_element_type=F32) for (h, sl, late, n, offset), ds in zip(todo, low)]
        for (h, sl, late, n, offset), a, b, d in zip(todo, dv, dk, dq):
            dv_s[h, sl][n] += a
            dk_s[h, sl][n] += b
            dq_s[h, sl][late] += d
        return 0

    lax.fori_loop(0, nb + 1, step, 0)
    for h, sl in chains:
        for half in range(2):
            lanes = slice(BLK * (2 * sl + half), BLK * (2 * sl + half + 1))
            cos, sin = cos_ref[:, lanes], sin_ref[:, lanes]
            for e in range(2):
                a = dq_s[h, sl][half, 0:48, BLK * e:BLK * (e + 1)] * SCALE
                b = dq_s[h, sl][half, 48:96, BLK * e:BLK * (e + 1)] * SCALE
                at = 192 * h + 96 * e
                dq_ref[at:at + 48, lanes] = (a * cos + b * sin).astype(BF)
                dq_ref[at + 48:at + 96, lanes] = (b * cos - a * sin).astype(BF)
    for h in range(heads):
        for n in range(nb):
            r, lanes = n // nq, slice(BLK * (n % nq), BLK * (n % nq + 1))
            dk = sum(dk_s[h, sl][n] for sl in range(slices))
            dv = sum(dv_s[h, sl][n] for sl in range(slices))
            dk_refs[r][96 * h:96 * (h + 1), lanes] = (dk * SCALE).astype(BF)
            dv_refs[r][96 * h:96 * (h + 1), lanes] = dv.astype(BF)


def attn_bwd(before, ids, inv, qT, oT, doT, lse, cosine, sine, ks, vs, heads):
    nchip = len(ks)
    T = qT.shape[1]
    nq = T // BLK
    nb = nchip * nq
    per = 4 if nb <= 16 else 2
    wide = pl.BlockSpec((192 * per, T), lambda g, *_: (g, 0))
    slim = pl.BlockSpec((96 * per, T), lambda g, *_: (g, 0))
    chain = [
        pltpu.VMEM((2, 96, 2 * BLK), BF),
        pltpu.VMEM((2, 96, 2 * BLK), BF),
        pltpu.VMEM((2, 2, 2 * BLK), F32),
        pltpu.VMEM((2, 96, 2 * BLK), F32),
        pltpu.VMEM((nb, 96, BLK), F32),
        pltpu.VMEM((nb, 96, BLK), F32),
    ]
    grid_spec = pltpu.PrefetchScalarGridSpec(
        num_scalar_prefetch=2,
        grid=(heads // per,),
        in_specs=[wide, wide, wide, pl.BlockSpec((per, nq, 1, 2 * BLK), lambda g, *_: (g, 0, 0, 0))]
        + [pl.BlockSpec((48, T), lambda g, *_: (0, 0))] * 2 + [pl.BlockSpec(memory_space=pltpu.HBM)] * (1 + 2 * nchip),
        out_specs=[wide] + [slim] * (2 * nchip),
        scratch_shapes=[
            pltpu.VMEM((2 * nchip, heads * 96, T), BF), pltpu.SemaphoreType.DMA((2 * nchip,)),
            pltpu.VMEM((per, nb, BLK, 96), BF), pltpu.VMEM((per, nb, 96, BLK), BF), pltpu.VMEM((per, nb, BLK, 96), BF),
        ]
        + chain * (per * nq // 2),
    )
    slab = jax.ShapeDtypeStruct((heads * 96, T), BF)
    outs = pl.pallas_call(
        functools.partial(bwd_kernel, nchip, per),
        grid_spec=grid_spec,
        out_shape=[jax.ShapeDtypeStruct((heads * 192, T), BF)] + [slab] * (2 * nchip),
        cost_estimate=NO_COST,
        compiler_params=pltpu.CompilerParams(vmem_limit_bytes=56 * 2**20),
        name="attention_backward",
    )(ids, inv, qT, oT, doT, lse, cosine, sine, before, *ks, *vs)
    return outs[0], outs[1:1 + nchip], outs[1 + nchip:]


def pack_width(rows, fine, zsize, width):
    return 2 * fine * zsize + width * fine // rows


def front_kernel(zsize, *refs):
    (tok, cot_in, gains, key_w, value_w, query_w, out_w, gate_w, up_w, down_w, cos, sin) = refs[:12]
    (kv_all, q_all, o_all, pack, rest, pack_x, pack_y, far_pack, cot, first_half, x_out, first, q_out, gains_out) = refs[12:26]
    (k0, k1, k2, k3, v0, v1, v2, v3) = refs[26:34]
    x_s, gain_s, full_kv, full_q, full_o, kv_s, first_s, pack_s, cot_s, ss, rs, ls, gs, gr = refs[34:]
    ks, vs = (k0, k1, k2, k3), (v0, v1, v2, v3)
    index, depth = lax.axis_index("ctx"), lax.axis_index("fsdp")
    chip, core = index // 2, lax.rem(index, 2)
    fine = down_w.shape[0] // 8
    chunk = fine * zsize
    folds = pack.shape[0] // fine
    fold = first.shape[1] // folds
    width = first.shape[1]
    length = first.shape[0]
    kv_rows = k0.shape[0]
    nxt, prv = lax.rem(depth + 1, zsize), lax.rem(depth + zsize - 1, zsize)
    to_next, to_prev = (index, nxt), (index, prv)
    chip_x, chip_y, chip_d = chip + 1 - 2 * lax.rem(chip, 2), lax.rem(chip + 2, 4), 3 - chip
    to_x, to_y, to_core = (chip_x * 2 + core, depth), (chip_y * 2 + core, depth), (chip * 2 + 1 - core, depth)

    barrier = pltpu.get_barrier_semaphore()
    for target in (to_next, to_prev, to_x, to_y, to_core):
        pl.semaphore_signal(barrier, inc=1, device_id=target, device_id_type=pl.DeviceIdType.MESH)
    pl.semaphore_wait(barrier, 5)

    count = [0, 0]
    sent = []

    def send(src, dst, target):
        k = count[0]
        count[0] += 1
        copy = pltpu.make_async_remote_copy(
            src_ref=src, dst_ref=dst, send_sem=ss.at[k], recv_sem=rs.at[k], device_id=target, device_id_type=pl.DeviceIdType.MESH
        )
        copy.start()
        sent.append(copy)
        return copy

    def local(src, dst):
        k = count[1]
        count[1] += 1
        copy = pltpu.make_async_copy(src, dst, ls.at[k])
        copy.start()
        return copy

    def slot(s):
        return lax.rem(depth + zsize - s, zsize)

    steps = range(1, zsize)
    last = zsize - 1
    tokens_there = send(tok.at[1 - core], x_s.at[1], to_core)
    own_kv = [local(key_w, full_kv.at[depth, :, :, :, pl.ds(0, kv_rows)]), local(value_w, full_kv.at[depth, :, :, :, pl.ds(kv_rows, kv_rows)])]
    gain_s[depth] = gains[...]

    weights = {"kv": full_kv, "q": full_q, "o": full_o}
    shards = {"q": query_w, "o": out_w}
    moves = {}

    def ring_step(name, s):
        full = weights[name]
        place = full.at[slot(s - 1), chip, core]
        if name == "kv" and s == 1:
            halves = ((key_w, pl.ds(0, kv_rows)), (value_w, pl.ds(kv_rows, kv_rows)))
            moves[name, "ring", s] = [send(ref.at[chip, core], full.at[slot(0), chip, core, :, cols], to_next) for ref, cols in halves]
        else:
            source = shards[name].at[chip, core] if name in shards and s == 1 else place
            moves[name, "ring", s] = [send(source, place, to_next)]

    def spread(name, s):
        place = weights[name].at[slot(s), chip, core]
        moves[name, "x", s] = send(place, place, to_x)
        moves[name, "y", s] = send(place, place, to_y)

    def forward(name, s):
        mid = width // 2
        moves[name, "x", s].wait_recv()
        left = weights[name].at[slot(s), chip_x, core, :, pl.ds(0, mid)]
        moves[name, "fy", s] = send(left, left, to_y)
        moves[name, "y", s].wait_recv()
        right = weights[name].at[slot(s), chip_y, core, :, pl.ds(mid, mid)]
        moves[name, "fx", s] = send(right, right, to_x)

    def cross(name, s):
        moves[name, "fx", s].wait_recv()
        moves[name, "fy", s].wait_recv()
        column = weights[name].at[slot(s), :, core]
        moves[name, "core", s] = send(column, column, to_core)

    def gain_step(s):
        place = gain_s.at[slot(s - 1)]
        copy = pltpu.make_async_remote_copy(
            src_ref=place, dst_ref=place, send_sem=gs.at[s], recv_sem=gr.at[s], device_id=to_next, device_id_type=pl.DeviceIdType.MESH
        )
        copy.start()
        sent.append(copy)
        moves["gain", s] = copy

    def ffn_step(s):
        moves["ffn", s] = send(pack_s.at[0] if s == 1 else rest.at[s - 2], rest.at[s - 1], to_next)

    ring_step("kv", 1)
    gain_step(1)
    own_late = [local(query_w, full_q.at[depth]), local(out_w, full_o.at[depth])]
    def cut_pack(which, target):
        copies = []
        for part in range(zsize):
            column = pl.multiple_of(part * (8 * fine) + core * (4 * fine) + which * fine, fine)
            copies.append(local(gate_w.at[:, pl.ds(column, fine)], target.at[:, pl.ds(part * fine, fine)]))
            copies.append(local(up_w.at[:, pl.ds(column, fine)], target.at[:, pl.ds(chunk + part * fine, fine)]))
        row = pl.multiple_of(core * (4 * fine) + which * fine, fine)
        for n in range(folds):
            copies.append(local(down_w.at[pl.ds(row, fine), pl.ds(n * fold, fold)], target.at[pl.ds(n * fine, fine), pl.ds(2 * chunk, fold)]))
        return copies

    own_ffn = cut_pack(chip, pack_s.at[0])
    far_ffn = cut_pack(chip_d, pack_s.at[1]) + cut_pack(chip_x, pack_s.at[2]) + cut_pack(chip_y, pack_s.at[3])
    far_ffn += [local(cot_in.at[core], cot_s.at[0]), local(cot_in.at[1 - core], cot_s.at[1])]
    cot_moves = [send(cot_in.at[1 - core], cot.at[1], to_core), send(cot_in.at[core], cot.at[2], to_core)]

    def around(name, s):
        for copy in moves[name, "ring", s]:
            copy.wait_recv()
        if s < last:
            ring_step(name, s + 1)

    ring_step("q", 1)
    ring_step("o", 1)
    for s in steps:
        moves["gain", s].wait_recv()
        if s < last:
            gain_step(s + 1)
        around("kv", s)
        spread("kv", s)
        around("q", s)
        around("o", s)
    for copy in own_ffn:
        copy.wait()
    ffn_step(1)
    for s in steps:
        forward("kv", s)
    for s in steps:
        spread("q", s)
    for s in steps:
        cross("kv", s)

    tokens_there.wait_recv()
    x_out[0:length // 2] = tok[core]
    x_out[length // 2:] = x_s[1]
    gain_rows = [gain_s[place] for place in range(zsize)]
    gains_full = jnp.concatenate(gain_rows, axis=1)
    gains_out[...] = gains_full
    gain = gains_full[0:1]
    rows = 64

    def normalize(t, _):
        part = pl.ds(pl.multiple_of(t * rows, rows), rows)
        v = x_out[part].astype(F32)
        inverse = lax.rsqrt(jnp.mean(v * v, -1, keepdims=True) + EPS)
        first[part] = (v * inverse * gain).astype(BF)
        return 0

    lax.fori_loop(0, length // rows, normalize, 0)

    for s in steps:
        spread("o", s)
    for s in steps:
        moves["kv", "core", s].wait_recv()
    for copy in own_kv:
        copy.wait()
    keep = [local(full_kv, kv_all)]
    tile = 384

    def project(weight, t, turn):
        cols = pl.ds(pl.multiple_of(t * tile, tile), tile)
        w = weight[:, :, :, :, cols].reshape(width, tile)
        r = jnp.dot(first[...], w, preferred_element_type=F32).T
        if turn:
            r = rotate(r, cos[...], sin[...])
        return r.astype(BF)

    def project_kv(t, turn):
        kv_s[pl.ds(pl.multiple_of(t * tile, tile), tile)] = project(full_kv, t, turn)
        return 0

    per = kv_rows // tile
    lax.fori_loop(0, per, lambda t, _: project_kv(t, True), 0)
    k_here, v_here = kv_s.at[pl.ds(0, kv_rows)], kv_s.at[pl.ds(kv_rows, kv_rows)]
    k_x, k_y = send(k_here, k1, to_x), send(k_here, k2, to_y)
    lax.fori_loop(per, 2 * per, lambda t, _: project_kv(t, False), 0)
    v_y, v_x = send(v_here, v2, to_y), send(v_here, v1, to_x)
    if last > 1:
        moves["ffn", 1].wait_recv()
        ffn_step(2)
    for s in steps:
        forward("q", s)
    keep += [local(k_here, k0), local(v_here, v0)]
    for copy in far_ffn:
        copy.wait()
    keep += [local(pack_s.at[n], out) for n, out in enumerate((pack, far_pack, pack_x, pack_y))]
    keep += [local(cot_s.at[0], cot.at[0]), local(cot_s.at[1], cot.at[3])]
    for z in range(zsize):
        strips = first[:, z * tile:(z + 1) * tile].astype(F32).T.astype(BF)
        first_s[z] = strips.reshape(4, 2, strips.shape[0] // 8, length)
    keep.append(local(first_s.at[:, :, core], first_half.at[:, :, :, pl.ds(0, length)]))
    half_move = send(first_s.at[:, :, 1 - core], first_half.at[:, :, :, pl.ds(length, length)], to_core)
    for s in steps:
        cross("q", s)
    for s in steps:
        forward("o", s)
    for s in range(2, last):
        moves["ffn", s].wait_recv()
        ffn_step(s + 1)
    k_x.wait_recv()
    k_d = send(k1, k3, to_y)
    v_y.wait_recv()
    v_d = send(v2, v3, to_x)
    for s in steps:
        moves["q", "core", s].wait_recv()
    for copy in own_late:
        copy.wait()
    keep.append(local(full_q, q_all))

    def project_q(t, _):
        q_out[pl.ds(pl.multiple_of(t * tile, tile), tile)] = project(full_q, t, True)
        return 0

    lax.fori_loop(0, width // tile, project_q, 0)
    for s in steps:
        cross("o", s)
    for s in steps:
        moves["o", "core", s].wait_recv()
    keep.append(local(full_o, o_all))
    moves["ffn", last].wait_recv()
    for copy in (k_y, v_x, k_d, v_d, half_move, *cot_moves):
        copy.wait_recv()
    for copy in keep:
        copy.wait()
    for copy in sent:
        copy.wait_send()


def front(tokens, cotangent, gains, key_w, value_w, query_w, out_w, gate_w, up_w, down_w, cosine, sine, zsize, ctx):
    width = tokens.shape[2]
    length = 2 * tokens.shape[1]
    rows = width // zsize
    strip = rows // ctx
    fine = down_w.shape[0] // ctx
    packed = pack_width(rows, fine, zsize, width)
    kv_rows = key_w.shape[1]
    chips = ctx // 2
    cut = lambda w: w.reshape(chips, 2, strip, w.shape[1])
    square = jax.ShapeDtypeStruct((zsize, chips, 2, strip, width), BF)
    flat = jax.ShapeDtypeStruct((kv_rows, length), BF)
    hbm, vmem = pl.BlockSpec(memory_space=pltpu.HBM), pl.BlockSpec(memory_space=pltpu.VMEM)
    copies = 19 * (zsize - 1) + 13
    return pl.pallas_call(
        functools.partial(front_kernel, zsize),
        out_shape=[
            square, square, square,
            jax.ShapeDtypeStruct((rows, packed), BF),
            jax.ShapeDtypeStruct((zsize - 1, rows, packed), BF),
            jax.ShapeDtypeStruct((rows, packed), BF),
            jax.ShapeDtypeStruct((rows, packed), BF),
            jax.ShapeDtypeStruct((rows, packed), BF),
            jax.ShapeDtypeStruct((4, length // 2, width), BF),
            jax.ShapeDtypeStruct((zsize, chips, strip, 2 * length), BF),
            jax.ShapeDtypeStruct((length, width), BF),
            jax.ShapeDtypeStruct((length, width), BF),
            jax.ShapeDtypeStruct((width, length), BF),
            jax.ShapeDtypeStruct((2, width), F32),
        ] + [flat] * 8,
        in_specs=[vmem, hbm, vmem] + [hbm] * 7 + [vmem] * 2,
        out_specs=[hbm] * 10 + [vmem] * 4 + [hbm] * 8,
        scratch_shapes=[
            pltpu.VMEM((2, length // 2, width), BF),
            pltpu.VMEM((zsize, 2, rows), F32),
            pltpu.VMEM(square.shape, BF),
            pltpu.VMEM(square.shape, BF),
            pltpu.VMEM(square.shape, BF),
            pltpu.VMEM((2 * kv_rows, length), BF),
            pltpu.VMEM((zsize, chips, 2, strip, length), BF),
            pltpu.VMEM((4, rows, packed), BF),
            pltpu.VMEM((2, length // 2, width), BF),
            pltpu.SemaphoreType.DMA((copies,)),
            pltpu.SemaphoreType.DMA((copies,)),
            pltpu.SemaphoreType.DMA((20 + 8 * zsize + 4 * (rows // fine),)),
            pltpu.SemaphoreType.DMA((zsize,)),
            pltpu.SemaphoreType.DMA((zsize,)),
        ],
        compiler_params=pltpu.CompilerParams(collective_id=0, has_side_effects=True, vmem_limit_bytes=50 * 2**20),
        name="front",
    )(tokens, cotangent, gains, cut(key_w), cut(value_w), cut(query_w), cut(out_w), gate_w, up_w, down_w, cosine, sine)


def tail_kernel(zsize, *refs):
    dk, dv = refs[0:4], refs[4:8]
    dq, cos, sin, first_half, att_half = refs[8:13]
    pack_in, far_in = refs[13:16], refs[16:19]
    mid_t, query_w, kv_w, x_in, middle, gain, second_part = refs[19:26]
    rest = refs[26:]
    o_all, q_all, kv_all, pack_all, tokens_out, gains_out = rest[:6]
    (got, held, dq_pair, kv_pair, half, grads, gl, gr, gx, gy, gz, piece,
     pack_s, pack_0, pack_z, far_s, far_r, pack_p, first_grad, tokens_s, gain_s, gain_r, ss, rs, ls) = rest[6:]
    index, depth = lax.axis_index("ctx"), lax.axis_index("fsdp")
    chip, core = index // 2, lax.rem(index, 2)
    chip_x, chip_y, chip_d = chip + 1 - 2 * lax.rem(chip, 2), lax.rem(chip + 2, 4), 3 - chip
    nxt, prv = lax.rem(depth + 1, zsize), lax.rem(depth + zsize - 1, zsize)
    to_next, to_prev = (index, nxt), (index, prv)
    to_x, to_y, to_core = (chip_x * 2 + core, depth), (chip_y * 2 + core, depth), (chip * 2 + 1 - core, depth)
    to_far = (chip_d * 2 + core, depth)
    last = zsize - 1
    kv_rows = dk[0].shape[0]
    width = kv_w.shape[2]
    strip = piece.shape[1]
    length = dq.shape[1]

    barrier = pltpu.get_barrier_semaphore()
    for target in (to_next, to_prev, to_x, to_y, to_core, to_far):
        pl.semaphore_signal(barrier, inc=1, device_id=target, device_id_type=pl.DeviceIdType.MESH)
    pl.semaphore_wait(barrier, 6)

    count = [0, 0]
    sent, kept = [], []

    def send(src, dst, target):
        k = count[0]
        count[0] += 1
        copy = pltpu.make_async_remote_copy(
            src_ref=src, dst_ref=dst, send_sem=ss.at[k], recv_sem=rs.at[k], device_id=target, device_id_type=pl.DeviceIdType.MESH
        )
        copy.start()
        sent.append(copy)
        return copy

    def settle(copy):
        copy.wait_send()
        sent[:] = [other for other in sent if other is not copy]

    def local(src, dst):
        k = count[1]
        count[1] += 1
        copy = pltpu.make_async_copy(src, dst, ls.at[k])
        copy.start()
        return copy

    def wait_all(copies):
        for copy in copies:
            copy.wait()

    def received(*copies):
        for copy in copies:
            copy.wait_recv()

    def add_rows(target, sources, block):
        def one(t, _):
            part = pl.ds(pl.multiple_of(t * block, block), block)
            total = target[part].astype(F32)
            for source in sources:
                total = total + source[part].astype(F32)
            target[part] = total.astype(BF)
            return 0

        lax.fori_loop(0, target.shape[0] // block, one, 0)

    def place_at(j):
        return lax.rem(depth + 2 * zsize - 1 - j, zsize)

    k3, v3 = send(dk[3], got.at[0], to_y), send(dv[3], got.at[1], to_x)
    mid_swap = send(mid_t, held.at[1], to_core)
    q_swap = send(dq, dq_pair.at[1], to_core)

    part = pack_0.shape[0] // 2
    parts = [pl.ds(h * part, part) for h in range(2)]

    def load_ffn(j):
        return [local(pack_in[n].at[place_at(j)], pack_s.at[j % 2, n]) for n in range(3)]

    ffn_loads = {0: load_ffn(0)}
    load_o = [local(mid_t, held.at[0]), local(att_half, half.at[0])]
    load_q = [local(dq, dq_pair.at[0]), local(first_half, half.at[1])]
    load_far = [local(far_in[n], far_s.at[n]) for n in range(3)]

    moves = {}

    def ffn_step(j):
        if j + 1 <= last:
            ffn_loads[j + 1] = load_ffn(j + 1)
        wait_all(ffn_loads[j])
        for h in range(2):
            mine = [pack_s.at[j % 2, n, parts[h]] for n in range(3)]
            if j == 0:
                sum_rows(pack_0.at[parts[h]], mine, 64)
                moves["pack", h, 0] = send(pack_0.at[parts[h]], pack_z.at[0, parts[h]], to_next)
                continue
            received(moves["pack", h, j - 1])
            here = pack_z.at[j - 1, parts[h]]
            add_rows(here, mine, 64)
            if j < last:
                moves["pack", h, j] = send(here, pack_z.at[j, parts[h]], to_next)

    def sum_rows(target, sources, block):
        def one(t, _):
            part = pl.ds(pl.multiple_of(t * block, block), block)
            total = sources[0][part].astype(F32)
            for source in sources[1:]:
                total = total + source[part].astype(F32)
            target[part] = total.astype(BF)
            return 0

        lax.fori_loop(0, target.shape[0] // block, one, 0)

    mid = width // 2
    tiles = 512

    def stage_1(m):
        moves["l", m] = send(grads.at[m, :, chip_d, :, pl.ds(0, mid)], gl.at[m], to_y)
        moves["r", m] = send(grads.at[m, :, chip_d, :, pl.ds(mid, mid)], gr.at[m], to_x)

    def stage_2(m):
        received(moves["l", m])

        def left(zz, _):
            grads[m, zz, chip_x, :, 0:mid] = (grads[m, zz, chip_x, :, 0:mid].astype(F32) + gl[m, zz].astype(F32)).astype(BF)
            return 0

        lax.fori_loop(0, zsize, left, 0)
        moves["x", m] = send(grads.at[m, :, chip_x], gx.at[m], to_x)
        received(moves["r", m])

        def right(zz, _):
            grads[m, zz, chip_y, :, mid:] = (grads[m, zz, chip_y, :, mid:].astype(F32) + gr[m, zz].astype(F32)).astype(BF)
            return 0

        lax.fori_loop(0, zsize, right, 0)
        moves["y", m] = send(grads.at[m, :, chip_y], gy.at[m], to_y)

    def stage_3(m):
        received(moves["x", m], moves["y", m])

        def own(zz, _):
            grads[m, zz, chip] = (grads[m, zz, chip].astype(F32) + gx[m, zz].astype(F32) + gy[m, zz].astype(F32)).astype(BF)
            return 0

        lax.fori_loop(0, zsize, own, 0)
        moves["z", m, 0] = send(grads.at[m, place_at(0), chip], gz.at[m, 0], to_next)

    def ring_step(m, j):
        received(moves["z", m, j - 1])
        total = gz[m, j - 1].astype(F32) + grads[m, place_at(j), chip].astype(F32)
        if j < last:
            gz[m, j - 1] = total.astype(BF)
            moves["z", m, j] = send(gz.at[m, j - 1], gz.at[m, j], to_next)
        else:
            piece[m] = total.astype(BF)

    def spread(name, source, target):
        kept.append(local(source, target(chip, core)))
        moves[name, "x"] = send(source, target(chip, core), to_x)
        moves[name, "y"] = send(source, target(chip, core), to_y)

    def forward(name, target):
        received(moves[name, "x"])
        left = target(chip_x, core, pl.ds(0, mid))
        moves[name, "fy"] = send(left, left, to_y)
        received(moves[name, "y"])
        right = target(chip_y, core, pl.ds(mid, mid))
        moves[name, "fx"] = send(right, right, to_x)

    def cross(name, target):
        received(moves[name, "fx"], moves[name, "fy"])
        column = target(slice(None), core)
        moves[name, "core"] = send(column, column, to_core)

    def whole(ref):
        def at(p, c, cols=None):
            return ref.at[p, c] if cols is None else ref.at[p, c, :, cols]

        return at

    def half_rows(ref, h):
        def at(p, c, cols=None):
            return ref.at[p, c, parts[h]] if cols is None else ref.at[p, c, parts[h], cols]

        return at

    def product(m, pair, which):
        per = width // tiles

        def one(t, _):
            zz = t // per
            cols = pl.ds(pl.multiple_of(lax.rem(t, per) * tiles, tiles), tiles)
            nt = (((1,), (1,)), ((), ()))
            left = half[which, zz].reshape(4 * strip, 2 * length)
            r = lax.dot_general(left[:, 0:length], pair[0, cols], nt, preferred_element_type=F32)
            r = r + lax.dot_general(left[:, length:], pair[1, cols], nt, preferred_element_type=F32)
            grads[m, zz, :, :, cols] = r.astype(BF).reshape(4, strip, tiles)
            return 0

        lax.fori_loop(0, zsize * per, one, 0)

    ffn_step(0)
    wait_all(load_far)
    add_rows(far_s.at[0], [far_s.at[1]], 64)
    far_ring = send(far_s.at[0], far_s.at[3], to_next)
    received(mid_swap)
    wait_all(load_o)
    product(0, held, 0)
    stage_1(0)
    keys_0, keys_1 = held.at[0, pl.ds(0, kv_rows)], held.at[0, pl.ds(kv_rows, kv_rows)]
    values_0, values_2 = held.at[1, pl.ds(0, kv_rows)], held.at[1, pl.ds(kv_rows, kv_rows)]
    load_kv = [local(dk[0], keys_0), local(dk[1], keys_1), local(dv[0], values_0), local(dv[2], values_2)]
    received(q_swap)
    wait_all(load_q)
    product(1, dq_pair, 1)
    stage_1(1)

    received(k3)
    wait_all(load_kv)
    add_rows(keys_1, [got.at[0]], 96)
    k1 = send(keys_1, got.at[2], to_x)
    received(v3)
    add_rows(values_2, [got.at[1]], 96)
    v2 = send(values_2, got.at[3], to_y)
    k2, v1 = send(dk[2], got.at[4], to_y), send(dv[1], got.at[5], to_x)
    if last > 1:
        ffn_step(1)
    received(k1, k2, v1, v2)

    def finish_keys(h, _):
        rows = pl.ds(pl.multiple_of(h * 96, 96), 96)
        v = keys_0[rows].astype(F32) + got[2, rows].astype(F32) + got[4, rows].astype(F32)
        kv_pair[0, rows] = rotate_back(v, cos[...], sin[...]).astype(BF)
        return 0

    def finish_values(h, _):
        rows = pl.ds(pl.multiple_of(h * 96, 96), 96)
        v = values_0[rows].astype(F32) + got[3, rows].astype(F32) + got[5, rows].astype(F32)
        kv_pair[0, pl.ds(pl.multiple_of(kv_rows + h * 96, 96), 96)] = v.astype(BF)
        return 0

    lax.fori_loop(0, kv_rows // 96, finish_keys, 0)
    lax.fori_loop(0, kv_rows // 96, finish_values, 0)
    kv_swap = send(kv_pair.at[0], kv_pair.at[1], to_core)
    stage_2(0)
    stage_2(1)
    if last > 2:
        ffn_step(2)
    received(far_ring)
    add_rows(far_s.at[2], [far_s.at[3]], 64)
    far = send(far_s.at[2], far_r, to_far)
    received(kv_swap)
    product(2, kv_pair, 1)
    stage_1(2)
    stage_3(0)
    stage_3(1)
    stage_2(2)
    for j in range(3, last):
        ffn_step(j)
    ffn_step(last)
    received(far)
    for h in range(2):
        sum_rows(pack_p.at[parts[h]], [pack_z.at[last - 1, parts[h]], far_r.at[parts[h]]], 64)
        spread(("pack", h), pack_p.at[parts[h]], half_rows(pack_all, h))
    for j in range(1, zsize):
        ring_step(0, j)
        ring_step(1, j)
        if j == 1:
            stage_3(2)
    spread(0, piece.at[0], whole(o_all))
    spread(1, piece.at[1], whole(q_all))
    for j in range(1, zsize):
        ring_step(2, j)
    spread(2, piece.at[2], whole(kv_all))
    settle(far)
    settle(far_ring)
    weight_at = [(pack_s.at[k // 3, k % 3], far_s.at[k]) for k in range(zsize)]
    loads = [(local(query_w.at[k], a), local(kv_w.at[k], b)) for k, (a, b) in enumerate(weight_at)]
    rows = width // zsize
    for k, (a, b) in enumerate(weight_at):
        wait_all(loads[k])
        r = jnp.dot(a[...], dq_pair[0], preferred_element_type=F32) + jnp.dot(b[...], kv_pair[0], preferred_element_type=F32)
        first_grad[:, k * rows:(k + 1) * rows] = r.T
    gain_s[...] = jnp.zeros(gain_s.shape, F32)
    gain_s[1:2] = second_part[...]

    def finish_tokens(t, _):
        at = pl.ds(pl.multiple_of(t * 64, 64), 64)
        v = x_in[at].astype(F32)
        inverse = lax.rsqrt(jnp.mean(v * v, -1, keepdims=True) + EPS)
        unit = v * inverse
        d = first_grad[at]
        gain_s[0:1] += jnp.sum(d * unit, axis=0, keepdims=True)
        scaled = d * gain[...]
        tokens_s[at] = (middle[at] + inverse * (scaled - unit * jnp.mean(scaled * unit, -1, keepdims=True))).astype(BF)
        return 0

    lax.fori_loop(0, length // 64, finish_tokens, 0)
    near_half = pl.ds(0, length // 2)
    kept.append(local(tokens_s.at[near_half], tokens_out.at[core]))
    tokens_swap = send(tokens_s.at[pl.ds(length // 2, length // 2)], tokens_out.at[core], to_core)
    gain_swap = send(gain_s, gain_r.at[0], to_core)

    targets = [(("pack", h), half_rows(pack_all, h)) for h in range(2)]
    targets += [(m, whole(ref)) for m, ref in enumerate((o_all, q_all, kv_all))]
    for name, target in targets[:2]:
        forward(name, target)
    received(gain_swap)
    settle(gain_swap)
    gain_s[...] += gain_r[0]
    for n, target in ((1, to_x), (2, to_y)):
        copy = send(gain_s, gain_r.at[n], target)
        for name, at in targets[2 * n:2 * n + 2]:
            forward(name, at)
        received(copy)
        settle(copy)
        gain_s[...] += gain_r[n]
    copy = send(gain_s, gain_r.at[3], to_next)
    wait_all(kept)
    for name, target in targets:
        cross(name, target)
    total = gain_s[...]
    for s in range(1, zsize):
        received(copy)
        total = total + gain_r[2 + s]
        if s < last:
            copy = send(gain_r.at[2 + s], gain_r.at[3 + s], to_next)
    gains_out[...] = total
    received(tokens_swap)
    for name, target in targets:
        received(moves[name, "core"])
    for copy in sent:
        copy.wait_send()


def tail(dk, dv, dq, cosine, sine, first_half, att_half, packs, far_packs, mid_t, query_w, kv_w, x, middle, gain, second_part, zsize, chips):
    kv_rows, length = dk[0].shape
    width = 2 * kv_rows
    strip = att_half.shape[2]
    rows, packed = packs[0].shape[1:]
    hbm, vmem = pl.BlockSpec(memory_space=pltpu.HBM), pl.BlockSpec(memory_space=pltpu.VMEM)
    shape = lambda *s: jax.ShapeDtypeStruct(s, BF)
    store = lambda *s: pltpu.VMEM(s, BF)
    copies = 16 + 3 * (zsize - 1) + 3 * (4 + zsize - 1) + 5 * 5
    cut = lambda w: w.reshape(zsize, rows, width)
    inputs = [*dk, *dv, dq, cosine, sine, first_half, att_half, *packs, *far_packs, mid_t, cut(query_w), cut(kv_w), x, middle, gain, second_part]
    last = zsize - 1
    return pl.pallas_call(
        functools.partial(tail_kernel, zsize),
        out_shape=[shape(chips, 2, strip, width)] * 3 + [
            shape(chips, 2, rows, packed), shape(2, length // 2, width), jax.ShapeDtypeStruct((8, width), F32)],
        in_specs=[hbm] * 9 + [vmem] * 2 + [hbm] * (len(inputs) - 15) + [vmem] * 4,
        out_specs=[hbm] * 5 + [vmem],
        scratch_shapes=[
            store(6, kv_rows, length), store(2, width, length), store(2, width, length), store(2, width, length),
            store(2, zsize, chips, strip, 2 * length), store(3, zsize, chips, strip, width),
            store(3, zsize, strip, width // 2), store(3, zsize, strip, width // 2),
            store(3, zsize, strip, width), store(3, zsize, strip, width),
            store(3, last, strip, width), store(3, strip, width),
            store(2, 3, rows, packed), store(rows, packed), store(last, rows, packed),
            store(max(4, zsize), rows, packed), store(rows, packed), store(rows, packed),
            pltpu.VMEM((length, width), F32), store(length, width), pltpu.VMEM((8, width), F32), pltpu.VMEM((zsize + 2, 8, width), F32),
            pltpu.SemaphoreType.DMA((copies,)), pltpu.SemaphoreType.DMA((copies,)),
            pltpu.SemaphoreType.DMA((6 * zsize + 14,)),
        ],
        compiler_params=pltpu.CompilerParams(collective_id=1, has_side_effects=True, vmem_limit_bytes=62 * 2**20),
        name="tail",
    )(*inputs)


def unfold(refs, wide, tall, start):
    zsize, fine = tall.shape[0], tall.shape[1]
    folds = wide.shape[1] // fine
    fold = tall.shape[2] // folds
    two = wide.shape[2]
    if len(refs) == 1:
        sources = [(refs[0], slice(None), (slice(None),))]
    else:
        depth = lax.axis_index("fsdp")
        pieces = [refs[0]] + ([refs[1].at[s] for s in range(zsize - 1)] if len(refs) == 2 else list(refs[1:]))
        sources = [(piece, lax.rem(depth + zsize - s, zsize), ()) for s, piece in enumerate(pieces)]
    for source, at, lead in sources:
        start(source.at[(*lead, slice(None), pl.ds(0, two))], wide.at[at])
        for n in range(folds):
            cols = pl.ds(n * fold, fold)
            start(source.at[(*lead, pl.ds(n * fine, fine), pl.ds(two, fold))], tall.at[at, :, cols])


def ffn_kernel(given, pieces, before, second, second_t, cot, *refs):
    weights, (hidden_o, low_o), grads = refs[:given], refs[given:given + 2], refs[given + 2:given + pieces + 2]
    s_v, st_v, c_v, wi_v, wo_v, h_v, ht_v, l_v, w_v, t_v, sem = refs[given + pieces + 2:]
    tokens, width = second.shape
    zsize, fine = wo_v.shape[:2]
    rows = wi_v.shape[1]
    chunk = zsize * fine
    loads = []

    def load(src, dst):
        copy = pltpu.make_async_copy(src, dst, sem.at[len(loads)])
        copy.start()
        loads.append(copy)

    tile = 256
    steps = tokens // tile
    unfold(weights, wi_v, wo_v, load)
    first = len(loads)
    for t in range(steps):
        part = pl.ds(t * tile, tile)
        load(second.at[part], s_v.at[part])
        load(cot.at[part], c_v.at[part])
    load(second_t, st_v)
    for copy in loads[:first]:
        copy.wait()
    nt = (((1,), (1,)), ((), ()))

    def one(t, _):
        part = pl.ds(t * tile, tile)
        pre = jnp.dot(s_v[part], wi_v[...].reshape(width, 2 * chunk), preferred_element_type=F32)
        hidden_grad = lax.dot_general(c_v[part], wo_v[...].reshape(chunk, width), nt, preferred_element_type=F32)
        gate, up = pre[:, :chunk], pre[:, chunk:]
        sigmoid = jax.nn.sigmoid(gate)
        silu = gate * sigmoid
        hidden = silu * up
        h_v[part] = hidden.astype(BF)
        ht_v[:, part] = hidden.T.astype(BF)
        l_v[part, 0:chunk] = (hidden_grad * up * sigmoid * (1.0 + gate * (1.0 - sigmoid))).astype(BF)
        l_v[part, chunk:] = (hidden_grad * silu).astype(BF)
        return 0

    for t in range(steps):
        loads[first + 2 * t].wait()
        loads[first + 2 * t + 1].wait()
        one(t, 0)
    stores = []

    def store(src, dst):
        copy = pltpu.make_async_copy(src, dst, sem.at[len(loads) + len(stores)])
        copy.start()
        stores.append(copy)

    store(h_v, hidden_o)
    store(l_v, low_o)
    loads[-1].wait()
    depth = 0 if pieces == 1 else lax.axis_index("fsdp")
    grad_at = lambda n: grads[0].at[n] if pieces == 1 else grads[n]

    def place(n):
        return n if pieces == 1 else lax.rem(depth + n, zsize)

    for n in range(zsize):
        z = place(n)
        part = pl.ds(pl.multiple_of(z * rows, rows), rows)
        w_v[z] = jnp.dot(st_v[part], l_v[...], preferred_element_type=F32).astype(BF)
        store(w_v.at[z], grad_at(n).at[:, pl.ds(0, 2 * chunk)])
    folds = rows // fine
    fold = width // folds
    for n in range(folds):
        cols = slice(fold * n, fold * (n + 1))
        t_v[:, :, cols] = jnp.dot(ht_v[...], c_v[:, cols], preferred_element_type=F32).astype(BF).reshape(zsize, fine, fold)
        if pieces == 1:
            store(t_v.at[:, :, cols], grads[0].at[:, pl.ds(n * fine, fine), pl.ds(2 * chunk, fold)])
        else:
            for k in range(zsize):
                store(t_v.at[place(k), :, cols], grads[k].at[pl.ds(n * fine, fine), pl.ds(2 * chunk, fold)])
    for copy in stores:
        copy.wait()


def ffn_chunk(before, second, second_t, cot, weights, split, cost, zsize, fine):
    pieces = zsize if split else 1
    tokens, width = second.shape
    chunk = zsize * fine
    rows = width // zsize
    folds = rows // fine
    shape = lambda *s: jax.ShapeDtypeStruct(s, BF)
    store = lambda *s: pltpu.VMEM(s, BF)
    hbm = pl.BlockSpec(memory_space=pltpu.HBM)
    packed = weights[0].shape[-1]
    piece = (rows, packed) if split else (zsize, rows, packed)
    out = pl.pallas_call(
        functools.partial(ffn_kernel, len(weights), pieces),
        out_shape=[shape(tokens, chunk), shape(tokens, 2 * chunk)] + [shape(*piece)] * pieces,
        in_specs=[hbm] * (4 + len(weights)),
        out_specs=[hbm] * (2 + pieces),
        scratch_shapes=[
            store(tokens, width), store(width, tokens), store(tokens, width), store(zsize, rows, 2 * chunk), store(zsize, fine, width),
            store(tokens, chunk), store(chunk, tokens), store(tokens, 2 * chunk), store(zsize, rows, 2 * chunk), store(zsize, fine, width),
            pltpu.SemaphoreType.DMA((5 + zsize + 2 * zsize * (folds + 1) + 2 * (tokens // 256),)),
        ],
        cost_estimate=cost,
        compiler_params=pltpu.CompilerParams(vmem_limit_bytes=50 * 2**20),
        name="ffn_chunk",
    )(before, second, second_t, cot, *weights)
    return out[0], out[1], out[2:]

def combine_kernel(counts, *refs):
    count = len(counts)
    hidden, low = refs[:count], refs[count:2 * count]
    weights, at = [], 2 * count
    for n in counts:
        weights.append(refs[at:at + n])
        at += n
    out, grad, h_v, l_v, wi_v, wo_v, o_v, g_v, sem = refs[at:]
    tokens, chunk = hidden[0].shape
    width = out.shape[1]
    loads = []

    def load(src, dst):
        copy = pltpu.make_async_copy(src, dst, sem.at[len(loads)])
        copy.start()
        loads.append(copy)

    for r in range(count):
        load(hidden[r], h_v.at[:, pl.ds(r * chunk, chunk)])
        unfold(weights[r], wi_v.at[:, :, pl.ds(2 * r * chunk, 2 * chunk)], wo_v.at[r], load)
    for r in range(count):
        load(low[r], l_v.at[:, pl.ds(2 * r * chunk, 2 * chunk)])
    nt = (((1,), (1,)), ((), ()))
    tile = 256
    steps = tokens // tile
    stores = []

    def store(src, dst):
        copy = pltpu.make_async_copy(src, dst, sem.at[len(loads) + len(stores)])
        copy.start()
        stores.append(copy)

    for copy in loads[:-count]:
        copy.wait()
    for t in range(steps):
        rows = slice(tile * t, tile * (t + 1))
        if t >= 2:
            stores[t - 2].wait()
        o_v[t % 2] = jnp.dot(h_v[rows], wo_v[...].reshape(count * chunk, width), preferred_element_type=F32)
        store(o_v.at[t % 2], out.at[rows])
    for copy in loads[-count:]:
        copy.wait()
    for t in range(steps):
        rows = slice(tile * t, tile * (t + 1))
        if t >= 2:
            stores[steps + t - 2].wait()
        g_v[t % 2] = lax.dot_general(l_v[rows], wi_v[...].reshape(width, 2 * count * chunk), nt, preferred_element_type=F32)
        store(g_v.at[t % 2], grad.at[rows])
    for t in range(max(steps - 2, 0), steps):
        stores[t].wait()
        stores[steps + t].wait()


def combine(hidden, low, weights, zsize, fine):
    counts = tuple(len(w) for w in weights)
    count = len(counts)
    tokens, chunk = hidden[0].shape
    rows = weights[0][0].shape[-2]
    width = rows * zsize
    hbm = pl.BlockSpec(memory_space=pltpu.HBM)
    shape = jax.ShapeDtypeStruct((tokens, width), F32)
    inputs = [*hidden, *low] + [piece for w in weights for piece in w]
    return pl.pallas_call(
        functools.partial(combine_kernel, counts),
        out_shape=[shape, shape],
        in_specs=[hbm] * len(inputs),
        out_specs=[hbm] * 2,
        scratch_shapes=[
            pltpu.VMEM((tokens, count * chunk), BF), pltpu.VMEM((tokens, 2 * count * chunk), BF),
            pltpu.VMEM((zsize, rows, 2 * count * chunk), BF), pltpu.VMEM((count, zsize, fine, width), BF),
            pltpu.VMEM((2, 256, width), F32), pltpu.VMEM((2, 256, width), F32),
            pltpu.SemaphoreType.DMA((2 * count + sum(counts) * (1 + rows // fine) + 2 * (tokens // 256),)),
        ],
        cost_estimate=NO_COST,
        compiler_params=pltpu.CompilerParams(vmem_limit_bytes=56 * 2**20),
        name="ffn_combine",
    )(*inputs)


def assemble_kernel(zsize, wide, tall, o, q, kv, gate_o, up_o, down_o, o_o, q_o, k_o, v_o):
    fold = tall.shape[3]
    folds = down_o.shape[1] // fold
    fine = tall.shape[2] // folds
    kv_rows = k_o.shape[1]
    for p in range(4):
        for c in range(2):
            for part in range(zsize):
                at = slice((part * 8 + c * 4 + p) * fine, (part * 8 + c * 4 + p + 1) * fine)
                gate_o[:, at] = wide[p, c, :, part * fine:(part + 1) * fine].astype(F32)
                up_o[:, at] = wide[p, c, :, (zsize + part) * fine:(zsize + part + 1) * fine].astype(F32)
    for p in range(2):
        for n in range(folds):
            down_o[p * fine:(p + 1) * fine, n * fold:(n + 1) * fold] = tall[p, 0, n * fine:(n + 1) * fine].astype(F32)
    o_o[...] = o[...].astype(F32)
    q_o[...] = q[...].astype(F32)
    k_o[...] = kv[:, 0:kv_rows].astype(F32)
    v_o[...] = kv[:, kv_rows:].astype(F32)


def assemble(packs, o, q, kv, zsize, fine):
    chips, cores, rows, packed = packs.shape
    width = o.shape[1]
    steps = 4
    block = rows // steps
    two = 2 * fine * zsize
    fold = packed - two
    flat = lambda n: pl.BlockSpec((block, n), lambda i: (i, 0))
    out = lambda r, c: jax.ShapeDtypeStruct((r, c), F32)
    ff = fine * chips * cores
    hbm = pl.BlockSpec(memory_space=pltpu.HBM)

    def kernel(pack, o_in, q_in, kv_in, *outs):
        pltpu.emit_pipeline(
            functools.partial(assemble_kernel, zsize),
            grid=(steps,),
            in_specs=[
                pl.BlockSpec((chips, cores, block, two), lambda i: (0, 0, i, 0)),
                pl.BlockSpec((2, 1, rows, fold), lambda i: (i % 2, i // 2, 0, two // fold)),
                flat(width), flat(width), flat(width),
            ],
            out_specs=[flat(ff * zsize), flat(ff * zsize), pl.BlockSpec((ff // steps, width), lambda i: (i, 0)), flat(width), flat(width), flat(width // 2), flat(width // 2)],
        )(pack, pack, o_in, q_in, kv_in, *outs)

    return pl.pallas_call(
        kernel,
        out_shape=[out(rows, ff * zsize), out(rows, ff * zsize), out(ff, width), out(rows, width), out(rows, width), out(rows, width // 2), out(rows, width // 2)],
        in_specs=[hbm] * 4,
        out_specs=[hbm] * 7,
        compiler_params=pltpu.CompilerParams(vmem_limit_bytes=40 * 2**20),
        name="assemble",
    )(packs, o, q, kv)


MESH = pl.DeviceIdType.MESH


class Mover:
    def __init__(self, send_sems, recv_sems, local_sems):
        self.sems = send_sems, recv_sems, local_sems
        self.sent, self.kept, self.counts = [], [], [0, 0]

    def send(self, src, dst, target):
        k = self.counts[0]
        self.counts[0] += 1
        copy = pltpu.make_async_remote_copy(
            src_ref=src, dst_ref=dst, send_sem=self.sems[0].at[k], recv_sem=self.sems[1].at[k], device_id=target, device_id_type=MESH
        )
        copy.start()
        self.sent.append(copy)
        return copy

    def local(self, src, dst):
        k = self.counts[1]
        self.counts[1] += 1
        copy = pltpu.make_async_copy(src, dst, self.sems[2].at[k])
        copy.start()
        return copy

    def settle(self, copy):
        copy.wait_send()
        self.sent = [other for other in self.sent if other is not copy]

    def finish(self):
        for copy in self.sent:
            copy.wait_send()
        for copy in self.kept:
            copy.wait()


def greet_other_core():
    index, depth = lax.axis_index("ctx"), lax.axis_index("fsdp")
    core = lax.rem(index, 2)
    other = (index + 1 - 2 * core, depth)
    barrier = pltpu.get_barrier_semaphore()
    pl.semaphore_signal(barrier, inc=1, device_id=other, device_id_type=MESH)
    pl.semaphore_wait(barrier, 1)
    return core, other


def bridge_kernel(att, weight, x, gain, middle_o, second, second_t, att_half, att_s, w_s, low_s, low_t, middle, ss, rs, ls):
    core, other = greet_other_core()
    move = Mover(ss, rs, ls)
    zsize, chips, _, strip, length = att.shape
    width = x.shape[1]
    loads = [move.local(att, att_s), move.local(weight, w_s)]
    arrive = [move.send(att.at[:, :, 1 - core], att_half.at[:, :, :, pl.ds(length, length)], other)]
    for copy in loads:
        copy.wait()
    move.kept.append(move.local(att_s.at[:, :, core], att_half.at[:, :, :, pl.ds(0, length)]))
    tile = 128
    for t in range(length // tile):
        rows = slice(tile * t, tile * (t + 1))
        left = att_s[:, :, :, :, rows].reshape(width, tile).astype(F32).T.astype(BF)
        y = x[rows].astype(F32) + jnp.dot(left, w_s[...], preferred_element_type=F32)
        middle[rows] = y
        inverse = lax.rsqrt(jnp.mean(y * y, -1, keepdims=True) + EPS)
        normed = y * inverse * gain[...]
        low_s[rows] = normed.astype(BF)
        low_t[:, rows] = normed.T.astype(BF)
        here, there = pl.ds(tile * t, tile), pl.ds(length + tile * t, tile)
        arrive.append(move.send(low_s.at[here], second.at[there], other))
        arrive.append(move.send(low_t.at[:, here], second_t.at[:, there], other))
    move.kept.append(move.local(middle, middle_o))
    move.kept.append(move.local(low_s, second.at[pl.ds(0, length)]))
    move.kept.append(move.local(low_t, second_t.at[:, pl.ds(0, length)]))
    for copy in arrive:
        copy.wait_recv()
    move.finish()


def bridge(attended, weight, x, gain, zsize, chips):
    width, length = attended.shape
    strip = width // (zsize * chips * 2)
    hbm, vmem = pl.BlockSpec(memory_space=pltpu.HBM), pl.BlockSpec(memory_space=pltpu.VMEM)
    steps = length // 128
    return pl.pallas_call(
        bridge_kernel,
        out_shape=[
            jax.ShapeDtypeStruct((length, width), F32), jax.ShapeDtypeStruct((2 * length, width), BF),
            jax.ShapeDtypeStruct((width, 2 * length), BF), jax.ShapeDtypeStruct((zsize, chips, strip, 2 * length), BF),
        ],
        in_specs=[hbm, hbm, vmem, vmem],
        out_specs=[hbm, hbm, hbm, hbm],
        scratch_shapes=[
            pltpu.VMEM((zsize, chips, 2, strip, length), BF), pltpu.VMEM((width, width), BF),
            pltpu.VMEM((length, width), BF), pltpu.VMEM((width, length), BF), pltpu.VMEM((length, width), F32),
            pltpu.SemaphoreType.DMA((1 + 2 * steps,)), pltpu.SemaphoreType.DMA((1 + 2 * steps,)), pltpu.SemaphoreType.DMA((6,)),
        ],
        compiler_params=pltpu.CompilerParams(collective_id=2, has_side_effects=True, vmem_limit_bytes=40 * 2**20),
        cost_estimate=NO_COST,
        name="bridge",
    )(attended.reshape(zsize, chips, 2, strip, length), weight, x, gain)


def middle_kernel(counts, *refs):
    count = len(counts)
    hidden, low = refs[:count], refs[count:2 * count]
    weights, at = [], 2 * count
    for n in counts:
        weights.append(refs[at:at + n])
        at += n
    y_in, cot_in, gain, out_w = refs[at:at + 4]
    layer_out, middle_grad, low_t, att_grad, gain_part = refs[at + 4:at + 9]
    h_v, l_v, wi_v, wo_v, send_s, got, own, out_s, y_s, cot_s, ss, rs, ls = refs[at + 9:]
    core, other = greet_other_core()
    move = Mover(ss, rs, ls)
    tokens, chunk = hidden[0].shape
    length, width = y_in.shape
    late, loads = [], []
    for r in range(count):
        chunk_loads = []
        load = lambda src, dst: chunk_loads.append(move.local(src, dst))
        load(low[r], l_v.at[r])
        unfold(weights[r], wi_v.at[:, :, pl.ds(2 * r * chunk, 2 * chunk)], wo_v.at[r], load)
        loads.append(chunk_loads)
    inputs = [move.local(y_in, y_s), move.local(cot_in.at[pl.ds(0, 2)], cot_s)]
    for r in range(count):
        late.append(move.local(hidden[r], h_v.at[:, pl.ds(r * chunk, chunk)]))
    nt = (((1,), (1,)), ((), ()))
    tile = tokens // 4

    def out_tile(t):
        return jnp.dot(h_v[tile * t:tile * (t + 1)], wo_v[...].reshape(count * chunk, width), preferred_element_type=F32)

    targets = (own.at[pl.ds(0, tile)], own.at[pl.ds(tile, tile)], send_s.at[0], send_s.at[1])
    there = []
    for r in range(count):
        for copy in loads[r]:
            copy.wait()
        for t in (2, 3, 0, 1):
            part = lax.dot_general(
                l_v[r, tile * t:tile * (t + 1)], wi_v[:, :, 2 * r * chunk:2 * (r + 1) * chunk].reshape(width, 2 * chunk), nt,
                preferred_element_type=F32,
            )
            targets[t][...] = part if r == 0 else targets[t][...] + part
            if r == count - 1 and t >= 2:
                there.append(move.send(send_s.at[t - 2], got.at[t - 2], other))
    for copy in inputs:
        copy.wait()
    load_out = move.local(out_w, wi_v.at[:, :, pl.ds(0, width)])
    for copy in late:
        copy.wait()
    for n in range(2):
        move.settle(there[n])
        send_s[n] = out_tile(2) if n == 0 else out_tile(1) + y_s[tile:2 * tile]
        there.append(move.send(send_s.at[n], got.at[2 + n], other))
    there[0].wait_recv()
    there[1].wait_recv()
    gain_part[...] = jnp.zeros(gain_part.shape, F32)
    step = 128

    for t in range(length // step):
        part = slice(step * t, step * (t + 1))
        y = y_s[part]
        inverse = lax.rsqrt(jnp.mean(y * y, -1, keepdims=True) + EPS)
        unit = y * inverse
        d = own[part] + got[step * t // tile, step * t % tile:step * t % tile + step]
        gain_part[...] += jnp.sum(d * unit, axis=0, keepdims=True)
        scaled = d * gain[...]
        g = cot_s[step * t // tile, step * t % tile:step * t % tile + step].astype(F32)
        g = g + inverse * (scaled - unit * jnp.mean(scaled * unit, -1, keepdims=True))
        middle_grad[part] = g
        low_t[:, part] = g.T.astype(BF)
    load_out.wait()
    rows = wi_v.shape[1]
    for z in range(wi_v.shape[0]):
        att_grad[z * rows:(z + 1) * rows] = jnp.dot(wi_v[z, :, 0:width], low_t[...], preferred_element_type=F32).astype(BF)
    first, last = out_tile(0) + y_s[0:tile], out_tile(3)
    there[2].wait_recv()
    out_s[0] = (first + got[2]).astype(BF)
    there[3].wait_recv()
    out_s[1] = (last + got[3]).astype(BF)
    move.kept.append(move.local(out_s.at[0], layer_out.at[core]))
    move.kept.append(move.local(out_s.at[1], layer_out.at[1 - core]))
    move.finish()


def middle_part(hidden, low, weights, y, cot, gain, out_w, zsize, fine):
    counts = tuple(len(w) for w in weights)
    count = len(counts)
    tokens, chunk = hidden[0].shape
    length, width = y.shape
    rows = width // zsize
    hbm, vmem = pl.BlockSpec(memory_space=pltpu.HBM), pl.BlockSpec(memory_space=pltpu.VMEM)
    inputs = [*hidden, *low] + [piece for w in weights for piece in w]
    tile = tokens // 4
    return pl.pallas_call(
        functools.partial(middle_kernel, counts),
        out_shape=[
            jax.ShapeDtypeStruct((2, length // 2, width), BF), jax.ShapeDtypeStruct((length, width), F32),
            jax.ShapeDtypeStruct((width, length), BF), jax.ShapeDtypeStruct((width, length), BF),
            jax.ShapeDtypeStruct((1, width), F32),
        ],
        in_specs=[hbm] * len(inputs) + [hbm, hbm, vmem, hbm],
        out_specs=[hbm] + [vmem] * 4,
        scratch_shapes=[
            pltpu.VMEM((tokens, count * chunk), BF), pltpu.VMEM((count, tokens, 2 * chunk), BF),
            pltpu.VMEM((zsize, rows, 2 * count * chunk), BF), pltpu.VMEM((count, zsize, fine, width), BF),
            pltpu.VMEM((2, tile, width), F32), pltpu.VMEM((4, tile, width), F32),
            pltpu.VMEM((length, width), F32), pltpu.VMEM((2, tile, width), BF),
            pltpu.VMEM((length, width), F32), pltpu.VMEM((2, tile, width), BF),
            pltpu.SemaphoreType.DMA((4,)), pltpu.SemaphoreType.DMA((4,)),
            pltpu.SemaphoreType.DMA((2 * count + count * zsize * (1 + rows // fine) + 5,)),
        ],
        compiler_params=pltpu.CompilerParams(collective_id=3, has_side_effects=True, vmem_limit_bytes=61 * 2**20),
        cost_estimate=NO_COST,
        name="middle",
    )(*inputs, y, cot, gain, out_w.reshape(zsize, rows, width))


def mm(left, right, left_dim, right_dim):
    return lax.dot_general(left, right, (((left_dim,), (right_dim,)), ((), ())), preferred_element_type=F32)


def swap(a):
    return lax.ppermute(a, "ctx", [(i, i ^ 1) for i in range(lax.axis_size("ctx"))])


def hop(a, r):
    return lax.ppermute(a, "ctx", [(i, i ^ (2 * r)) for i in range(lax.axis_size("ctx"))])


def ring(a):
    n = lax.axis_size("fsdp")
    return lax.ppermute(a, "fsdp", [(i, (i + 1) % n) for i in range(n)])


def pick(a, index, axis=0):
    return lax.dynamic_index_in_dim(a, index, axis, keepdims=False)


def place(buffer, piece, index, axis=0):
    return lax.dynamic_update_slice_in_dim(buffer, jnp.expand_dims(piece, axis), index, axis)


def shift(a, s):
    n = lax.axis_size("fsdp")
    return lax.ppermute(a, "fsdp", [(i, (i + s) % n) for i in range(n)])


def depth_gather(piece, depth):
    n = lax.axis_size("fsdp")
    buffer = place(jnp.zeros((n,) + piece.shape, piece.dtype), piece, depth)
    for s in range(1, n):
        piece = ring(piece)
        buffer = place(buffer, piece, lax.rem(depth + n - s, n))
    return buffer


def depth_scatter(parts, depth):
    n = lax.axis_size("fsdp")
    total = pick(parts, lax.rem(depth + n - 1, n))
    for s in range(n - 1):
        total = ring(total.astype(BF))
        total = total.astype(F32) + pick(parts, lax.rem(depth + 2 * n - 2 - s, n)).astype(F32)
    return total


def plane_gather(piece, index):
    n = lax.axis_size("ctx")
    chips = n // 2
    pieces = jnp.stack([piece] + [hop(piece, r) for r in range(1, chips)])
    others = swap(pieces)
    buffer = jnp.zeros((n,) + piece.shape, piece.dtype)
    for r in range(chips):
        buffer = place(buffer, pieces[r], index ^ (2 * r))
        buffer = place(buffer, others[r], index ^ (2 * r + 1))
    return buffer


def rotate(v, cosine, sine):
    heads = v.reshape(-1, 2, HEAD_WIDTH // 2, v.shape[-1])
    a, b = heads[:, 0], heads[:, 1]
    return jnp.stack([a * cosine - b * sine, b * cosine + a * sine], 1).reshape(v.shape)


def rotate_back(v, cosine, sine):
    heads = v.reshape(-1, 2, HEAD_WIDTH // 2, v.shape[-1])
    a, b = heads[:, 0], heads[:, 1]
    return jnp.stack([a * cosine + b * sine, b * cosine - a * sine], 1).reshape(v.shape)


def norm_back(incoming, unit, inverse, gain):
    scaled = incoming * gain
    return inverse * (scaled - unit * jnp.mean(scaled * unit, -1, keepdims=True))


def body(
    tokens,
    block_pairs,
    cotangent,
    attention_gain,
    query_weight,
    key_matrix,
    value_matrix,
    output_weight,
    feedforward_gain,
    gate_weight,
    up_weight,
    down_weight,
):
    slice_len, width = tokens.shape[1], tokens.shape[2]
    ctx = lax.axis_size("ctx")
    zsize = lax.axis_size("fsdp")
    chips = ctx // 2
    diag = chips - 1
    near = range(1, chips - 1)
    index = lax.axis_index("ctx")
    chip, core = index // 2, lax.rem(index, 2)
    depth = lax.axis_index("fsdp")
    rows = width // zsize
    strip = rows // ctx
    hidden_rows = down_weight.shape[0]
    fine = hidden_rows // ctx
    chunk = fine * zsize
    kv_rows = KEY_HEADS * HEAD_WIDTH

    length = 2 * slice_len

    ids_all = jnp.concatenate([pick(block_pairs, index ^ r) for r in range(ctx)])
    ids = ids_all[:4]
    blocks = ids_all.shape[0]
    order = jnp.sum(
        jnp.where(ids_all[None, :] == jnp.arange(blocks, dtype=jnp.int32)[:, None], jnp.arange(blocks, dtype=jnp.int32)[None, :], 0), 1
    )
    positions = (ids[:, None] * BLK + jnp.arange(BLK, dtype=jnp.int32)[None, :]).reshape(length)
    half = HEAD_WIDTH // 2
    frequency = THETA ** (-jnp.arange(half, dtype=F32) * 2.0 / HEAD_WIDTH)
    angles = frequency[:, None] * positions.astype(F32)[None, :]
    cosine, sine = jnp.cos(angles), jnp.sin(angles)

    packs, keys, values = {}, {}, {}
    folds = rows // fine
    fast = chips == 4 and strip % 16 == 0 and fine % 128 == 0 and pack_width(rows, fine, zsize, width) == width
    if fast:
        (key_value_full, query_full, output_full, pack, rest, pack_x, pack_y, far_pack, cot, first_half, x_low, first, query, gains_full, *kv) = front(
            tokens, cotangent, jnp.stack([attention_gain, feedforward_gain]).astype(F32), key_matrix, value_matrix, query_weight,
            output_weight, gate_weight, up_weight, down_weight, cosine, sine, zsize, ctx,
        )
        key_value_full, query_full, output_full = (w.reshape(width, width) for w in (key_value_full, query_full, output_full))
        packs[0], packs[1], packs[2] = [pack, rest], [pack_x, hop(rest, 1)], [pack_y, hop(rest, 2)]
        for r in range(chips):
            keys[r], values[r] = kv[r], kv[chips + r]
        gain_first, gain_second = gains_full[0], gains_full[1]
        packs[diag] = [far_pack] + [shift(far_pack, s) for s in range(1, zsize)]
    else:
        gate_cut = gate_weight.reshape(rows, zsize, 2, chips, fine)
        up_cut = up_weight.reshape(rows, zsize, 2, chips, fine)
        down_cut = down_weight.reshape(2, chips, fine, width)

        def own_piece(r):
            gate = pick(pick(gate_cut, core, 2), chip ^ r, 2).reshape(rows, chunk)
            up = pick(pick(up_cut, core, 2), chip ^ r, 2).reshape(rows, chunk)
            down = pick(pick(down_cut, core), chip ^ r)
            folded = jnp.transpose(down.reshape(fine, folds, width // folds), (1, 0, 2)).reshape(rows, width // folds)
            return jnp.concatenate([gate, up, folded], 1)

        gains = jnp.stack([attention_gain, feedforward_gain])
        gain_buffer = place(jnp.zeros((zsize, 2, rows), BF), gains, depth)
        for s in range(1, zsize):
            moved = lax.ppermute(gains, "fsdp", [(k, (k + s) % zsize) for k in range(zsize)])
            gain_buffer = place(gain_buffer, moved, lax.rem(depth + zsize - s, zsize))
        gains_full = jnp.transpose(gain_buffer, (1, 0, 2)).reshape(2, width).astype(F32)
        gain_first, gain_second = gains_full[0], gains_full[1]

        def gather_square(shard):
            strips = shard.reshape(ctx, strip, shard.shape[1])
            pair = jnp.stack([pick(strips, index), pick(strips, index ^ (2 * diag))])
            pair = depth_gather(pair, depth)
            own, far = pair[:, 0], pair[:, 1]
            found = {0: own, diag: far}
            for r in near:
                found[r] = hop(own, r)
            full = jnp.zeros((zsize, ctx, strip, shard.shape[1]), BF)
            for r in range(chips):
                full = place(full, found[r], index ^ (2 * r), 1)
                full = place(full, swap(found[r]), index ^ (2 * r + 1), 1)
            return full.reshape(width, shard.shape[1])

        key_value_full = gather_square(jnp.concatenate([key_matrix, value_matrix], 1))
        query_full = gather_square(query_weight)
        output_full = gather_square(output_weight)

        x = jnp.concatenate([pick(tokens, core), swap(pick(tokens, 1 - core))]).astype(F32)
        packs[0] = [depth_gather(own_piece(0), depth)]
        inverse_first = lax.rsqrt(jnp.mean(x * x, -1, keepdims=True) + EPS)
        unit_first = x * inverse_first
        first = (unit_first * gain_first).astype(BF)
        first_t = jnp.transpose(first)
        kv = mm(key_value_full, first_t, 0, 0)
        keys[0] = rotate(kv[:kv_rows], cosine, sine).astype(BF)
        values[0] = kv[kv_rows:].astype(BF)
        for r in range(1, chips):
            high = 1 << (r.bit_length() - 1)
            low = r & -r
            keys[r] = hop(keys[r ^ high], high)
            values[r] = hop(values[r ^ low], low)
        query = rotate(mm(query_full, first_t, 0, 0), cosine, sine).astype(BF)
        packs[diag] = [depth_gather(own_piece(diag), depth)]

        for r in near:
            packs[r] = [hop(packs[0][0], r)]
        cot_there = swap(cotangent)
        cot = jnp.concatenate(
            [pick(cotangent, core), pick(cot_there, core), pick(cot_there, 1 - core), pick(cotangent, 1 - core)]
        )

    key_list = [keys[r] for r in range(chips)]
    value_list = [values[r] for r in range(chips)]
    attended, log_total = attn_fwd(ids, order, query, key_list, value_list, KEY_HEADS)

    if fast:
        middle, second, second_t, att_half = bridge(attended, output_full, x_low, gain_second[None], zsize, chips)
    else:
        middle = x + mm(attended, output_full, 0, 0)
        inverse_second = lax.rsqrt(jnp.mean(middle * middle, -1, keepdims=True) + EPS)
        unit_second = middle * inverse_second
        second = (unit_second * gain_second).astype(BF)
        second = jnp.concatenate([second, swap(second)])
        second_t = jnp.transpose(second)
    grads, hidden, low = {}, {}, {}
    before = second
    for r in [0] + list(near) + [diag]:
        before, low[r], grads[r] = ffn_chunk(
            before, second, second_t, cot.reshape(2 * length, width), packs[r], fast and r == diag, LONG if r == diag else NO_COST, zsize, fine
        )
        hidden[r] = before
    every = range(chips)
    hidden, low, packs = ([a[r] for r in every] for a in (hidden, low, packs))

    if fast:
        layer_out, middle_grad, middle_t, attended_grad, gain_second_part = middle_part(
            hidden, low, packs, middle, cot, gain_second[None], output_full, zsize, fine
        )
    else:
        out_part, second_grad = combine(hidden, low, packs, zsize, fine)

        q = slice_len
        out_part = jnp.concatenate([out_part[:length] + middle, out_part[length:]])
        came = swap(jnp.concatenate([out_part[2 * q:3 * q], out_part[q:2 * q]]))
        out_here = (out_part[:q] + came[:q]).astype(BF)
        out_there = (out_part[3 * q:] + came[q:]).astype(BF)

        def stored(here, there):
            return jnp.where(core == 0, jnp.stack([here, there]), jnp.stack([there, here]))

        layer_out = stored(out_here, out_there)

        second_grad = second_grad[:length] + swap(second_grad[length:])
        gain_second_part = jnp.sum(second_grad * unit_second, 0)
        middle_grad = cot[:length].astype(F32) + norm_back(second_grad, unit_second, inverse_second, gain_second)

        def halves(a):
            cut = a.reshape(zsize, chips, 2, strip, length)
            here = pick(cut, core, 2).reshape(-1, length)
            there = swap(pick(cut, 1 - core, 2).reshape(-1, length))
            return jnp.concatenate([here, there], 1)

        first_half = halves(first_t)
        middle_low = middle_grad.astype(BF)
        out_part_grad = mm(halves(attended), jnp.concatenate([middle_low, swap(middle_low)]), 1, 0)
        attended_grad = mm(output_full, middle_low, 1, 1).astype(BF)

    far_sum = middle_grad
    if fast:
        far_sum = grads[diag][zsize - 1]
        for s in range(zsize - 2, 0, -1):
            far_moved = shift(far_sum, 1)
            if s > 1:
                share, middle_t = lax.optimization_barrier((grads[diag][s], middle_t))
                far_sum = (far_moved.astype(F32) + share.astype(F32)).astype(BF)

    query_low, key_parts, value_parts = attn_bwd(
        far_sum, ids, order, query, attended, attended_grad, log_total, cosine, sine, key_list, value_list, KEY_HEADS
    )
    if fast:
        o_all, q_all, kv_all, pack_all, tokens_grad, gain_sums = tail(
            key_parts, value_parts, query_low, cosine, sine, first_half,
            att_half,
            [grads[0][0], hop(grads[1][0], 1), hop(grads[2][0], 2)],
            [far_moved, grads[diag][1], grads[diag][0]],
            middle_t, query_full, key_value_full, x_low, middle_grad, gain_first[None], gain_second_part, zsize, chips,
        )
        gain_first_grad, gain_second_grad = (
            lax.dynamic_slice_in_dim(gain_sums[n], depth * rows, rows) for n in range(2)
        )
        gate_grad, up_grad, down_grad, output_grad, query_grad, key_grad, value_grad = assemble(
            pack_all, *(a.reshape(rows, width) for a in (o_all, q_all, kv_all)), zsize, fine
        )
    else:
        key_sum = [part for part in key_parts]
        value_sum = [part for part in value_parts]
        for r in range(chips - 1, 0, -1):
            high = 1 << (r.bit_length() - 1)
            low = r & -r
            key_sum[r ^ high] = key_sum[r ^ high].astype(F32) + hop(key_sum[r].astype(BF), high).astype(F32)
            value_sum[r ^ low] = value_sum[r ^ low].astype(F32) + hop(value_sum[r].astype(BF), low).astype(F32)
        key_low = rotate_back(key_sum[0], cosine, sine).astype(BF)
        value_low = value_sum[0].astype(BF)
        kv_low = jnp.concatenate([key_low, value_low])

        def scatter(parts):
            total = parts[0].astype(F32)
            for r in near:
                total = total + hop(parts[r], r).astype(F32)
            far = hop(depth_scatter(parts[diag], depth).astype(BF), diag)
            total = depth_scatter(total.astype(BF), depth) + far.astype(F32)
            return total.astype(BF)

        pack_all = plane_gather(scatter({r: grads[r][0] for r in range(chips)}), index)
        wide_all = pack_all[:, :, :2 * chunk]
        tall_all = jnp.transpose(pack_all[:, :, 2 * chunk:].reshape(ctx, folds, fine, width // folds), (0, 2, 1, 3))
        def square_grad(product):
            parts = product.astype(BF).reshape(zsize, chips, strip, width)
            piece = scatter({r: pick(parts, chip ^ r, 1) for r in range(chips)})
            return plane_gather(piece, index).reshape(rows, width).astype(F32)

        output_grad = square_grad(out_part_grad)
        query_grad = square_grad(mm(first_half, jnp.concatenate([query_low, swap(query_low)], 1), 1, 1))
        kv_grad = square_grad(mm(first_half, jnp.concatenate([kv_low, swap(kv_low)], 1), 1, 1))
        down_grad = jnp.transpose(tall_all.reshape(chips, 2, fine, width), (1, 0, 2, 3)).reshape(hidden_rows, width).astype(F32)
        wide_all = wide_all.reshape(chips, 2, rows, 2, zsize, fine)
        gate_grad = jnp.transpose(wide_all[:, :, :, 0], (2, 3, 1, 0, 4)).reshape(rows, -1).astype(F32)
        up_grad = jnp.transpose(wide_all[:, :, :, 1], (2, 3, 1, 0, 4)).reshape(rows, -1).astype(F32)
        key_grad, value_grad = kv_grad[:, :kv_rows], kv_grad[:, kv_rows:]

        def gain_total(part):
            cut = part.reshape(zsize, rows)
            total = pick(cut, depth)
            for s in range(1, zsize):
                total = total + lax.ppermute(
                    pick(cut, lax.rem(depth + s, zsize)), "fsdp", [(k, (k + s) % zsize) for k in range(zsize)]
                )
            total = total + swap(total)
            bit = 1
            while bit < chips:
                total = total + hop(total, bit)
                bit *= 2
            return total

        first_grad = mm(query_low, query_full, 0, 1) + mm(kv_low, key_value_full, 0, 1)
        gain_first_part = jnp.sum(first_grad * unit_first, 0)
        tokens_part = (middle_grad + norm_back(first_grad, unit_first, inverse_first, gain_first)).astype(BF)
        tokens_grad = stored(tokens_part[:q], swap(tokens_part[q:]))
        gain_first_grad, gain_second_grad = gain_total(gain_first_part), gain_total(gain_second_part)

    return (
        layer_out,
        tokens_grad,
        gain_first_grad,
        query_grad,
        key_grad,
        value_grad,
        output_grad,
        gain_second_grad,
        gate_grad,
        up_grad,
        down_grad,
    )


def solution(mesh):
    line, square, grid = P("fsdp"), P("fsdp", None), P("fsdp", "ctx", None)
    in_specs = (grid, P(), grid, line, square, square, square, square, line, square, square, square)
    out_specs = (grid, grid, line, square, square, square, square, line, square, square, square)
    return jax.shard_map(body, mesh=mesh, in_specs=in_specs, out_specs=out_specs, check_vma=False)
```

```python
import functools

import jax
import jax.numpy as jnp
from jax import lax
from jax.experimental import pallas as pl
from jax.experimental.pallas import tpu as pltpu
from jax.sharding import PartitionSpec as P

QUERY_HEADS = 16
KEY_HEADS = 8
HEAD_WIDTH = 96
EPS = 1e-05
THETA = 100000.0
BLK = 128
SCALE = HEAD_WIDTH ** -0.5
BF = jnp.bfloat16
F32 = jnp.float32
NO_COST = pl.CostEstimate(flops=0, bytes_accessed=0, transcendentals=0)
LONG = pl.CostEstimate(flops=52 * 10**9, bytes_accessed=0, transcendentals=0)
ALL_VMEM = 62 * 2**20

LOG2E = 1.4426950408889634
NT = (((1,), (1,)), ((), ()))


def block_tasks(ids_ref, inv_ref, slices, t):
    tasks = []
    for sl in range(slices):
        first = ids_ref[2 * sl]
        late = (t > first).astype(jnp.int32)
        kpos = t - late * (first + 1)
        tasks.append((sl, late, inv_ref[kpos], (ids_ref[2 * sl + late] - kpos) * BLK))
    return tasks


def causal_difference():
    return lax.broadcasted_iota(jnp.int32, (BLK, 2 * BLK), 0) - lax.rem(lax.broadcasted_iota(jnp.int32, (BLK, 2 * BLK), 1), BLK)


def load_keys(refs, scratch, sem):
    copies = [pltpu.make_async_copy(ref, scratch.at[n], sem.at[n]) for n, ref in enumerate(refs)]

    @pl.when(pl.program_id(0) == 0)
    def _():
        for copy in copies:
            copy.start()
        for copy in copies:
            copy.wait()


def fwd_kernel(nchip, heads, ids_ref, inv_ref, q_ref, *rest):
    o_ref, lse_ref, kv_s, sem, knat, vtr = rest[2 * nchip:2 * nchip + 6]
    state = rest[2 * nchip + 6:]
    load_keys(rest[:2 * nchip], kv_s, sem)
    base = pl.program_id(0) * (96 * heads)
    nq = q_ref.shape[1] // BLK
    slices = nq // 2
    nb = nchip * nq
    c = SCALE * LOG2E
    chains = [(h, sl) for h in range(heads) for sl in range(slices)]
    qs, m_s, l_s, acc = ({chain: state[4 * n + k] for n, chain in enumerate(chains)} for k in range(4))
    for h in range(heads):
        for n in range(nb):
            r, lanes = n // nq, slice(BLK * (n % nq), BLK * (n % nq + 1))
            part = pl.ds(pl.multiple_of(base + 96 * h, 96), 96)
            knat[h, n] = kv_s[r, part, lanes].T
            vtr[h, n] = kv_s[nchip + r, part, lanes]
        for sl in range(slices):
            for half in range(2):
                lanes = slice(BLK * (2 * sl + half), BLK * (2 * sl + half + 1))
                qs[h, sl][half] = jnp.concatenate([q_ref[192 * h:192 * h + 96, lanes], q_ref[192 * h + 96:192 * h + 192, lanes]], axis=1)
            m_s[h, sl][...] = jnp.full((2, 1, 2 * BLK), -1e30, F32)
            l_s[h, sl][...] = jnp.zeros((2, 1, 2 * BLK), F32)
            acc[h, sl][...] = jnp.zeros((2, 96, 2 * BLK), F32)
    diff = causal_difference()

    def step(t, _):
        tasks = block_tasks(ids_ref, inv_ref, slices, t)
        todo = [(h, *task) for h in range(heads) for task in tasks]
        scores = [
            jnp.where(diff <= offset, jnp.dot(knat[h, n], qs[h, sl][late], preferred_element_type=F32), -jnp.inf)
            for h, sl, late, n, offset in todo
        ]
        old = [(m_s[h, sl][late], l_s[h, sl][late], acc[h, sl][late]) for h, sl, late, n, offset in todo]
        peaks = [jnp.maximum(m, jnp.max(s, axis=0, keepdims=True)) for s, (m, _l, _a) in zip(scores, old)]
        weights = [jnp.exp2((s - peak) * c) for s, peak in zip(scores, peaks)]
        shrink = [jnp.exp2((m - peak) * c) for peak, (m, _l, _a) in zip(peaks, old)]
        totals = [l * a + jnp.sum(p, axis=0, keepdims=True) for (_m, l, _a), a, p in zip(old, shrink, weights)]
        mixed = [
            o * a + jnp.dot(vtr[h, n], p.astype(BF), preferred_element_type=F32)
            for (h, sl, late, n, offset), (_m, _l, o), a, p in zip(todo, old, shrink, weights)
        ]
        for (h, sl, late, n, offset), peak, total, o in zip(todo, peaks, totals, mixed):
            m_s[h, sl][late] = peak
            l_s[h, sl][late] = total
            acc[h, sl][late] = o
        return 0

    lax.fori_loop(0, nb + 1, step, 0)
    for h, sl in chains:
        for half in range(2):
            lanes = slice(BLK * (2 * sl + half), BLK * (2 * sl + half + 1))
            l = l_s[h, sl][half]
            o = acc[h, sl][half] / l
            lse_ref[h, 2 * sl + half] = m_s[h, sl][half] * c + jnp.log2(l)
            o_ref[192 * h:192 * h + 96, lanes] = o[:, :BLK].astype(BF)
            o_ref[192 * h + 96:192 * h + 192, lanes] = o[:, BLK:].astype(BF)


def attn_fwd(ids, inv, qT, ks, vs, heads):
    nchip = len(ks)
    T = qT.shape[1]
    nq = T // BLK
    nb = nchip * nq
    per = 4 if nb <= 16 else 2
    wide = pl.BlockSpec((192 * per, T), lambda g, *_: (g, 0))
    slim = pl.BlockSpec((96 * per, T), lambda g, *_: (g, 0))
    chain = [
        pltpu.VMEM((2, 96, 2 * BLK), BF),
        pltpu.VMEM((2, 1, 2 * BLK), F32),
        pltpu.VMEM((2, 1, 2 * BLK), F32),
        pltpu.VMEM((2, 96, 2 * BLK), F32),
    ]
    grid_spec = pltpu.PrefetchScalarGridSpec(
        num_scalar_prefetch=2,
        grid=(heads // per,),
        in_specs=[wide] + [pl.BlockSpec(memory_space=pltpu.HBM)] * (2 * nchip),
        out_specs=[wide, pl.BlockSpec((per, nq, 1, 2 * BLK), lambda g, *_: (g, 0, 0, 0))],
        scratch_shapes=[
            pltpu.VMEM((2 * nchip, heads * 96, T), BF), pltpu.SemaphoreType.DMA((2 * nchip,)),
            pltpu.VMEM((per, nb, BLK, 96), BF), pltpu.VMEM((per, nb, 96, BLK), BF),
        ] + chain * (per * nq // 2),
    )
    return pl.pallas_call(
        functools.partial(fwd_kernel, nchip, per),
        grid_spec=grid_spec,
        out_shape=[jax.ShapeDtypeStruct((heads * 192, T), BF), jax.ShapeDtypeStruct((heads, nq, 1, 2 * BLK), F32)],
        cost_estimate=NO_COST,
        compiler_params=pltpu.CompilerParams(vmem_limit_bytes=ALL_VMEM),
        name="attention_forward",
    )(ids, inv, qT, *ks, *vs)


def bwd_kernel(nchip, heads, ids_ref, inv_ref, q_ref, o_ref, do_ref, lse_ref, cos_ref, sin_ref, before, *rest):
    dq_ref = rest[2 * nchip]
    dk_refs, dv_refs = rest[2 * nchip + 1:3 * nchip + 1], rest[3 * nchip + 1:4 * nchip + 1]
    kv_s, sem, knat, ktr, vnat = rest[4 * nchip + 1:4 * nchip + 6]
    state = rest[4 * nchip + 6:]
    load_keys(rest[:2 * nchip], kv_s, sem)
    base = pl.program_id(0) * (96 * heads)
    nq = q_ref.shape[1] // BLK
    slices = nq // 2
    nb = nchip * nq
    c = SCALE * LOG2E
    chains = [(h, sl) for h in range(heads) for sl in range(slices)]
    qs, dos, stat, dq_s, dk_s, dv_s = ({chain: state[6 * n + k] for n, chain in enumerate(chains)} for k in range(6))
    for h in range(heads):
        for n in range(nb):
            r, lanes = n // nq, slice(BLK * (n % nq), BLK * (n % nq + 1))
            part = pl.ds(pl.multiple_of(base + 96 * h, 96), 96)
            block = kv_s[r, part, lanes]
            knat[h, n] = block.T
            ktr[h, n] = block
            vnat[h, n] = kv_s[nchip + r, part, lanes].T
    for h, sl in chains:
        for half in range(2):
            lanes = slice(BLK * (2 * sl + half), BLK * (2 * sl + half + 1))
            pair = lambda ref: jnp.concatenate([ref[192 * h:192 * h + 96, lanes], ref[192 * h + 96:192 * h + 192, lanes]], axis=1)
            do = pair(do_ref)
            qs[h, sl][half] = pair(q_ref)
            dos[h, sl][half] = do
            stat[h, sl][half, 0:1] = lse_ref[h, 2 * sl + half]
            stat[h, sl][half, 1:2] = jnp.sum(pair(o_ref).astype(F32) * do.astype(F32), axis=0, keepdims=True)
        dq_s[h, sl][...] = jnp.zeros((2, 96, 2 * BLK), F32)
        dk_s[h, sl][...] = jnp.zeros((nb, 96, BLK), F32)
        dv_s[h, sl][...] = jnp.zeros((nb, 96, BLK), F32)
    diff = causal_difference()

    def step(t, _):
        tasks = block_tasks(ids_ref, inv_ref, slices, t)
        todo = [(h, *task) for h in range(heads) for task in tasks]
        q = [qs[h, sl][late] for h, sl, late, n, offset in todo]
        do = [dos[h, sl][late] for h, sl, late, n, offset in todo]
        scores = [jnp.dot(knat[h, n], x, preferred_element_type=F32) for (h, sl, late, n, offset), x in zip(todo, q)]
        grads = [jnp.dot(vnat[h, n], x, preferred_element_type=F32) for (h, sl, late, n, offset), x in zip(todo, do)]
        weights = [
            jnp.exp2(jnp.where(diff <= offset, s * c - stat[h, sl][late, 0:1], -jnp.inf))
            for (h, sl, late, n, offset), s in zip(todo, scores)
        ]
        low = [(p * (g - stat[h, sl][late, 1:2])).astype(BF) for (h, sl, late, n, offset), p, g in zip(todo, weights, grads)]
        dv = [lax.dot_general(x, p.astype(BF), NT, preferred_element_type=F32) for x, p in zip(do, weights)]
        dk = [lax.dot_general(x, ds, NT, preferred_element_type=F32) for x, ds in zip(q, low)]
        dq = [jnp.dot(ktr[h, n], ds, preferred_element_type=F32) for (h, sl, late, n, offset), ds in zip(todo, low)]
        for (h, sl, late, n, offset), a, b, d in zip(todo, dv, dk, dq):
            dv_s[h, sl][n] += a
            dk_s[h, sl][n] += b
            dq_s[h, sl][late] += d
        return 0

    lax.fori_loop(0, nb + 1, step, 0)
    for h, sl in chains:
        for half in range(2):
            lanes = slice(BLK * (2 * sl + half), BLK * (2 * sl + half + 1))
            cos, sin = cos_ref[:, lanes], sin_ref[:, lanes]
            for e in range(2):
                a = dq_s[h, sl][half, 0:48, BLK * e:BLK * (e + 1)] * SCALE
                b = dq_s[h, sl][half, 48:96, BLK * e:BLK * (e + 1)] * SCALE
                at = 192 * h + 96 * e
                dq_ref[at:at + 48, lanes] = (a * cos + b * sin).astype(BF)
                dq_ref[at + 48:at + 96, lanes] = (b * cos - a * sin).astype(BF)
    for h in range(heads):
        for n in range(nb):
            r, lanes = n // nq, slice(BLK * (n % nq), BLK * (n % nq + 1))
            dk = sum(dk_s[h, sl][n] for sl in range(slices))
            dv = sum(dv_s[h, sl][n] for sl in range(slices))
            dk_refs[r][96 * h:96 * (h + 1), lanes] = (dk * SCALE).astype(BF)
            dv_refs[r][96 * h:96 * (h + 1), lanes] = dv.astype(BF)


def attn_bwd(before, ids, inv, qT, oT, doT, lse, cosine, sine, ks, vs, heads):
    nchip = len(ks)
    T = qT.shape[1]
    nq = T // BLK
    nb = nchip * nq
    per = 4 if nb <= 16 else 2
    wide = pl.BlockSpec((192 * per, T), lambda g, *_: (g, 0))
    slim = pl.BlockSpec((96 * per, T), lambda g, *_: (g, 0))
    chain = [
        pltpu.VMEM((2, 96, 2 * BLK), BF),
        pltpu.VMEM((2, 96, 2 * BLK), BF),
        pltpu.VMEM((2, 2, 2 * BLK), F32),
        pltpu.VMEM((2, 96, 2 * BLK), F32),
        pltpu.VMEM((nb, 96, BLK), F32),
        pltpu.VMEM((nb, 96, BLK), F32),
    ]
    grid_spec = pltpu.PrefetchScalarGridSpec(
        num_scalar_prefetch=2,
        grid=(heads // per,),
        in_specs=[wide, wide, wide, pl.BlockSpec((per, nq, 1, 2 * BLK), lambda g, *_: (g, 0, 0, 0))]
        + [pl.BlockSpec((48, T), lambda g, *_: (0, 0))] * 2 + [pl.BlockSpec(memory_space=pltpu.HBM)] * (1 + 2 * nchip),
        out_specs=[wide] + [slim] * (2 * nchip),
        scratch_shapes=[
            pltpu.VMEM((2 * nchip, heads * 96, T), BF), pltpu.SemaphoreType.DMA((2 * nchip,)),
            pltpu.VMEM((per, nb, BLK, 96), BF), pltpu.VMEM((per, nb, 96, BLK), BF), pltpu.VMEM((per, nb, BLK, 96), BF),
        ]
        + chain * (per * nq // 2),
    )
    slab = jax.ShapeDtypeStruct((heads * 96, T), BF)
    outs = pl.pallas_call(
        functools.partial(bwd_kernel, nchip, per),
        grid_spec=grid_spec,
        out_shape=[jax.ShapeDtypeStruct((heads * 192, T), BF)] + [slab] * (2 * nchip),
        cost_estimate=NO_COST,
        compiler_params=pltpu.CompilerParams(vmem_limit_bytes=ALL_VMEM),
        name="attention_backward",
    )(ids, inv, qT, oT, doT, lse, cosine, sine, before, *ks, *vs)
    return outs[0], outs[1:1 + nchip], outs[1 + nchip:]


def pack_width(rows, fine, zsize, width):
    return 2 * fine * zsize + width * fine // rows


def front_kernel(zsize, *refs):
    (tok, cot_in, gains, key_w, value_w, query_w, out_w, gate_w, up_w, down_w, cos, sin) = refs[:12]
    (kv_all, q_all, o_all, pack, rest, pack_x, pack_y, far_pack, cot, first_half, x_out, first, q_out, gains_out) = refs[12:26]
    (k0, k1, k2, k3, v0, v1, v2, v3) = refs[26:34]
    x_s, gain_s, full_kv, full_q, full_o, kv_s, first_s, pack_s, cot_s, ss, rs, ls, gs, gr = refs[34:]
    ks, vs = (k0, k1, k2, k3), (v0, v1, v2, v3)
    index, depth = lax.axis_index("ctx"), lax.axis_index("fsdp")
    chip, core = index // 2, lax.rem(index, 2)
    fine = down_w.shape[0] // 8
    chunk = fine * zsize
    folds = pack.shape[0] // fine
    fold = first.shape[1] // folds
    width = first.shape[1]
    length = first.shape[0]
    kv_rows = k0.shape[0]
    nxt, prv = lax.rem(depth + 1, zsize), lax.rem(depth + zsize - 1, zsize)
    to_next, to_prev = (index, nxt), (index, prv)
    chip_x, chip_y, chip_d = chip + 1 - 2 * lax.rem(chip, 2), lax.rem(chip + 2, 4), 3 - chip
    to_x, to_y, to_core = (chip_x * 2 + core, depth), (chip_y * 2 + core, depth), (chip * 2 + 1 - core, depth)

    barrier = pltpu.get_barrier_semaphore()
    for target in (to_next, to_prev, to_x, to_y, to_core):
        pl.semaphore_signal(barrier, inc=1, device_id=target, device_id_type=pl.DeviceIdType.MESH)
    pl.semaphore_wait(barrier, 5)

    count = [0, 0]
    sent = []

    def send(src, dst, target):
        k = count[0]
        count[0] += 1
        copy = pltpu.make_async_remote_copy(
            src_ref=src, dst_ref=dst, send_sem=ss.at[k], recv_sem=rs.at[k], device_id=target, device_id_type=pl.DeviceIdType.MESH
        )
        copy.start()
        sent.append(copy)
        return copy

    def local(src, dst):
        k = count[1]
        count[1] += 1
        copy = pltpu.make_async_copy(src, dst, ls.at[k])
        copy.start()
        return copy

    def slot(s):
        return lax.rem(depth + zsize - s, zsize)

    steps = range(1, zsize)
    last = zsize - 1
    tokens_there = send(tok.at[1 - core], x_s.at[1], to_core)
    own_kv = [local(key_w, full_kv.at[depth, :, :, :, pl.ds(0, kv_rows)]), local(value_w, full_kv.at[depth, :, :, :, pl.ds(kv_rows, kv_rows)])]
    gain_s[depth] = gains[...]

    weights = {"kv": full_kv, "q": full_q, "o": full_o}
    shards = {"q": query_w, "o": out_w}
    moves = {}

    def ring_step(name, s):
        full = weights[name]
        place = full.at[slot(s - 1), chip, core]
        if name == "kv" and s == 1:
            halves = ((key_w, pl.ds(0, kv_rows)), (value_w, pl.ds(kv_rows, kv_rows)))
            moves[name, "ring", s] = [send(ref.at[chip, core], full.at[slot(0), chip, core, :, cols], to_next) for ref, cols in halves]
        else:
            source = shards[name].at[chip, core] if name in shards and s == 1 else place
            moves[name, "ring", s] = [send(source, place, to_next)]

    def spread(name, s):
        place = weights[name].at[slot(s), chip, core]
        moves[name, "x", s] = send(place, place, to_x)
        moves[name, "y", s] = send(place, place, to_y)

    def forward(name, s):
        mid = width // 2
        moves[name, "x", s].wait_recv()
        left = weights[name].at[slot(s), chip_x, core, :, pl.ds(0, mid)]
        moves[name, "fy", s] = send(left, left, to_y)
        moves[name, "y", s].wait_recv()
        right = weights[name].at[slot(s), chip_y, core, :, pl.ds(mid, mid)]
        moves[name, "fx", s] = send(right, right, to_x)

    def cross(name, s):
        moves[name, "fx", s].wait_recv()
        moves[name, "fy", s].wait_recv()
        column = weights[name].at[slot(s), :, core]
        moves[name, "core", s] = send(column, column, to_core)

    def gain_step(s):
        place = gain_s.at[slot(s - 1)]
        copy = pltpu.make_async_remote_copy(
            src_ref=place, dst_ref=place, send_sem=gs.at[s], recv_sem=gr.at[s], device_id=to_next, device_id_type=pl.DeviceIdType.MESH
        )
        copy.start()
        sent.append(copy)
        moves["gain", s] = copy

    def ffn_step(s):
        moves["ffn", s] = send(pack_s.at[0] if s == 1 else rest.at[s - 2], rest.at[s - 1], to_next)

    ring_step("kv", 1)
    gain_step(1)
    own_late = [local(query_w, full_q.at[depth]), local(out_w, full_o.at[depth])]
    def cut_pack(which, target):
        copies = []
        for part in range(zsize):
            column = pl.multiple_of(part * (8 * fine) + core * (4 * fine) + which * fine, fine)
            copies.append(local(gate_w.at[:, pl.ds(column, fine)], target.at[:, pl.ds(part * fine, fine)]))
            copies.append(local(up_w.at[:, pl.ds(column, fine)], target.at[:, pl.ds(chunk + part * fine, fine)]))
        row = pl.multiple_of(core * (4 * fine) + which * fine, fine)
        for n in range(folds):
            copies.append(local(down_w.at[pl.ds(row, fine), pl.ds(n * fold, fold)], target.at[pl.ds(n * fine, fine), pl.ds(2 * chunk, fold)]))
        return copies

    own_ffn = cut_pack(chip, pack_s.at[0])
    far_ffn = cut_pack(chip_d, pack_s.at[1]) + cut_pack(chip_x, pack_s.at[2]) + cut_pack(chip_y, pack_s.at[3])
    far_ffn += [local(cot_in.at[core], cot_s.at[0]), local(cot_in.at[1 - core], cot_s.at[1])]
    cot_moves = [send(cot_in.at[1 - core], cot.at[1], to_core), send(cot_in.at[core], cot.at[2], to_core)]

    def around(name, s):
        for copy in moves[name, "ring", s]:
            copy.wait_recv()
        if s < last:
            ring_step(name, s + 1)

    ring_step("q", 1)
    ring_step("o", 1)
    for s in steps:
        moves["gain", s].wait_recv()
        if s < last:
            gain_step(s + 1)
        around("kv", s)
        spread("kv", s)
        around("q", s)
        around("o", s)
    for copy in own_ffn:
        copy.wait()
    ffn_step(1)
    for s in steps:
        forward("kv", s)
    for s in steps:
        spread("q", s)
    for s in steps:
        cross("kv", s)

    tokens_there.wait_recv()
    x_out[0:length // 2] = tok[core]
    x_out[length // 2:] = x_s[1]
    gain_rows = [gain_s[place] for place in range(zsize)]
    gains_full = jnp.concatenate(gain_rows, axis=1)
    gains_out[...] = gains_full
    gain = gains_full[0:1]
    rows = 64

    def normalize(t, _):
        part = pl.ds(pl.multiple_of(t * rows, rows), rows)
        v = x_out[part].astype(F32)
        inverse = lax.rsqrt(jnp.mean(v * v, -1, keepdims=True) + EPS)
        first[part] = (v * inverse * gain).astype(BF)
        return 0

    lax.fori_loop(0, length // rows, normalize, 0)

    for s in steps:
        spread("o", s)
    for s in steps:
        moves["kv", "core", s].wait_recv()
    for copy in own_kv:
        copy.wait()
    keep = [local(full_kv, kv_all)]
    tile = 384

    def project(weight, t, turn):
        cols = pl.ds(pl.multiple_of(t * tile, tile), tile)
        w = weight[:, :, :, :, cols].reshape(width, tile)
        r = jnp.dot(first[...], w, preferred_element_type=F32).T
        if turn:
            r = rotate(r, cos[...], sin[...])
        return r.astype(BF)

    def project_kv(t, turn):
        kv_s[pl.ds(pl.multiple_of(t * tile, tile), tile)] = project(full_kv, t, turn)
        return 0

    per = kv_rows // tile
    lax.fori_loop(0, per, lambda t, _: project_kv(t, True), 0)
    k_here, v_here = kv_s.at[pl.ds(0, kv_rows)], kv_s.at[pl.ds(kv_rows, kv_rows)]
    k_x, k_y = send(k_here, k1, to_x), send(k_here, k2, to_y)
    lax.fori_loop(per, 2 * per, lambda t, _: project_kv(t, False), 0)
    v_y, v_x = send(v_here, v2, to_y), send(v_here, v1, to_x)
    if last > 1:
        moves["ffn", 1].wait_recv()
        ffn_step(2)
    for s in steps:
        forward("q", s)
    keep += [local(k_here, k0), local(v_here, v0)]
    for copy in far_ffn:
        copy.wait()
    keep += [local(pack_s.at[n], out) for n, out in enumerate((pack, far_pack, pack_x, pack_y))]
    keep += [local(cot_s.at[0], cot.at[0]), local(cot_s.at[1], cot.at[3])]
    for z in range(zsize):
        strips = first[:, z * tile:(z + 1) * tile].astype(F32).T.astype(BF)
        first_s[z] = strips.reshape(4, 2, strips.shape[0] // 8, length)
    keep.append(local(first_s.at[:, :, core], first_half.at[:, :, :, pl.ds(0, length)]))
    half_move = send(first_s.at[:, :, 1 - core], first_half.at[:, :, :, pl.ds(length, length)], to_core)
    for s in steps:
        cross("q", s)
    for s in steps:
        forward("o", s)
    for s in range(2, last):
        moves["ffn", s].wait_recv()
        ffn_step(s + 1)
    k_x.wait_recv()
    k_d = send(k1, k3, to_y)
    v_y.wait_recv()
    v_d = send(v2, v3, to_x)
    for s in steps:
        moves["q", "core", s].wait_recv()
    for copy in own_late:
        copy.wait()
    keep.append(local(full_q, q_all))

    def project_q(t, _):
        q_out[pl.ds(pl.multiple_of(t * tile, tile), tile)] = project(full_q, t, True)
        return 0

    lax.fori_loop(0, width // tile, project_q, 0)
    for s in steps:
        cross("o", s)
    for s in steps:
        moves["o", "core", s].wait_recv()
    keep.append(local(full_o, o_all))
    moves["ffn", last].wait_recv()
    for copy in (k_y, v_x, k_d, v_d, half_move, *cot_moves):
        copy.wait_recv()
    for copy in keep:
        copy.wait()
    for copy in sent:
        copy.wait_send()


def front(tokens, cotangent, gains, key_w, value_w, query_w, out_w, gate_w, up_w, down_w, cosine, sine, zsize, ctx):
    width = tokens.shape[2]
    length = 2 * tokens.shape[1]
    rows = width // zsize
    strip = rows // ctx
    fine = down_w.shape[0] // ctx
    packed = pack_width(rows, fine, zsize, width)
    kv_rows = key_w.shape[1]
    chips = ctx // 2
    cut = lambda w: w.reshape(chips, 2, strip, w.shape[1])
    square = jax.ShapeDtypeStruct((zsize, chips, 2, strip, width), BF)
    flat = jax.ShapeDtypeStruct((kv_rows, length), BF)
    hbm, vmem = pl.BlockSpec(memory_space=pltpu.HBM), pl.BlockSpec(memory_space=pltpu.VMEM)
    copies = 19 * (zsize - 1) + 13
    return pl.pallas_call(
        functools.partial(front_kernel, zsize),
        out_shape=[
            square, square, square,
            jax.ShapeDtypeStruct((rows, packed), BF),
            jax.ShapeDtypeStruct((zsize - 1, rows, packed), BF),
            jax.ShapeDtypeStruct((rows, packed), BF),
            jax.ShapeDtypeStruct((rows, packed), BF),
            jax.ShapeDtypeStruct((rows, packed), BF),
            jax.ShapeDtypeStruct((4, length // 2, width), BF),
            jax.ShapeDtypeStruct((zsize, chips, strip, 2 * length), BF),
            jax.ShapeDtypeStruct((length, width), BF),
            jax.ShapeDtypeStruct((length, width), BF),
            jax.ShapeDtypeStruct((width, length), BF),
            jax.ShapeDtypeStruct((2, width), F32),
        ] + [flat] * 8,
        in_specs=[vmem, hbm, vmem] + [hbm] * 7 + [vmem] * 2,
        out_specs=[hbm] * 10 + [vmem] * 4 + [hbm] * 8,
        scratch_shapes=[
            pltpu.VMEM((2, length // 2, width), BF),
            pltpu.VMEM((zsize, 2, rows), F32),
            pltpu.VMEM(square.shape, BF),
            pltpu.VMEM(square.shape, BF),
            pltpu.VMEM(square.shape, BF),
            pltpu.VMEM((2 * kv_rows, length), BF),
            pltpu.VMEM((zsize, chips, 2, strip, length), BF),
            pltpu.VMEM((4, rows, packed), BF),
            pltpu.VMEM((2, length // 2, width), BF),
            pltpu.SemaphoreType.DMA((copies,)),
            pltpu.SemaphoreType.DMA((copies,)),
            pltpu.SemaphoreType.DMA((20 + 8 * zsize + 4 * (rows // fine),)),
            pltpu.SemaphoreType.DMA((zsize,)),
            pltpu.SemaphoreType.DMA((zsize,)),
        ],
        compiler_params=pltpu.CompilerParams(collective_id=0, has_side_effects=True, vmem_limit_bytes=ALL_VMEM),
        name="front",
    )(tokens, cotangent, gains, cut(key_w), cut(value_w), cut(query_w), cut(out_w), gate_w, up_w, down_w, cosine, sine)


def tail_kernel(zsize, *refs):
    dk, dv = refs[0:4], refs[4:8]
    dq, cos, sin, first_half, att_half = refs[8:13]
    pack_in, far_in = refs[13:16], refs[16:19]
    mid_t, query_w, kv_w, x_in, middle, gain, second_part = refs[19:26]
    rest = refs[26:]
    o_all, q_all, kv_all, pack_all, tokens_out, gains_out = rest[:6]
    (got, held, dq_pair, kv_pair, half, grads, gl, gr, gx, gy, gz, piece,
     pack_s, pack_0, pack_z, far_s, far_r, pack_p, first_grad, tokens_s, gain_s, gain_r, ss, rs, ls) = rest[6:]
    index, depth = lax.axis_index("ctx"), lax.axis_index("fsdp")
    chip, core = index // 2, lax.rem(index, 2)
    chip_x, chip_y, chip_d = chip + 1 - 2 * lax.rem(chip, 2), lax.rem(chip + 2, 4), 3 - chip
    nxt, prv = lax.rem(depth + 1, zsize), lax.rem(depth + zsize - 1, zsize)
    to_next, to_prev = (index, nxt), (index, prv)
    to_x, to_y, to_core = (chip_x * 2 + core, depth), (chip_y * 2 + core, depth), (chip * 2 + 1 - core, depth)
    to_far = (chip_d * 2 + core, depth)
    last = zsize - 1
    kv_rows = dk[0].shape[0]
    width = kv_w.shape[2]
    strip = piece.shape[1]
    length = dq.shape[1]

    barrier = pltpu.get_barrier_semaphore()
    for target in (to_next, to_prev, to_x, to_y, to_core, to_far):
        pl.semaphore_signal(barrier, inc=1, device_id=target, device_id_type=pl.DeviceIdType.MESH)
    pl.semaphore_wait(barrier, 6)

    count = [0, 0]
    sent, kept = [], []

    def send(src, dst, target):
        k = count[0]
        count[0] += 1
        copy = pltpu.make_async_remote_copy(
            src_ref=src, dst_ref=dst, send_sem=ss.at[k], recv_sem=rs.at[k], device_id=target, device_id_type=pl.DeviceIdType.MESH
        )
        copy.start()
        sent.append(copy)
        return copy

    def settle(copy):
        copy.wait_send()
        sent[:] = [other for other in sent if other is not copy]

    def local(src, dst):
        k = count[1]
        count[1] += 1
        copy = pltpu.make_async_copy(src, dst, ls.at[k])
        copy.start()
        return copy

    def wait_all(copies):
        for copy in copies:
            copy.wait()

    def received(*copies):
        for copy in copies:
            copy.wait_recv()

    def add_rows(target, sources, block):
        def one(t, _):
            part = pl.ds(pl.multiple_of(t * block, block), block)
            total = target[part].astype(F32)
            for source in sources:
                total = total + source[part].astype(F32)
            target[part] = total.astype(BF)
            return 0

        lax.fori_loop(0, target.shape[0] // block, one, 0)

    def place_at(j):
        return lax.rem(depth + 2 * zsize - 1 - j, zsize)

    k3, v3 = send(dk[3], got.at[0], to_y), send(dv[3], got.at[1], to_x)
    mid_swap = send(mid_t, held.at[1], to_core)
    q_swap = send(dq, dq_pair.at[1], to_core)

    part = pack_0.shape[0] // 2
    parts = [pl.ds(h * part, part) for h in range(2)]

    def load_ffn(j):
        return [local(pack_in[n].at[place_at(j)], pack_s.at[j % 2, n]) for n in range(3)]

    ffn_loads = {0: load_ffn(0)}
    load_o = [local(mid_t, held.at[0]), local(att_half, half.at[0])]
    load_q = [local(dq, dq_pair.at[0]), local(first_half, half.at[1])]
    load_far = [local(far_in[n], far_s.at[n]) for n in range(3)]

    moves = {}

    def ffn_step(j):
        if j + 1 <= last:
            ffn_loads[j + 1] = load_ffn(j + 1)
        wait_all(ffn_loads[j])
        for h in range(2):
            mine = [pack_s.at[j % 2, n, parts[h]] for n in range(3)]
            if j == 0:
                sum_rows(pack_0.at[parts[h]], mine, 64)
                moves["pack", h, 0] = send(pack_0.at[parts[h]], pack_z.at[0, parts[h]], to_next)
                continue
            received(moves["pack", h, j - 1])
            here = pack_z.at[j - 1, parts[h]]
            add_rows(here, mine, 64)
            if j < last:
                moves["pack", h, j] = send(here, pack_z.at[j, parts[h]], to_next)

    def sum_rows(target, sources, block):
        def one(t, _):
            part = pl.ds(pl.multiple_of(t * block, block), block)
            total = sources[0][part].astype(F32)
            for source in sources[1:]:
                total = total + source[part].astype(F32)
            target[part] = total.astype(BF)
            return 0

        lax.fori_loop(0, target.shape[0] // block, one, 0)

    mid = width // 2
    tiles = 512

    def stage_1(m):
        moves["l", m] = send(grads.at[m, :, chip_d, :, pl.ds(0, mid)], gl.at[m], to_y)
        moves["r", m] = send(grads.at[m, :, chip_d, :, pl.ds(mid, mid)], gr.at[m], to_x)

    def stage_2(m):
        received(moves["l", m])

        def left(zz, _):
            grads[m, zz, chip_x, :, 0:mid] = (grads[m, zz, chip_x, :, 0:mid].astype(F32) + gl[m, zz].astype(F32)).astype(BF)
            return 0

        lax.fori_loop(0, zsize, left, 0)
        moves["x", m] = send(grads.at[m, :, chip_x], gx.at[m], to_x)
        received(moves["r", m])

        def right(zz, _):
            grads[m, zz, chip_y, :, mid:] = (grads[m, zz, chip_y, :, mid:].astype(F32) + gr[m, zz].astype(F32)).astype(BF)
            return 0

        lax.fori_loop(0, zsize, right, 0)
        moves["y", m] = send(grads.at[m, :, chip_y], gy.at[m], to_y)

    def stage_3(m):
        received(moves["x", m], moves["y", m])

        def own(zz, _):
            grads[m, zz, chip] = (grads[m, zz, chip].astype(F32) + gx[m, zz].astype(F32) + gy[m, zz].astype(F32)).astype(BF)
            return 0

        lax.fori_loop(0, zsize, own, 0)
        moves["z", m, 0] = send(grads.at[m, place_at(0), chip], gz.at[m, 0], to_next)

    def ring_step(m, j):
        received(moves["z", m, j - 1])
        total = gz[m, j - 1].astype(F32) + grads[m, place_at(j), chip].astype(F32)
        if j < last:
            gz[m, j - 1] = total.astype(BF)
            moves["z", m, j] = send(gz.at[m, j - 1], gz.at[m, j], to_next)
        else:
            piece[m] = total.astype(BF)

    def spread(name, source, target):
        kept.append(local(source, target(chip, core)))
        moves[name, "x"] = send(source, target(chip, core), to_x)
        moves[name, "y"] = send(source, target(chip, core), to_y)

    def forward(name, target):
        received(moves[name, "x"])
        left = target(chip_x, core, pl.ds(0, mid))
        moves[name, "fy"] = send(left, left, to_y)
        received(moves[name, "y"])
        right = target(chip_y, core, pl.ds(mid, mid))
        moves[name, "fx"] = send(right, right, to_x)

    def cross(name, target):
        received(moves[name, "fx"], moves[name, "fy"])
        column = target(slice(None), core)
        moves[name, "core"] = send(column, column, to_core)

    def whole(ref):
        def at(p, c, cols=None):
            return ref.at[p, c] if cols is None else ref.at[p, c, :, cols]

        return at

    def half_rows(ref, h):
        def at(p, c, cols=None):
            return ref.at[p, c, parts[h]] if cols is None else ref.at[p, c, parts[h], cols]

        return at

    def product(m, pair, which):
        per = width // tiles

        def one(t, _):
            zz = t // per
            cols = pl.ds(pl.multiple_of(lax.rem(t, per) * tiles, tiles), tiles)
            nt = (((1,), (1,)), ((), ()))
            left = half[which, zz].reshape(4 * strip, 2 * length)
            r = lax.dot_general(left[:, 0:length], pair[0, cols], nt, preferred_element_type=F32)
            r = r + lax.dot_general(left[:, length:], pair[1, cols], nt, preferred_element_type=F32)
            grads[m, zz, :, :, cols] = r.astype(BF).reshape(4, strip, tiles)
            return 0

        lax.fori_loop(0, zsize * per, one, 0)

    ffn_step(0)
    wait_all(load_far)
    add_rows(far_s.at[0], [far_s.at[1]], 64)
    far_ring = send(far_s.at[0], far_s.at[3], to_next)
    received(mid_swap)
    wait_all(load_o)
    product(0, held, 0)
    stage_1(0)
    keys_0, keys_1 = held.at[0, pl.ds(0, kv_rows)], held.at[0, pl.ds(kv_rows, kv_rows)]
    values_0, values_2 = held.at[1, pl.ds(0, kv_rows)], held.at[1, pl.ds(kv_rows, kv_rows)]
    load_kv = [local(dk[0], keys_0), local(dk[1], keys_1), local(dv[0], values_0), local(dv[2], values_2)]
    received(q_swap)
    wait_all(load_q)
    product(1, dq_pair, 1)
    stage_1(1)

    received(k3)
    wait_all(load_kv)
    add_rows(keys_1, [got.at[0]], 96)
    k1 = send(keys_1, got.at[2], to_x)
    received(v3)
    add_rows(values_2, [got.at[1]], 96)
    v2 = send(values_2, got.at[3], to_y)
    k2, v1 = send(dk[2], got.at[4], to_y), send(dv[1], got.at[5], to_x)
    if last > 1:
        ffn_step(1)
    received(far_ring)
    add_rows(far_s.at[2], [far_s.at[3]], 64)
    far = send(far_s.at[2], far_r, to_far)
    received(k1, k2, v1, v2)

    def finish_keys(h, _):
        rows = pl.ds(pl.multiple_of(h * 96, 96), 96)
        v = keys_0[rows].astype(F32) + got[2, rows].astype(F32) + got[4, rows].astype(F32)
        kv_pair[0, rows] = rotate_back(v, cos[...], sin[...]).astype(BF)
        return 0

    def finish_values(h, _):
        rows = pl.ds(pl.multiple_of(h * 96, 96), 96)
        v = values_0[rows].astype(F32) + got[3, rows].astype(F32) + got[5, rows].astype(F32)
        kv_pair[0, pl.ds(pl.multiple_of(kv_rows + h * 96, 96), 96)] = v.astype(BF)
        return 0

    lax.fori_loop(0, kv_rows // 96, finish_keys, 0)
    lax.fori_loop(0, kv_rows // 96, finish_values, 0)
    kv_swap = send(kv_pair.at[0], kv_pair.at[1], to_core)
    stage_2(0)
    stage_2(1)
    if last > 2:
        ffn_step(2)
    received(kv_swap)
    product(2, kv_pair, 1)
    stage_1(2)
    for j in range(3, last):
        ffn_step(j)
    ffn_step(last)
    stage_3(0)
    stage_3(1)
    stage_2(2)
    received(far)
    for h in range(2):
        sum_rows(pack_p.at[parts[h]], [pack_z.at[last - 1, parts[h]], far_r.at[parts[h]]], 64)
        spread(("pack", h), pack_p.at[parts[h]], half_rows(pack_all, h))
    for j in range(1, zsize):
        ring_step(0, j)
        ring_step(1, j)
        if j == 1:
            stage_3(2)
    spread(0, piece.at[0], whole(o_all))
    spread(1, piece.at[1], whole(q_all))
    for j in range(1, zsize):
        ring_step(2, j)
    spread(2, piece.at[2], whole(kv_all))
    settle(far)
    settle(far_ring)
    weight_at = [(pack_s.at[k // 3, k % 3], far_s.at[k]) for k in range(zsize)]
    loads = [(local(query_w.at[k], a), local(kv_w.at[k], b)) for k, (a, b) in enumerate(weight_at)]
    rows = width // zsize
    for k, (a, b) in enumerate(weight_at):
        wait_all(loads[k])
        r = jnp.dot(a[...], dq_pair[0], preferred_element_type=F32) + jnp.dot(b[...], kv_pair[0], preferred_element_type=F32)
        first_grad[:, k * rows:(k + 1) * rows] = r.T
    gain_s[...] = jnp.zeros(gain_s.shape, F32)
    gain_s[1:2] = second_part[...]

    def finish_tokens(t, _):
        at = pl.ds(pl.multiple_of(t * 64, 64), 64)
        v = x_in[at].astype(F32)
        inverse = lax.rsqrt(jnp.mean(v * v, -1, keepdims=True) + EPS)
        unit = v * inverse
        d = first_grad[at]
        gain_s[0:1] += jnp.sum(d * unit, axis=0, keepdims=True)
        scaled = d * gain[...]
        tokens_s[at] = (middle[at] + inverse * (scaled - unit * jnp.mean(scaled * unit, -1, keepdims=True))).astype(BF)
        return 0

    lax.fori_loop(0, length // 64, finish_tokens, 0)
    near_half = pl.ds(0, length // 2)
    kept.append(local(tokens_s.at[near_half], tokens_out.at[core]))
    tokens_swap = send(tokens_s.at[pl.ds(length // 2, length // 2)], tokens_out.at[core], to_core)
    gain_swap = send(gain_s, gain_r.at[0], to_core)

    targets = [(("pack", h), half_rows(pack_all, h)) for h in range(2)]
    targets += [(m, whole(ref)) for m, ref in enumerate((o_all, q_all, kv_all))]
    for name, target in targets[:2]:
        forward(name, target)
    received(gain_swap)
    settle(gain_swap)
    gain_s[...] += gain_r[0]
    for n, target in ((1, to_x), (2, to_y)):
        copy = send(gain_s, gain_r.at[n], target)
        for name, at in targets[2 * n:2 * n + 2]:
            forward(name, at)
        received(copy)
        settle(copy)
        gain_s[...] += gain_r[n]
    copy = send(gain_s, gain_r.at[3], to_next)
    wait_all(kept)
    for name, target in targets:
        cross(name, target)
    total = gain_s[...]
    for s in range(1, zsize):
        received(copy)
        total = total + gain_r[2 + s]
        if s < last:
            copy = send(gain_r.at[2 + s], gain_r.at[3 + s], to_next)
    gains_out[...] = total
    received(tokens_swap)
    for name, target in targets:
        received(moves[name, "core"])
    for copy in sent:
        copy.wait_send()


def tail(dk, dv, dq, cosine, sine, first_half, att_half, packs, far_packs, mid_t, query_w, kv_w, x, middle, gain, second_part, zsize, chips):
    kv_rows, length = dk[0].shape
    width = 2 * kv_rows
    strip = att_half.shape[2]
    rows, packed = packs[0].shape[1:]
    hbm, vmem = pl.BlockSpec(memory_space=pltpu.HBM), pl.BlockSpec(memory_space=pltpu.VMEM)
    shape = lambda *s: jax.ShapeDtypeStruct(s, BF)
    store = lambda *s: pltpu.VMEM(s, BF)
    copies = 16 + 3 * (zsize - 1) + 3 * (4 + zsize - 1) + 5 * 5
    cut = lambda w: w.reshape(zsize, rows, width)
    inputs = [*dk, *dv, dq, cosine, sine, first_half, att_half, *packs, *far_packs, mid_t, cut(query_w), cut(kv_w), x, middle, gain, second_part]
    last = zsize - 1
    return pl.pallas_call(
        functools.partial(tail_kernel, zsize),
        out_shape=[shape(chips, 2, strip, width)] * 3 + [
            shape(chips, 2, rows, packed), shape(2, length // 2, width), jax.ShapeDtypeStruct((8, width), F32)],
        in_specs=[hbm] * 9 + [vmem] * 2 + [hbm] * (len(inputs) - 15) + [vmem] * 4,
        out_specs=[hbm] * 5 + [vmem],
        scratch_shapes=[
            store(6, kv_rows, length), store(2, width, length), store(2, width, length), store(2, width, length),
            store(2, zsize, chips, strip, 2 * length), store(3, zsize, chips, strip, width),
            store(3, zsize, strip, width // 2), store(3, zsize, strip, width // 2),
            store(3, zsize, strip, width), store(3, zsize, strip, width),
            store(3, last, strip, width), store(3, strip, width),
            store(2, 3, rows, packed), store(rows, packed), store(last, rows, packed),
            store(max(4, zsize), rows, packed), store(rows, packed), store(rows, packed),
            pltpu.VMEM((length, width), F32), store(length, width), pltpu.VMEM((8, width), F32), pltpu.VMEM((zsize + 2, 8, width), F32),
            pltpu.SemaphoreType.DMA((copies,)), pltpu.SemaphoreType.DMA((copies,)),
            pltpu.SemaphoreType.DMA((6 * zsize + 14,)),
        ],
        compiler_params=pltpu.CompilerParams(collective_id=1, has_side_effects=True, vmem_limit_bytes=ALL_VMEM),
        name="tail",
    )(*inputs)


def unfold(refs, wide, tall, start):
    zsize, fine = tall.shape[0], tall.shape[1]
    folds = wide.shape[1] // fine
    fold = tall.shape[2] // folds
    two = wide.shape[2]
    if len(refs) == 1:
        sources = [(refs[0], slice(None), (slice(None),))]
    else:
        depth = lax.axis_index("fsdp")
        pieces = [refs[0]] + ([refs[1].at[s] for s in range(zsize - 1)] if len(refs) == 2 else list(refs[1:]))
        sources = [(piece, lax.rem(depth + zsize - s, zsize), ()) for s, piece in enumerate(pieces)]
    for source, at, lead in sources:
        start(source.at[(*lead, slice(None), pl.ds(0, two))], wide.at[at])
        for n in range(folds):
            cols = pl.ds(n * fold, fold)
            start(source.at[(*lead, pl.ds(n * fine, fine), pl.ds(two, fold))], tall.at[at, :, cols])


def ffn_kernel(given, pieces, before, second, second_t, cot, *refs):
    weights, (hidden_o, low_o), grads = refs[:given], refs[given:given + 2], refs[given + 2:given + pieces + 2]
    s_v, st_v, c_v, wi_v, wo_v, h_v, ht_v, l_v, w_v, t_v, sem = refs[given + pieces + 2:]
    tokens, width = second.shape
    zsize, fine = wo_v.shape[:2]
    rows = wi_v.shape[1]
    chunk = zsize * fine
    loads = []

    def load(src, dst):
        copy = pltpu.make_async_copy(src, dst, sem.at[len(loads)])
        copy.start()
        loads.append(copy)

    tile = 256
    steps = tokens // tile
    unfold(weights, wi_v, wo_v, load)
    first = len(loads)
    for t in range(steps):
        part = pl.ds(t * tile, tile)
        load(second.at[part], s_v.at[part])
        load(cot.at[part], c_v.at[part])
    load(second_t, st_v)
    for copy in loads[:first]:
        copy.wait()
    nt = (((1,), (1,)), ((), ()))

    def one(t, _):
        part = pl.ds(t * tile, tile)
        pre = jnp.dot(s_v[part], wi_v[...].reshape(width, 2 * chunk), preferred_element_type=F32)
        hidden_grad = lax.dot_general(c_v[part], wo_v[...].reshape(chunk, width), nt, preferred_element_type=F32)
        gate, up = pre[:, :chunk], pre[:, chunk:]
        sigmoid = jax.nn.sigmoid(gate)
        silu = gate * sigmoid
        hidden = silu * up
        h_v[part] = hidden.astype(BF)
        ht_v[:, part] = hidden.T.astype(BF)
        l_v[part, 0:chunk] = (hidden_grad * up * sigmoid * (1.0 + gate * (1.0 - sigmoid))).astype(BF)
        l_v[part, chunk:] = (hidden_grad * silu).astype(BF)
        return 0

    for t in range(steps):
        loads[first + 2 * t].wait()
        loads[first + 2 * t + 1].wait()
        one(t, 0)
    stores = []

    def store(src, dst):
        copy = pltpu.make_async_copy(src, dst, sem.at[len(loads) + len(stores)])
        copy.start()
        stores.append(copy)

    store(h_v, hidden_o)
    store(l_v, low_o)
    loads[-1].wait()
    depth = 0 if pieces == 1 else lax.axis_index("fsdp")
    grad_at = lambda n: grads[0].at[n] if pieces == 1 else grads[n]

    def place(n):
        return n if pieces == 1 else lax.rem(depth + n, zsize)

    for n in range(zsize):
        z = place(n)
        part = pl.ds(pl.multiple_of(z * rows, rows), rows)
        w_v[z] = jnp.dot(st_v[part], l_v[...], preferred_element_type=F32).astype(BF)
        store(w_v.at[z], grad_at(n).at[:, pl.ds(0, 2 * chunk)])
    folds = rows // fine
    fold = width // folds
    for n in range(folds):
        cols = slice(fold * n, fold * (n + 1))
        t_v[:, :, cols] = jnp.dot(ht_v[...], c_v[:, cols], preferred_element_type=F32).astype(BF).reshape(zsize, fine, fold)
        if pieces == 1:
            store(t_v.at[:, :, cols], grads[0].at[:, pl.ds(n * fine, fine), pl.ds(2 * chunk, fold)])
        else:
            for k in range(zsize):
                store(t_v.at[place(k), :, cols], grads[k].at[pl.ds(n * fine, fine), pl.ds(2 * chunk, fold)])
    for copy in stores:
        copy.wait()


def ffn_chunk(before, second, second_t, cot, weights, split, cost, zsize, fine):
    pieces = zsize if split else 1
    tokens, width = second.shape
    chunk = zsize * fine
    rows = width // zsize
    folds = rows // fine
    shape = lambda *s: jax.ShapeDtypeStruct(s, BF)
    store = lambda *s: pltpu.VMEM(s, BF)
    hbm = pl.BlockSpec(memory_space=pltpu.HBM)
    packed = weights[0].shape[-1]
    piece = (rows, packed) if split else (zsize, rows, packed)
    out = pl.pallas_call(
        functools.partial(ffn_kernel, len(weights), pieces),
        out_shape=[shape(tokens, chunk), shape(tokens, 2 * chunk)] + [shape(*piece)] * pieces,
        in_specs=[hbm] * (4 + len(weights)),
        out_specs=[hbm] * (2 + pieces),
        scratch_shapes=[
            store(tokens, width), store(width, tokens), store(tokens, width), store(zsize, rows, 2 * chunk), store(zsize, fine, width),
            store(tokens, chunk), store(chunk, tokens), store(tokens, 2 * chunk), store(zsize, rows, 2 * chunk), store(zsize, fine, width),
            pltpu.SemaphoreType.DMA((5 + zsize + 2 * zsize * (folds + 1) + 2 * (tokens // 256),)),
        ],
        cost_estimate=cost,
        compiler_params=pltpu.CompilerParams(vmem_limit_bytes=ALL_VMEM),
        name="ffn_chunk",
    )(before, second, second_t, cot, *weights)
    return out[0], out[1], out[2:]

def combine_kernel(counts, *refs):
    count = len(counts)
    hidden, low = refs[:count], refs[count:2 * count]
    weights, at = [], 2 * count
    for n in counts:
        weights.append(refs[at:at + n])
        at += n
    out, grad, h_v, l_v, wi_v, wo_v, o_v, g_v, sem = refs[at:]
    tokens, chunk = hidden[0].shape
    width = out.shape[1]
    loads = []

    def load(src, dst):
        copy = pltpu.make_async_copy(src, dst, sem.at[len(loads)])
        copy.start()
        loads.append(copy)

    for r in range(count):
        load(hidden[r], h_v.at[:, pl.ds(r * chunk, chunk)])
        unfold(weights[r], wi_v.at[:, :, pl.ds(2 * r * chunk, 2 * chunk)], wo_v.at[r], load)
    for r in range(count):
        load(low[r], l_v.at[:, pl.ds(2 * r * chunk, 2 * chunk)])
    nt = (((1,), (1,)), ((), ()))
    tile = 256
    steps = tokens // tile
    stores = []

    def store(src, dst):
        copy = pltpu.make_async_copy(src, dst, sem.at[len(loads) + len(stores)])
        copy.start()
        stores.append(copy)

    for copy in loads[:-count]:
        copy.wait()
    for t in range(steps):
        rows = slice(tile * t, tile * (t + 1))
        if t >= 2:
            stores[t - 2].wait()
        o_v[t % 2] = jnp.dot(h_v[rows], wo_v[...].reshape(count * chunk, width), preferred_element_type=F32)
        store(o_v.at[t % 2], out.at[rows])
    for copy in loads[-count:]:
        copy.wait()
    for t in range(steps):
        rows = slice(tile * t, tile * (t + 1))
        if t >= 2:
            stores[steps + t - 2].wait()
        g_v[t % 2] = lax.dot_general(l_v[rows], wi_v[...].reshape(width, 2 * count * chunk), nt, preferred_element_type=F32)
        store(g_v.at[t % 2], grad.at[rows])
    for t in range(max(steps - 2, 0), steps):
        stores[t].wait()
        stores[steps + t].wait()


def combine(hidden, low, weights, zsize, fine):
    counts = tuple(len(w) for w in weights)
    count = len(counts)
    tokens, chunk = hidden[0].shape
    rows = weights[0][0].shape[-2]
    width = rows * zsize
    hbm = pl.BlockSpec(memory_space=pltpu.HBM)
    shape = jax.ShapeDtypeStruct((tokens, width), F32)
    inputs = [*hidden, *low] + [piece for w in weights for piece in w]
    return pl.pallas_call(
        functools.partial(combine_kernel, counts),
        out_shape=[shape, shape],
        in_specs=[hbm] * len(inputs),
        out_specs=[hbm] * 2,
        scratch_shapes=[
            pltpu.VMEM((tokens, count * chunk), BF), pltpu.VMEM((tokens, 2 * count * chunk), BF),
            pltpu.VMEM((zsize, rows, 2 * count * chunk), BF), pltpu.VMEM((count, zsize, fine, width), BF),
            pltpu.VMEM((2, 256, width), F32), pltpu.VMEM((2, 256, width), F32),
            pltpu.SemaphoreType.DMA((2 * count + sum(counts) * (1 + rows // fine) + 2 * (tokens // 256),)),
        ],
        cost_estimate=NO_COST,
        compiler_params=pltpu.CompilerParams(vmem_limit_bytes=ALL_VMEM),
        name="ffn_combine",
    )(*inputs)


def assemble_kernel(zsize, wide, tall, o, q, kv, gate_o, up_o, down_o, o_o, q_o, k_o, v_o):
    fold = tall.shape[3]
    folds = down_o.shape[1] // fold
    fine = tall.shape[2] // folds
    kv_rows = k_o.shape[1]
    for p in range(4):
        for c in range(2):
            for part in range(zsize):
                at = slice((part * 8 + c * 4 + p) * fine, (part * 8 + c * 4 + p + 1) * fine)
                gate_o[:, at] = wide[p, c, :, part * fine:(part + 1) * fine].astype(F32)
                up_o[:, at] = wide[p, c, :, (zsize + part) * fine:(zsize + part + 1) * fine].astype(F32)
    for p in range(2):
        for n in range(folds):
            down_o[p * fine:(p + 1) * fine, n * fold:(n + 1) * fold] = tall[p, 0, n * fine:(n + 1) * fine].astype(F32)
    o_o[...] = o[...].astype(F32)
    q_o[...] = q[...].astype(F32)
    k_o[...] = kv[:, 0:kv_rows].astype(F32)
    v_o[...] = kv[:, kv_rows:].astype(F32)


def assemble(packs, o, q, kv, zsize, fine):
    chips, cores, rows, packed = packs.shape
    width = o.shape[1]
    steps = 4
    block = rows // steps
    two = 2 * fine * zsize
    fold = packed - two
    flat = lambda n: pl.BlockSpec((block, n), lambda i: (i, 0))
    out = lambda r, c: jax.ShapeDtypeStruct((r, c), F32)
    ff = fine * chips * cores
    hbm = pl.BlockSpec(memory_space=pltpu.HBM)

    def kernel(pack, o_in, q_in, kv_in, *outs):
        pltpu.emit_pipeline(
            functools.partial(assemble_kernel, zsize),
            grid=(steps,),
            in_specs=[
                pl.BlockSpec((chips, cores, block, two), lambda i: (0, 0, i, 0)),
                pl.BlockSpec((2, 1, rows, fold), lambda i: (i % 2, i // 2, 0, two // fold)),
                flat(width), flat(width), flat(width),
            ],
            out_specs=[flat(ff * zsize), flat(ff * zsize), pl.BlockSpec((ff // steps, width), lambda i: (i, 0)), flat(width), flat(width), flat(width // 2), flat(width // 2)],
        )(pack, pack, o_in, q_in, kv_in, *outs)

    return pl.pallas_call(
        kernel,
        out_shape=[out(rows, ff * zsize), out(rows, ff * zsize), out(ff, width), out(rows, width), out(rows, width), out(rows, width // 2), out(rows, width // 2)],
        in_specs=[hbm] * 4,
        out_specs=[hbm] * 7,
        compiler_params=pltpu.CompilerParams(vmem_limit_bytes=ALL_VMEM),
        name="assemble",
    )(packs, o, q, kv)


MESH = pl.DeviceIdType.MESH


class Mover:
    def __init__(self, send_sems, recv_sems, local_sems):
        self.sems = send_sems, recv_sems, local_sems
        self.sent, self.kept, self.counts = [], [], [0, 0]

    def send(self, src, dst, target):
        k = self.counts[0]
        self.counts[0] += 1
        copy = pltpu.make_async_remote_copy(
            src_ref=src, dst_ref=dst, send_sem=self.sems[0].at[k], recv_sem=self.sems[1].at[k], device_id=target, device_id_type=MESH
        )
        copy.start()
        self.sent.append(copy)
        return copy

    def local(self, src, dst):
        k = self.counts[1]
        self.counts[1] += 1
        copy = pltpu.make_async_copy(src, dst, self.sems[2].at[k])
        copy.start()
        return copy

    def settle(self, copy):
        copy.wait_send()
        self.sent = [other for other in self.sent if other is not copy]

    def finish(self):
        for copy in self.sent:
            copy.wait_send()
        for copy in self.kept:
            copy.wait()


def greet_other_core():
    index, depth = lax.axis_index("ctx"), lax.axis_index("fsdp")
    core = lax.rem(index, 2)
    other = (index + 1 - 2 * core, depth)
    barrier = pltpu.get_barrier_semaphore()
    pl.semaphore_signal(barrier, inc=1, device_id=other, device_id_type=MESH)
    pl.semaphore_wait(barrier, 1)
    return core, other


def bridge_kernel(att, weight, x, gain, middle_o, second, second_t, att_half, att_s, w_s, low_s, low_t, middle, ss, rs, ls):
    core, other = greet_other_core()
    move = Mover(ss, rs, ls)
    zsize, chips, _, strip, length = att.shape
    width = x.shape[1]
    loads = [move.local(att, att_s), move.local(weight, w_s)]
    arrive = [move.send(att.at[:, :, 1 - core], att_half.at[:, :, :, pl.ds(length, length)], other)]
    for copy in loads:
        copy.wait()
    move.kept.append(move.local(att_s.at[:, :, core], att_half.at[:, :, :, pl.ds(0, length)]))
    tile = 128
    for t in range(length // tile):
        rows = slice(tile * t, tile * (t + 1))
        left = att_s[:, :, :, :, rows].reshape(width, tile).astype(F32).T.astype(BF)
        y = x[rows].astype(F32) + jnp.dot(left, w_s[...], preferred_element_type=F32)
        middle[rows] = y
        inverse = lax.rsqrt(jnp.mean(y * y, -1, keepdims=True) + EPS)
        normed = y * inverse * gain[...]
        low_s[rows] = normed.astype(BF)
        low_t[:, rows] = normed.T.astype(BF)
        here, there = pl.ds(tile * t, tile), pl.ds(length + tile * t, tile)
        arrive.append(move.send(low_s.at[here], second.at[there], other))
        arrive.append(move.send(low_t.at[:, here], second_t.at[:, there], other))
    move.kept.append(move.local(middle, middle_o))
    move.kept.append(move.local(low_s, second.at[pl.ds(0, length)]))
    move.kept.append(move.local(low_t, second_t.at[:, pl.ds(0, length)]))
    for copy in arrive:
        copy.wait_recv()
    move.finish()


def bridge(attended, weight, x, gain, zsize, chips):
    width, length = attended.shape
    strip = width // (zsize * chips * 2)
    hbm, vmem = pl.BlockSpec(memory_space=pltpu.HBM), pl.BlockSpec(memory_space=pltpu.VMEM)
    steps = length // 128
    return pl.pallas_call(
        bridge_kernel,
        out_shape=[
            jax.ShapeDtypeStruct((length, width), F32), jax.ShapeDtypeStruct((2 * length, width), BF),
            jax.ShapeDtypeStruct((width, 2 * length), BF), jax.ShapeDtypeStruct((zsize, chips, strip, 2 * length), BF),
        ],
        in_specs=[hbm, hbm, vmem, vmem],
        out_specs=[hbm, hbm, hbm, hbm],
        scratch_shapes=[
            pltpu.VMEM((zsize, chips, 2, strip, length), BF), pltpu.VMEM((width, width), BF),
            pltpu.VMEM((length, width), BF), pltpu.VMEM((width, length), BF), pltpu.VMEM((length, width), F32),
            pltpu.SemaphoreType.DMA((1 + 2 * steps,)), pltpu.SemaphoreType.DMA((1 + 2 * steps,)), pltpu.SemaphoreType.DMA((6,)),
        ],
        compiler_params=pltpu.CompilerParams(collective_id=2, has_side_effects=True, vmem_limit_bytes=ALL_VMEM),
        cost_estimate=NO_COST,
        name="bridge",
    )(attended.reshape(zsize, chips, 2, strip, length), weight, x, gain)


def middle_kernel(counts, *refs):
    count = len(counts)
    hidden, low = refs[:count], refs[count:2 * count]
    weights, at = [], 2 * count
    for n in counts:
        weights.append(refs[at:at + n])
        at += n
    y_in, cot_in, gain, out_w = refs[at:at + 4]
    layer_out, middle_grad, low_t, att_grad, gain_part = refs[at + 4:at + 9]
    h_v, l_v, wi_v, wo_v, send_s, got, own, out_s, y_s, cot_s, ss, rs, ls = refs[at + 9:]
    core, other = greet_other_core()
    move = Mover(ss, rs, ls)
    tokens, chunk = hidden[0].shape
    length, width = y_in.shape
    late, loads = [], []
    for r in range(count):
        chunk_loads = []
        load = lambda src, dst: chunk_loads.append(move.local(src, dst))
        load(low[r], l_v.at[r])
        unfold(weights[r], wi_v.at[:, :, pl.ds(2 * r * chunk, 2 * chunk)], wo_v.at[r], load)
        loads.append(chunk_loads)
    inputs = [move.local(y_in, y_s), move.local(cot_in.at[pl.ds(0, 2)], cot_s)]
    for r in range(count):
        late.append(move.local(hidden[r], h_v.at[:, pl.ds(r * chunk, chunk)]))
    nt = (((1,), (1,)), ((), ()))
    tile = tokens // 4

    def out_tile(t):
        return jnp.dot(h_v[tile * t:tile * (t + 1)], wo_v[...].reshape(count * chunk, width), preferred_element_type=F32)

    targets = (own.at[pl.ds(0, tile)], own.at[pl.ds(tile, tile)], send_s.at[0], send_s.at[1])
    there = []
    for r in range(count):
        for copy in loads[r]:
            copy.wait()
        for t in (2, 3, 0, 1):
            part = lax.dot_general(
                l_v[r, tile * t:tile * (t + 1)], wi_v[:, :, 2 * r * chunk:2 * (r + 1) * chunk].reshape(width, 2 * chunk), nt,
                preferred_element_type=F32,
            )
            targets[t][...] = part if r == 0 else targets[t][...] + part
            if r == count - 1 and t >= 2:
                there.append(move.send(send_s.at[t - 2], got.at[t - 2], other))
    for copy in inputs:
        copy.wait()
    load_out = move.local(out_w, wi_v.at[:, :, pl.ds(0, width)])
    for copy in late:
        copy.wait()
    for n in range(2):
        move.settle(there[n])
        send_s[n] = out_tile(2) if n == 0 else out_tile(1) + y_s[tile:2 * tile]
        there.append(move.send(send_s.at[n], got.at[2 + n], other))
    there[0].wait_recv()
    there[1].wait_recv()
    gain_part[...] = jnp.zeros(gain_part.shape, F32)
    step = 128

    for t in range(length // step):
        part = slice(step * t, step * (t + 1))
        y = y_s[part]
        inverse = lax.rsqrt(jnp.mean(y * y, -1, keepdims=True) + EPS)
        unit = y * inverse
        d = own[part] + got[step * t // tile, step * t % tile:step * t % tile + step]
        gain_part[...] += jnp.sum(d * unit, axis=0, keepdims=True)
        scaled = d * gain[...]
        g = cot_s[step * t // tile, step * t % tile:step * t % tile + step].astype(F32)
        g = g + inverse * (scaled - unit * jnp.mean(scaled * unit, -1, keepdims=True))
        middle_grad[part] = g
        low_t[:, part] = g.T.astype(BF)
    load_out.wait()
    rows = wi_v.shape[1]
    for z in range(wi_v.shape[0]):
        att_grad[z * rows:(z + 1) * rows] = jnp.dot(wi_v[z, :, 0:width], low_t[...], preferred_element_type=F32).astype(BF)
    first, last = out_tile(0) + y_s[0:tile], out_tile(3)
    there[2].wait_recv()
    out_s[0] = (first + got[2]).astype(BF)
    there[3].wait_recv()
    out_s[1] = (last + got[3]).astype(BF)
    move.kept.append(move.local(out_s.at[0], layer_out.at[core]))
    move.kept.append(move.local(out_s.at[1], layer_out.at[1 - core]))
    move.finish()


def middle_part(hidden, low, weights, y, cot, gain, out_w, zsize, fine):
    counts = tuple(len(w) for w in weights)
    count = len(counts)
    tokens, chunk = hidden[0].shape
    length, width = y.shape
    rows = width // zsize
    hbm, vmem = pl.BlockSpec(memory_space=pltpu.HBM), pl.BlockSpec(memory_space=pltpu.VMEM)
    inputs = [*hidden, *low] + [piece for w in weights for piece in w]
    tile = tokens // 4
    return pl.pallas_call(
        functools.partial(middle_kernel, counts),
        out_shape=[
            jax.ShapeDtypeStruct((2, length // 2, width), BF), jax.ShapeDtypeStruct((length, width), F32),
            jax.ShapeDtypeStruct((width, length), BF), jax.ShapeDtypeStruct((width, length), BF),
            jax.ShapeDtypeStruct((1, width), F32),
        ],
        in_specs=[hbm] * len(inputs) + [hbm, hbm, vmem, hbm],
        out_specs=[hbm] + [vmem] * 4,
        scratch_shapes=[
            pltpu.VMEM((tokens, count * chunk), BF), pltpu.VMEM((count, tokens, 2 * chunk), BF),
            pltpu.VMEM((zsize, rows, 2 * count * chunk), BF), pltpu.VMEM((count, zsize, fine, width), BF),
            pltpu.VMEM((2, tile, width), F32), pltpu.VMEM((4, tile, width), F32),
            pltpu.VMEM((length, width), F32), pltpu.VMEM((2, tile, width), BF),
            pltpu.VMEM((length, width), F32), pltpu.VMEM((2, tile, width), BF),
            pltpu.SemaphoreType.DMA((4,)), pltpu.SemaphoreType.DMA((4,)),
            pltpu.SemaphoreType.DMA((2 * count + count * zsize * (1 + rows // fine) + 5,)),
        ],
        compiler_params=pltpu.CompilerParams(collective_id=3, has_side_effects=True, vmem_limit_bytes=ALL_VMEM),
        cost_estimate=NO_COST,
        name="middle",
    )(*inputs, y, cot, gain, out_w.reshape(zsize, rows, width))


def mm(left, right, left_dim, right_dim):
    return lax.dot_general(left, right, (((left_dim,), (right_dim,)), ((), ())), preferred_element_type=F32)


def swap(a):
    return lax.ppermute(a, "ctx", [(i, i ^ 1) for i in range(lax.axis_size("ctx"))])


def hop(a, r):
    return lax.ppermute(a, "ctx", [(i, i ^ (2 * r)) for i in range(lax.axis_size("ctx"))])


def ring(a):
    n = lax.axis_size("fsdp")
    return lax.ppermute(a, "fsdp", [(i, (i + 1) % n) for i in range(n)])


def pick(a, index, axis=0):
    return lax.dynamic_index_in_dim(a, index, axis, keepdims=False)


def place(buffer, piece, index, axis=0):
    return lax.dynamic_update_slice_in_dim(buffer, jnp.expand_dims(piece, axis), index, axis)


def shift(a, s):
    n = lax.axis_size("fsdp")
    return lax.ppermute(a, "fsdp", [(i, (i + s) % n) for i in range(n)])


def depth_gather(piece, depth):
    n = lax.axis_size("fsdp")
    buffer = place(jnp.zeros((n,) + piece.shape, piece.dtype), piece, depth)
    for s in range(1, n):
        piece = ring(piece)
        buffer = place(buffer, piece, lax.rem(depth + n - s, n))
    return buffer


def depth_scatter(parts, depth):
    n = lax.axis_size("fsdp")
    total = pick(parts, lax.rem(depth + n - 1, n))
    for s in range(n - 1):
        total = ring(total.astype(BF))
        total = total.astype(F32) + pick(parts, lax.rem(depth + 2 * n - 2 - s, n)).astype(F32)
    return total


def plane_gather(piece, index):
    n = lax.axis_size("ctx")
    chips = n // 2
    pieces = jnp.stack([piece] + [hop(piece, r) for r in range(1, chips)])
    others = swap(pieces)
    buffer = jnp.zeros((n,) + piece.shape, piece.dtype)
    for r in range(chips):
        buffer = place(buffer, pieces[r], index ^ (2 * r))
        buffer = place(buffer, others[r], index ^ (2 * r + 1))
    return buffer


def rotate(v, cosine, sine):
    heads = v.reshape(-1, 2, HEAD_WIDTH // 2, v.shape[-1])
    a, b = heads[:, 0], heads[:, 1]
    return jnp.stack([a * cosine - b * sine, b * cosine + a * sine], 1).reshape(v.shape)


def rotate_back(v, cosine, sine):
    heads = v.reshape(-1, 2, HEAD_WIDTH // 2, v.shape[-1])
    a, b = heads[:, 0], heads[:, 1]
    return jnp.stack([a * cosine + b * sine, b * cosine - a * sine], 1).reshape(v.shape)


def norm_back(incoming, unit, inverse, gain):
    scaled = incoming * gain
    return inverse * (scaled - unit * jnp.mean(scaled * unit, -1, keepdims=True))


def body(
    tokens,
    block_pairs,
    cotangent,
    attention_gain,
    query_weight,
    key_matrix,
    value_matrix,
    output_weight,
    feedforward_gain,
    gate_weight,
    up_weight,
    down_weight,
):
    slice_len, width = tokens.shape[1], tokens.shape[2]
    ctx = lax.axis_size("ctx")
    zsize = lax.axis_size("fsdp")
    chips = ctx // 2
    diag = chips - 1
    near = range(1, chips - 1)
    index = lax.axis_index("ctx")
    chip, core = index // 2, lax.rem(index, 2)
    depth = lax.axis_index("fsdp")
    rows = width // zsize
    strip = rows // ctx
    hidden_rows = down_weight.shape[0]
    fine = hidden_rows // ctx
    chunk = fine * zsize
    kv_rows = KEY_HEADS * HEAD_WIDTH

    length = 2 * slice_len

    ids_all = jnp.concatenate([pick(block_pairs, index ^ r) for r in range(ctx)])
    ids = ids_all[:4]
    blocks = ids_all.shape[0]
    order = jnp.sum(
        jnp.where(ids_all[None, :] == jnp.arange(blocks, dtype=jnp.int32)[:, None], jnp.arange(blocks, dtype=jnp.int32)[None, :], 0), 1
    )
    positions = (ids[:, None] * BLK + jnp.arange(BLK, dtype=jnp.int32)[None, :]).reshape(length)
    half = HEAD_WIDTH // 2
    frequency = THETA ** (-jnp.arange(half, dtype=F32) * 2.0 / HEAD_WIDTH)
    angles = frequency[:, None] * positions.astype(F32)[None, :]
    cosine, sine = jnp.cos(angles), jnp.sin(angles)

    packs, keys, values = {}, {}, {}
    folds = rows // fine
    fast = chips == 4 and strip % 16 == 0 and fine % 128 == 0 and pack_width(rows, fine, zsize, width) == width
    if fast:
        (key_value_full, query_full, output_full, pack, rest, pack_x, pack_y, far_pack, cot, first_half, x_low, first, query, gains_full, *kv) = front(
            tokens, cotangent, jnp.stack([attention_gain, feedforward_gain]).astype(F32), key_matrix, value_matrix, query_weight,
            output_weight, gate_weight, up_weight, down_weight, cosine, sine, zsize, ctx,
        )
        key_value_full, query_full, output_full = (w.reshape(width, width) for w in (key_value_full, query_full, output_full))
        packs[0], packs[1], packs[2] = [pack, rest], [pack_x, hop(rest, 1)], [pack_y, hop(rest, 2)]
        for r in range(chips):
            keys[r], values[r] = kv[r], kv[chips + r]
        gain_first, gain_second = gains_full[0], gains_full[1]
        packs[diag] = [far_pack] + [shift(far_pack, s) for s in range(1, zsize)]
    else:
        gate_cut = gate_weight.reshape(rows, zsize, 2, chips, fine)
        up_cut = up_weight.reshape(rows, zsize, 2, chips, fine)
        down_cut = down_weight.reshape(2, chips, fine, width)

        def own_piece(r):
            gate = pick(pick(gate_cut, core, 2), chip ^ r, 2).reshape(rows, chunk)
            up = pick(pick(up_cut, core, 2), chip ^ r, 2).reshape(rows, chunk)
            down = pick(pick(down_cut, core), chip ^ r)
            folded = jnp.transpose(down.reshape(fine, folds, width // folds), (1, 0, 2)).reshape(rows, width // folds)
            return jnp.concatenate([gate, up, folded], 1)

        gains = jnp.stack([attention_gain, feedforward_gain])
        gain_buffer = place(jnp.zeros((zsize, 2, rows), BF), gains, depth)
        for s in range(1, zsize):
            moved = lax.ppermute(gains, "fsdp", [(k, (k + s) % zsize) for k in range(zsize)])
            gain_buffer = place(gain_buffer, moved, lax.rem(depth + zsize - s, zsize))
        gains_full = jnp.transpose(gain_buffer, (1, 0, 2)).reshape(2, width).astype(F32)
        gain_first, gain_second = gains_full[0], gains_full[1]

        def gather_square(shard):
            strips = shard.reshape(ctx, strip, shard.shape[1])
            pair = jnp.stack([pick(strips, index), pick(strips, index ^ (2 * diag))])
            pair = depth_gather(pair, depth)
            own, far = pair[:, 0], pair[:, 1]
            found = {0: own, diag: far}
            for r in near:
                found[r] = hop(own, r)
            full = jnp.zeros((zsize, ctx, strip, shard.shape[1]), BF)
            for r in range(chips):
                full = place(full, found[r], index ^ (2 * r), 1)
                full = place(full, swap(found[r]), index ^ (2 * r + 1), 1)
            return full.reshape(width, shard.shape[1])

        key_value_full = gather_square(jnp.concatenate([key_matrix, value_matrix], 1))
        query_full = gather_square(query_weight)
        output_full = gather_square(output_weight)

        x = jnp.concatenate([pick(tokens, core), swap(pick(tokens, 1 - core))]).astype(F32)
        packs[0] = [depth_gather(own_piece(0), depth)]
        inverse_first = lax.rsqrt(jnp.mean(x * x, -1, keepdims=True) + EPS)
        unit_first = x * inverse_first
        first = (unit_first * gain_first).astype(BF)
        first_t = jnp.transpose(first)
        kv = mm(key_value_full, first_t, 0, 0)
        keys[0] = rotate(kv[:kv_rows], cosine, sine).astype(BF)
        values[0] = kv[kv_rows:].astype(BF)
        for r in range(1, chips):
            high = 1 << (r.bit_length() - 1)
            low = r & -r
            keys[r] = hop(keys[r ^ high], high)
            values[r] = hop(values[r ^ low], low)
        query = rotate(mm(query_full, first_t, 0, 0), cosine, sine).astype(BF)
        packs[diag] = [depth_gather(own_piece(diag), depth)]

        for r in near:
            packs[r] = [hop(packs[0][0], r)]
        cot_there = swap(cotangent)
        cot = jnp.concatenate(
            [pick(cotangent, core), pick(cot_there, core), pick(cot_there, 1 - core), pick(cotangent, 1 - core)]
        )

    key_list = [keys[r] for r in range(chips)]
    value_list = [values[r] for r in range(chips)]
    attended, log_total = attn_fwd(ids, order, query, key_list, value_list, KEY_HEADS)

    if fast:
        middle, second, second_t, att_half = bridge(attended, output_full, x_low, gain_second[None], zsize, chips)
    else:
        middle = x + mm(attended, output_full, 0, 0)
        inverse_second = lax.rsqrt(jnp.mean(middle * middle, -1, keepdims=True) + EPS)
        unit_second = middle * inverse_second
        second = (unit_second * gain_second).astype(BF)
        second = jnp.concatenate([second, swap(second)])
        second_t = jnp.transpose(second)
    grads, hidden, low = {}, {}, {}
    before = second
    for r in [0] + list(near) + [diag]:
        before, low[r], grads[r] = ffn_chunk(
            before, second, second_t, cot.reshape(2 * length, width), packs[r], fast and r == diag, LONG if r == diag else NO_COST, zsize, fine
        )
        hidden[r] = before
    every = range(chips)
    hidden, low, packs = ([a[r] for r in every] for a in (hidden, low, packs))

    if fast:
        layer_out, middle_grad, middle_t, attended_grad, gain_second_part = middle_part(
            hidden, low, packs, middle, cot, gain_second[None], output_full, zsize, fine
        )
    else:
        out_part, second_grad = combine(hidden, low, packs, zsize, fine)

        q = slice_len
        out_part = jnp.concatenate([out_part[:length] + middle, out_part[length:]])
        came = swap(jnp.concatenate([out_part[2 * q:3 * q], out_part[q:2 * q]]))
        out_here = (out_part[:q] + came[:q]).astype(BF)
        out_there = (out_part[3 * q:] + came[q:]).astype(BF)

        def stored(here, there):
            return jnp.where(core == 0, jnp.stack([here, there]), jnp.stack([there, here]))

        layer_out = stored(out_here, out_there)

        second_grad = second_grad[:length] + swap(second_grad[length:])
        gain_second_part = jnp.sum(second_grad * unit_second, 0)
        middle_grad = cot[:length].astype(F32) + norm_back(second_grad, unit_second, inverse_second, gain_second)

        def halves(a):
            cut = a.reshape(zsize, chips, 2, strip, length)
            here = pick(cut, core, 2).reshape(-1, length)
            there = swap(pick(cut, 1 - core, 2).reshape(-1, length))
            return jnp.concatenate([here, there], 1)

        first_half = halves(first_t)
        middle_low = middle_grad.astype(BF)
        out_part_grad = mm(halves(attended), jnp.concatenate([middle_low, swap(middle_low)]), 1, 0)
        attended_grad = mm(output_full, middle_low, 1, 1).astype(BF)

    far_sum = middle_grad
    if fast:
        far_sum = grads[diag][zsize - 1]
        for s in range(zsize - 2, 0, -1):
            far_moved = shift(far_sum, 1)
            if s > 1:
                share, middle_t = lax.optimization_barrier((grads[diag][s], middle_t))
                far_sum = (far_moved.astype(F32) + share.astype(F32)).astype(BF)

    query_low, key_parts, value_parts = attn_bwd(
        far_sum, ids, order, query, attended, attended_grad, log_total, cosine, sine, key_list, value_list, KEY_HEADS
    )
    if fast:
        o_all, q_all, kv_all, pack_all, tokens_grad, gain_sums = tail(
            key_parts, value_parts, query_low, cosine, sine, first_half,
            att_half,
            [grads[0][0], hop(grads[1][0], 1), hop(grads[2][0], 2)],
            [far_moved, grads[diag][1], grads[diag][0]],
            middle_t, query_full, key_value_full, x_low, middle_grad, gain_first[None], gain_second_part, zsize, chips,
        )
        gain_first_grad, gain_second_grad = (
            lax.dynamic_slice_in_dim(gain_sums[n], depth * rows, rows) for n in range(2)
        )
        gate_grad, up_grad, down_grad, output_grad, query_grad, key_grad, value_grad = assemble(
            pack_all, *(a.reshape(rows, width) for a in (o_all, q_all, kv_all)), zsize, fine
        )
    else:
        key_sum = [part for part in key_parts]
        value_sum = [part for part in value_parts]
        for r in range(chips - 1, 0, -1):
            high = 1 << (r.bit_length() - 1)
            low = r & -r
            key_sum[r ^ high] = key_sum[r ^ high].astype(F32) + hop(key_sum[r].astype(BF), high).astype(F32)
            value_sum[r ^ low] = value_sum[r ^ low].astype(F32) + hop(value_sum[r].astype(BF), low).astype(F32)
        key_low = rotate_back(key_sum[0], cosine, sine).astype(BF)
        value_low = value_sum[0].astype(BF)
        kv_low = jnp.concatenate([key_low, value_low])

        def scatter(parts):
            total = parts[0].astype(F32)
            for r in near:
                total = total + hop(parts[r], r).astype(F32)
            far = hop(depth_scatter(parts[diag], depth).astype(BF), diag)
            total = depth_scatter(total.astype(BF), depth) + far.astype(F32)
            return total.astype(BF)

        pack_all = plane_gather(scatter({r: grads[r][0] for r in range(chips)}), index)
        wide_all = pack_all[:, :, :2 * chunk]
        tall_all = jnp.transpose(pack_all[:, :, 2 * chunk:].reshape(ctx, folds, fine, width // folds), (0, 2, 1, 3))
        def square_grad(product):
            parts = product.astype(BF).reshape(zsize, chips, strip, width)
            piece = scatter({r: pick(parts, chip ^ r, 1) for r in range(chips)})
            return plane_gather(piece, index).reshape(rows, width).astype(F32)

        output_grad = square_grad(out_part_grad)
        query_grad = square_grad(mm(first_half, jnp.concatenate([query_low, swap(query_low)], 1), 1, 1))
        kv_grad = square_grad(mm(first_half, jnp.concatenate([kv_low, swap(kv_low)], 1), 1, 1))
        down_grad = jnp.transpose(tall_all.reshape(chips, 2, fine, width), (1, 0, 2, 3)).reshape(hidden_rows, width).astype(F32)
        wide_all = wide_all.reshape(chips, 2, rows, 2, zsize, fine)
        gate_grad = jnp.transpose(wide_all[:, :, :, 0], (2, 3, 1, 0, 4)).reshape(rows, -1).astype(F32)
        up_grad = jnp.transpose(wide_all[:, :, :, 1], (2, 3, 1, 0, 4)).reshape(rows, -1).astype(F32)
        key_grad, value_grad = kv_grad[:, :kv_rows], kv_grad[:, kv_rows:]

        def gain_total(part):
            cut = part.reshape(zsize, rows)
            total = pick(cut, depth)
            for s in range(1, zsize):
                total = total + lax.ppermute(
                    pick(cut, lax.rem(depth + s, zsize)), "fsdp", [(k, (k + s) % zsize) for k in range(zsize)]
                )
            total = total + swap(total)
            bit = 1
            while bit < chips:
                total = total + hop(total, bit)
                bit *= 2
            return total

        first_grad = mm(query_low, query_full, 0, 1) + mm(kv_low, key_value_full, 0, 1)
        gain_first_part = jnp.sum(first_grad * unit_first, 0)
        tokens_part = (middle_grad + norm_back(first_grad, unit_first, inverse_first, gain_first)).astype(BF)
        tokens_grad = stored(tokens_part[:q], swap(tokens_part[q:]))
        gain_first_grad, gain_second_grad = gain_total(gain_first_part), gain_total(gain_second_part)

    return (
        layer_out,
        tokens_grad,
        gain_first_grad,
        query_grad,
        key_grad,
        value_grad,
        output_grad,
        gain_second_grad,
        gate_grad,
        up_grad,
        down_grad,
    )


def solution(mesh):
    line, square, grid = P("fsdp"), P("fsdp", None), P("fsdp", "ctx", None)
    in_specs = (grid, P(), grid, line, square, square, square, square, line, square, square, square)
    out_specs = (grid, grid, line, square, square, square, square, line, square, square, square)
    return jax.shard_map(body, mesh=mesh, in_specs=in_specs, out_specs=out_specs, check_vma=False)
```

```python
import functools

import jax
import jax.numpy as jnp
from jax import lax
from jax.experimental import pallas as pl
from jax.experimental.pallas import tpu as pltpu
from jax.sharding import PartitionSpec as P

QUERY_HEADS = 16
KEY_HEADS = 8
HEAD_WIDTH = 96
EPS = 1e-05
THETA = 100000.0
BLK = 128
SCALE = HEAD_WIDTH ** -0.5
BF = jnp.bfloat16
F32 = jnp.float32
NO_COST = pl.CostEstimate(flops=0, bytes_accessed=0, transcendentals=0)
LONG = pl.CostEstimate(flops=52 * 10**9, bytes_accessed=0, transcendentals=0)
ALL_VMEM = 62 * 2**20

LOG2E = 1.4426950408889634
NT = (((1,), (1,)), ((), ()))


def block_tasks(ids_ref, inv_ref, slices, t):
    tasks = []
    for sl in range(slices):
        first = ids_ref[2 * sl]
        late = (t > first).astype(jnp.int32)
        kpos = t - late * (first + 1)
        tasks.append((sl, late, inv_ref[kpos], (ids_ref[2 * sl + late] - kpos) * BLK))
    return tasks


def causal_difference():
    return lax.broadcasted_iota(jnp.int32, (BLK, 2 * BLK), 0) - lax.rem(lax.broadcasted_iota(jnp.int32, (BLK, 2 * BLK), 1), BLK)


def load_keys(refs, scratch, sem):
    copies = [pltpu.make_async_copy(ref, scratch.at[n], sem.at[n]) for n, ref in enumerate(refs)]

    @pl.when(pl.program_id(0) == 0)
    def _():
        for copy in copies:
            copy.start()
        for copy in copies:
            copy.wait()


def fwd_kernel(nchip, heads, ids_ref, inv_ref, q_ref, *rest):
    o_ref, lse_ref, kv_s, sem, knat, vtr = rest[2 * nchip:2 * nchip + 6]
    state = rest[2 * nchip + 6:]
    load_keys(rest[:2 * nchip], kv_s, sem)
    base = pl.program_id(0) * (96 * heads)
    nq = q_ref.shape[1] // BLK
    slices = nq // 2
    nb = nchip * nq
    c = SCALE * LOG2E
    chains = [(h, sl) for h in range(heads) for sl in range(slices)]
    qs, m_s, l_s, acc = ({chain: state[4 * n + k] for n, chain in enumerate(chains)} for k in range(4))
    for h in range(heads):
        for n in range(nb):
            r, lanes = n // nq, slice(BLK * (n % nq), BLK * (n % nq + 1))
            part = pl.ds(pl.multiple_of(base + 96 * h, 96), 96)
            knat[h, n] = kv_s[r, part, lanes].T
            vtr[h, n] = kv_s[nchip + r, part, lanes]
        for sl in range(slices):
            for half in range(2):
                lanes = slice(BLK * (2 * sl + half), BLK * (2 * sl + half + 1))
                qs[h, sl][half] = jnp.concatenate([q_ref[192 * h:192 * h + 96, lanes], q_ref[192 * h + 96:192 * h + 192, lanes]], axis=1)
            m_s[h, sl][...] = jnp.full((2, 1, 2 * BLK), -1e30, F32)
            l_s[h, sl][...] = jnp.zeros((2, 1, 2 * BLK), F32)
            acc[h, sl][...] = jnp.zeros((2, 96, 2 * BLK), F32)
    diff = causal_difference()

    def step(t, _):
        tasks = block_tasks(ids_ref, inv_ref, slices, t)
        todo = [(h, *task) for h in range(heads) for task in tasks]
        scores = [
            jnp.where(diff <= offset, jnp.dot(knat[h, n], qs[h, sl][late], preferred_element_type=F32), -jnp.inf)
            for h, sl, late, n, offset in todo
        ]
        old = [(m_s[h, sl][late], l_s[h, sl][late], acc[h, sl][late]) for h, sl, late, n, offset in todo]
        peaks = [jnp.maximum(m, jnp.max(s, axis=0, keepdims=True)) for s, (m, _l, _a) in zip(scores, old)]
        weights = [jnp.exp2((s - peak) * c) for s, peak in zip(scores, peaks)]
        shrink = [jnp.exp2((m - peak) * c) for peak, (m, _l, _a) in zip(peaks, old)]
        totals = [l * a + jnp.sum(p, axis=0, keepdims=True) for (_m, l, _a), a, p in zip(old, shrink, weights)]
        mixed = [
            o * a + jnp.dot(vtr[h, n], p.astype(BF), preferred_element_type=F32)
            for (h, sl, late, n, offset), (_m, _l, o), a, p in zip(todo, old, shrink, weights)
        ]
        for (h, sl, late, n, offset), peak, total, o in zip(todo, peaks, totals, mixed):
            m_s[h, sl][late] = peak
            l_s[h, sl][late] = total
            acc[h, sl][late] = o
        return 0

    lax.fori_loop(0, nb + 1, step, 0, unroll=2)
    for h, sl in chains:
        for half in range(2):
            lanes = slice(BLK * (2 * sl + half), BLK * (2 * sl + half + 1))
            l = l_s[h, sl][half]
            o = acc[h, sl][half] / l
            lse_ref[h, 2 * sl + half] = m_s[h, sl][half] * c + jnp.log2(l)
            o_ref[192 * h:192 * h + 96, lanes] = o[:, :BLK].astype(BF)
            o_ref[192 * h + 96:192 * h + 192, lanes] = o[:, BLK:].astype(BF)


def attn_fwd(ids, inv, qT, ks, vs, heads):
    nchip = len(ks)
    T = qT.shape[1]
    nq = T // BLK
    nb = nchip * nq
    per = 4 if nb <= 16 else 2
    wide = pl.BlockSpec((192 * per, T), lambda g, *_: (g, 0))
    slim = pl.BlockSpec((96 * per, T), lambda g, *_: (g, 0))
    chain = [
        pltpu.VMEM((2, 96, 2 * BLK), BF),
        pltpu.VMEM((2, 1, 2 * BLK), F32),
        pltpu.VMEM((2, 1, 2 * BLK), F32),
        pltpu.VMEM((2, 96, 2 * BLK), F32),
    ]
    grid_spec = pltpu.PrefetchScalarGridSpec(
        num_scalar_prefetch=2,
        grid=(heads // per,),
        in_specs=[wide] + [pl.BlockSpec(memory_space=pltpu.HBM)] * (2 * nchip),
        out_specs=[wide, pl.BlockSpec((per, nq, 1, 2 * BLK), lambda g, *_: (g, 0, 0, 0))],
        scratch_shapes=[
            pltpu.VMEM((2 * nchip, heads * 96, T), BF), pltpu.SemaphoreType.DMA((2 * nchip,)),
            pltpu.VMEM((per, nb, BLK, 96), BF), pltpu.VMEM((per, nb, 96, BLK), BF),
        ] + chain * (per * nq // 2),
    )
    return pl.pallas_call(
        functools.partial(fwd_kernel, nchip, per),
        grid_spec=grid_spec,
        out_shape=[jax.ShapeDtypeStruct((heads * 192, T), BF), jax.ShapeDtypeStruct((heads, nq, 1, 2 * BLK), F32)],
        cost_estimate=NO_COST,
        compiler_params=pltpu.CompilerParams(vmem_limit_bytes=ALL_VMEM),
        name="attention_forward",
    )(ids, inv, qT, *ks, *vs)


def bwd_kernel(nchip, heads, ids_ref, inv_ref, q_ref, o_ref, do_ref, lse_ref, cos_ref, sin_ref, before, *rest):
    dq_ref = rest[2 * nchip]
    dk_refs, dv_refs = rest[2 * nchip + 1:3 * nchip + 1], rest[3 * nchip + 1:4 * nchip + 1]
    kv_s, sem, knat, ktr, vnat = rest[4 * nchip + 1:4 * nchip + 6]
    state = rest[4 * nchip + 6:]
    load_keys(rest[:2 * nchip], kv_s, sem)
    base = pl.program_id(0) * (96 * heads)
    nq = q_ref.shape[1] // BLK
    slices = nq // 2
    nb = nchip * nq
    c = SCALE * LOG2E
    chains = [(h, sl) for h in range(heads) for sl in range(slices)]
    qs, dos, stat, dq_s, dk_s, dv_s = ({chain: state[6 * n + k] for n, chain in enumerate(chains)} for k in range(6))
    for h in range(heads):
        for n in range(nb):
            r, lanes = n // nq, slice(BLK * (n % nq), BLK * (n % nq + 1))
            part = pl.ds(pl.multiple_of(base + 96 * h, 96), 96)
            block = kv_s[r, part, lanes]
            knat[h, n] = block.T
            ktr[h, n] = block
            vnat[h, n] = kv_s[nchip + r, part, lanes].T
    for h, sl in chains:
        for half in range(2):
            lanes = slice(BLK * (2 * sl + half), BLK * (2 * sl + half + 1))
            pair = lambda ref: jnp.concatenate([ref[192 * h:192 * h + 96, lanes], ref[192 * h + 96:192 * h + 192, lanes]], axis=1)
            do = pair(do_ref)
            qs[h, sl][half] = pair(q_ref)
            dos[h, sl][half] = do
            stat[h, sl][half, 0:1] = lse_ref[h, 2 * sl + half]
            stat[h, sl][half, 1:2] = jnp.sum(pair(o_ref).astype(F32) * do.astype(F32), axis=0, keepdims=True)
        dq_s[h, sl][...] = jnp.zeros((2, 96, 2 * BLK), F32)
        dk_s[h, sl][...] = jnp.zeros((nb, 96, BLK), F32)
        dv_s[h, sl][...] = jnp.zeros((nb, 96, BLK), F32)
    diff = causal_difference()

    def step(t, _):
        tasks = block_tasks(ids_ref, inv_ref, slices, t)
        todo = [(h, *task) for h in range(heads) for task in tasks]
        q = [qs[h, sl][late] for h, sl, late, n, offset in todo]
        do = [dos[h, sl][late] for h, sl, late, n, offset in todo]
        scores = [jnp.dot(knat[h, n], x, preferred_element_type=F32) for (h, sl, late, n, offset), x in zip(todo, q)]
        grads = [jnp.dot(vnat[h, n], x, preferred_element_type=F32) for (h, sl, late, n, offset), x in zip(todo, do)]
        weights = [
            jnp.exp2(jnp.where(diff <= offset, s * c - stat[h, sl][late, 0:1], -jnp.inf))
            for (h, sl, late, n, offset), s in zip(todo, scores)
        ]
        low = [(p * (g - stat[h, sl][late, 1:2])).astype(BF) for (h, sl, late, n, offset), p, g in zip(todo, weights, grads)]
        dv = [lax.dot_general(x, p.astype(BF), NT, preferred_element_type=F32) for x, p in zip(do, weights)]
        dk = [lax.dot_general(x, ds, NT, preferred_element_type=F32) for x, ds in zip(q, low)]
        dq = [jnp.dot(ktr[h, n], ds, preferred_element_type=F32) for (h, sl, late, n, offset), ds in zip(todo, low)]
        for (h, sl, late, n, offset), a, b, d in zip(todo, dv, dk, dq):
            dv_s[h, sl][n] += a
            dk_s[h, sl][n] += b
            dq_s[h, sl][late] += d
        return 0

    lax.fori_loop(0, nb + 1, step, 0, unroll=2)
    for h, sl in chains:
        for half in range(2):
            lanes = slice(BLK * (2 * sl + half), BLK * (2 * sl + half + 1))
            cos, sin = cos_ref[:, lanes], sin_ref[:, lanes]
            for e in range(2):
                a = dq_s[h, sl][half, 0:48, BLK * e:BLK * (e + 1)] * SCALE
                b = dq_s[h, sl][half, 48:96, BLK * e:BLK * (e + 1)] * SCALE
                at = 192 * h + 96 * e
                dq_ref[at:at + 48, lanes] = (a * cos + b * sin).astype(BF)
                dq_ref[at + 48:at + 96, lanes] = (b * cos - a * sin).astype(BF)
    for h in range(heads):
        for n in range(nb):
            r, lanes = n // nq, slice(BLK * (n % nq), BLK * (n % nq + 1))
            dk = sum(dk_s[h, sl][n] for sl in range(slices))
            dv = sum(dv_s[h, sl][n] for sl in range(slices))
            dk_refs[r][96 * h:96 * (h + 1), lanes] = (dk * SCALE).astype(BF)
            dv_refs[r][96 * h:96 * (h + 1), lanes] = dv.astype(BF)


def attn_bwd(before, ids, inv, qT, oT, doT, lse, cosine, sine, ks, vs, heads):
    nchip = len(ks)
    T = qT.shape[1]
    nq = T // BLK
    nb = nchip * nq
    per = 4 if nb <= 16 else 2
    wide = pl.BlockSpec((192 * per, T), lambda g, *_: (g, 0))
    slim = pl.BlockSpec((96 * per, T), lambda g, *_: (g, 0))
    chain = [
        pltpu.VMEM((2, 96, 2 * BLK), BF),
        pltpu.VMEM((2, 96, 2 * BLK), BF),
        pltpu.VMEM((2, 2, 2 * BLK), F32),
        pltpu.VMEM((2, 96, 2 * BLK), F32),
        pltpu.VMEM((nb, 96, BLK), F32),
        pltpu.VMEM((nb, 96, BLK), F32),
    ]
    grid_spec = pltpu.PrefetchScalarGridSpec(
        num_scalar_prefetch=2,
        grid=(heads // per,),
        in_specs=[wide, wide, wide, pl.BlockSpec((per, nq, 1, 2 * BLK), lambda g, *_: (g, 0, 0, 0))]
        + [pl.BlockSpec((48, T), lambda g, *_: (0, 0))] * 2 + [pl.BlockSpec(memory_space=pltpu.HBM)] * (1 + 2 * nchip),
        out_specs=[wide] + [slim] * (2 * nchip),
        scratch_shapes=[
            pltpu.VMEM((2 * nchip, heads * 96, T), BF), pltpu.SemaphoreType.DMA((2 * nchip,)),
            pltpu.VMEM((per, nb, BLK, 96), BF), pltpu.VMEM((per, nb, 96, BLK), BF), pltpu.VMEM((per, nb, BLK, 96), BF),
        ]
        + chain * (per * nq // 2),
    )
    slab = jax.ShapeDtypeStruct((heads * 96, T), BF)
    outs = pl.pallas_call(
        functools.partial(bwd_kernel, nchip, per),
        grid_spec=grid_spec,
        out_shape=[jax.ShapeDtypeStruct((heads * 192, T), BF)] + [slab] * (2 * nchip),
        cost_estimate=NO_COST,
        compiler_params=pltpu.CompilerParams(vmem_limit_bytes=ALL_VMEM),
        name="attention_backward",
    )(ids, inv, qT, oT, doT, lse, cosine, sine, before, *ks, *vs)
    return outs[0], outs[1:1 + nchip], outs[1 + nchip:]


def pack_width(rows, fine, zsize, width):
    return 2 * fine * zsize + width * fine // rows


def front_kernel(zsize, *refs):
    (tok, cot_in, gains, key_w, value_w, query_w, out_w, gate_w, up_w, down_w, cos, sin) = refs[:12]
    (kv_all, q_all, o_all, pack, rest, pack_x, pack_y, far_pack, cot, first_half, x_out, first, q_out, gains_out) = refs[12:26]
    (k0, k1, k2, k3, v0, v1, v2, v3) = refs[26:34]
    x_s, gain_s, full_kv, full_q, full_o, kv_s, first_s, pack_s, cot_s, ss, rs, ls, gs, gr = refs[34:]
    ks, vs = (k0, k1, k2, k3), (v0, v1, v2, v3)
    index, depth = lax.axis_index("ctx"), lax.axis_index("fsdp")
    chip, core = index // 2, lax.rem(index, 2)
    fine = down_w.shape[0] // 8
    chunk = fine * zsize
    folds = pack.shape[0] // fine
    fold = first.shape[1] // folds
    width = first.shape[1]
    length = first.shape[0]
    kv_rows = k0.shape[0]
    nxt, prv = lax.rem(depth + 1, zsize), lax.rem(depth + zsize - 1, zsize)
    to_next, to_prev = (index, nxt), (index, prv)
    chip_x, chip_y, chip_d = chip + 1 - 2 * lax.rem(chip, 2), lax.rem(chip + 2, 4), 3 - chip
    to_x, to_y, to_core = (chip_x * 2 + core, depth), (chip_y * 2 + core, depth), (chip * 2 + 1 - core, depth)

    barrier = pltpu.get_barrier_semaphore()
    for target in (to_next, to_prev, to_x, to_y, to_core):
        pl.semaphore_signal(barrier, inc=1, device_id=target, device_id_type=pl.DeviceIdType.MESH)
    pl.semaphore_wait(barrier, 5)

    count = [0, 0]
    sent = []

    def send(src, dst, target):
        k = count[0]
        count[0] += 1
        copy = pltpu.make_async_remote_copy(
            src_ref=src, dst_ref=dst, send_sem=ss.at[k], recv_sem=rs.at[k], device_id=target, device_id_type=pl.DeviceIdType.MESH
        )
        copy.start()
        sent.append(copy)
        return copy

    def local(src, dst):
        k = count[1]
        count[1] += 1
        copy = pltpu.make_async_copy(src, dst, ls.at[k])
        copy.start()
        return copy

    def slot(s):
        return lax.rem(depth + zsize - s, zsize)

    steps = range(1, zsize)
    last = zsize - 1
    tokens_there = send(tok.at[1 - core], x_s.at[1], to_core)
    own_kv = [local(key_w, full_kv.at[depth, :, :, :, pl.ds(0, kv_rows)]), local(value_w, full_kv.at[depth, :, :, :, pl.ds(kv_rows, kv_rows)])]
    gain_s[depth] = gains[...]

    weights = {"kv": full_kv, "q": full_q, "o": full_o}
    shards = {"q": query_w, "o": out_w}
    moves = {}

    def ring_step(name, s):
        full = weights[name]
        place = full.at[slot(s - 1), chip, core]
        if name == "kv" and s == 1:
            halves = ((key_w, pl.ds(0, kv_rows)), (value_w, pl.ds(kv_rows, kv_rows)))
            moves[name, "ring", s] = [send(ref.at[chip, core], full.at[slot(0), chip, core, :, cols], to_next) for ref, cols in halves]
        else:
            source = shards[name].at[chip, core] if name in shards and s == 1 else place
            moves[name, "ring", s] = [send(source, place, to_next)]

    def spread(name, s):
        place = weights[name].at[slot(s), chip, core]
        moves[name, "x", s] = send(place, place, to_x)
        moves[name, "y", s] = send(place, place, to_y)

    def forward(name, s):
        mid = width // 2
        moves[name, "x", s].wait_recv()
        left = weights[name].at[slot(s), chip_x, core, :, pl.ds(0, mid)]
        moves[name, "fy", s] = send(left, left, to_y)
        moves[name, "y", s].wait_recv()
        right = weights[name].at[slot(s), chip_y, core, :, pl.ds(mid, mid)]
        moves[name, "fx", s] = send(right, right, to_x)

    def cross(name, s):
        moves[name, "fx", s].wait_recv()
        moves[name, "fy", s].wait_recv()
        column = weights[name].at[slot(s), :, core]
        moves[name, "core", s] = send(column, column, to_core)

    def gain_step(s):
        place = gain_s.at[slot(s - 1)]
        copy = pltpu.make_async_remote_copy(
            src_ref=place, dst_ref=place, send_sem=gs.at[s], recv_sem=gr.at[s], device_id=to_next, device_id_type=pl.DeviceIdType.MESH
        )
        copy.start()
        sent.append(copy)
        moves["gain", s] = copy

    def ffn_step(s):
        moves["ffn", s] = send(pack_s.at[0] if s == 1 else rest.at[s - 2], rest.at[s - 1], to_next)

    ring_step("kv", 1)
    gain_step(1)
    own_late = [local(query_w, full_q.at[depth]), local(out_w, full_o.at[depth])]
    def cut_pack(which, target):
        copies = []
        for part in range(zsize):
            column = pl.multiple_of(part * (8 * fine) + core * (4 * fine) + which * fine, fine)
            copies.append(local(gate_w.at[:, pl.ds(column, fine)], target.at[:, pl.ds(part * fine, fine)]))
            copies.append(local(up_w.at[:, pl.ds(column, fine)], target.at[:, pl.ds(chunk + part * fine, fine)]))
        row = pl.multiple_of(core * (4 * fine) + which * fine, fine)
        for n in range(folds):
            copies.append(local(down_w.at[pl.ds(row, fine), pl.ds(n * fold, fold)], target.at[pl.ds(n * fine, fine), pl.ds(2 * chunk, fold)]))
        return copies

    own_ffn = cut_pack(chip, pack_s.at[0])
    far_ffn = cut_pack(chip_d, pack_s.at[1]) + cut_pack(chip_x, pack_s.at[2]) + cut_pack(chip_y, pack_s.at[3])
    far_ffn += [local(cot_in.at[core], cot_s.at[0]), local(cot_in.at[1 - core], cot_s.at[1])]
    cot_moves = [send(cot_in.at[1 - core], cot.at[1], to_core), send(cot_in.at[core], cot.at[2], to_core)]

    def around(name, s):
        for copy in moves[name, "ring", s]:
            copy.wait_recv()
        if s < last:
            ring_step(name, s + 1)

    ring_step("q", 1)
    ring_step("o", 1)
    for s in steps:
        moves["gain", s].wait_recv()
        if s < last:
            gain_step(s + 1)
        around("kv", s)
        spread("kv", s)
        around("q", s)
        around("o", s)
    for copy in own_ffn:
        copy.wait()
    ffn_step(1)
    for s in steps:
        forward("kv", s)
    for s in steps:
        spread("q", s)
    for s in steps:
        cross("kv", s)

    tokens_there.wait_recv()
    x_out[0:length // 2] = tok[core]
    x_out[length // 2:] = x_s[1]
    gain_rows = [gain_s[place] for place in range(zsize)]
    gains_full = jnp.concatenate(gain_rows, axis=1)
    gains_out[...] = gains_full
    gain = gains_full[0:1]
    rows = 64

    def normalize(t, _):
        part = pl.ds(pl.multiple_of(t * rows, rows), rows)
        v = x_out[part].astype(F32)
        inverse = lax.rsqrt(jnp.mean(v * v, -1, keepdims=True) + EPS)
        first[part] = (v * inverse * gain).astype(BF)
        return 0

    lax.fori_loop(0, length // rows, normalize, 0)

    for s in steps:
        spread("o", s)
    for s in steps:
        moves["kv", "core", s].wait_recv()
    for copy in own_kv:
        copy.wait()
    keep = [local(full_kv, kv_all)]
    tile = 384

    def project(weight, t, turn):
        cols = pl.ds(pl.multiple_of(t * tile, tile), tile)
        w = weight[:, :, :, :, cols].reshape(width, tile)
        r = jnp.dot(first[...], w, preferred_element_type=F32).T
        if turn:
            r = rotate(r, cos[...], sin[...])
        return r.astype(BF)

    def project_kv(t, turn):
        kv_s[pl.ds(pl.multiple_of(t * tile, tile), tile)] = project(full_kv, t, turn)
        return 0

    per = kv_rows // tile
    lax.fori_loop(0, per, lambda t, _: project_kv(t, True), 0)
    k_here, v_here = kv_s.at[pl.ds(0, kv_rows)], kv_s.at[pl.ds(kv_rows, kv_rows)]
    k_x, k_y = send(k_here, k1, to_x), send(k_here, k2, to_y)
    lax.fori_loop(per, 2 * per, lambda t, _: project_kv(t, False), 0)
    v_y, v_x = send(v_here, v2, to_y), send(v_here, v1, to_x)
    if last > 1:
        moves["ffn", 1].wait_recv()
        ffn_step(2)
    for s in steps:
        forward("q", s)
    keep += [local(k_here, k0), local(v_here, v0)]
    for copy in far_ffn:
        copy.wait()
    keep += [local(pack_s.at[n], out) for n, out in enumerate((pack, far_pack, pack_x, pack_y))]
    keep += [local(cot_s.at[0], cot.at[0]), local(cot_s.at[1], cot.at[3])]
    for z in range(zsize):
        strips = first[:, z * tile:(z + 1) * tile].astype(F32).T.astype(BF)
        first_s[z] = strips.reshape(4, 2, strips.shape[0] // 8, length)
    keep.append(local(first_s.at[:, :, core], first_half.at[:, :, :, pl.ds(0, length)]))
    half_move = send(first_s.at[:, :, 1 - core], first_half.at[:, :, :, pl.ds(length, length)], to_core)
    for s in steps:
        cross("q", s)
    for s in steps:
        forward("o", s)
    for s in range(2, last):
        moves["ffn", s].wait_recv()
        ffn_step(s + 1)
    k_x.wait_recv()
    k_d = send(k1, k3, to_y)
    v_y.wait_recv()
    v_d = send(v2, v3, to_x)
    for s in steps:
        moves["q", "core", s].wait_recv()
    for copy in own_late:
        copy.wait()
    keep.append(local(full_q, q_all))

    def project_q(t, _):
        q_out[pl.ds(pl.multiple_of(t * tile, tile), tile)] = project(full_q, t, True)
        return 0

    lax.fori_loop(0, width // tile, project_q, 0)
    for s in steps:
        cross("o", s)
    for s in steps:
        moves["o", "core", s].wait_recv()
    keep.append(local(full_o, o_all))
    moves["ffn", last].wait_recv()
    for copy in (k_y, v_x, k_d, v_d, half_move, *cot_moves):
        copy.wait_recv()
    for copy in keep:
        copy.wait()
    for copy in sent:
        copy.wait_send()


def front(tokens, cotangent, gains, key_w, value_w, query_w, out_w, gate_w, up_w, down_w, cosine, sine, zsize, ctx):
    width = tokens.shape[2]
    length = 2 * tokens.shape[1]
    rows = width // zsize
    strip = rows // ctx
    fine = down_w.shape[0] // ctx
    packed = pack_width(rows, fine, zsize, width)
    kv_rows = key_w.shape[1]
    chips = ctx // 2
    cut = lambda w: w.reshape(chips, 2, strip, w.shape[1])
    square = jax.ShapeDtypeStruct((zsize, chips, 2, strip, width), BF)
    flat = jax.ShapeDtypeStruct((kv_rows, length), BF)
    hbm, vmem = pl.BlockSpec(memory_space=pltpu.HBM), pl.BlockSpec(memory_space=pltpu.VMEM)
    copies = 19 * (zsize - 1) + 13
    return pl.pallas_call(
        functools.partial(front_kernel, zsize),
        out_shape=[
            square, square, square,
            jax.ShapeDtypeStruct((rows, packed), BF),
            jax.ShapeDtypeStruct((zsize - 1, rows, packed), BF),
            jax.ShapeDtypeStruct((rows, packed), BF),
            jax.ShapeDtypeStruct((rows, packed), BF),
            jax.ShapeDtypeStruct((rows, packed), BF),
            jax.ShapeDtypeStruct((4, length // 2, width), BF),
            jax.ShapeDtypeStruct((zsize, chips, strip, 2 * length), BF),
            jax.ShapeDtypeStruct((length, width), BF),
            jax.ShapeDtypeStruct((length, width), BF),
            jax.ShapeDtypeStruct((width, length), BF),
            jax.ShapeDtypeStruct((2, width), F32),
        ] + [flat] * 8,
        in_specs=[vmem, hbm, vmem] + [hbm] * 7 + [vmem] * 2,
        out_specs=[hbm] * 10 + [vmem] * 4 + [hbm] * 8,
        scratch_shapes=[
            pltpu.VMEM((2, length // 2, width), BF),
            pltpu.VMEM((zsize, 2, rows), F32),
            pltpu.VMEM(square.shape, BF),
            pltpu.VMEM(square.shape, BF),
            pltpu.VMEM(square.shape, BF),
            pltpu.VMEM((2 * kv_rows, length), BF),
            pltpu.VMEM((zsize, chips, 2, strip, length), BF),
            pltpu.VMEM((4, rows, packed), BF),
            pltpu.VMEM((2, length // 2, width), BF),
            pltpu.SemaphoreType.DMA((copies,)),
            pltpu.SemaphoreType.DMA((copies,)),
            pltpu.SemaphoreType.DMA((20 + 8 * zsize + 4 * (rows // fine),)),
            pltpu.SemaphoreType.DMA((zsize,)),
            pltpu.SemaphoreType.DMA((zsize,)),
        ],
        compiler_params=pltpu.CompilerParams(collective_id=0, has_side_effects=True, vmem_limit_bytes=ALL_VMEM),
        name="front",
    )(tokens, cotangent, gains, cut(key_w), cut(value_w), cut(query_w), cut(out_w), gate_w, up_w, down_w, cosine, sine)


def tail_kernel(zsize, *refs):
    dk, dv = refs[0:4], refs[4:8]
    dq, cos, sin, first_half, att_half = refs[8:13]
    pack_in, far_in = refs[13:16], refs[16:19]
    mid_t, query_w, kv_w, x_in, middle, gain, second_part = refs[19:26]
    rest = refs[26:]
    o_all, q_all, kv_all, pack_all, tokens_out, gains_out = rest[:6]
    (got, held, dq_pair, kv_pair, half, grads, gl, gr, gx, gy, gz, piece,
     pack_s, pack_0, pack_z, far_s, far_r, pack_p, first_grad, tokens_s, gain_s, gain_r, ss, rs, ls) = rest[6:]
    index, depth = lax.axis_index("ctx"), lax.axis_index("fsdp")
    chip, core = index // 2, lax.rem(index, 2)
    chip_x, chip_y, chip_d = chip + 1 - 2 * lax.rem(chip, 2), lax.rem(chip + 2, 4), 3 - chip
    nxt, prv = lax.rem(depth + 1, zsize), lax.rem(depth + zsize - 1, zsize)
    to_next, to_prev = (index, nxt), (index, prv)
    to_x, to_y, to_core = (chip_x * 2 + core, depth), (chip_y * 2 + core, depth), (chip * 2 + 1 - core, depth)
    to_far = (chip_d * 2 + core, depth)
    last = zsize - 1
    kv_rows = dk[0].shape[0]
    width = kv_w.shape[2]
    strip = piece.shape[1]
    length = dq.shape[1]

    barrier = pltpu.get_barrier_semaphore()
    for target in (to_next, to_prev, to_x, to_y, to_core, to_far):
        pl.semaphore_signal(barrier, inc=1, device_id=target, device_id_type=pl.DeviceIdType.MESH)
    pl.semaphore_wait(barrier, 6)

    count = [0, 0]
    sent, kept = [], []

    def send(src, dst, target):
        k = count[0]
        count[0] += 1
        copy = pltpu.make_async_remote_copy(
            src_ref=src, dst_ref=dst, send_sem=ss.at[k], recv_sem=rs.at[k], device_id=target, device_id_type=pl.DeviceIdType.MESH
        )
        copy.start()
        sent.append(copy)
        return copy

    def settle(copy):
        copy.wait_send()
        sent[:] = [other for other in sent if other is not copy]

    def local(src, dst):
        k = count[1]
        count[1] += 1
        copy = pltpu.make_async_copy(src, dst, ls.at[k])
        copy.start()
        return copy

    def wait_all(copies):
        for copy in copies:
            copy.wait()

    def received(*copies):
        for copy in copies:
            copy.wait_recv()

    def add_rows(target, sources, block):
        def one(t, _):
            part = pl.ds(pl.multiple_of(t * block, block), block)
            total = target[part].astype(F32)
            for source in sources:
                total = total + source[part].astype(F32)
            target[part] = total.astype(BF)
            return 0

        lax.fori_loop(0, target.shape[0] // block, one, 0)

    def place_at(j):
        return lax.rem(depth + 2 * zsize - 1 - j, zsize)

    k3, v3 = send(dk[3], got.at[0], to_y), send(dv[3], got.at[1], to_x)
    mid_swap = send(mid_t, held.at[1], to_core)
    q_swap = send(dq, dq_pair.at[1], to_core)

    part = pack_0.shape[0] // 2
    parts = [pl.ds(h * part, part) for h in range(2)]

    def load_ffn(j):
        return [local(pack_in[n].at[place_at(j)], pack_s.at[j % 2, n]) for n in range(3)]

    ffn_loads = {0: load_ffn(0)}
    load_o = [local(mid_t, held.at[0]), local(att_half, half.at[0])]
    load_q = [local(dq, dq_pair.at[0]), local(first_half, half.at[1])]
    load_far = [local(far_in[n], far_s.at[n]) for n in range(3)]

    moves = {}

    def ffn_step(j):
        if j + 1 <= last:
            ffn_loads[j + 1] = load_ffn(j + 1)
        wait_all(ffn_loads[j])
        for h in range(2):
            mine = [pack_s.at[j % 2, n, parts[h]] for n in range(3)]
            if j == 0:
                sum_rows(pack_0.at[parts[h]], mine, 64)
                moves["pack", h, 0] = send(pack_0.at[parts[h]], pack_z.at[0, parts[h]], to_next)
                continue
            received(moves["pack", h, j - 1])
            here = pack_z.at[j - 1, parts[h]]
            add_rows(here, mine, 64)
            if j < last:
                moves["pack", h, j] = send(here, pack_z.at[j, parts[h]], to_next)

    def sum_rows(target, sources, block):
        def one(t, _):
            part = pl.ds(pl.multiple_of(t * block, block), block)
            total = sources[0][part].astype(F32)
            for source in sources[1:]:
                total = total + source[part].astype(F32)
            target[part] = total.astype(BF)
            return 0

        lax.fori_loop(0, target.shape[0] // block, one, 0)

    mid = width // 2
    tiles = 512

    def stage_1(m):
        moves["l", m] = send(grads.at[m, :, chip_d, :, pl.ds(0, mid)], gl.at[m], to_y)
        moves["r", m] = send(grads.at[m, :, chip_d, :, pl.ds(mid, mid)], gr.at[m], to_x)

    def stage_2(m):
        received(moves["l", m])

        def left(zz, _):
            grads[m, zz, chip_x, :, 0:mid] = (grads[m, zz, chip_x, :, 0:mid].astype(F32) + gl[m, zz].astype(F32)).astype(BF)
            return 0

        lax.fori_loop(0, zsize, left, 0)
        moves["x", m] = send(grads.at[m, :, chip_x], gx.at[m], to_x)
        received(moves["r", m])

        def right(zz, _):
            grads[m, zz, chip_y, :, mid:] = (grads[m, zz, chip_y, :, mid:].astype(F32) + gr[m, zz].astype(F32)).astype(BF)
            return 0

        lax.fori_loop(0, zsize, right, 0)
        moves["y", m] = send(grads.at[m, :, chip_y], gy.at[m], to_y)

    def stage_3(m):
        received(moves["x", m], moves["y", m])

        def own(zz, _):
            grads[m, zz, chip] = (grads[m, zz, chip].astype(F32) + gx[m, zz].astype(F32) + gy[m, zz].astype(F32)).astype(BF)
            return 0

        lax.fori_loop(0, zsize, own, 0)
        moves["z", m, 0] = send(grads.at[m, place_at(0), chip], gz.at[m, 0], to_next)

    def ring_step(m, j):
        received(moves["z", m, j - 1])
        total = gz[m, j - 1].astype(F32) + grads[m, place_at(j), chip].astype(F32)
        if j < last:
            gz[m, j - 1] = total.astype(BF)
            moves["z", m, j] = send(gz.at[m, j - 1], gz.at[m, j], to_next)
        else:
            piece[m] = total.astype(BF)

    def spread(name, source, target):
        kept.append(local(source, target(chip, core)))
        moves[name, "x"] = send(source, target(chip, core), to_x)
        moves[name, "y"] = send(source, target(chip, core), to_y)

    def forward(name, target):
        received(moves[name, "x"])
        left = target(chip_x, core, pl.ds(0, mid))
        moves[name, "fy"] = send(left, left, to_y)
        received(moves[name, "y"])
        right = target(chip_y, core, pl.ds(mid, mid))
        moves[name, "fx"] = send(right, right, to_x)

    def cross(name, target):
        received(moves[name, "fx"], moves[name, "fy"])
        column = target(slice(None), core)
        moves[name, "core"] = send(column, column, to_core)

    def whole(ref):
        def at(p, c, cols=None):
            return ref.at[p, c] if cols is None else ref.at[p, c, :, cols]

        return at

    def half_rows(ref, h):
        def at(p, c, cols=None):
            return ref.at[p, c, parts[h]] if cols is None else ref.at[p, c, parts[h], cols]

        return at

    def product(m, pair, which):
        per = width // tiles

        def one(t, _):
            zz = t // per
            cols = pl.ds(pl.multiple_of(lax.rem(t, per) * tiles, tiles), tiles)
            nt = (((1,), (1,)), ((), ()))
            left = half[which, zz].reshape(4 * strip, 2 * length)
            r = lax.dot_general(left[:, 0:length], pair[0, cols], nt, preferred_element_type=F32)
            r = r + lax.dot_general(left[:, length:], pair[1, cols], nt, preferred_element_type=F32)
            grads[m, zz, :, :, cols] = r.astype(BF).reshape(4, strip, tiles)
            return 0

        lax.fori_loop(0, zsize * per, one, 0)

    ffn_step(0)
    wait_all(load_far)
    add_rows(far_s.at[0], [far_s.at[1]], 64)
    far_ring = send(far_s.at[0], far_s.at[3], to_next)
    received(mid_swap)
    wait_all(load_o)
    product(0, held, 0)
    stage_1(0)
    keys_0, keys_1 = held.at[0, pl.ds(0, kv_rows)], held.at[0, pl.ds(kv_rows, kv_rows)]
    values_0, values_2 = held.at[1, pl.ds(0, kv_rows)], held.at[1, pl.ds(kv_rows, kv_rows)]
    load_kv = [local(dk[0], keys_0), local(dk[1], keys_1), local(dv[0], values_0), local(dv[2], values_2)]
    received(q_swap)
    wait_all(load_q)
    product(1, dq_pair, 1)
    stage_1(1)

    received(k3)
    wait_all(load_kv)
    add_rows(keys_1, [got.at[0]], 96)
    k1 = send(keys_1, got.at[2], to_x)
    received(v3)
    add_rows(values_2, [got.at[1]], 96)
    v2 = send(values_2, got.at[3], to_y)
    k2, v1 = send(dk[2], got.at[4], to_y), send(dv[1], got.at[5], to_x)
    if last > 1:
        ffn_step(1)
    received(far_ring)
    add_rows(far_s.at[2], [far_s.at[3]], 64)
    far = send(far_s.at[2], far_r, to_far)
    received(k1, k2, v1, v2)

    def finish_keys(h, _):
        rows = pl.ds(pl.multiple_of(h * 96, 96), 96)
        v = keys_0[rows].astype(F32) + got[2, rows].astype(F32) + got[4, rows].astype(F32)
        kv_pair[0, rows] = rotate_back(v, cos[...], sin[...]).astype(BF)
        return 0

    def finish_values(h, _):
        rows = pl.ds(pl.multiple_of(h * 96, 96), 96)
        v = values_0[rows].astype(F32) + got[3, rows].astype(F32) + got[5, rows].astype(F32)
        kv_pair[0, pl.ds(pl.multiple_of(kv_rows + h * 96, 96), 96)] = v.astype(BF)
        return 0

    lax.fori_loop(0, kv_rows // 96, finish_keys, 0)
    lax.fori_loop(0, kv_rows // 96, finish_values, 0)
    kv_swap = send(kv_pair.at[0], kv_pair.at[1], to_core)
    stage_2(0)
    stage_2(1)
    if last > 2:
        ffn_step(2)
    received(kv_swap)
    product(2, kv_pair, 1)
    stage_1(2)
    for j in range(3, last):
        ffn_step(j)
    ffn_step(last)
    stage_3(0)
    stage_3(1)
    stage_2(2)
    received(far)
    for h in range(2):
        sum_rows(pack_p.at[parts[h]], [pack_z.at[last - 1, parts[h]], far_r.at[parts[h]]], 64)
        spread(("pack", h), pack_p.at[parts[h]], half_rows(pack_all, h))
    for j in range(1, zsize):
        ring_step(0, j)
        ring_step(1, j)
        if j == 1:
            stage_3(2)
    spread(0, piece.at[0], whole(o_all))
    spread(1, piece.at[1], whole(q_all))
    for j in range(1, zsize):
        ring_step(2, j)
    spread(2, piece.at[2], whole(kv_all))
    settle(far)
    settle(far_ring)
    weight_at = [(pack_s.at[k // 3, k % 3], far_s.at[k]) for k in range(zsize)]
    loads = [(local(query_w.at[k], a), local(kv_w.at[k], b)) for k, (a, b) in enumerate(weight_at)]
    rows = width // zsize
    for k, (a, b) in enumerate(weight_at):
        wait_all(loads[k])
        r = jnp.dot(a[...], dq_pair[0], preferred_element_type=F32) + jnp.dot(b[...], kv_pair[0], preferred_element_type=F32)
        first_grad[:, k * rows:(k + 1) * rows] = r.T
    gain_s[...] = jnp.zeros(gain_s.shape, F32)
    gain_s[1:2] = second_part[...]

    def finish_tokens(t, _):
        at = pl.ds(pl.multiple_of(t * 64, 64), 64)
        v = x_in[at].astype(F32)
        inverse = lax.rsqrt(jnp.mean(v * v, -1, keepdims=True) + EPS)
        unit = v * inverse
        d = first_grad[at]
        gain_s[0:1] += jnp.sum(d * unit, axis=0, keepdims=True)
        scaled = d * gain[...]
        tokens_s[at] = (middle[at] + inverse * (scaled - unit * jnp.mean(scaled * unit, -1, keepdims=True))).astype(BF)
        return 0

    lax.fori_loop(0, length // 64, finish_tokens, 0)
    near_half = pl.ds(0, length // 2)
    kept.append(local(tokens_s.at[near_half], tokens_out.at[core]))
    tokens_swap = send(tokens_s.at[pl.ds(length // 2, length // 2)], tokens_out.at[core], to_core)
    gain_swap = send(gain_s, gain_r.at[0], to_core)

    targets = [(("pack", h), half_rows(pack_all, h)) for h in range(2)]
    targets += [(m, whole(ref)) for m, ref in enumerate((o_all, q_all, kv_all))]
    for name, target in targets[:2]:
        forward(name, target)
    received(gain_swap)
    settle(gain_swap)
    gain_s[...] += gain_r[0]
    for n, target in ((1, to_x), (2, to_y)):
        copy = send(gain_s, gain_r.at[n], target)
        for name, at in targets[2 * n:2 * n + 2]:
            forward(name, at)
        received(copy)
        settle(copy)
        gain_s[...] += gain_r[n]
    copy = send(gain_s, gain_r.at[3], to_next)
    wait_all(kept)
    for name, target in targets:
        cross(name, target)
    total = gain_s[...]
    for s in range(1, zsize):
        received(copy)
        total = total + gain_r[2 + s]
        if s < last:
            copy = send(gain_r.at[2 + s], gain_r.at[3 + s], to_next)
    gains_out[...] = total
    received(tokens_swap)
    for name, target in targets:
        received(moves[name, "core"])
    for copy in sent:
        copy.wait_send()


def tail(dk, dv, dq, cosine, sine, first_half, att_half, packs, far_packs, mid_t, query_w, kv_w, x, middle, gain, second_part, zsize, chips):
    kv_rows, length = dk[0].shape
    width = 2 * kv_rows
    strip = att_half.shape[2]
    rows, packed = packs[0].shape[1:]
    hbm, vmem = pl.BlockSpec(memory_space=pltpu.HBM), pl.BlockSpec(memory_space=pltpu.VMEM)
    shape = lambda *s: jax.ShapeDtypeStruct(s, BF)
    store = lambda *s: pltpu.VMEM(s, BF)
    copies = 16 + 3 * (zsize - 1) + 3 * (4 + zsize - 1) + 5 * 5
    cut = lambda w: w.reshape(zsize, rows, width)
    inputs = [*dk, *dv, dq, cosine, sine, first_half, att_half, *packs, *far_packs, mid_t, cut(query_w), cut(kv_w), x, middle, gain, second_part]
    last = zsize - 1
    return pl.pallas_call(
        functools.partial(tail_kernel, zsize),
        out_shape=[shape(chips, 2, strip, width)] * 3 + [
            shape(chips, 2, rows, packed), shape(2, length // 2, width), jax.ShapeDtypeStruct((8, width), F32)],
        in_specs=[hbm] * 9 + [vmem] * 2 + [hbm] * (len(inputs) - 15) + [vmem] * 4,
        out_specs=[hbm] * 5 + [vmem],
        scratch_shapes=[
            store(6, kv_rows, length), store(2, width, length), store(2, width, length), store(2, width, length),
            store(2, zsize, chips, strip, 2 * length), store(3, zsize, chips, strip, width),
            store(3, zsize, strip, width // 2), store(3, zsize, strip, width // 2),
            store(3, zsize, strip, width), store(3, zsize, strip, width),
            store(3, last, strip, width), store(3, strip, width),
            store(2, 3, rows, packed), store(rows, packed), store(last, rows, packed),
            store(max(4, zsize), rows, packed), store(rows, packed), store(rows, packed),
            pltpu.VMEM((length, width), F32), store(length, width), pltpu.VMEM((8, width), F32), pltpu.VMEM((zsize + 2, 8, width), F32),
            pltpu.SemaphoreType.DMA((copies,)), pltpu.SemaphoreType.DMA((copies,)),
            pltpu.SemaphoreType.DMA((6 * zsize + 14,)),
        ],
        compiler_params=pltpu.CompilerParams(collective_id=1, has_side_effects=True, vmem_limit_bytes=ALL_VMEM),
        name="tail",
    )(*inputs)


def unfold(refs, wide, tall, start):
    zsize, fine = tall.shape[0], tall.shape[1]
    folds = wide.shape[1] // fine
    fold = tall.shape[2] // folds
    two = wide.shape[2]
    if len(refs) == 1:
        sources = [(refs[0], slice(None), (slice(None),))]
    else:
        depth = lax.axis_index("fsdp")
        pieces = [refs[0]] + ([refs[1].at[s] for s in range(zsize - 1)] if len(refs) == 2 else list(refs[1:]))
        sources = [(piece, lax.rem(depth + zsize - s, zsize), ()) for s, piece in enumerate(pieces)]
    for source, at, lead in sources:
        start(source.at[(*lead, slice(None), pl.ds(0, two))], wide.at[at])
        for n in range(folds):
            cols = pl.ds(n * fold, fold)
            start(source.at[(*lead, pl.ds(n * fine, fine), pl.ds(two, fold))], tall.at[at, :, cols])


def ffn_kernel(given, pieces, before, second, second_t, cot, *refs):
    weights, (hidden_o, low_o), grads = refs[:given], refs[given:given + 2], refs[given + 2:given + pieces + 2]
    s_v, st_v, c_v, wi_v, wo_v, h_v, ht_v, l_v, w_v, t_v, sem = refs[given + pieces + 2:]
    tokens, width = second.shape
    zsize, fine = wo_v.shape[:2]
    rows = wi_v.shape[1]
    chunk = zsize * fine
    loads = []

    def load(src, dst):
        copy = pltpu.make_async_copy(src, dst, sem.at[len(loads)])
        copy.start()
        loads.append(copy)

    tile = 256
    steps = tokens // tile
    unfold(weights, wi_v, wo_v, load)
    first = len(loads)
    for t in range(steps):
        part = pl.ds(t * tile, tile)
        load(second.at[part], s_v.at[part])
        load(cot.at[part], c_v.at[part])
    load(second_t, st_v)
    for copy in loads[:first]:
        copy.wait()
    nt = (((1,), (1,)), ((), ()))

    def one(t, _):
        part = pl.ds(t * tile, tile)
        pre = jnp.dot(s_v[part], wi_v[...].reshape(width, 2 * chunk), preferred_element_type=F32)
        hidden_grad = lax.dot_general(c_v[part], wo_v[...].reshape(chunk, width), nt, preferred_element_type=F32)
        gate, up = pre[:, :chunk], pre[:, chunk:]
        sigmoid = jax.nn.sigmoid(gate)
        silu = gate * sigmoid
        hidden = silu * up
        h_v[part] = hidden.astype(BF)
        ht_v[:, part] = hidden.T.astype(BF)
        l_v[part, 0:chunk] = (hidden_grad * up * sigmoid * (1.0 + gate * (1.0 - sigmoid))).astype(BF)
        l_v[part, chunk:] = (hidden_grad * silu).astype(BF)
        return 0

    for t in range(steps):
        loads[first + 2 * t].wait()
        loads[first + 2 * t + 1].wait()
        one(t, 0)
    stores = []

    def store(src, dst):
        copy = pltpu.make_async_copy(src, dst, sem.at[len(loads) + len(stores)])
        copy.start()
        stores.append(copy)

    store(h_v, hidden_o)
    store(l_v, low_o)
    loads[-1].wait()
    depth = 0 if pieces == 1 else lax.axis_index("fsdp")
    grad_at = lambda n: grads[0].at[n] if pieces == 1 else grads[n]

    def place(n):
        return n if pieces == 1 else lax.rem(depth + n, zsize)

    for n in range(zsize):
        z = place(n)
        part = pl.ds(pl.multiple_of(z * rows, rows), rows)
        w_v[z] = jnp.dot(st_v[part], l_v[...], preferred_element_type=F32).astype(BF)
        store(w_v.at[z], grad_at(n).at[:, pl.ds(0, 2 * chunk)])
    folds = rows // fine
    fold = width // folds
    for n in range(folds):
        cols = slice(fold * n, fold * (n + 1))
        t_v[:, :, cols] = jnp.dot(ht_v[...], c_v[:, cols], preferred_element_type=F32).astype(BF).reshape(zsize, fine, fold)
        if pieces == 1:
            store(t_v.at[:, :, cols], grads[0].at[:, pl.ds(n * fine, fine), pl.ds(2 * chunk, fold)])
        else:
            for k in range(zsize):
                store(t_v.at[place(k), :, cols], grads[k].at[pl.ds(n * fine, fine), pl.ds(2 * chunk, fold)])
    for copy in stores:
        copy.wait()


def ffn_chunk(before, second, second_t, cot, weights, split, cost, zsize, fine):
    pieces = zsize if split else 1
    tokens, width = second.shape
    chunk = zsize * fine
    rows = width // zsize
    folds = rows // fine
    shape = lambda *s: jax.ShapeDtypeStruct(s, BF)
    store = lambda *s: pltpu.VMEM(s, BF)
    hbm = pl.BlockSpec(memory_space=pltpu.HBM)
    packed = weights[0].shape[-1]
    piece = (rows, packed) if split else (zsize, rows, packed)
    out = pl.pallas_call(
        functools.partial(ffn_kernel, len(weights), pieces),
        out_shape=[shape(tokens, chunk), shape(tokens, 2 * chunk)] + [shape(*piece)] * pieces,
        in_specs=[hbm] * (4 + len(weights)),
        out_specs=[hbm] * (2 + pieces),
        scratch_shapes=[
            store(tokens, width), store(width, tokens), store(tokens, width), store(zsize, rows, 2 * chunk), store(zsize, fine, width),
            store(tokens, chunk), store(chunk, tokens), store(tokens, 2 * chunk), store(zsize, rows, 2 * chunk), store(zsize, fine, width),
            pltpu.SemaphoreType.DMA((5 + zsize + 2 * zsize * (folds + 1) + 2 * (tokens // 256),)),
        ],
        cost_estimate=cost,
        compiler_params=pltpu.CompilerParams(vmem_limit_bytes=ALL_VMEM),
        name="ffn_chunk",
    )(before, second, second_t, cot, *weights)
    return out[0], out[1], out[2:]

def combine_kernel(counts, *refs):
    count = len(counts)
    hidden, low = refs[:count], refs[count:2 * count]
    weights, at = [], 2 * count
    for n in counts:
        weights.append(refs[at:at + n])
        at += n
    out, grad, h_v, l_v, wi_v, wo_v, o_v, g_v, sem = refs[at:]
    tokens, chunk = hidden[0].shape
    width = out.shape[1]
    loads = []

    def load(src, dst):
        copy = pltpu.make_async_copy(src, dst, sem.at[len(loads)])
        copy.start()
        loads.append(copy)

    for r in range(count):
        load(hidden[r], h_v.at[:, pl.ds(r * chunk, chunk)])
        unfold(weights[r], wi_v.at[:, :, pl.ds(2 * r * chunk, 2 * chunk)], wo_v.at[r], load)
    for r in range(count):
        load(low[r], l_v.at[:, pl.ds(2 * r * chunk, 2 * chunk)])
    nt = (((1,), (1,)), ((), ()))
    tile = 256
    steps = tokens // tile
    stores = []

    def store(src, dst):
        copy = pltpu.make_async_copy(src, dst, sem.at[len(loads) + len(stores)])
        copy.start()
        stores.append(copy)

    for copy in loads[:-count]:
        copy.wait()
    for t in range(steps):
        rows = slice(tile * t, tile * (t + 1))
        if t >= 2:
            stores[t - 2].wait()
        o_v[t % 2] = jnp.dot(h_v[rows], wo_v[...].reshape(count * chunk, width), preferred_element_type=F32)
        store(o_v.at[t % 2], out.at[rows])
    for copy in loads[-count:]:
        copy.wait()
    for t in range(steps):
        rows = slice(tile * t, tile * (t + 1))
        if t >= 2:
            stores[steps + t - 2].wait()
        g_v[t % 2] = lax.dot_general(l_v[rows], wi_v[...].reshape(width, 2 * count * chunk), nt, preferred_element_type=F32)
        store(g_v.at[t % 2], grad.at[rows])
    for t in range(max(steps - 2, 0), steps):
        stores[t].wait()
        stores[steps + t].wait()


def combine(hidden, low, weights, zsize, fine):
    counts = tuple(len(w) for w in weights)
    count = len(counts)
    tokens, chunk = hidden[0].shape
    rows = weights[0][0].shape[-2]
    width = rows * zsize
    hbm = pl.BlockSpec(memory_space=pltpu.HBM)
    shape = jax.ShapeDtypeStruct((tokens, width), F32)
    inputs = [*hidden, *low] + [piece for w in weights for piece in w]
    return pl.pallas_call(
        functools.partial(combine_kernel, counts),
        out_shape=[shape, shape],
        in_specs=[hbm] * len(inputs),
        out_specs=[hbm] * 2,
        scratch_shapes=[
            pltpu.VMEM((tokens, count * chunk), BF), pltpu.VMEM((tokens, 2 * count * chunk), BF),
            pltpu.VMEM((zsize, rows, 2 * count * chunk), BF), pltpu.VMEM((count, zsize, fine, width), BF),
            pltpu.VMEM((2, 256, width), F32), pltpu.VMEM((2, 256, width), F32),
            pltpu.SemaphoreType.DMA((2 * count + sum(counts) * (1 + rows // fine) + 2 * (tokens // 256),)),
        ],
        cost_estimate=NO_COST,
        compiler_params=pltpu.CompilerParams(vmem_limit_bytes=ALL_VMEM),
        name="ffn_combine",
    )(*inputs)


def assemble_kernel(zsize, wide, tall, o, q, kv, gate_o, up_o, down_o, o_o, q_o, k_o, v_o):
    fold = tall.shape[3]
    folds = down_o.shape[1] // fold
    fine = tall.shape[2] // folds
    kv_rows = k_o.shape[1]
    for p in range(4):
        for c in range(2):
            for part in range(zsize):
                at = slice((part * 8 + c * 4 + p) * fine, (part * 8 + c * 4 + p + 1) * fine)
                gate_o[:, at] = wide[p, c, :, part * fine:(part + 1) * fine].astype(F32)
                up_o[:, at] = wide[p, c, :, (zsize + part) * fine:(zsize + part + 1) * fine].astype(F32)
    for p in range(tall.shape[0]):
        for n in range(folds):
            down_o[p * fine:(p + 1) * fine, n * fold:(n + 1) * fold] = tall[p, 0, n * fine:(n + 1) * fine].astype(F32)
    o_o[...] = o[...].astype(F32)
    q_o[...] = q[...].astype(F32)
    k_o[...] = kv[:, 0:kv_rows].astype(F32)
    v_o[...] = kv[:, kv_rows:].astype(F32)


def assemble(packs, o, q, kv, zsize, fine):
    chips, cores, rows, packed = packs.shape
    width = o.shape[1]
    steps = chips * cores
    block = rows // steps
    two = 2 * fine * zsize
    fold = packed - two
    flat = lambda n: pl.BlockSpec((block, n), lambda i: (i, 0))
    out = lambda r, c: jax.ShapeDtypeStruct((r, c), F32)
    ff = fine * chips * cores
    hbm = pl.BlockSpec(memory_space=pltpu.HBM)

    def kernel(pack, o_in, q_in, kv_in, *outs):
        pltpu.emit_pipeline(
            functools.partial(assemble_kernel, zsize),
            grid=(steps,),
            in_specs=[
                pl.BlockSpec((chips, cores, block, two), lambda i: (0, 0, i, 0)),
                pl.BlockSpec((1, 1, rows, fold), lambda i: (i % chips, i // chips, 0, two // fold)),
                flat(width), flat(width), flat(width),
            ],
            out_specs=[flat(ff * zsize), flat(ff * zsize), pl.BlockSpec((ff // steps, width), lambda i: (i, 0)), flat(width), flat(width), flat(width // 2), flat(width // 2)],
        )(pack, pack, o_in, q_in, kv_in, *outs)

    return pl.pallas_call(
        kernel,
        out_shape=[out(rows, ff * zsize), out(rows, ff * zsize), out(ff, width), out(rows, width), out(rows, width), out(rows, width // 2), out(rows, width // 2)],
        in_specs=[hbm] * 4,
        out_specs=[hbm] * 7,
        compiler_params=pltpu.CompilerParams(vmem_limit_bytes=ALL_VMEM),
        name="assemble",
    )(packs, o, q, kv)


MESH = pl.DeviceIdType.MESH


class Mover:
    def __init__(self, send_sems, recv_sems, local_sems):
        self.sems = send_sems, recv_sems, local_sems
        self.sent, self.kept, self.counts = [], [], [0, 0]

    def send(self, src, dst, target):
        k = self.counts[0]
        self.counts[0] += 1
        copy = pltpu.make_async_remote_copy(
            src_ref=src, dst_ref=dst, send_sem=self.sems[0].at[k], recv_sem=self.sems[1].at[k], device_id=target, device_id_type=MESH
        )
        copy.start()
        self.sent.append(copy)
        return copy

    def local(self, src, dst):
        k = self.counts[1]
        self.counts[1] += 1
        copy = pltpu.make_async_copy(src, dst, self.sems[2].at[k])
        copy.start()
        return copy

    def settle(self, copy):
        copy.wait_send()
        self.sent = [other for other in self.sent if other is not copy]

    def finish(self):
        for copy in self.sent:
            copy.wait_send()
        for copy in self.kept:
            copy.wait()


def greet_other_core():
    index, depth = lax.axis_index("ctx"), lax.axis_index("fsdp")
    core = lax.rem(index, 2)
    other = (index + 1 - 2 * core, depth)
    barrier = pltpu.get_barrier_semaphore()
    pl.semaphore_signal(barrier, inc=1, device_id=other, device_id_type=MESH)
    pl.semaphore_wait(barrier, 1)
    return core, other


def bridge_kernel(att, weight, x, gain, middle_o, second, second_t, att_half, att_s, w_s, low_s, low_t, middle, ss, rs, ls):
    core, other = greet_other_core()
    move = Mover(ss, rs, ls)
    zsize, chips, _, strip, length = att.shape
    width = x.shape[1]
    loads = [move.local(att, att_s), move.local(weight, w_s)]
    arrive = [move.send(att.at[:, :, 1 - core], att_half.at[:, :, :, pl.ds(length, length)], other)]
    for copy in loads:
        copy.wait()
    move.kept.append(move.local(att_s.at[:, :, core], att_half.at[:, :, :, pl.ds(0, length)]))
    tile = 128
    for t in range(length // tile):
        rows = slice(tile * t, tile * (t + 1))
        left = att_s[:, :, :, :, rows].reshape(width, tile).astype(F32).T.astype(BF)
        y = x[rows].astype(F32) + jnp.dot(left, w_s[...], preferred_element_type=F32)
        middle[rows] = y
        inverse = lax.rsqrt(jnp.mean(y * y, -1, keepdims=True) + EPS)
        normed = y * inverse * gain[...]
        low_s[rows] = normed.astype(BF)
        low_t[:, rows] = normed.T.astype(BF)
        here, there = pl.ds(tile * t, tile), pl.ds(length + tile * t, tile)
        arrive.append(move.send(low_s.at[here], second.at[there], other))
        arrive.append(move.send(low_t.at[:, here], second_t.at[:, there], other))
    move.kept.append(move.local(middle, middle_o))
    move.kept.append(move.local(low_s, second.at[pl.ds(0, length)]))
    move.kept.append(move.local(low_t, second_t.at[:, pl.ds(0, length)]))
    for copy in arrive:
        copy.wait_recv()
    move.finish()


def bridge(attended, weight, x, gain, zsize, chips):
    width, length = attended.shape
    strip = width // (zsize * chips * 2)
    hbm, vmem = pl.BlockSpec(memory_space=pltpu.HBM), pl.BlockSpec(memory_space=pltpu.VMEM)
    steps = length // 128
    return pl.pallas_call(
        bridge_kernel,
        out_shape=[
            jax.ShapeDtypeStruct((length, width), F32), jax.ShapeDtypeStruct((2 * length, width), BF),
            jax.ShapeDtypeStruct((width, 2 * length), BF), jax.ShapeDtypeStruct((zsize, chips, strip, 2 * length), BF),
        ],
        in_specs=[hbm, hbm, vmem, vmem],
        out_specs=[hbm, hbm, hbm, hbm],
        scratch_shapes=[
            pltpu.VMEM((zsize, chips, 2, strip, length), BF), pltpu.VMEM((width, width), BF),
            pltpu.VMEM((length, width), BF), pltpu.VMEM((width, length), BF), pltpu.VMEM((length, width), F32),
            pltpu.SemaphoreType.DMA((1 + 2 * steps,)), pltpu.SemaphoreType.DMA((1 + 2 * steps,)), pltpu.SemaphoreType.DMA((6,)),
        ],
        compiler_params=pltpu.CompilerParams(collective_id=2, has_side_effects=True, vmem_limit_bytes=ALL_VMEM),
        cost_estimate=NO_COST,
        name="bridge",
    )(attended.reshape(zsize, chips, 2, strip, length), weight, x, gain)


def middle_kernel(counts, *refs):
    count = len(counts)
    hidden, low = refs[:count], refs[count:2 * count]
    weights, at = [], 2 * count
    for n in counts:
        weights.append(refs[at:at + n])
        at += n
    y_in, cot_in, gain, out_w = refs[at:at + 4]
    layer_out, middle_grad, low_t, att_grad, gain_part = refs[at + 4:at + 9]
    h_v, l_v, wi_v, wo_v, send_s, got, own, out_s, y_s, cot_s, ss, rs, ls = refs[at + 9:]
    core, other = greet_other_core()
    move = Mover(ss, rs, ls)
    tokens, chunk = hidden[0].shape
    length, width = y_in.shape
    late, loads = [], []
    for r in range(count):
        chunk_loads = []
        load = lambda src, dst: chunk_loads.append(move.local(src, dst))
        load(low[r], l_v.at[r])
        unfold(weights[r], wi_v.at[:, :, pl.ds(2 * r * chunk, 2 * chunk)], wo_v.at[r], load)
        loads.append(chunk_loads)
    inputs = [move.local(y_in, y_s), move.local(cot_in.at[pl.ds(0, 2)], cot_s)]
    for r in range(count):
        late.append(move.local(hidden[r], h_v.at[:, pl.ds(r * chunk, chunk)]))
    nt = (((1,), (1,)), ((), ()))
    tile = tokens // 4

    def out_tile(t):
        return jnp.dot(h_v[tile * t:tile * (t + 1)], wo_v[...].reshape(count * chunk, width), preferred_element_type=F32)

    targets = (own.at[pl.ds(0, tile)], own.at[pl.ds(tile, tile)], send_s.at[0], send_s.at[1])
    there = []
    for r in range(count):
        for copy in loads[r]:
            copy.wait()
        for t in (2, 3, 0, 1):
            part = lax.dot_general(
                l_v[r, tile * t:tile * (t + 1)], wi_v[:, :, 2 * r * chunk:2 * (r + 1) * chunk].reshape(width, 2 * chunk), nt,
                preferred_element_type=F32,
            )
            targets[t][...] = part if r == 0 else targets[t][...] + part
            if r == count - 1 and t >= 2:
                there.append(move.send(send_s.at[t - 2], got.at[t - 2], other))
    for copy in inputs:
        copy.wait()
    load_out = move.local(out_w, wi_v.at[:, :, pl.ds(0, width)])
    for copy in late:
        copy.wait()
    for n in range(2):
        move.settle(there[n])
        send_s[n] = out_tile(2) if n == 0 else out_tile(1) + y_s[tile:2 * tile]
        there.append(move.send(send_s.at[n], got.at[2 + n], other))
    there[0].wait_recv()
    there[1].wait_recv()
    gain_part[...] = jnp.zeros(gain_part.shape, F32)
    step = 128

    for t in range(length // step):
        part = slice(step * t, step * (t + 1))
        y = y_s[part]
        inverse = lax.rsqrt(jnp.mean(y * y, -1, keepdims=True) + EPS)
        unit = y * inverse
        d = own[part] + got[step * t // tile, step * t % tile:step * t % tile + step]
        gain_part[...] += jnp.sum(d * unit, axis=0, keepdims=True)
        scaled = d * gain[...]
        g = cot_s[step * t // tile, step * t % tile:step * t % tile + step].astype(F32)
        g = g + inverse * (scaled - unit * jnp.mean(scaled * unit, -1, keepdims=True))
        middle_grad[part] = g
        low_t[:, part] = g.T.astype(BF)
    load_out.wait()
    rows = wi_v.shape[1]
    for z in range(wi_v.shape[0]):
        att_grad[z * rows:(z + 1) * rows] = jnp.dot(wi_v[z, :, 0:width], low_t[...], preferred_element_type=F32).astype(BF)
    first, last = out_tile(0) + y_s[0:tile], out_tile(3)
    there[2].wait_recv()
    out_s[0] = (first + got[2]).astype(BF)
    there[3].wait_recv()
    out_s[1] = (last + got[3]).astype(BF)
    move.kept.append(move.local(out_s.at[0], layer_out.at[core]))
    move.kept.append(move.local(out_s.at[1], layer_out.at[1 - core]))
    move.finish()


def middle_part(hidden, low, weights, y, cot, gain, out_w, zsize, fine):
    counts = tuple(len(w) for w in weights)
    count = len(counts)
    tokens, chunk = hidden[0].shape
    length, width = y.shape
    rows = width // zsize
    hbm, vmem = pl.BlockSpec(memory_space=pltpu.HBM), pl.BlockSpec(memory_space=pltpu.VMEM)
    inputs = [*hidden, *low] + [piece for w in weights for piece in w]
    tile = tokens // 4
    return pl.pallas_call(
        functools.partial(middle_kernel, counts),
        out_shape=[
            jax.ShapeDtypeStruct((2, length // 2, width), BF), jax.ShapeDtypeStruct((length, width), F32),
            jax.ShapeDtypeStruct((width, length), BF), jax.ShapeDtypeStruct((width, length), BF),
            jax.ShapeDtypeStruct((1, width), F32),
        ],
        in_specs=[hbm] * len(inputs) + [hbm, hbm, vmem, hbm],
        out_specs=[hbm] + [vmem] * 4,
        scratch_shapes=[
            pltpu.VMEM((tokens, count * chunk), BF), pltpu.VMEM((count, tokens, 2 * chunk), BF),
            pltpu.VMEM((zsize, rows, 2 * count * chunk), BF), pltpu.VMEM((count, zsize, fine, width), BF),
            pltpu.VMEM((2, tile, width), F32), pltpu.VMEM((4, tile, width), F32),
            pltpu.VMEM((length, width), F32), pltpu.VMEM((2, tile, width), BF),
            pltpu.VMEM((length, width), F32), pltpu.VMEM((2, tile, width), BF),
            pltpu.SemaphoreType.DMA((4,)), pltpu.SemaphoreType.DMA((4,)),
            pltpu.SemaphoreType.DMA((2 * count + count * zsize * (1 + rows // fine) + 5,)),
        ],
        compiler_params=pltpu.CompilerParams(collective_id=3, has_side_effects=True, vmem_limit_bytes=ALL_VMEM),
        cost_estimate=NO_COST,
        name="middle",
    )(*inputs, y, cot, gain, out_w.reshape(zsize, rows, width))


def mm(left, right, left_dim, right_dim):
    return lax.dot_general(left, right, (((left_dim,), (right_dim,)), ((), ())), preferred_element_type=F32)


def swap(a):
    return lax.ppermute(a, "ctx", [(i, i ^ 1) for i in range(lax.axis_size("ctx"))])


def hop(a, r):
    return lax.ppermute(a, "ctx", [(i, i ^ (2 * r)) for i in range(lax.axis_size("ctx"))])


def ring(a):
    n = lax.axis_size("fsdp")
    return lax.ppermute(a, "fsdp", [(i, (i + 1) % n) for i in range(n)])


def pick(a, index, axis=0):
    return lax.dynamic_index_in_dim(a, index, axis, keepdims=False)


def place(buffer, piece, index, axis=0):
    return lax.dynamic_update_slice_in_dim(buffer, jnp.expand_dims(piece, axis), index, axis)


def shift(a, s):
    n = lax.axis_size("fsdp")
    return lax.ppermute(a, "fsdp", [(i, (i + s) % n) for i in range(n)])


def depth_gather(piece, depth):
    n = lax.axis_size("fsdp")
    buffer = place(jnp.zeros((n,) + piece.shape, piece.dtype), piece, depth)
    for s in range(1, n):
        piece = ring(piece)
        buffer = place(buffer, piece, lax.rem(depth + n - s, n))
    return buffer


def depth_scatter(parts, depth):
    n = lax.axis_size("fsdp")
    total = pick(parts, lax.rem(depth + n - 1, n))
    for s in range(n - 1):
        total = ring(total.astype(BF))
        total = total.astype(F32) + pick(parts, lax.rem(depth + 2 * n - 2 - s, n)).astype(F32)
    return total


def plane_gather(piece, index):
    n = lax.axis_size("ctx")
    chips = n // 2
    pieces = jnp.stack([piece] + [hop(piece, r) for r in range(1, chips)])
    others = swap(pieces)
    buffer = jnp.zeros((n,) + piece.shape, piece.dtype)
    for r in range(chips):
        buffer = place(buffer, pieces[r], index ^ (2 * r))
        buffer = place(buffer, others[r], index ^ (2 * r + 1))
    return buffer


def rotate(v, cosine, sine):
    heads = v.reshape(-1, 2, HEAD_WIDTH // 2, v.shape[-1])
    a, b = heads[:, 0], heads[:, 1]
    return jnp.stack([a * cosine - b * sine, b * cosine + a * sine], 1).reshape(v.shape)


def rotate_back(v, cosine, sine):
    heads = v.reshape(-1, 2, HEAD_WIDTH // 2, v.shape[-1])
    a, b = heads[:, 0], heads[:, 1]
    return jnp.stack([a * cosine + b * sine, b * cosine - a * sine], 1).reshape(v.shape)


def norm_back(incoming, unit, inverse, gain):
    scaled = incoming * gain
    return inverse * (scaled - unit * jnp.mean(scaled * unit, -1, keepdims=True))


def body(
    tokens,
    block_pairs,
    cotangent,
    attention_gain,
    query_weight,
    key_matrix,
    value_matrix,
    output_weight,
    feedforward_gain,
    gate_weight,
    up_weight,
    down_weight,
):
    slice_len, width = tokens.shape[1], tokens.shape[2]
    ctx = lax.axis_size("ctx")
    zsize = lax.axis_size("fsdp")
    chips = ctx // 2
    diag = chips - 1
    near = range(1, chips - 1)
    index = lax.axis_index("ctx")
    chip, core = index // 2, lax.rem(index, 2)
    depth = lax.axis_index("fsdp")
    rows = width // zsize
    strip = rows // ctx
    hidden_rows = down_weight.shape[0]
    fine = hidden_rows // ctx
    chunk = fine * zsize
    kv_rows = KEY_HEADS * HEAD_WIDTH

    length = 2 * slice_len

    ids_all = jnp.concatenate([pick(block_pairs, index ^ r) for r in range(ctx)])
    ids = ids_all[:4]
    blocks = ids_all.shape[0]
    order = jnp.sum(
        jnp.where(ids_all[None, :] == jnp.arange(blocks, dtype=jnp.int32)[:, None], jnp.arange(blocks, dtype=jnp.int32)[None, :], 0), 1
    )
    positions = (ids[:, None] * BLK + jnp.arange(BLK, dtype=jnp.int32)[None, :]).reshape(length)
    half = HEAD_WIDTH // 2
    frequency = THETA ** (-jnp.arange(half, dtype=F32) * 2.0 / HEAD_WIDTH)
    angles = frequency[:, None] * positions.astype(F32)[None, :]
    cosine, sine = jnp.cos(angles), jnp.sin(angles)

    packs, keys, values = {}, {}, {}
    folds = rows // fine
    fast = chips == 4 and strip % 16 == 0 and fine % 128 == 0 and pack_width(rows, fine, zsize, width) == width
    if fast:
        (key_value_full, query_full, output_full, pack, rest, pack_x, pack_y, far_pack, cot, first_half, x_low, first, query, gains_full, *kv) = front(
            tokens, cotangent, jnp.stack([attention_gain, feedforward_gain]).astype(F32), key_matrix, value_matrix, query_weight,
            output_weight, gate_weight, up_weight, down_weight, cosine, sine, zsize, ctx,
        )
        key_value_full, query_full, output_full = (w.reshape(width, width) for w in (key_value_full, query_full, output_full))
        packs[0], packs[1], packs[2] = [pack, rest], [pack_x, hop(rest, 1)], [pack_y, hop(rest, 2)]
        for r in range(chips):
            keys[r], values[r] = kv[r], kv[chips + r]
        gain_first, gain_second = gains_full[0], gains_full[1]
        packs[diag] = [far_pack] + [shift(far_pack, s) for s in range(1, zsize)]
    else:
        gate_cut = gate_weight.reshape(rows, zsize, 2, chips, fine)
        up_cut = up_weight.reshape(rows, zsize, 2, chips, fine)
        down_cut = down_weight.reshape(2, chips, fine, width)

        def own_piece(r):
            gate = pick(pick(gate_cut, core, 2), chip ^ r, 2).reshape(rows, chunk)
            up = pick(pick(up_cut, core, 2), chip ^ r, 2).reshape(rows, chunk)
            down = pick(pick(down_cut, core), chip ^ r)
            folded = jnp.transpose(down.reshape(fine, folds, width // folds), (1, 0, 2)).reshape(rows, width // folds)
            return jnp.concatenate([gate, up, folded], 1)

        gains = jnp.stack([attention_gain, feedforward_gain])
        gain_buffer = place(jnp.zeros((zsize, 2, rows), BF), gains, depth)
        for s in range(1, zsize):
            moved = lax.ppermute(gains, "fsdp", [(k, (k + s) % zsize) for k in range(zsize)])
            gain_buffer = place(gain_buffer, moved, lax.rem(depth + zsize - s, zsize))
        gains_full = jnp.transpose(gain_buffer, (1, 0, 2)).reshape(2, width).astype(F32)
        gain_first, gain_second = gains_full[0], gains_full[1]

        def gather_square(shard):
            strips = shard.reshape(ctx, strip, shard.shape[1])
            pair = jnp.stack([pick(strips, index), pick(strips, index ^ (2 * diag))])
            pair = depth_gather(pair, depth)
            own, far = pair[:, 0], pair[:, 1]
            found = {0: own, diag: far}
            for r in near:
                found[r] = hop(own, r)
            full = jnp.zeros((zsize, ctx, strip, shard.shape[1]), BF)
            for r in range(chips):
                full = place(full, found[r], index ^ (2 * r), 1)
                full = place(full, swap(found[r]), index ^ (2 * r + 1), 1)
            return full.reshape(width, shard.shape[1])

        key_value_full = gather_square(jnp.concatenate([key_matrix, value_matrix], 1))
        query_full = gather_square(query_weight)
        output_full = gather_square(output_weight)

        x = jnp.concatenate([pick(tokens, core), swap(pick(tokens, 1 - core))]).astype(F32)
        packs[0] = [depth_gather(own_piece(0), depth)]
        inverse_first = lax.rsqrt(jnp.mean(x * x, -1, keepdims=True) + EPS)
        unit_first = x * inverse_first
        first = (unit_first * gain_first).astype(BF)
        first_t = jnp.transpose(first)
        kv = mm(key_value_full, first_t, 0, 0)
        keys[0] = rotate(kv[:kv_rows], cosine, sine).astype(BF)
        values[0] = kv[kv_rows:].astype(BF)
        for r in range(1, chips):
            high = 1 << (r.bit_length() - 1)
            low = r & -r
            keys[r] = hop(keys[r ^ high], high)
            values[r] = hop(values[r ^ low], low)
        query = rotate(mm(query_full, first_t, 0, 0), cosine, sine).astype(BF)
        packs[diag] = [depth_gather(own_piece(diag), depth)]

        for r in near:
            packs[r] = [hop(packs[0][0], r)]
        cot_there = swap(cotangent)
        cot = jnp.concatenate(
            [pick(cotangent, core), pick(cot_there, core), pick(cot_there, 1 - core), pick(cotangent, 1 - core)]
        )

    key_list = [keys[r] for r in range(chips)]
    value_list = [values[r] for r in range(chips)]
    attended, log_total = attn_fwd(ids, order, query, key_list, value_list, KEY_HEADS)

    if fast:
        middle, second, second_t, att_half = bridge(attended, output_full, x_low, gain_second[None], zsize, chips)
    else:
        middle = x + mm(attended, output_full, 0, 0)
        inverse_second = lax.rsqrt(jnp.mean(middle * middle, -1, keepdims=True) + EPS)
        unit_second = middle * inverse_second
        second = (unit_second * gain_second).astype(BF)
        second = jnp.concatenate([second, swap(second)])
        second_t = jnp.transpose(second)
    grads, hidden, low = {}, {}, {}
    before = second
    for r in [0] + list(near) + [diag]:
        before, low[r], grads[r] = ffn_chunk(
            before, second, second_t, cot.reshape(2 * length, width), packs[r], fast and r == diag, LONG if r == diag else NO_COST, zsize, fine
        )
        hidden[r] = before
    every = range(chips)
    hidden, low, packs = ([a[r] for r in every] for a in (hidden, low, packs))

    if fast:
        layer_out, middle_grad, middle_t, attended_grad, gain_second_part = middle_part(
            hidden, low, packs, middle, cot, gain_second[None], output_full, zsize, fine
        )
    else:
        out_part, second_grad = combine(hidden, low, packs, zsize, fine)

        q = slice_len
        out_part = jnp.concatenate([out_part[:length] + middle, out_part[length:]])
        came = swap(jnp.concatenate([out_part[2 * q:3 * q], out_part[q:2 * q]]))
        out_here = (out_part[:q] + came[:q]).astype(BF)
        out_there = (out_part[3 * q:] + came[q:]).astype(BF)

        def stored(here, there):
            return jnp.where(core == 0, jnp.stack([here, there]), jnp.stack([there, here]))

        layer_out = stored(out_here, out_there)

        second_grad = second_grad[:length] + swap(second_grad[length:])
        gain_second_part = jnp.sum(second_grad * unit_second, 0)
        middle_grad = cot[:length].astype(F32) + norm_back(second_grad, unit_second, inverse_second, gain_second)

        def halves(a):
            cut = a.reshape(zsize, chips, 2, strip, length)
            here = pick(cut, core, 2).reshape(-1, length)
            there = swap(pick(cut, 1 - core, 2).reshape(-1, length))
            return jnp.concatenate([here, there], 1)

        first_half = halves(first_t)
        middle_low = middle_grad.astype(BF)
        out_part_grad = mm(halves(attended), jnp.concatenate([middle_low, swap(middle_low)]), 1, 0)
        attended_grad = mm(output_full, middle_low, 1, 1).astype(BF)

    far_sum = middle_grad
    if fast:
        far_sum = grads[diag][zsize - 1]
        for s in range(zsize - 2, 0, -1):
            far_moved = shift(far_sum, 1)
            if s > 1:
                share, middle_t = lax.optimization_barrier((grads[diag][s], middle_t))
                far_sum = (far_moved.astype(F32) + share.astype(F32)).astype(BF)

    query_low, key_parts, value_parts = attn_bwd(
        far_sum, ids, order, query, attended, attended_grad, log_total, cosine, sine, key_list, value_list, KEY_HEADS
    )
    if fast:
        o_all, q_all, kv_all, pack_all, tokens_grad, gain_sums = tail(
            key_parts, value_parts, query_low, cosine, sine, first_half,
            att_half,
            [grads[0][0], hop(grads[1][0], 1), hop(grads[2][0], 2)],
            [far_moved, grads[diag][1], grads[diag][0]],
            middle_t, query_full, key_value_full, x_low, middle_grad, gain_first[None], gain_second_part, zsize, chips,
        )
        gain_first_grad, gain_second_grad = (
            lax.dynamic_slice_in_dim(gain_sums[n], depth * rows, rows) for n in range(2)
        )
        gate_grad, up_grad, down_grad, output_grad, query_grad, key_grad, value_grad = assemble(
            pack_all, *(a.reshape(rows, width) for a in (o_all, q_all, kv_all)), zsize, fine
        )
    else:
        key_sum = [part for part in key_parts]
        value_sum = [part for part in value_parts]
        for r in range(chips - 1, 0, -1):
            high = 1 << (r.bit_length() - 1)
            low = r & -r
            key_sum[r ^ high] = key_sum[r ^ high].astype(F32) + hop(key_sum[r].astype(BF), high).astype(F32)
            value_sum[r ^ low] = value_sum[r ^ low].astype(F32) + hop(value_sum[r].astype(BF), low).astype(F32)
        key_low = rotate_back(key_sum[0], cosine, sine).astype(BF)
        value_low = value_sum[0].astype(BF)
        kv_low = jnp.concatenate([key_low, value_low])

        def scatter(parts):
            total = parts[0].astype(F32)
            for r in near:
                total = total + hop(parts[r], r).astype(F32)
            far = hop(depth_scatter(parts[diag], depth).astype(BF), diag)
            total = depth_scatter(total.astype(BF), depth) + far.astype(F32)
            return total.astype(BF)

        pack_all = plane_gather(scatter({r: grads[r][0] for r in range(chips)}), index)
        wide_all = pack_all[:, :, :2 * chunk]
        tall_all = jnp.transpose(pack_all[:, :, 2 * chunk:].reshape(ctx, folds, fine, width // folds), (0, 2, 1, 3))
        def square_grad(product):
            parts = product.astype(BF).reshape(zsize, chips, strip, width)
            piece = scatter({r: pick(parts, chip ^ r, 1) for r in range(chips)})
            return plane_gather(piece, index).reshape(rows, width).astype(F32)

        output_grad = square_grad(out_part_grad)
        query_grad = square_grad(mm(first_half, jnp.concatenate([query_low, swap(query_low)], 1), 1, 1))
        kv_grad = square_grad(mm(first_half, jnp.concatenate([kv_low, swap(kv_low)], 1), 1, 1))
        down_grad = jnp.transpose(tall_all.reshape(chips, 2, fine, width), (1, 0, 2, 3)).reshape(hidden_rows, width).astype(F32)
        wide_all = wide_all.reshape(chips, 2, rows, 2, zsize, fine)
        gate_grad = jnp.transpose(wide_all[:, :, :, 0], (2, 3, 1, 0, 4)).reshape(rows, -1).astype(F32)
        up_grad = jnp.transpose(wide_all[:, :, :, 1], (2, 3, 1, 0, 4)).reshape(rows, -1).astype(F32)
        key_grad, value_grad = kv_grad[:, :kv_rows], kv_grad[:, kv_rows:]

        def gain_total(part):
            cut = part.reshape(zsize, rows)
            total = pick(cut, depth)
            for s in range(1, zsize):
                total = total + lax.ppermute(
                    pick(cut, lax.rem(depth + s, zsize)), "fsdp", [(k, (k + s) % zsize) for k in range(zsize)]
                )
            total = total + swap(total)
            bit = 1
            while bit < chips:
                total = total + hop(total, bit)
                bit *= 2
            return total

        first_grad = mm(query_low, query_full, 0, 1) + mm(kv_low, key_value_full, 0, 1)
        gain_first_part = jnp.sum(first_grad * unit_first, 0)
        tokens_part = (middle_grad + norm_back(first_grad, unit_first, inverse_first, gain_first)).astype(BF)
        tokens_grad = stored(tokens_part[:q], swap(tokens_part[q:]))
        gain_first_grad, gain_second_grad = gain_total(gain_first_part), gain_total(gain_second_part)

    return (
        layer_out,
        tokens_grad,
        gain_first_grad,
        query_grad,
        key_grad,
        value_grad,
        output_grad,
        gain_second_grad,
        gate_grad,
        up_grad,
        down_grad,
    )


def solution(mesh):
    line, square, grid = P("fsdp"), P("fsdp", None), P("fsdp", "ctx", None)
    in_specs = (grid, P(), grid, line, square, square, square, square, line, square, square, square)
    out_specs = (grid, grid, line, square, square, square, square, line, square, square, square)
    return jax.shard_map(body, mesh=mesh, in_specs=in_specs, out_specs=out_specs, check_vma=False)
```
